32 devices in a mesh: groups: 2 (over x), view: 16 (over z, y, core).
Axes of the slice: x: 2, y: 2, z: 4, core: 2. Of those that a mesh axis runs over, the one named last changes fastest.
Arguments:
- ref_features: bfloat16 [256, 32, 384], P(('groups', 'view')), parts along dimension 0, may hold values from -6 to 6
- source_tiles: bfloat16 [1024, 2, 32, 384], P(('groups', 'view')), parts along dimension 0, may hold values from -6 to 6
- pair_lists: int32 [32, 4, 4], P(('groups', 'view')), parts along dimension 0, may hold values from -1 to 511, as said below
- view_counts: int32 [32], P(('groups', 'view')), parts along dimension 0, may hold values from 3 to 4, as said below
- disparities: int32 [16, 4], P('groups'), parts along dimension 0, may hold values from -48 to 48
- conv_first: bfloat16 [3, 3, 8, 3, 32], replicated, may hold values from -0.21875 to 0.21875
- bias_first: float32 [8], replicated, may hold values from -3 to 3
- conv_second: bfloat16 [16, 3, 3, 3, 8], replicated, may hold values from -0.4375 to 0.4375
- bias_second: float32 [16], replicated, may hold values from -3 to 3
Outputs:
- cost_features: float32 [8, 64, 16, 192], P('groups', 'view'), parts along dimension 0
The draws below stay inside these ranges and needn't reach their ends.
There are 2 independent parts, one for each index of `groups`. The reference program is written for one: setup_inputs(seed, part) draws one part's arguments, and reference() takes and returns one part's arrays. A program takes and returns all parts, laid end to end along the dimension named above; an argument that names none is the same for every part. Nothing has to cross between parts.
Inputs may be any that keep to these rules, and one draw needn't show every extreme that they name: pair_lists[v, s, b] is the tile holding rows 2b and 2b + 1 of source s of strip v; it is -1 exactly when s >= view_counts[v]; tile t lies on device t // 32 of the view axis; no strip takes more than 2 tiles from one device, and some strip takes exactly 2 from some device. `view_counts`: some strip uses 3 sources and some uses 4.
All inputs are finite; a program needn't handle non-finite values.
Results may differ from the reference program's by a relative error of at most 0.0028.
Values may be sent and summed in bfloat16 or wider, within the bound.
No kernel may reach another device: no remote copies, remote signals or barrier semaphores. Data moves between devices by JAX's collectives and lax.ppermute only.
A program may use at most 128 MiB of HBM per device.

```python
import jax
import jax.numpy as jnp
from jax import lax

C = 32
C1 = 8
C2 = 16
COLS = 384
ROWS = 8
PLANES = 8
SOURCES = 4
SHIFT = 48
TILES_DEV = 32
STRIPS = 16
TILES = 512
HEIGHT = 128
BLOCKS = 4
CAP = 2


def survey_pairs(key):
    base_key = jax.random.fold_in(key, 7331)
    key_count, key_pick, key_pop, key_rows = jax.random.split(base_key, 4)
    view_counts = jax.random.randint(key_count, (STRIPS,), 3, 5)
    full_strip = jax.random.randint(key_pick, (), 0, STRIPS)
    strip_ids = jnp.arange(STRIPS)
    view_counts = jnp.where(strip_ids == full_strip, 4, view_counts)
    view_counts = jnp.where(strip_ids == (full_strip + 1) % STRIPS, 3, view_counts)
    popular = jax.random.randint(key_pop, (STRIPS,), 0, 4) * (STRIPS // 2 + 1)
    requests = SOURCES * BLOCKS
    least_full = max(-((STRIPS - requests) // (CAP - 1)), 1)
    most_full = requests // CAP

    def one_strip(strip_key):
        key_jitter, key_shuffle, key_tile, key_twins = jax.random.split(strip_key, 4)
        jitter = jax.random.randint(key_jitter, (STRIPS,), 0, 2 * STRIPS)
        ranking = popular + jitter
        ranked = jnp.argsort(-ranking, stable=True)
        full_count = jax.random.randint(key_twins, (), least_full, most_full + 1)
        shuffled = jax.random.permutation(key_shuffle, requests)
        owner_slot = jnp.where(shuffled < CAP * full_count, shuffled // CAP, shuffled - CAP * full_count + full_count)
        owners = ranked[owner_slot]
        local_ids = jax.random.randint(key_tile, (requests,), 0, TILES_DEV)
        return owners * TILES_DEV + local_ids
    tile_ids = jax.vmap(one_strip)(jax.random.split(key_rows, STRIPS)).reshape(STRIPS, SOURCES, BLOCKS)
    source_ids = jnp.arange(SOURCES)
    in_use = source_ids[None, :, None] < view_counts[:, None, None]
    pair_ids = jnp.where(in_use, tile_ids, -1)
    return (pair_ids.astype(jnp.int32), view_counts.astype(jnp.int32))


def draw_pair_lists(key, part):
    return survey_pairs(key)[0]


def draw_view_counts(key, part):
    return survey_pairs(key)[1]


def touch_ends(result, own_key, low, top_value):
    extent = result.shape
    spot = [jax.random.randint(jax.random.fold_in(own_key, axis), (), 0, extent[axis]) for axis in range(len(extent))]
    result = result.at[tuple(spot)].set(low)
    longest = extent.index(max(extent))
    spot[longest] = (spot[longest] + 1) % extent[longest]
    return result.at[tuple(spot)].set(top_value)


def block_scale(own_key, extent, cuts, low, largest):
    loudness, own = 1.0, jax.random.fold_in(own_key, 6)
    for axis_at, blocks in cuts:
        draws = jnp.exp(jax.random.uniform(jax.random.fold_in(own, axis_at), (blocks,), jnp.float32, low / len(cuts), largest / len(cuts)))
        loudness = loudness * jnp.repeat(draws, extent[axis_at] // blocks).reshape([-1 if axis == axis_at else 1 for axis in range(len(extent))])
    return loudness


def bell_draw(stream_key, shape, width, bound, pieces=(), held_as=jnp.bfloat16):
    values = width * jax.random.normal(stream_key, shape, jnp.float32)
    if pieces:
        values = values * block_scale(stream_key, shape, pieces, -0.22, 0.18)
    return jnp.clip(values, -bound, bound).astype(held_as)


def setup_inputs(seed: int = 0, part: int = 0) -> dict:
    splits = jax.random.split(jax.random.key(seed), 10)
    part_splits = jax.random.split(jax.random.fold_in(splits[9], part), 10)
    return {
        "ref_features": bell_draw(part_splits[0], (HEIGHT, C, COLS), 1.0, 6.0, ((0, 16),)),
        "source_tiles": bell_draw(part_splits[1], (TILES, 2, C, COLS), 1.0, 6.0, ((0, 16),)),
        "pair_lists": draw_pair_lists(jax.random.fold_in(jax.random.fold_in(splits[9], part), 71), part),
        "view_counts": draw_view_counts(jax.random.fold_in(jax.random.fold_in(splits[9], part), 71), part),
        "disparities": touch_ends(jax.random.randint(part_splits[4], (PLANES, SOURCES), 0 - SHIFT, SHIFT + 1), jax.random.fold_in(part_splits[4], 1), 0 - SHIFT, SHIFT).astype(jnp.int32),
        "conv_first": bell_draw(splits[5], (3, 3, C1, 3, C), (27 * C) ** -0.5, 0.21875),
        "bias_first": bell_draw(splits[6], (C1,), 0.5, 3.0, (), jnp.float32),
        "conv_second": bell_draw(splits[7], (C2, 3, 3, 3, C1), (27 * C1) ** -0.5, 0.4375),
        "bias_second": bell_draw(splits[8], (C2,), 0.5, 3.0, (), jnp.float32),
    }


def shifted(rows, offset):
    padded = jnp.pad(rows, ((0, 0), (0, 0), (SHIFT, SHIFT)))
    return lax.dynamic_slice_in_dim(padded, (SHIFT - offset).astype(jnp.int32), COLS, 2)


def strip_variance(ref_rows, pair_row, live_count, source_tiles, disparities):
    ref_wide = ref_rows.astype(jnp.float32)
    summed = jnp.broadcast_to(ref_wide, (PLANES,) + ref_wide.shape)
    squares = summed * summed
    for source in range(SOURCES):
        picked = source_tiles[jnp.maximum(pair_row[source], 0)].reshape(ROWS, C, COLS)
        warped = jax.vmap(lambda offset: shifted(picked, offset))(disparities[:, source]).astype(jnp.float32)
        weight = (source < live_count).astype(jnp.float32)
        summed = summed + weight * warped
        squares = squares + weight * warped * warped
    view_total = live_count.astype(jnp.float32) + 1.0
    view_mean = summed / view_total
    return (squares / view_total - view_mean * view_mean).astype(jnp.bfloat16)


def reference(ref_features, source_tiles, pair_lists, view_counts, disparities, conv_first, bias_first, conv_second, bias_second):
    strips = ref_features.reshape(STRIPS, ROWS, C, COLS)
    volume = lax.map(lambda packed: strip_variance(packed[0], packed[1], packed[2], source_tiles, disparities), (strips, pair_lists, view_counts))
    volume_wide = jnp.transpose(volume, (3, 1, 0, 2, 4)).reshape(1, C, PLANES, HEIGHT, COLS).astype(jnp.float32)
    kernel_one = jnp.transpose(conv_first, (2, 4, 0, 1, 3)).astype(jnp.float32)
    first_out = lax.conv_general_dilated(volume_wide, kernel_one, (1, 1, 1), ((1, 1), (1, 1), (1, 1)), dimension_numbers=("NCDHW", "OIDHW", "NCDHW"), precision=lax.Precision.HIGHEST)
    cost_first = jnp.maximum(first_out + bias_first[None, :, None, None, None], 0.0).astype(jnp.bfloat16)
    kernel_two = jnp.transpose(conv_second, (0, 4, 1, 2, 3)).astype(jnp.float32)
    second = lax.conv_general_dilated(cost_first.astype(jnp.float32), kernel_two, (2, 2, 2), ((1, 1), (1, 1), (1, 1)), dimension_numbers=("NCDHW", "OIDHW", "NCDHW"), precision=lax.Precision.HIGHEST)
    second = second + bias_second[None, :, None, None, None]
    return jnp.transpose(second[0], (1, 2, 0, 3))
```

```python
import functools

import numpy as np

import jax
import jax.numpy as jnp
from jax import lax
from jax.experimental import pallas as pl
from jax.experimental.pallas import tpu as pltpu
from jax.sharding import PartitionSpec as P

SHIFT = 48
CAP = 2
LANES = 128
PAD = 8
CHUNK = 64
VMEM_LIMIT = 40 * 1024 * 1024


def passed_along(x, axis, by):
    count = lax.axis_size(axis)
    pairs = [(i, i + by) for i in range(count) if 0 <= i + by < count]
    return lax.ppermute(x, axis, pairs)


def spread(stage_value, scale, wide, at, cols):
    band = jnp.zeros((SHIFT, LANES), jnp.float32)
    wide[at, 0:SHIFT, :] = band
    wide[at, SHIFT + cols : 2 * SHIFT + cols, :] = band
    wide[at, SHIFT : SHIFT + cols, :] = stage_value.astype(jnp.float32).T * scale


def plane_variance(p, at, sources, cols, disp, wide, ref_wide, ref_at, inv, store):
    for x0 in range(0, cols, CHUNK):
        ref = ref_wide[ref_at, x0 : x0 + CHUNK, :]
        summed = ref
        squares = ref * ref
        for s in range(sources):
            warped = wide[at + s, pl.ds(SHIFT + x0 - disp[p, s], CHUNK), :]
            summed = summed + warped
            squares = squares + warped * warped
        mean = summed * inv
        store(x0, (squares * inv - mean * mean).astype(jnp.bfloat16))


def own_kernel(slots, disp, live, arrived, ref, var, stage, wide, ref_wide, sem):
    planes, cols, lanes = var.shape
    groups = lanes // LANES
    sources = stage.shape[0]
    tile_rows = arrived.shape[1]
    per_group = LANES // tile_rows
    blocks = groups * per_group
    copies = {}
    for g in range(groups):
        for s in range(sources):
            for b in range(per_group):
                copies[g, s, b] = pltpu.make_async_copy(
                    arrived.at[slots[s * blocks + g * per_group + b]],
                    stage.at[s, g, pl.ds(b * tile_rows, tile_rows)],
                    sem.at[g, s, b],
                )
                copies[g, s, b].start()
    for g in range(groups):
        ref_wide[g] = ref[g].astype(jnp.float32).T
    for g in range(groups):
        for s in range(sources):
            for b in range(per_group):
                copies[g, s, b].wait()
            scale = (s < live[0]).astype(jnp.float32)
            spread(stage[s, g], scale, wide, g * sources + s, cols)
    inv = 1.0 / (live[0].astype(jnp.float32) + 1.0)
    for g in range(groups):

        def step(p, carry):
            def store(x0, value):
                var[p, x0 : x0 + CHUNK, g * LANES : (g + 1) * LANES] = value

            plane_variance(p, g * sources, sources, cols, disp, wide, ref_wide, g, inv, store)
            return carry

        lax.fori_loop(0, planes, step, 0)


def rim_kernel(
    width,
    disp,
    lane_info,
    rim,
    var,
    kernel_one,
    bias_one,
    kernel_two,
    bias_two,
    out,
    wide,
    ref_wide,
    rim_var,
    left,
    right,
    cost,
):
    planes, cols, lanes = var.shape
    sources = rim.shape[0] - 1
    ref_wide[0] = rim[sources].astype(jnp.float32).T
    for s in range(sources):
        spread(rim[s], lane_info[s + 1 : s + 2, :], wide, s, cols)
    inv = lane_info[0:1, :]

    def step(p, carry):
        def store(x0, value):
            rim_var[p, x0 : x0 + CHUNK, :] = value

        plane_variance(p, 0, sources, cols, disp, wide, ref_wide, 0, inv, store)
        return carry

    lax.fori_loop(0, planes, step, 0)

    deep = lanes + LANES
    info_rows = lane_info.shape[0]
    keep = lane_info[info_rows - 1 : info_rows, :]
    held = LANES - width
    lane_at = lax.broadcasted_iota(jnp.int32, (cols, LANES), 1)
    zeros = jnp.zeros((PAD, LANES), jnp.float32)
    left[0:PAD, :] = zeros
    right[PAD + cols : 2 * PAD + cols, :] = zeros
    for p in range(planes):
        cost[p, 0:PAD, :] = zeros
    out_w = out.shape[2]
    for p in range(planes):
        first, last = max(p - 1, 0), min(p + 2, planes)
        lhs = jnp.concatenate(
            [part for q in range(first, last) for part in (var[q], rim_var[q])], axis=1
        )
        a0 = first - (p - 1)
        rhs = kernel_one[a0 * deep : (a0 + last - first) * deep, :]
        taps = jnp.dot(lhs, rhs, preferred_element_type=jnp.float32)
        t_left, t_right = taps[:, 0:LANES], taps[:, LANES : 2 * LANES]
        left[PAD : PAD + cols, :] = t_left
        right[PAD : PAD + cols, :] = t_right
        center = jnp.where(
            lane_at < held,
            pltpu.roll(t_left, LANES - width, 1),
            pltpu.roll(t_right, LANES - (width - held), 1),
        )
        total = left[PAD - 1 : PAD - 1 + cols, :] + center + right[PAD + 1 : PAD + 1 + cols, :]
        cost[p, PAD : PAD + cols, :] = jnp.maximum(total + bias_one[...], 0.0) * keep

    for q in range(planes // 2):
        parts = []
        a0 = 0
        for a in range(3):
            plane = 2 * q + a - 1
            if plane < 0:
                a0 = 1
                continue
            for d in range(3):
                parts.append(cost[plane, pl.ds(PAD + d - 1, out_w, stride=2), :].astype(jnp.bfloat16))
        lhs = jnp.concatenate(parts, axis=1)
        rhs = kernel_two[:, a0 * 3 * LANES :]
        result = lax.dot_general(rhs, lhs, (((1,), (1,)), ((), ())), preferred_element_type=jnp.float32)
        out[q] = result + bias_two[...]


def on_device(
    ref_features,
    source_tiles,
    pair_lists,
    view_counts,
    disparities,
    conv_first,
    bias_first,
    conv_second,
    bias_second,
):
    n_view = lax.axis_size("view")
    me = lax.axis_index("view")
    rows_n, channels, cols = ref_features.shape
    tiles_dev, tile_rows = source_tiles.shape[0], source_tiles.shape[1]
    sources, blocks = pair_lists.shape[1], pair_lists.shape[2]
    planes = disparities.shape[0]
    requests = sources * blocks
    slab = tile_rows * channels
    groups = rows_n * channels // LANES

    def ranked(ids):
        owner = jnp.where(ids >= 0, ids // tiles_dev, -1)
        order = np.arange(requests)
        earlier = order[None, :] < order[:, None]
        same = (owner[..., :, None] == owner[..., None, :]) & earlier
        return owner, jnp.sum(same.astype(jnp.int32), axis=-1)

    own_ids = pair_lists.reshape(requests)
    every = lax.all_gather(own_ids, "view")
    owner, rank = ranked(every)
    asked = (owner == me)[:, None, :] & (rank[:, None, :] == np.arange(CAP)[None, :, None])
    wanted = jnp.sum(jnp.where(asked, (every % tiles_dev)[:, None, :], 0), axis=2)
    outgoing = source_tiles.reshape(tiles_dev, slab, cols)[wanted]
    arrived = lax.all_to_all(outgoing, "view", split_axis=0, concat_axis=0, tiled=True)
    arrived = arrived.reshape(n_view * CAP, slab, cols)
    own_owner, own_rank = ranked(own_ids)
    slots = jnp.where(own_owner >= 0, own_owner * CAP + own_rank, 0)

    ref_slabs = ref_features.reshape(blocks, slab, cols)
    block_slots = slots.reshape(sources, blocks)
    last_block = jnp.concatenate([arrived[block_slots[:, blocks - 1]], ref_slabs[blocks - 1 :]], axis=0)
    first_block = jnp.concatenate([arrived[block_slots[:, 0]], ref_slabs[:1]], axis=0)
    above = passed_along(last_block, "view", 1)
    below = passed_along(first_block, "view", -1)

    var = pl.pallas_call(
        own_kernel,
        out_shape=jax.ShapeDtypeStruct((planes, cols, groups * LANES), jnp.bfloat16),
        in_specs=[
            pl.BlockSpec(memory_space=pltpu.SMEM),
            pl.BlockSpec(memory_space=pltpu.SMEM),
            pl.BlockSpec(memory_space=pltpu.SMEM),
            pl.BlockSpec(memory_space=pl.ANY),
            pl.BlockSpec(memory_space=pltpu.VMEM),
        ],
        out_specs=pl.BlockSpec(memory_space=pltpu.VMEM),
        scratch_shapes=[
            pltpu.VMEM((sources, groups, LANES, cols), jnp.bfloat16),
            pltpu.VMEM((groups * sources, cols + 2 * SHIFT, LANES), jnp.float32),
            pltpu.VMEM((groups, cols, LANES), jnp.float32),
            pltpu.SemaphoreType.DMA((groups, sources, LANES // slab)),
        ],
        compiler_params=pltpu.CompilerParams(vmem_limit_bytes=VMEM_LIMIT),
        name="own_rows",
    )(slots, disparities, view_counts, arrived, ref_features.reshape(groups, LANES, cols))

    rim = jnp.concatenate([above, below], axis=1)
    counts = jnp.sum((every.reshape(n_view, sources, blocks)[:, :, 0] >= 0).astype(jnp.int32), axis=1)
    strip_ids = np.arange(n_view)
    count_above = jnp.sum(jnp.where(strip_ids == me - 1, counts, 0))
    count_below = jnp.sum(jnp.where(strip_ids == me + 1, counts, 0))
    lane_count = jnp.where(np.arange(LANES) < slab, count_above, count_below)
    out_rows = rows_n + 1
    c1 = conv_first.shape[2]
    c2 = conv_second.shape[0]
    width = out_rows * c1
    keep = jnp.where((np.arange(LANES) < width) & ((np.arange(LANES) >= c1) | (me > 0)), 1.0, 0.0)
    lane_info = jnp.concatenate(
        [
            (1.0 / (lane_count.astype(jnp.float32) + 1.0))[None],
            (np.arange(sources)[:, None] < lane_count[None, :]).astype(jnp.float32),
            jnp.zeros((2, LANES), jnp.float32),
            keep[None].astype(jnp.float32),
        ],
        axis=0,
    )

    in_rows = list(range(rows_n)) + [-2, -1, rows_n, rows_n + 1]
    hits = np.zeros((len(in_rows), out_rows, 3), np.float32)
    for i, row in enumerate(in_rows):
        for r in range(out_rows):
            tap = row - (r - 1) + 1
            if 0 <= tap < 3:
                hits[i, r, tap] = 1.0
    held = LANES - width
    kernel_one = jnp.einsum("irb,abodc->aicdro", jnp.asarray(hits, jnp.bfloat16), conv_first)
    kernel_one = kernel_one.reshape(3 * len(in_rows) * channels, 3, width)
    kernel_one = jnp.concatenate(
        [
            kernel_one[:, 0],
            kernel_one[:, 1, :held],
            kernel_one[:, 2],
            kernel_one[:, 1, held:],
            jnp.zeros((kernel_one.shape[0], 2 * LANES - 3 * width), jnp.bfloat16),
        ],
        axis=1,
    )
    half_r = rows_n // 2
    hits_two = np.zeros((out_rows, half_r, 3), np.float32)
    for g in range(half_r):
        for b in range(3):
            hits_two[2 * g + b, g, b] = 1.0
    kernel_two = jnp.einsum("rgb,kabdo->gkadro", jnp.asarray(hits_two, jnp.bfloat16), conv_second)
    kernel_two = kernel_two.reshape(half_r * c2, 9, width)
    kernel_two = jnp.pad(kernel_two, ((0, 0), (0, 0), (0, LANES - width))).reshape(half_r * c2, 9 * LANES)
    bias_lanes = jnp.pad(jnp.tile(bias_first, out_rows), (0, LANES - width))[None]
    bias_two = jnp.tile(bias_second, half_r)[:, None]

    out = pl.pallas_call(
        functools.partial(rim_kernel, width),
        out_shape=jax.ShapeDtypeStruct((planes // 2, half_r * c2, cols // 2), jnp.float32),
        in_specs=[pl.BlockSpec(memory_space=pltpu.SMEM)] + [pl.BlockSpec(memory_space=pltpu.VMEM)] * 7,
        out_specs=pl.BlockSpec(memory_space=pltpu.VMEM),
        scratch_shapes=[
            pltpu.VMEM((sources, cols + 2 * SHIFT, LANES), jnp.float32),
            pltpu.VMEM((1, cols, LANES), jnp.float32),
            pltpu.VMEM((planes, cols, LANES), jnp.bfloat16),
            pltpu.VMEM((cols + 2 * PAD, LANES), jnp.float32),
            pltpu.VMEM((cols + 2 * PAD, LANES), jnp.float32),
            pltpu.VMEM((planes, cols + PAD, LANES), jnp.float32),
        ],
        compiler_params=pltpu.CompilerParams(vmem_limit_bytes=VMEM_LIMIT),
        name="rim_and_convolutions",
    )(disparities, lane_info, rim, var, kernel_one, bias_lanes, kernel_two, bias_two)
    return out.reshape(planes // 2, half_r, c2, cols // 2)


def solution(mesh):
    return jax.shard_map(
        on_device,
        mesh=mesh,
        in_specs=(
            P(("groups", "view"), None, None),
            P(("groups", "view"), None, None, None),
            P(("groups", "view"), None, None),
            P(("groups", "view")),
            P("groups", None),
            P(),
            P(),
            P(),
            P(),
        ),
        out_specs=P("groups", "view", None, None),
        check_vma=False,
    )
```

```python
import functools

import numpy as np

import jax
import jax.numpy as jnp
from jax import lax
from jax.experimental import pallas as pl
from jax.experimental.pallas import tpu as pltpu
from jax.sharding import PartitionSpec as P

SHIFT = 48
CAP = 2
LANES = 128
PAD = 8
CHUNK = 64
VMEM_LIMIT = 40 * 1024 * 1024


def passed_along(x, axis, by):
    count = lax.axis_size(axis)
    pairs = [(i, i + by) for i in range(count) if 0 <= i + by < count]
    return lax.ppermute(x, axis, pairs)


def spread(stage_value, scale, wide, at, cols):
    band = jnp.zeros((SHIFT, LANES), jnp.float32)
    wide[at, 0:SHIFT, :] = band
    wide[at, SHIFT + cols : 2 * SHIFT + cols, :] = band
    wide[at, SHIFT : SHIFT + cols, :] = stage_value.astype(jnp.float32).T * scale


def plane_variance(p, at, sources, cols, disp, wide, ref_wide, ref_at, inv, store):
    for x0 in range(0, cols, CHUNK):
        ref = ref_wide[ref_at, x0 : x0 + CHUNK, :]
        summed = ref
        squares = ref * ref
        for s in range(sources):
            warped = wide[at + s, pl.ds(SHIFT + x0 - disp[p * sources + s], CHUNK), :]
            summed = summed + warped
            squares = squares + warped * warped
        mean = summed * inv
        store(x0, (squares * inv - mean * mean).astype(jnp.bfloat16))


def layout_kernel(first, second, bias_first, bias_second, kernel_one, kernel_two, bias_one, bias_two, turned):
    deep = turned.shape[1]
    c1, channels = first.shape[3], first.shape[4]
    c2 = second.shape[4]
    half_r = bias_two.shape[0] // c2
    out_rows = 2 * half_r + 1
    width = out_rows * c1
    held = (LANES - width) // c1
    turned[...] = jnp.zeros(turned.shape, jnp.float32)
    for a in range(3):
        for d in range(3):
            band = jnp.concatenate(
                [first[a, b, d].astype(jnp.float32) for b in range(3)]
                + [jnp.zeros((c1, deep - 3 * channels), jnp.float32)],
                axis=1,
            )
            for r in range(out_rows):
                at = r * c1 + (LANES if d == 2 else 0)
                if d == 1:
                    at = width + (r * c1 if r < held else LANES + (r - held) * c1)
                turned[at : at + c1, :] = pltpu.roll(band, ((r - 2) * channels) % deep, 1)
        kernel_one[a * deep : (a + 1) * deep, :] = turned[...].T.astype(jnp.bfloat16)
    none = jnp.zeros((c1, c2), jnp.float32)
    for a in range(3):
        for d in range(3):
            taps = [second[a, b, d].astype(jnp.float32) for b in range(3)]
            stacked = jnp.concatenate(
                [
                    jnp.concatenate(
                        [taps[r - 2 * g] if 0 <= r - 2 * g < 3 else none for g in range(half_r)]
                        + [jnp.zeros((c1, LANES - half_r * c2), jnp.float32)],
                        axis=1,
                    )
                    for r in range(out_rows)
                ]
                + [jnp.zeros((LANES - width, LANES), jnp.float32)],
                axis=0,
            )
            at = (a * 3 + d) * LANES
            kernel_two[:, at : at + LANES] = stacked.T[: half_r * c2].astype(jnp.bfloat16)
    lane = lax.broadcasted_iota(jnp.int32, bias_one.shape, 1)
    total = jnp.zeros(bias_one.shape, jnp.float32)
    for o in range(c1):
        total = jnp.where(lane % c1 == o, bias_first[o], total)
    bias_one[...] = total
    row = lax.broadcasted_iota(jnp.int32, bias_two.shape, 0)
    total = jnp.zeros(bias_two.shape, jnp.float32)
    for k in range(c2):
        total = jnp.where(row % c2 == k, bias_second[k], total)
    bias_two[...] = total


def pick_kernel(sources, blocks, at_slots, scalars, arrived, ref, *rest):
    last, first, sem = rest[-3:]
    copies = []
    for s in range(sources):
        for j, (into, block) in enumerate(((last, blocks - 1), (first, 0))):
            slot = scalars[at_slots + s * blocks + block]
            copies.append(pltpu.make_async_copy(arrived.at[slot], into.at[s], sem.at[j, s]))
    for j, (into, block) in enumerate(((last, blocks - 1), (first, 0))):
        copies.append(pltpu.make_async_copy(ref.at[block], into.at[sources], sem.at[j, sources]))
    for copy in copies:
        copy.start()
    for copy in copies:
        copy.wait()


def own_kernel(at_slots, at_live, scalars, arrived, ref, var, stage, wide, ref_wide, sem):
    planes, cols, lanes = var.shape
    groups = lanes // LANES
    sources = stage.shape[0]
    tile_rows = arrived.shape[1]
    per_group = LANES // tile_rows
    blocks = groups * per_group
    copies = {}
    for g in range(groups):
        for s in range(sources):
            for b in range(per_group):
                copies[g, s, b] = pltpu.make_async_copy(
                    arrived.at[scalars[at_slots + s * blocks + g * per_group + b]],
                    stage.at[s, g, pl.ds(b * tile_rows, tile_rows)],
                    sem.at[g, s, b],
                )
                copies[g, s, b].start()
    live = scalars[at_live]
    for g in range(groups):
        ref_wide[g] = ref[g].astype(jnp.float32).T
    for g in range(groups):
        for s in range(sources):
            for b in range(per_group):
                copies[g, s, b].wait()
            scale = (s < live).astype(jnp.float32)
            spread(stage[s, g], scale, wide, g * sources + s, cols)
    inv = 1.0 / (live.astype(jnp.float32) + 1.0)
    for g in range(groups):

        def step(p, carry):
            def store(x0, value):
                var[p, x0 : x0 + CHUNK, g * LANES : (g + 1) * LANES] = value

            plane_variance(p, g * sources, sources, cols, scalars, wide, ref_wide, g, inv, store)
            return carry

        lax.fori_loop(0, planes, step, 0)


def rim_kernel(
    c1,
    width,
    at_live,
    scalars,
    below,
    above,
    var,
    kernel_one,
    bias_one,
    kernel_two,
    bias_two,
    out,
    wide,
    ref_wide,
    rim_var,
    left,
    right,
    cost,
):
    planes, cols, lanes = var.shape
    sources = below.shape[0] - 1
    is_below = lax.broadcasted_iota(jnp.int32, (1, LANES), 1) < below.shape[1]
    live = jnp.where(is_below, scalars[at_live + 2], scalars[at_live + 1])

    def both(s):
        return jnp.concatenate([below[s], above[s]], axis=0)

    ref_wide[0] = both(sources).astype(jnp.float32).T
    for s in range(sources):
        spread(both(s), (s < live).astype(jnp.float32), wide, s, cols)
    inv = 1.0 / (live.astype(jnp.float32) + 1.0)

    def step(p, carry):
        def store(x0, value):
            rim_var[p, x0 : x0 + CHUNK, :] = value

        plane_variance(p, 0, sources, cols, scalars, wide, ref_wide, 0, inv, store)
        return carry

    lax.fori_loop(0, planes, step, 0)

    deep = lanes + LANES
    held = LANES - width
    lane_at = lax.broadcasted_iota(jnp.int32, (cols, LANES), 1)
    keep = jnp.where((lane_at[:1] >= c1) | (scalars[at_live + 3] > 0), 1.0, 0.0)
    zeros = jnp.zeros((PAD, LANES), jnp.float32)
    left[0:PAD, :] = zeros
    right[PAD + cols : 2 * PAD + cols, :] = zeros
    for p in range(planes):
        cost[p, 0:PAD, :] = zeros
    out_w = out.shape[2]
    for p in range(planes):
        first, last = max(p - 1, 0), min(p + 2, planes)
        lhs = jnp.concatenate(
            [part for q in range(first, last) for part in (var[q], rim_var[q])], axis=1
        )
        a0 = first - (p - 1)
        rhs = kernel_one[a0 * deep : (a0 + last - first) * deep, :]
        taps = jnp.dot(lhs, rhs, preferred_element_type=jnp.float32)
        t_left, t_right = taps[:, 0:LANES], taps[:, LANES : 2 * LANES]
        left[PAD : PAD + cols, :] = t_left
        right[PAD : PAD + cols, :] = t_right
        center = jnp.where(
            lane_at < held,
            pltpu.roll(t_left, LANES - width, 1),
            pltpu.roll(t_right, LANES - (width - held), 1),
        )
        total = left[PAD - 1 : PAD - 1 + cols, :] + center + right[PAD + 1 : PAD + 1 + cols, :]
        cost[p, PAD : PAD + cols, :] = jnp.maximum(total + bias_one[...], 0.0) * keep

    for q in range(planes // 2):
        parts = []
        a0 = 0
        for a in range(3):
            plane = 2 * q + a - 1
            if plane < 0:
                a0 = 1
                continue
            for d in range(3):
                parts.append(cost[plane, pl.ds(PAD + d - 1, out_w, stride=2), :].astype(jnp.bfloat16))
        lhs = jnp.concatenate(parts, axis=1)
        rhs = kernel_two[:, a0 * 3 * LANES :]
        result = lax.dot_general(rhs, lhs, (((1,), (1,)), ((), ())), preferred_element_type=jnp.float32)
        out[q] = result + bias_two[...]


def on_device(
    ref_features,
    source_tiles,
    pair_lists,
    view_counts,
    disparities,
    conv_first,
    bias_first,
    conv_second,
    bias_second,
):
    n_view = lax.axis_size("view")
    me = lax.axis_index("view")
    rows_n, channels, cols = ref_features.shape
    tiles_dev, tile_rows = source_tiles.shape[0], source_tiles.shape[1]
    sources, blocks = pair_lists.shape[1], pair_lists.shape[2]
    planes = disparities.shape[0]
    requests = sources * blocks
    slab = tile_rows * channels
    groups = rows_n * channels // LANES
    c1, c2 = conv_first.shape[2], conv_second.shape[0]
    out_rows = rows_n + 1
    width = out_rows * c1
    half_r, half_p, half_x = rows_n // 2, planes // 2, cols // 2
    deep = (groups + 1) * LANES
    smem = pl.BlockSpec(memory_space=pltpu.SMEM)
    vmem = pl.BlockSpec(memory_space=pltpu.VMEM)
    anywhere = pl.BlockSpec(memory_space=pl.ANY)
    params = pltpu.CompilerParams(vmem_limit_bytes=VMEM_LIMIT)

    ids = pair_lists.reshape(requests)
    owner = jnp.where(ids >= 0, ids // tiles_dev, -1)
    order = np.arange(requests)
    same = (owner[:, None] == owner[None, :]) & (order[None, :] < order[:, None])
    slots = jnp.where(ids >= 0, owner * CAP + jnp.sum(same.astype(jnp.int32), axis=1), -1)
    asked = slots[:, None] == np.arange(n_view * CAP)[None, :]
    wanted = jnp.sum(jnp.where(asked, (ids % tiles_dev)[:, None], 0), axis=0)
    table = jnp.concatenate(
        [wanted.reshape(n_view, CAP), jnp.broadcast_to(view_counts[:, None], (n_view, 1))], axis=1
    )
    table = lax.all_to_all(table, "view", split_axis=0, concat_axis=0, tiled=True)
    outgoing = source_tiles.reshape(tiles_dev, slab, cols)[table[:, :CAP]]
    arrived = lax.all_to_all(outgoing, "view", split_axis=0, concat_axis=0, tiled=True)
    arrived = arrived.reshape(n_view * CAP, slab, cols)

    strips = np.arange(n_view)
    neighbours = jnp.sum(
        jnp.where(strips[None, :] == jnp.stack([me - 1, me + 1])[:, None], table[None, :, CAP], 0), axis=1
    )
    scalars = jnp.concatenate(
        [
            disparities.reshape(planes * sources),
            jnp.maximum(slots, 0),
            view_counts,
            neighbours,
            (me > 0).astype(jnp.int32)[None],
        ]
    )
    at_slots = planes * sources
    at_live = at_slots + requests

    layouts = pl.pallas_call(
        layout_kernel,
        out_shape=[
            jax.ShapeDtypeStruct((3 * deep, 2 * LANES), jnp.bfloat16),
            jax.ShapeDtypeStruct((half_r * c2, 9 * LANES), jnp.bfloat16),
            jax.ShapeDtypeStruct((1, LANES), jnp.float32),
            jax.ShapeDtypeStruct((half_r * c2, half_x), jnp.float32),
        ],
        in_specs=[vmem, vmem, smem, smem],
        out_specs=[vmem] * 4,
        scratch_shapes=[pltpu.VMEM((2 * LANES, deep), jnp.float32)],
        compiler_params=params,
        name="weight_layout",
    )(conv_first.transpose(0, 1, 3, 2, 4), conv_second.transpose(1, 2, 3, 4, 0), bias_first, bias_second)
    kernel_one, kernel_two, bias_one, bias_two = layouts

    payload = jax.ShapeDtypeStruct((sources + 1, slab, cols), jnp.bfloat16)
    last_block, first_block = pl.pallas_call(
        functools.partial(pick_kernel, sources, blocks, at_slots),
        out_shape=[payload, payload],
        in_specs=[smem] + [anywhere] * 4,
        out_specs=[anywhere] * 2,
        scratch_shapes=[pltpu.SemaphoreType.DMA((2, sources + 1))],
        compiler_params=params,
        name="edge_blocks",
    )(scalars, arrived, ref_features.reshape(blocks, slab, cols), kernel_one, kernel_two)
    above = passed_along(last_block, "view", 1)
    below = passed_along(first_block, "view", -1)

    var = pl.pallas_call(
        functools.partial(own_kernel, at_slots, at_live),
        out_shape=jax.ShapeDtypeStruct((planes, cols, groups * LANES), jnp.bfloat16),
        in_specs=[smem, anywhere, vmem],
        out_specs=vmem,
        scratch_shapes=[
            pltpu.VMEM((sources, groups, LANES, cols), jnp.bfloat16),
            pltpu.VMEM((groups * sources, cols + 2 * SHIFT, LANES), jnp.float32),
            pltpu.VMEM((groups, cols, LANES), jnp.float32),
            pltpu.SemaphoreType.DMA((groups, sources, LANES // slab)),
        ],
        compiler_params=params,
        name="own_rows",
    )(scalars, arrived, ref_features.reshape(groups, LANES, cols))

    out = pl.pallas_call(
        functools.partial(rim_kernel, c1, width, at_live),
        out_shape=jax.ShapeDtypeStruct((half_p, half_r * c2, half_x), jnp.float32),
        in_specs=[smem] + [vmem] * 7,
        out_specs=vmem,
        scratch_shapes=[
            pltpu.VMEM((sources, cols + 2 * SHIFT, LANES), jnp.float32),
            pltpu.VMEM((1, cols, LANES), jnp.float32),
            pltpu.VMEM((planes, cols, LANES), jnp.bfloat16),
            pltpu.VMEM((cols + 2 * PAD, LANES), jnp.float32),
            pltpu.VMEM((cols + 2 * PAD, LANES), jnp.float32),
            pltpu.VMEM((planes, cols + PAD, LANES), jnp.float32),
        ],
        compiler_params=params,
        name="rim_and_convolutions",
    )(scalars, below, above, var, kernel_one, bias_one, kernel_two, bias_two)
    return out.reshape(half_p, half_r, c2, half_x)


def solution(mesh):
    return jax.shard_map(
        on_device,
        mesh=mesh,
        in_specs=(
            P(("groups", "view"), None, None),
            P(("groups", "view"), None, None, None),
            P(("groups", "view"), None, None),
            P(("groups", "view")),
            P("groups", None),
            P(),
            P(),
            P(),
            P(),
        ),
        out_specs=P("groups", "view", None, None),
        check_vma=False,
    )
```

```python
import functools

import numpy as np

import jax
import jax.numpy as jnp
from jax import lax
from jax.experimental import pallas as pl
from jax.experimental.pallas import tpu as pltpu
from jax.sharding import PartitionSpec as P

SHIFT = 48
CAP = 2
LANES = 128
PAD = 8
CHUNK = 64
VMEM_LIMIT = 40 * 1024 * 1024


def passed_along(x, axis, by):
    count = lax.axis_size(axis)
    pairs = [(i, i + by) for i in range(count) if 0 <= i + by < count]
    return lax.ppermute(x, axis, pairs)


def spread(stage_value, scale, wide, at, cols):
    band = jnp.zeros((SHIFT, LANES), jnp.float32)
    wide[at, 0:SHIFT, :] = band
    wide[at, SHIFT + cols : 2 * SHIFT + cols, :] = band
    wide[at, SHIFT : SHIFT + cols, :] = stage_value.astype(jnp.float32).T * scale


def plane_variance(p, at, sources, cols, disp, wide, ref_wide, ref_at, inv, store):
    for x0 in range(0, cols, CHUNK):
        ref = ref_wide[ref_at, x0 : x0 + CHUNK, :]
        summed = ref
        squares = ref * ref
        for s in range(sources):
            warped = wide[at + s, pl.ds(SHIFT + x0 - disp[p * sources + s], CHUNK), :]
            summed = summed + warped
            squares = squares + warped * warped
        mean = summed * inv
        store(x0, (squares * inv - mean * mean).astype(jnp.bfloat16))


def layout_kernel(places, first, second, bias_first, bias_second, kernel_one, kernel_two, bias_one, bias_two, turned):
    deep = turned.shape[1]
    c1, channels = first.shape[3], first.shape[4]
    c2 = second.shape[4]
    half_r = bias_two.shape[0] // c2
    out_rows = 2 * half_r + 1
    width = out_rows * c1
    held = (LANES - width) // c1
    per_group = LANES // channels
    turned[...] = jnp.zeros(turned.shape, jnp.float32)
    filler = jnp.zeros((c1, LANES - channels), jnp.float32)
    for a in range(3):
        for d in range(3):
            taps = [jnp.concatenate([first[a, b, d].astype(jnp.float32), filler], axis=1) for b in range(3)]
            for r in range(out_rows):
                at = r * c1 + (LANES if d == 2 else 0)
                if d == 1:
                    at = width + (r * c1 if r < held else LANES + (r - held) * c1)
                for b in range(3):
                    place = places[r - 2 + b]
                    group, lane = place // per_group * LANES, place % per_group * channels
                    block = pltpu.roll(taps[b], lane, 1) if lane else taps[b]
                    turned[at : at + c1, group : group + LANES] += block
        kernel_one[a * deep : (a + 1) * deep, :] = turned[...].T.astype(jnp.bfloat16)
        turned[...] = jnp.zeros(turned.shape, jnp.float32)
    none = jnp.zeros((c1, c2), jnp.float32)
    for a in range(3):
        for d in range(3):
            taps = [second[a, b, d].astype(jnp.float32) for b in range(3)]
            stacked = jnp.concatenate(
                [
                    jnp.concatenate(
                        [taps[r - 2 * g] if 0 <= r - 2 * g < 3 else none for g in range(half_r)]
                        + [jnp.zeros((c1, LANES - half_r * c2), jnp.float32)],
                        axis=1,
                    )
                    for r in range(out_rows)
                ]
                + [jnp.zeros((LANES - width, LANES), jnp.float32)],
                axis=0,
            )
            at = (a * 3 + d) * LANES
            kernel_two[:, at : at + LANES] = stacked.T[: half_r * c2].astype(jnp.bfloat16)
    lane = lax.broadcasted_iota(jnp.int32, bias_one.shape, 1)
    total = jnp.zeros(bias_one.shape, jnp.float32)
    for o in range(c1):
        total = jnp.where(lane % c1 == o, bias_first[o], total)
    bias_one[...] = total
    row = lax.broadcasted_iota(jnp.int32, bias_two.shape, 0)
    total = jnp.zeros(bias_two.shape, jnp.float32)
    for k in range(c2):
        total = jnp.where(row % c2 == k, bias_second[k], total)
    bias_two[...] = total


def pick_kernel(sources, blocks, at_slots, picks, scalars, arrived, ref, *rest):
    payloads, sem = rest[-1 - len(picks) : -1], rest[-1]
    copies = []
    for j, (into, (block, row)) in enumerate(zip(payloads, picks)):
        for s in range(sources):
            slot = scalars[at_slots + s * blocks + block]
            copies.append(pltpu.make_async_copy(arrived.at[slot], into.at[s], sem.at[j, s]))
        copies.append(pltpu.make_async_copy(ref.at[row], into.at[sources], sem.at[j, sources]))
    for copy in copies:
        copy.start()
    for copy in copies:
        copy.wait()


def own_kernel(at_slots, at_live, row, scalars, arrived, ref, var, stage, wide, ref_wide, sem):
    planes, cols, lanes = var.shape
    sources = stage.shape[0]
    channels = arrived.shape[1]
    blocks = lanes // channels
    tile_rows = ref.shape[0] // blocks
    copies = {}
    for s in range(sources):
        for b in range(blocks):
            copies[s, b] = pltpu.make_async_copy(
                arrived.at[scalars[at_slots + s * blocks + b]],
                stage.at[s, pl.ds(b * channels, channels)],
                sem.at[s, b],
            )
            copies[s, b].start()
    live = scalars[at_live]
    slab = jnp.concatenate([ref[tile_rows * b + row] for b in range(blocks)], axis=0)
    ref_wide[0] = slab.astype(jnp.float32).T
    for s in range(sources):
        for b in range(blocks):
            copies[s, b].wait()
        spread(stage[s], (s < live).astype(jnp.float32), wide, s, cols)
    inv = 1.0 / (live.astype(jnp.float32) + 1.0)

    def step(p, carry):
        def store(x0, value):
            var[p, x0 : x0 + CHUNK, :] = value

        plane_variance(p, 0, sources, cols, scalars, wide, ref_wide, 0, inv, store)
        return carry

    lax.fori_loop(0, planes, step, 0)


def rim_kernel(
    c1,
    width,
    at_live,
    scalars,
    below,
    above,
    nearest,
    even,
    odd,
    kernel_one,
    bias_one,
    kernel_two,
    bias_two,
    out,
    wide,
    ref_wide,
    rim_var,
    left,
    right,
    cost,
):
    planes, cols, lanes = even.shape
    sources = below.shape[0] - 1
    channels = below.shape[1]
    is_below = lax.broadcasted_iota(jnp.int32, (1, LANES), 1) < channels
    live = jnp.where(is_below, scalars[at_live + 2], scalars[at_live + 1])
    filler = jnp.zeros((LANES - 3 * channels, cols), jnp.bfloat16)

    def slab(s):
        return jnp.concatenate([below[s], above[s], nearest[s], filler], axis=0)

    ref_wide[0] = slab(sources).astype(jnp.float32).T
    for s in range(sources):
        spread(slab(s), (s < live).astype(jnp.float32), wide, s, cols)
    inv = 1.0 / (live.astype(jnp.float32) + 1.0)

    def step(p, carry):
        def store(x0, value):
            rim_var[p, x0 : x0 + CHUNK, :] = value

        plane_variance(p, 0, sources, cols, scalars, wide, ref_wide, 0, inv, store)
        return carry

    lax.fori_loop(0, planes, step, 0)

    deep = 3 * lanes
    held = LANES - width
    lane_at = lax.broadcasted_iota(jnp.int32, (cols, LANES), 1)
    keep = jnp.where((lane_at[:1] >= c1) | (scalars[at_live + 3] > 0), 1.0, 0.0)
    zeros = jnp.zeros((PAD, LANES), jnp.float32)
    left[0:PAD, :] = zeros
    right[PAD + cols : 2 * PAD + cols, :] = zeros
    for p in range(planes):
        cost[p, 0:PAD, :] = zeros
    out_w = out.shape[2]
    for p in range(planes):
        first, last = max(p - 1, 0), min(p + 2, planes)
        lhs = jnp.concatenate(
            [part for q in range(first, last) for part in (even[q], odd[q], rim_var[q])], axis=1
        )
        a0 = first - (p - 1)
        rhs = kernel_one[a0 * deep : (a0 + last - first) * deep, :]
        taps = jnp.dot(lhs, rhs, preferred_element_type=jnp.float32)
        t_left, t_right = taps[:, 0:LANES], taps[:, LANES : 2 * LANES]
        left[PAD : PAD + cols, :] = t_left
        right[PAD : PAD + cols, :] = t_right
        center = jnp.where(
            lane_at < held,
            pltpu.roll(t_left, LANES - width, 1),
            pltpu.roll(t_right, LANES - (width - held), 1),
        )
        total = left[PAD - 1 : PAD - 1 + cols, :] + center + right[PAD + 1 : PAD + 1 + cols, :]
        cost[p, PAD : PAD + cols, :] = jnp.maximum(total + bias_one[...], 0.0) * keep

    for q in range(planes // 2):
        parts = []
        a0 = 0
        for a in range(3):
            plane = 2 * q + a - 1
            if plane < 0:
                a0 = 1
                continue
            for d in range(3):
                parts.append(cost[plane, pl.ds(PAD + d - 1, out_w, stride=2), :].astype(jnp.bfloat16))
        lhs = jnp.concatenate(parts, axis=1)
        rhs = kernel_two[:, a0 * 3 * LANES :]
        result = lax.dot_general(rhs, lhs, (((1,), (1,)), ((), ())), preferred_element_type=jnp.float32)
        out[q] = result + bias_two[...]


def on_device(
    ref_features,
    source_tiles,
    pair_lists,
    view_counts,
    disparities,
    conv_first,
    bias_first,
    conv_second,
    bias_second,
):
    n_view = lax.axis_size("view")
    me = lax.axis_index("view")
    rows_n, channels, cols = ref_features.shape
    tiles_dev, tile_rows = source_tiles.shape[0], source_tiles.shape[1]
    sources, blocks = pair_lists.shape[1], pair_lists.shape[2]
    planes = disparities.shape[0]
    requests = sources * blocks
    groups = rows_n * channels // LANES
    c1, c2 = conv_first.shape[2], conv_second.shape[0]
    out_rows = rows_n + 1
    width = out_rows * c1
    half_r, half_p, half_x = rows_n // 2, planes // 2, cols // 2
    deep = (groups + 1) * LANES
    smem = pl.BlockSpec(memory_space=pltpu.SMEM)
    vmem = pl.BlockSpec(memory_space=pltpu.VMEM)
    anywhere = pl.BlockSpec(memory_space=pl.ANY)
    params = pltpu.CompilerParams(vmem_limit_bytes=VMEM_LIMIT)

    ids = pair_lists.reshape(requests)
    owner = jnp.where(ids >= 0, ids // tiles_dev, -1)
    order = np.arange(requests)
    same = (owner[:, None] == owner[None, :]) & (order[None, :] < order[:, None])
    slots = jnp.where(ids >= 0, owner * CAP + jnp.sum(same.astype(jnp.int32), axis=1), -1)
    asked = slots[:, None] == np.arange(n_view * CAP)[None, :]
    wanted = jnp.sum(jnp.where(asked, (ids % tiles_dev)[:, None], 0), axis=0)
    table = jnp.concatenate(
        [wanted.reshape(n_view, CAP), jnp.broadcast_to(view_counts[:, None], (n_view, 1))], axis=1
    )
    table = lax.all_to_all(table, "view", split_axis=0, concat_axis=0, tiled=True)
    flat_rows = source_tiles.reshape(tiles_dev * tile_rows, channels, cols)
    arrived = []
    for row in range(tile_rows):
        outgoing = flat_rows[table[:, :CAP] * tile_rows + row]
        moved = lax.all_to_all(outgoing, "view", split_axis=0, concat_axis=0, tiled=True)
        arrived.append(moved.reshape(n_view * CAP, channels, cols))

    strips = np.arange(n_view)
    neighbours = jnp.sum(
        jnp.where(strips[None, :] == jnp.stack([me - 1, me + 1])[:, None], table[None, :, CAP], 0), axis=1
    )
    scalars = jnp.concatenate(
        [
            disparities.reshape(planes * sources),
            jnp.maximum(slots, 0),
            view_counts,
            neighbours,
            (me > 0).astype(jnp.int32)[None],
        ]
    )
    at_slots = planes * sources
    at_live = at_slots + requests

    per_group = rows_n // tile_rows
    places = {row: row % tile_rows * per_group + row // tile_rows for row in range(rows_n)}
    places.update({rows_n: rows_n, -2: rows_n + 1, -1: rows_n + 2})
    layouts = pl.pallas_call(
        functools.partial(layout_kernel, places),
        out_shape=[
            jax.ShapeDtypeStruct((3 * deep, 2 * LANES), jnp.bfloat16),
            jax.ShapeDtypeStruct((half_r * c2, 9 * LANES), jnp.bfloat16),
            jax.ShapeDtypeStruct((1, LANES), jnp.float32),
            jax.ShapeDtypeStruct((half_r * c2, half_x), jnp.float32),
        ],
        in_specs=[vmem, vmem, smem, smem],
        out_specs=[vmem] * 4,
        scratch_shapes=[pltpu.VMEM((2 * LANES, deep), jnp.float32)],
        compiler_params=params,
        name="weight_layout",
    )(conv_first.transpose(0, 1, 3, 2, 4), conv_second.transpose(1, 2, 3, 4, 0), bias_first, bias_second)
    kernel_one, kernel_two, bias_one, bias_two = layouts

    payload = jax.ShapeDtypeStruct((sources + 1, channels, cols), jnp.bfloat16)

    def edges(row, picks, *after):
        return pl.pallas_call(
            functools.partial(pick_kernel, sources, blocks, at_slots, picks),
            out_shape=[payload] * len(picks),
            in_specs=[smem] + [anywhere] * (2 + len(after)),
            out_specs=[anywhere] * len(picks),
            scratch_shapes=[pltpu.SemaphoreType.DMA((len(picks), sources + 1))],
            compiler_params=params,
            name=f"edge_rows_{row}",
        )(scalars, arrived[row], ref_features, *after)

    def own(row):
        return pl.pallas_call(
            functools.partial(own_kernel, at_slots, at_live, row),
            out_shape=jax.ShapeDtypeStruct((planes, cols, LANES), jnp.bfloat16),
            in_specs=[smem, anywhere, vmem],
            out_specs=vmem,
            scratch_shapes=[
                pltpu.VMEM((sources, LANES, cols), jnp.bfloat16),
                pltpu.VMEM((sources, cols + 2 * SHIFT, LANES), jnp.float32),
                pltpu.VMEM((1, cols, LANES), jnp.float32),
                pltpu.SemaphoreType.DMA((sources, blocks)),
            ],
            compiler_params=params,
            name=f"own_rows_{row}",
        )(scalars, arrived[row], ref_features)

    last_even, first_even = edges(0, ((blocks - 1, rows_n - 2), (0, 0)), bias_one)
    above = passed_along(last_even, "view", 1)
    below = passed_along(first_even, "view", -1)
    even = own(0)
    (last_odd,) = edges(1, ((blocks - 1, rows_n - 1),), even)
    nearest = passed_along(last_odd, "view", 1)
    odd = own(1)

    out = pl.pallas_call(
        functools.partial(rim_kernel, c1, width, at_live),
        out_shape=jax.ShapeDtypeStruct((half_p, half_r * c2, half_x), jnp.float32),
        in_specs=[smem] + [vmem] * 9,
        out_specs=vmem,
        scratch_shapes=[
            pltpu.VMEM((sources, cols + 2 * SHIFT, LANES), jnp.float32),
            pltpu.VMEM((1, cols, LANES), jnp.float32),
            pltpu.VMEM((planes, cols, LANES), jnp.bfloat16),
            pltpu.VMEM((cols + 2 * PAD, LANES), jnp.float32),
            pltpu.VMEM((cols + 2 * PAD, LANES), jnp.float32),
            pltpu.VMEM((planes, cols + PAD, LANES), jnp.float32),
        ],
        compiler_params=params,
        name="rim_and_convolutions",
    )(scalars, below, above, nearest, even, odd, kernel_one, bias_one, kernel_two, bias_two)
    return out.reshape(half_p, half_r, c2, half_x)


def solution(mesh):
    return jax.shard_map(
        on_device,
        mesh=mesh,
        in_specs=(
            P(("groups", "view"), None, None),
            P(("groups", "view"), None, None, None),
            P(("groups", "view"), None, None),
            P(("groups", "view")),
            P("groups", None),
            P(),
            P(),
            P(),
            P(),
        ),
        out_specs=P("groups", "view", None, None),
        check_vma=False,
    )
```

```python
import functools

import numpy as np

import jax
import jax.numpy as jnp
from jax import lax
from jax.experimental import pallas as pl
from jax.experimental.pallas import tpu as pltpu
from jax.sharding import PartitionSpec as P

SHIFT = 48
CAP = 2
LANES = 128
PAD = 8
CHUNK = 64
VMEM_LIMIT = 40 * 1024 * 1024


def passed_along(x, axis, by):
    count = lax.axis_size(axis)
    pairs = [(i, i + by) for i in range(count) if 0 <= i + by < count]
    return lax.ppermute(x, axis, pairs)


def request_places(pair_lists, tiles_dev):
    owners, ranks, tiles = [], [], []
    for s in range(pair_lists.shape[1]):
        for b in range(pair_lists.shape[2]):
            tile = pair_lists[0, s, b]
            whole = jnp.maximum(tile, 0)
            owner = jnp.where(tile >= 0, lax.div(whole, tiles_dev), -1)
            rank = jnp.int32(0)
            for other in owners:
                rank = rank + jnp.where(other == owner, 1, 0)
            owners.append(owner)
            ranks.append(rank)
            tiles.append(lax.rem(whole, tiles_dev))
    return owners, ranks, tiles


def request_kernel(tiles_dev, pair_lists, view_counts, table):
    owners, ranks, tiles = request_places(pair_lists, tiles_dev)
    row = lax.broadcasted_iota(jnp.int32, table.shape, 0)
    lane = lax.broadcasted_iota(jnp.int32, table.shape, 2)
    total = jnp.where(lane == CAP, view_counts[0], 0)
    for owner, rank, tile in zip(owners, ranks, tiles):
        total = jnp.where((row == owner) & (lane == rank), tile, total)
    table[...] = total


def gather_kernel(table, tiles, outgoing):
    for d in range(outgoing.shape[0]):
        for k in range(CAP):
            outgoing[d, k] = tiles[table[d, 0, k]]


def prepare_kernel(
    tiles_dev,
    places,
    first,
    second,
    bias_first,
    bias_second,
    disparities,
    pair_lists,
    view_counts,
    table,
    me,
    ref,
    kernel_own,
    kernel_rim,
    kernel_two,
    bias_one,
    bias_two,
    ref_last,
    ref_first,
    scalars,
    turned,
):
    planes, sources = disparities.shape
    blocks = pair_lists.shape[2]
    owners, ranks, _ = request_places(pair_lists, tiles_dev)
    at = 0
    for p in range(planes):
        for s in range(sources):
            scalars[at] = disparities[p, s]
            at += 1
    for owner, rank in zip(owners, ranks):
        scalars[at] = jnp.where(owner >= 0, owner * CAP + rank, 0)
        at += 1
    n_view = table.shape[0]
    up, down = jnp.maximum(me[0] - 1, 0), jnp.minimum(me[0] + 1, n_view - 1)
    scalars[at] = view_counts[0]
    scalars[at + 1] = table[up, 0, CAP]
    scalars[at + 2] = table[down, 0, CAP]
    scalars[at + 3] = me[0]

    rows_n = ref.shape[0]
    edge = ref_last.shape[0]
    for i in range(edge):
        ref_last[i] = ref[rows_n - edge + i]
    ref_first[0] = ref[0]

    deep = turned.shape[1]
    own_deep = kernel_own.shape[0] // 3
    rim_deep = kernel_rim.shape[0] // 3
    c1, channels = first.shape[3], first.shape[4]
    c2 = second.shape[4]
    half_r = bias_two.shape[0] // c2
    out_rows = 2 * half_r + 1
    width = out_rows * c1
    held = (LANES - width) // c1
    per_group = LANES // channels
    filler = jnp.zeros((c1, LANES - channels), jnp.float32)
    for a in range(3):
        turned[...] = jnp.zeros(turned.shape, jnp.float32)
        for d in range(3):
            taps = [jnp.concatenate([first[a, b, d].astype(jnp.float32), filler], axis=1) for b in range(3)]
            for r in range(out_rows):
                at = r * c1 + (LANES if d == 2 else 0)
                if d == 1:
                    at = width + (r * c1 if r < held else LANES + (r - held) * c1)
                for b in range(3):
                    place = places[r - 2 + b]
                    group, lane = place // per_group * LANES, place % per_group * channels
                    block = pltpu.roll(taps[b], lane, 1) if lane else taps[b]
                    turned[at : at + c1, group : group + LANES] += block
        band = turned[...].T.astype(jnp.bfloat16)
        kernel_own[a * own_deep : (a + 1) * own_deep, :] = band[:own_deep]
        kernel_rim[a * rim_deep : (a + 1) * rim_deep, :] = band[own_deep:]
    none = jnp.zeros((c1, c2), jnp.float32)
    for a in range(3):
        for d in range(3):
            taps = [second[a, b, d].astype(jnp.float32) for b in range(3)]
            stacked = jnp.concatenate(
                [
                    jnp.concatenate(
                        [taps[r - 2 * g] if 0 <= r - 2 * g < 3 else none for g in range(half_r)]
                        + [jnp.zeros((c1, LANES - half_r * c2), jnp.float32)],
                        axis=1,
                    )
                    for r in range(out_rows)
                ]
                + [jnp.zeros((LANES - width, LANES), jnp.float32)],
                axis=0,
            )
            at = (a * 3 + d) * LANES
            kernel_two[:, at : at + LANES] = stacked.T[: half_r * c2].astype(jnp.bfloat16)
    lane = lax.broadcasted_iota(jnp.int32, bias_one.shape, 1)
    total = jnp.zeros(bias_one.shape, jnp.float32)
    for o in range(c1):
        total = jnp.where(lane % c1 == o, bias_first[o], total)
    bias_one[...] = total
    row = lax.broadcasted_iota(jnp.int32, bias_two.shape, 0)
    total = jnp.zeros(bias_two.shape, jnp.float32)
    for k in range(c2):
        total = jnp.where(row % c2 == k, bias_second[k], total)
    bias_two[...] = total


def edge_kernel(blocks, at_slots, scalars, arrived, *rest):
    last, first = rest[-2:]
    channels = first.shape[1]
    for s in range(last.shape[0]):
        last[s] = arrived[scalars[at_slots + s * blocks + blocks - 1]]
        first[s] = arrived[scalars[at_slots + s * blocks], 0:channels, :]


def spread(slab, scale, wide, at):
    cols = slab.shape[1]
    band = jnp.zeros((SHIFT, LANES), jnp.float32)
    wide[at, 0:SHIFT, :] = band
    wide[at, SHIFT + cols : 2 * SHIFT + cols, :] = band
    wide[at, SHIFT : SHIFT + cols, :] = slab.astype(jnp.float32).T * scale


def plane_variance(p, at, sources, cols, disp, wide, ref_wide, ref_at, inv, store):
    for x0 in range(0, cols, CHUNK):
        ref = ref_wide[ref_at, x0 : x0 + CHUNK, :]
        summed = ref
        squares = ref * ref
        for s in range(sources):
            warped = wide[at + s, pl.ds(SHIFT + x0 - disp[p * sources + s], CHUNK), :]
            summed = summed + warped
            squares = squares + warped * warped
        mean = summed * inv
        store(x0, (squares * inv - mean * mean).astype(jnp.bfloat16))


def plane_taps(p, planes, var, kernel):
    deep = kernel.shape[0] // 3
    first, last = max(p - 1, 0), min(p + 2, planes)
    lhs = jnp.concatenate([var[q] for q in range(first, last)], axis=1)
    a0 = first - (p - 1)
    rhs = kernel[a0 * deep : (a0 + last - first) * deep, :]
    return jnp.dot(lhs, rhs, preferred_element_type=jnp.float32)


def own_kernel(at_slots, at_live, sources, scalars, arrived, ref, kernel, taps, wide, ref_wide, var):
    planes, cols, lanes = var.shape
    groups = lanes // LANES
    channels = ref.shape[1]
    per_group = LANES // channels
    blocks = ref.shape[0] * channels // arrived.shape[1]
    group_blocks = blocks // groups
    live = scalars[at_live]
    for g in range(groups):
        rows = [ref[g * per_group + i] for i in range(per_group)]
        ref_wide[g] = jnp.concatenate(rows, axis=0).astype(jnp.float32).T
        for s in range(sources):
            at = at_slots + s * blocks + g * group_blocks
            slab = jnp.concatenate([arrived[scalars[at + b]] for b in range(group_blocks)], axis=0)
            spread(slab, (s < live).astype(jnp.float32), wide, g * sources + s)
    inv = 1.0 / (live.astype(jnp.float32) + 1.0)
    for step in range(planes + 1):
        if step < planes:
            for g in range(groups):

                def store(x0, value):
                    var[step, x0 : x0 + CHUNK, g * LANES : (g + 1) * LANES] = value

                plane_variance(step, g * sources, sources, cols, scalars, wide, ref_wide, g, inv, store)
        if step > 0:
            taps[step - 1] = plane_taps(step - 1, planes, var, kernel)


def rim_kernel(
    c1,
    width,
    at_live,
    scalars,
    below,
    above,
    ref_below,
    ref_above,
    own_taps,
    kernel,
    bias_one,
    kernel_two,
    bias_two,
    out,
    wide,
    ref_wide,
    var,
    left,
    right,
    cost,
):
    planes, cols, _ = var.shape
    sources, channels = below.shape[0], below.shape[1]
    edge = ref_above.shape[0]
    is_below = lax.broadcasted_iota(jnp.int32, (1, LANES), 1) < channels
    live = jnp.where(is_below, scalars[at_live + 2], scalars[at_live + 1])
    filler = jnp.zeros((LANES - (edge + 1) * channels, cols), jnp.bfloat16)
    slab = jnp.concatenate([ref_below[0]] + [ref_above[i] for i in range(edge)] + [filler], axis=0)
    ref_wide[0] = slab.astype(jnp.float32).T
    for s in range(sources):
        slab = jnp.concatenate([below[s], above[s], filler], axis=0)
        spread(slab, (s < live).astype(jnp.float32), wide, s)
    inv = 1.0 / (live.astype(jnp.float32) + 1.0)

    held = LANES - width
    lane_at = lax.broadcasted_iota(jnp.int32, (cols, LANES), 1)
    keep = jnp.where((lane_at[:1] >= c1) | (scalars[at_live + 3] > 0), 1.0, 0.0)
    zeros = jnp.zeros((PAD, LANES), jnp.float32)
    out_w = out.shape[2]
    for step in range(planes + 1):
        if step < planes:

            def store(x0, value):
                var[step, x0 : x0 + CHUNK, :] = value

            plane_variance(step, 0, sources, cols, scalars, wide, ref_wide, 0, inv, store)
        if step == 0:
            continue
        p = step - 1
        taps = own_taps[p] + plane_taps(p, planes, var, kernel)
        t_left, t_right = taps[:, 0:LANES], taps[:, LANES : 2 * LANES]
        left[p, 0:PAD, :] = zeros
        left[p, PAD : PAD + cols, :] = t_left
        right[p, PAD : PAD + cols, :] = t_right
        right[p, PAD + cols : 2 * PAD + cols, :] = zeros
        center = jnp.where(
            lane_at < held,
            pltpu.roll(t_left, LANES - width, 1),
            pltpu.roll(t_right, LANES - (width - held), 1),
        )
        total = left[p, PAD - 1 : PAD - 1 + cols, :] + center + right[p, PAD + 1 : PAD + 1 + cols, :]
        cost[p, 0:PAD, :] = zeros
        cost[p, PAD : PAD + cols, :] = jnp.maximum(total + bias_one[...], 0.0) * keep
        if p % 2 == 0:
            continue
        q = p // 2
        parts = []
        a0 = 0
        for a in range(3):
            plane = 2 * q + a - 1
            if plane < 0:
                a0 = 1
                continue
            for d in range(3):
                parts.append(cost[plane, pl.ds(PAD + d - 1, out_w, stride=2), :].astype(jnp.bfloat16))
        lhs = jnp.concatenate(parts, axis=1)
        rhs = kernel_two[:, a0 * 3 * LANES :]
        result = lax.dot_general(rhs, lhs, (((1,), (1,)), ((), ())), preferred_element_type=jnp.float32)
        out[q] = result + bias_two[...]


def on_device(
    ref_features,
    source_tiles,
    pair_lists,
    view_counts,
    disparities,
    conv_first,
    bias_first,
    conv_second,
    bias_second,
):
    n_view = lax.axis_size("view")
    me = lax.axis_index("view").reshape(1)
    rows_n, channels, cols = ref_features.shape
    tiles_dev, tile_rows = source_tiles.shape[0], source_tiles.shape[1]
    sources, blocks = pair_lists.shape[1], pair_lists.shape[2]
    planes = disparities.shape[0]
    slab = tile_rows * channels
    groups = rows_n * channels // LANES
    c1, c2 = conv_first.shape[2], conv_second.shape[0]
    width = (rows_n + 1) * c1
    half_r, half_p, half_x = rows_n // 2, planes // 2, cols // 2
    own_deep = groups * LANES
    smem = pl.BlockSpec(memory_space=pltpu.SMEM)
    vmem = pl.BlockSpec(memory_space=pltpu.VMEM)
    anywhere = pl.BlockSpec(memory_space=pl.ANY)
    params = pltpu.CompilerParams(vmem_limit_bytes=VMEM_LIMIT)
    bf16, f32, i32 = jnp.bfloat16, jnp.float32, jnp.int32

    table = pl.pallas_call(
        functools.partial(request_kernel, tiles_dev),
        out_shape=jax.ShapeDtypeStruct((n_view, 1, CAP + 1), i32),
        in_specs=[smem, smem],
        out_specs=vmem,
        compiler_params=params,
        name="request_table",
    )(pair_lists, view_counts)
    table = lax.all_to_all(table, "view", split_axis=0, concat_axis=0, tiled=True)
    outgoing = pl.pallas_call(
        gather_kernel,
        out_shape=jax.ShapeDtypeStruct((n_view, CAP, slab, cols), bf16),
        in_specs=[smem, vmem],
        out_specs=vmem,
        compiler_params=params,
        name="requested_tiles",
    )(table, source_tiles.reshape(tiles_dev, slab, cols))
    arrived = lax.all_to_all(outgoing, "view", split_axis=0, concat_axis=0, tiled=True)
    arrived = arrived.reshape(n_view * CAP, slab, cols)

    at_slots = planes * sources
    at_live = at_slots + sources * blocks
    places = {row: row for row in range(rows_n + 1)}
    places.update({row - tile_rows: rows_n + 1 + row for row in range(tile_rows)})
    shape = jax.ShapeDtypeStruct
    prepared = pl.pallas_call(
        functools.partial(prepare_kernel, tiles_dev, places),
        out_shape=[
            shape((3 * own_deep, 2 * LANES), bf16),
            shape((3 * LANES, 2 * LANES), bf16),
            shape((half_r * c2, 9 * LANES), bf16),
            shape((1, LANES), f32),
            shape((half_r * c2, half_x), f32),
            shape((tile_rows, channels, cols), bf16),
            shape((1, channels, cols), bf16),
            shape((at_live + 4,), i32),
        ],
        in_specs=[vmem, vmem] + [smem] * 7 + [vmem],
        out_specs=[vmem] * 7 + [smem],
        scratch_shapes=[pltpu.VMEM((2 * LANES, own_deep + LANES), f32)],
        compiler_params=params,
        name="weights_and_scalars",
    )(
        conv_first.transpose(0, 1, 3, 2, 4),
        conv_second.transpose(1, 2, 3, 4, 0),
        bias_first,
        bias_second,
        disparities,
        pair_lists,
        view_counts,
        table,
        me,
        ref_features,
    )
    kernel_own, kernel_rim, kernel_two, bias_one, bias_two, ref_last, ref_first, scalars = prepared
    ref_above = passed_along(ref_last, "view", 1)
    ref_below = passed_along(ref_first, "view", -1)

    last, first = pl.pallas_call(
        functools.partial(edge_kernel, blocks, at_slots),
        out_shape=[shape((sources, slab, cols), bf16), shape((sources, channels, cols), bf16)],
        in_specs=[smem, vmem, anywhere, anywhere],
        out_specs=[vmem, vmem],
        compiler_params=params,
        name="edge_tiles",
    )(scalars, arrived, ref_above, ref_below)
    above = passed_along(last, "view", 1)
    below = passed_along(first, "view", -1)

    own_taps = pl.pallas_call(
        functools.partial(own_kernel, at_slots, at_live, sources),
        out_shape=shape((planes, cols, 2 * LANES), f32),
        in_specs=[smem] + [vmem] * 3,
        out_specs=vmem,
        scratch_shapes=[
            pltpu.VMEM((groups * sources, cols + 2 * SHIFT, LANES), f32),
            pltpu.VMEM((groups, cols, LANES), f32),
            pltpu.VMEM((planes, cols, own_deep), bf16),
        ],
        compiler_params=params,
        name="own_rows",
    )(scalars, arrived, ref_features, kernel_own)

    out = pl.pallas_call(
        functools.partial(rim_kernel, c1, width, at_live),
        out_shape=shape((half_p, half_r * c2, half_x), f32),
        in_specs=[smem] + [vmem] * 9,
        out_specs=vmem,
        scratch_shapes=[
            pltpu.VMEM((sources, cols + 2 * SHIFT, LANES), f32),
            pltpu.VMEM((1, cols, LANES), f32),
            pltpu.VMEM((planes, cols, LANES), bf16),
            pltpu.VMEM((planes, cols + 2 * PAD, LANES), f32),
            pltpu.VMEM((planes, cols + 2 * PAD, LANES), f32),
            pltpu.VMEM((planes, cols + PAD, LANES), f32),
        ],
        compiler_params=params,
        name="rim_and_convolutions",
    )(scalars, below, above, ref_below, ref_above, own_taps, kernel_rim, bias_one, kernel_two, bias_two)
    return out.reshape(half_p, half_r, c2, half_x)


def solution(mesh):
    return jax.shard_map(
        on_device,
        mesh=mesh,
        in_specs=(
            P(("groups", "view"), None, None),
            P(("groups", "view"), None, None, None),
            P(("groups", "view"), None, None),
            P(("groups", "view")),
            P("groups", None),
            P(),
            P(),
            P(),
            P(),
        ),
        out_specs=P("groups", "view", None, None),
        check_vma=False,
    )
```

```python
import functools

import numpy as np

import jax
import jax.numpy as jnp
from jax import lax
from jax.experimental import pallas as pl
from jax.experimental.pallas import tpu as pltpu
from jax.sharding import PartitionSpec as P

SHIFT = 48
CAP = 2
LANES = 128
PAD = 8
CHUNK = 64
VMEM_LIMIT = 40 * 1024 * 1024


def passed_along(x, axis, by):
    count = lax.axis_size(axis)
    pairs = [(i, i + by) for i in range(count) if 0 <= i + by < count]
    return lax.ppermute(x, axis, pairs)


def request_places(pair_lists, tiles_dev):
    owners, ranks, tiles = [], [], []
    for s in range(pair_lists.shape[1]):
        for b in range(pair_lists.shape[2]):
            tile = pair_lists[0, s, b]
            whole = jnp.maximum(tile, 0)
            owner = jnp.where(tile >= 0, lax.div(whole, tiles_dev), -1)
            rank = jnp.int32(0)
            for other in owners:
                rank = rank + jnp.where(other == owner, 1, 0)
            owners.append(owner)
            ranks.append(rank)
            tiles.append(lax.rem(whole, tiles_dev))
    return owners, ranks, tiles


def request_kernel(tiles_dev, pair_lists, view_counts, table):
    owners, ranks, tiles = request_places(pair_lists, tiles_dev)
    row = lax.broadcasted_iota(jnp.int32, table.shape, 0)
    lane = lax.broadcasted_iota(jnp.int32, table.shape, 2)
    total = jnp.where(lane == CAP, view_counts[0], 0)
    for owner, rank, tile in zip(owners, ranks, tiles):
        total = jnp.where((row == owner) & (lane == rank), tile, total)
    table[...] = total


def gather_kernel(table, me, tiles, *rest):
    n_view = table.shape[0]
    outgoing, sem = rest[:n_view], rest[n_view]
    copies = []
    for k in range(n_view):
        d = lax.rem(me[0] + k, n_view)
        for j in range(CAP):
            copies.append(pltpu.make_async_copy(tiles.at[table[d, 0, j]], outgoing[k].at[j], sem.at[k, j]))
            copies[-1].start()
    for copy in copies:
        copy.wait()


def prepare_kernel(
    tiles_dev,
    places,
    first,
    second,
    bias_first,
    bias_second,
    disparities,
    pair_lists,
    view_counts,
    table,
    me,
    ref,
    _,
    kernel_own,
    kernel_rim,
    kernel_two,
    bias_one,
    bias_two,
    ref_last,
    ref_first,
    scalars,
    turned,
):
    planes, sources = disparities.shape
    n_view = table.shape[0]
    owners, ranks, _ = request_places(pair_lists, tiles_dev)
    at = 0
    for p in range(planes):
        for s in range(sources):
            scalars[at] = disparities[p, s]
            at += 1
    for owner, rank in zip(owners, ranks):
        back = lax.rem(me[0] - owner + n_view, n_view)
        scalars[at] = jnp.where(owner >= 0, back * CAP + rank, 0)
        at += 1
    up, down = jnp.maximum(me[0] - 1, 0), jnp.minimum(me[0] + 1, n_view - 1)
    scalars[at] = view_counts[0]
    scalars[at + 1] = table[up, 0, CAP]
    scalars[at + 2] = table[down, 0, CAP]
    scalars[at + 3] = me[0]

    rows_n = ref.shape[0]
    edge = ref_last.shape[0]
    for i in range(edge):
        ref_last[i] = ref[rows_n - edge + i]
    ref_first[0] = ref[0]

    deep = turned.shape[1]
    own_deep = kernel_own.shape[0] // 3
    rim_deep = kernel_rim.shape[0] // 3
    c1, channels = first.shape[3], first.shape[4]
    c2 = second.shape[4]
    half_r = bias_two.shape[0] // c2
    out_rows = 2 * half_r + 1
    width = out_rows * c1
    held = (LANES - width) // c1
    per_group = LANES // channels
    filler = jnp.zeros((c1, LANES - channels), jnp.float32)
    for a in range(3):
        turned[...] = jnp.zeros(turned.shape, jnp.float32)
        for d in range(3):
            taps = [jnp.concatenate([first[a, b, d].astype(jnp.float32), filler], axis=1) for b in range(3)]
            for r in range(out_rows):
                at = r * c1 + (LANES if d == 2 else 0)
                if d == 1:
                    at = width + (r * c1 if r < held else LANES + (r - held) * c1)
                for b in range(3):
                    place = places[r - 2 + b]
                    group, lane = place // per_group * LANES, place % per_group * channels
                    block = pltpu.roll(taps[b], lane, 1) if lane else taps[b]
                    turned[at : at + c1, group : group + LANES] += block
        band = turned[...].T.astype(jnp.bfloat16)
        kernel_own[a * own_deep : (a + 1) * own_deep, :] = band[:own_deep]
        kernel_rim[a * rim_deep : (a + 1) * rim_deep, :] = band[own_deep:]
    none = jnp.zeros((c1, c2), jnp.float32)
    for a in range(3):
        for d in range(3):
            taps = [second[a, b, d].astype(jnp.float32) for b in range(3)]
            stacked = jnp.concatenate(
                [
                    jnp.concatenate(
                        [taps[r - 2 * g] if 0 <= r - 2 * g < 3 else none for g in range(half_r)]
                        + [jnp.zeros((c1, LANES - half_r * c2), jnp.float32)],
                        axis=1,
                    )
                    for r in range(out_rows)
                ]
                + [jnp.zeros((LANES - width, LANES), jnp.float32)],
                axis=0,
            )
            at = (a * 3 + d) * LANES
            kernel_two[:, at : at + LANES] = stacked.T[: half_r * c2].astype(jnp.bfloat16)
    lane = lax.broadcasted_iota(jnp.int32, bias_one.shape, 1)
    total = jnp.zeros(bias_one.shape, jnp.float32)
    for o in range(c1):
        total = jnp.where(lane % c1 == o, bias_first[o], total)
    bias_one[...] = total
    row = lax.broadcasted_iota(jnp.int32, bias_two.shape, 0)
    total = jnp.zeros(bias_two.shape, jnp.float32)
    for k in range(c2):
        total = jnp.where(row % c2 == k, bias_second[k], total)
    bias_two[...] = total


def edge_kernel(n_view, blocks, at_slots, scalars, *rest):
    arrived, last, first = rest[-3:]
    channels = first.shape[1]
    for k in range(n_view):
        for j in range(CAP):
            arrived[k * CAP + j] = rest[k][j]
    for s in range(last.shape[0]):
        last[s] = arrived[scalars[at_slots + s * blocks + blocks - 1]]
        first[s] = arrived[scalars[at_slots + s * blocks], 0:channels, :]


def spread(slab, scale, wide, at):
    cols = slab.shape[1]
    band = jnp.zeros((SHIFT, LANES), jnp.float32)
    wide[at, 0:SHIFT, :] = band
    wide[at, SHIFT + cols : 2 * SHIFT + cols, :] = band
    wide[at, SHIFT : SHIFT + cols, :] = slab.astype(jnp.float32).T * scale


def plane_variance(p, at, sources, cols, disp, wide, ref_wide, ref_at, inv, store):
    for x0 in range(0, cols, CHUNK):
        ref = ref_wide[ref_at, x0 : x0 + CHUNK, :]
        summed = ref
        squares = ref * ref
        for s in range(sources):
            warped = wide[at + s, pl.ds(SHIFT + x0 - disp[p * sources + s], CHUNK), :]
            summed = summed + warped
            squares = squares + warped * warped
        mean = summed * inv
        store(x0, (squares * inv - mean * mean).astype(jnp.bfloat16))


def plane_taps(p, planes, var, kernel):
    deep = kernel.shape[0] // 3
    first, last = max(p - 1, 0), min(p + 2, planes)
    lhs = jnp.concatenate([var[q] for q in range(first, last)], axis=1)
    a0 = first - (p - 1)
    rhs = kernel[a0 * deep : (a0 + last - first) * deep, :]
    return jnp.dot(lhs, rhs, preferred_element_type=jnp.float32)


def own_kernel(at_slots, at_live, sources, scalars, arrived, ref, kernel, taps, wide, ref_wide, var):
    planes, cols, lanes = var.shape
    groups = lanes // LANES
    channels = ref.shape[1]
    per_group = LANES // channels
    blocks = ref.shape[0] * channels // arrived.shape[1]
    group_blocks = blocks // groups
    live = scalars[at_live]
    for g in range(groups):
        rows = [ref[g * per_group + i] for i in range(per_group)]
        ref_wide[g] = jnp.concatenate(rows, axis=0).astype(jnp.float32).T
        for s in range(sources):
            at = at_slots + s * blocks + g * group_blocks
            slab = jnp.concatenate([arrived[scalars[at + b]] for b in range(group_blocks)], axis=0)
            spread(slab, (s < live).astype(jnp.float32), wide, g * sources + s)
    inv = 1.0 / (live.astype(jnp.float32) + 1.0)
    for step in range(planes + 1):
        if step < planes:
            for g in range(groups):

                def store(x0, value):
                    var[step, x0 : x0 + CHUNK, g * LANES : (g + 1) * LANES] = value

                plane_variance(step, g * sources, sources, cols, scalars, wide, ref_wide, g, inv, store)
        if step > 0:
            taps[step - 1] = plane_taps(step - 1, planes, var, kernel)


def rim_kernel(
    c1,
    width,
    at_live,
    scalars,
    below,
    above,
    ref_below,
    ref_above,
    own_taps,
    kernel,
    bias_one,
    kernel_two,
    bias_two,
    out,
    wide,
    ref_wide,
    var,
    left,
    right,
    cost,
):
    planes, cols, _ = var.shape
    sources, channels = below.shape[0], below.shape[1]
    edge = ref_above.shape[0]
    is_below = lax.broadcasted_iota(jnp.int32, (1, LANES), 1) < channels
    live = jnp.where(is_below, scalars[at_live + 2], scalars[at_live + 1])
    filler = jnp.zeros((LANES - (edge + 1) * channels, cols), jnp.bfloat16)
    slab = jnp.concatenate([ref_below[0]] + [ref_above[i] for i in range(edge)] + [filler], axis=0)
    ref_wide[0] = slab.astype(jnp.float32).T
    for s in range(sources):
        slab = jnp.concatenate([below[s], above[s], filler], axis=0)
        spread(slab, (s < live).astype(jnp.float32), wide, s)
    inv = 1.0 / (live.astype(jnp.float32) + 1.0)

    held = LANES - width
    lane_at = lax.broadcasted_iota(jnp.int32, (cols, LANES), 1)
    keep = jnp.where((lane_at[:1] >= c1) | (scalars[at_live + 3] > 0), 1.0, 0.0)
    zeros = jnp.zeros((PAD, LANES), jnp.float32)
    out_w = out.shape[2]
    for step in range(planes + 1):
        if step < planes:

            def store(x0, value):
                var[step, x0 : x0 + CHUNK, :] = value

            plane_variance(step, 0, sources, cols, scalars, wide, ref_wide, 0, inv, store)
        if step == 0:
            continue
        p = step - 1
        taps = own_taps[p] + plane_taps(p, planes, var, kernel)
        t_left, t_right = taps[:, 0:LANES], taps[:, LANES : 2 * LANES]
        left[p, 0:PAD, :] = zeros
        left[p, PAD : PAD + cols, :] = t_left
        right[p, PAD : PAD + cols, :] = t_right
        right[p, PAD + cols : 2 * PAD + cols, :] = zeros
        center = jnp.where(
            lane_at < held,
            pltpu.roll(t_left, LANES - width, 1),
            pltpu.roll(t_right, LANES - (width - held), 1),
        )
        total = left[p, PAD - 1 : PAD - 1 + cols, :] + center + right[p, PAD + 1 : PAD + 1 + cols, :]
        cost[p, 0:PAD, :] = zeros
        cost[p, PAD : PAD + cols, :] = jnp.maximum(total + bias_one[...], 0.0) * keep
        if p % 2 == 0:
            continue
        q = p // 2
        parts = []
        a0 = 0
        for a in range(3):
            plane = 2 * q + a - 1
            if plane < 0:
                a0 = 1
                continue
            for d in range(3):
                parts.append(cost[plane, pl.ds(PAD + d - 1, out_w, stride=2), :].astype(jnp.bfloat16))
        lhs = jnp.concatenate(parts, axis=1)
        rhs = kernel_two[:, a0 * 3 * LANES :]
        result = lax.dot_general(rhs, lhs, (((1,), (1,)), ((), ())), preferred_element_type=jnp.float32)
        out[q] = result + bias_two[...]


def on_device(
    ref_features,
    source_tiles,
    pair_lists,
    view_counts,
    disparities,
    conv_first,
    bias_first,
    conv_second,
    bias_second,
):
    n_view = lax.axis_size("view")
    me = lax.axis_index("view").reshape(1)
    rows_n, channels, cols = ref_features.shape
    tiles_dev, tile_rows = source_tiles.shape[0], source_tiles.shape[1]
    sources, blocks = pair_lists.shape[1], pair_lists.shape[2]
    planes = disparities.shape[0]
    slab = tile_rows * channels
    groups = rows_n * channels // LANES
    c1, c2 = conv_first.shape[2], conv_second.shape[0]
    width = (rows_n + 1) * c1
    half_r, half_p, half_x = rows_n // 2, planes // 2, cols // 2
    own_deep = groups * LANES
    smem = pl.BlockSpec(memory_space=pltpu.SMEM)
    vmem = pl.BlockSpec(memory_space=pltpu.VMEM)
    anywhere = pl.BlockSpec(memory_space=pl.ANY)
    params = pltpu.CompilerParams(vmem_limit_bytes=VMEM_LIMIT)
    bf16, f32, i32 = jnp.bfloat16, jnp.float32, jnp.int32

    table = pl.pallas_call(
        functools.partial(request_kernel, tiles_dev),
        out_shape=jax.ShapeDtypeStruct((n_view, 1, CAP + 1), i32),
        in_specs=[smem, smem],
        out_specs=vmem,
        compiler_params=params,
        name="request_table",
    )(pair_lists, view_counts)
    table = lax.all_to_all(table, "view", split_axis=0, concat_axis=0, tiled=True)
    bundle = jax.ShapeDtypeStruct((CAP, slab, cols), bf16)
    outgoing = pl.pallas_call(
        gather_kernel,
        out_shape=[bundle] * n_view,
        in_specs=[smem, smem, anywhere],
        out_specs=[vmem] * n_view,
        scratch_shapes=[pltpu.SemaphoreType.DMA((n_view, CAP))],
        compiler_params=params,
        name="requested_tiles",
    )(table, me, source_tiles.reshape(tiles_dev, slab, cols))
    bundles = list(outgoing)
    for k in sorted(range(1, n_view), key=lambda k: -min(k, n_view - k)):
        bundles[k] = lax.ppermute(outgoing[k], "view", [(i, (i + k) % n_view) for i in range(n_view)])

    at_slots = planes * sources
    at_live = at_slots + sources * blocks
    places = {row: row for row in range(rows_n + 1)}
    places.update({row - tile_rows: rows_n + 1 + row for row in range(tile_rows)})
    shape = jax.ShapeDtypeStruct
    prepared = pl.pallas_call(
        functools.partial(prepare_kernel, tiles_dev, places),
        out_shape=[
            shape((3 * own_deep, 2 * LANES), bf16),
            shape((3 * LANES, 2 * LANES), bf16),
            shape((half_r * c2, 9 * LANES), bf16),
            shape((1, LANES), f32),
            shape((half_r * c2, half_x), f32),
            shape((tile_rows, channels, cols), bf16),
            shape((1, channels, cols), bf16),
            shape((at_live + 4,), i32),
        ],
        in_specs=[vmem, vmem] + [smem] * 7 + [vmem, anywhere],
        out_specs=[vmem] * 7 + [smem],
        scratch_shapes=[pltpu.VMEM((2 * LANES, own_deep + LANES), f32)],
        compiler_params=params,
        name="weights_and_scalars",
    )(
        conv_first.transpose(0, 1, 3, 2, 4),
        conv_second.transpose(1, 2, 3, 4, 0),
        bias_first,
        bias_second,
        disparities,
        pair_lists,
        view_counts,
        table,
        me,
        ref_features,
        bundles[n_view // 2],
    )
    kernel_own, kernel_rim, kernel_two, bias_one, bias_two, ref_last, ref_first, scalars = prepared
    ref_above = passed_along(ref_last, "view", 1)
    ref_below = passed_along(ref_first, "view", -1)

    arrived, last, first = pl.pallas_call(
        functools.partial(edge_kernel, n_view, blocks, at_slots),
        out_shape=[
            shape((n_view * CAP, slab, cols), bf16),
            shape((sources, slab, cols), bf16),
            shape((sources, channels, cols), bf16),
        ],
        in_specs=[smem] + [vmem] * n_view + [anywhere, anywhere],
        out_specs=[vmem] * 3,
        compiler_params=params,
        name="edge_tiles",
    )(scalars, *bundles, ref_above, ref_below)
    above = passed_along(last, "view", 1)
    below = passed_along(first, "view", -1)

    own_taps = pl.pallas_call(
        functools.partial(own_kernel, at_slots, at_live, sources),
        out_shape=shape((planes, cols, 2 * LANES), f32),
        in_specs=[smem] + [vmem] * 3,
        out_specs=vmem,
        scratch_shapes=[
            pltpu.VMEM((groups * sources, cols + 2 * SHIFT, LANES), f32),
            pltpu.VMEM((groups, cols, LANES), f32),
            pltpu.VMEM((planes, cols, own_deep), bf16),
        ],
        compiler_params=params,
        name="own_rows",
    )(scalars, arrived, ref_features, kernel_own)

    out = pl.pallas_call(
        functools.partial(rim_kernel, c1, width, at_live),
        out_shape=shape((half_p, half_r * c2, half_x), f32),
        in_specs=[smem] + [vmem] * 9,
        out_specs=vmem,
        scratch_shapes=[
            pltpu.VMEM((sources, cols + 2 * SHIFT, LANES), f32),
            pltpu.VMEM((1, cols, LANES), f32),
            pltpu.VMEM((planes, cols, LANES), bf16),
            pltpu.VMEM((planes, cols + 2 * PAD, LANES), f32),
            pltpu.VMEM((planes, cols + 2 * PAD, LANES), f32),
            pltpu.VMEM((planes, cols + PAD, LANES), f32),
        ],
        compiler_params=params,
        name="rim_and_convolutions",
    )(scalars, below, above, ref_below, ref_above, own_taps, kernel_rim, bias_one, kernel_two, bias_two)
    return out.reshape(half_p, half_r, c2, half_x)


def solution(mesh):
    return jax.shard_map(
        on_device,
        mesh=mesh,
        in_specs=(
            P(("groups", "view"), None, None),
            P(("groups", "view"), None, None, None),
            P(("groups", "view"), None, None),
            P(("groups", "view")),
            P("groups", None),
            P(),
            P(),
            P(),
            P(),
        ),
        out_specs=P("groups", "view", None, None),
        check_vma=False,
    )
```

```python
import functools

import numpy as np

import jax
import jax.numpy as jnp
from jax import lax
from jax.experimental import pallas as pl
from jax.experimental.pallas import tpu as pltpu
from jax.sharding import PartitionSpec as P

SHIFT = 48
CAP = 2
LANES = 128
PAD = 8
CHUNK = 64
VMEM_LIMIT = 40 * 1024 * 1024


def swapped(x, axis, parity):
    count = lax.axis_size(axis)
    pairs = [(i, i + 1) for i in range(parity, count - 1, 2)]
    return lax.ppermute(x, axis, pairs + [(j, i) for i, j in pairs])


def request_places(pair_lists, tiles_dev):
    owners, ranks, tiles = [], [], []
    for s in range(pair_lists.shape[1]):
        for b in range(pair_lists.shape[2]):
            tile = pair_lists[0, s, b]
            whole = jnp.maximum(tile, 0)
            owner = jnp.where(tile >= 0, lax.div(whole, tiles_dev), -1)
            rank = jnp.int32(0)
            for other in owners:
                rank = rank + jnp.where(other == owner, 1, 0)
            owners.append(owner)
            ranks.append(rank)
            tiles.append(lax.rem(whole, tiles_dev))
    return owners, ranks, tiles


def request_kernel(tiles_dev, pair_lists, view_counts, table):
    owners, ranks, tiles = request_places(pair_lists, tiles_dev)
    row = lax.broadcasted_iota(jnp.int32, table.shape, 0)
    lane = lax.broadcasted_iota(jnp.int32, table.shape, 2)
    total = jnp.where(lane == CAP, view_counts[0], 0)
    for owner, rank, tile in zip(owners, ranks, tiles):
        total = jnp.where((row == owner) & (lane == rank), tile, total)
    table[...] = total


def prepare_kernel(
    tiles_dev,
    places,
    first,
    second,
    bias_first,
    bias_second,
    disparities,
    pair_lists,
    view_counts,
    table,
    me,
    kernel_own,
    kernel_rim,
    kernel_two,
    bias_one,
    bias_two,
    scalars,
    turned,
):
    planes, sources = disparities.shape
    blocks = pair_lists.shape[2]
    owners, ranks, _ = request_places(pair_lists, tiles_dev)
    at = 0
    for p in range(planes):
        for s in range(sources):
            scalars[at] = disparities[p, s]
            at += 1
    for owner, rank in zip(owners, ranks):
        scalars[at] = jnp.where(owner >= 0, owner * CAP + rank, 0)
        at += 1
    n_view = table.shape[0]
    up, down = jnp.maximum(me[0] - 1, 0), jnp.minimum(me[0] + 1, n_view - 1)
    scalars[at] = view_counts[0]
    scalars[at + 1] = table[up, 0, CAP]
    scalars[at + 2] = table[down, 0, CAP]
    scalars[at + 3] = me[0]
    scalars[at + 4] = lax.rem(me[0], 2)

    deep = turned.shape[1]
    own_deep = kernel_own.shape[0] // 3
    rim_deep = kernel_rim.shape[0] // 3
    c1, channels = first.shape[3], first.shape[4]
    c2 = second.shape[4]
    half_r = bias_two.shape[0] // c2
    out_rows = 2 * half_r + 1
    width = out_rows * c1
    held = (LANES - width) // c1
    per_group = LANES // channels
    filler = jnp.zeros((c1, LANES - channels), jnp.float32)
    for a in range(3):
        turned[...] = jnp.zeros(turned.shape, jnp.float32)
        for d in range(3):
            taps = [jnp.concatenate([first[a, b, d].astype(jnp.float32), filler], axis=1) for b in range(3)]
            for r in range(out_rows):
                at = r * c1 + (LANES if d == 2 else 0)
                if d == 1:
                    at = width + (r * c1 if r < held else LANES + (r - held) * c1)
                for b in range(3):
                    place = places[r - 2 + b]
                    group, lane = place // per_group * LANES, place % per_group * channels
                    block = pltpu.roll(taps[b], lane, 1) if lane else taps[b]
                    turned[at : at + c1, group : group + LANES] += block
        band = turned[...].T.astype(jnp.bfloat16)
        kernel_own[a * own_deep : (a + 1) * own_deep, :] = band[:own_deep]
        kernel_rim[a * rim_deep : (a + 1) * rim_deep, :] = band[own_deep:]
    none = jnp.zeros((c1, c2), jnp.float32)
    for a in range(3):
        for d in range(3):
            taps = [second[a, b, d].astype(jnp.float32) for b in range(3)]
            stacked = jnp.concatenate(
                [
                    jnp.concatenate(
                        [taps[r - 2 * g] if 0 <= r - 2 * g < 3 else none for g in range(half_r)]
                        + [jnp.zeros((c1, LANES - half_r * c2), jnp.float32)],
                        axis=1,
                    )
                    for r in range(out_rows)
                ]
                + [jnp.zeros((LANES - width, LANES), jnp.float32)],
                axis=0,
            )
            at = (a * 3 + d) * LANES
            kernel_two[:, at : at + LANES] = stacked.T[: half_r * c2].astype(jnp.bfloat16)
    lane = lax.broadcasted_iota(jnp.int32, bias_one.shape, 1)
    total = jnp.zeros(bias_one.shape, jnp.float32)
    for o in range(c1):
        total = jnp.where(lane % c1 == o, bias_first[o], total)
    bias_one[...] = total
    row = lax.broadcasted_iota(jnp.int32, bias_two.shape, 0)
    total = jnp.zeros(bias_two.shape, jnp.float32)
    for k in range(c2):
        total = jnp.where(row % c2 == k, bias_second[k], total)
    bias_two[...] = total


def edge_kernel(blocks, at_slots, at_live, scalars, arrived, ref, *rest):
    far, near = rest[-2:]
    sources = far.shape[0] - 1
    odd = scalars[at_live + 4]
    for into, block in ((far, odd * (blocks - 1)), (near, (1 - odd) * (blocks - 1))):
        for s in range(sources):
            into[s] = arrived[scalars[at_slots + s * blocks + block]]
        into[sources] = ref[block]


def spread(slab, scale, wide, at):
    cols = slab.shape[1]
    band = jnp.zeros((SHIFT, LANES), jnp.float32)
    wide[at, 0:SHIFT, :] = band
    wide[at, SHIFT + cols : 2 * SHIFT + cols, :] = band
    wide[at, SHIFT : SHIFT + cols, :] = slab.astype(jnp.float32).T * scale


def plane_variance(p, at, sources, cols, disp, wide, ref_wide, ref_at, inv, store):
    for x0 in range(0, cols, CHUNK):
        ref = ref_wide[ref_at, x0 : x0 + CHUNK, :]
        summed = ref
        squares = ref * ref
        for s in range(sources):
            warped = wide[at + s, pl.ds(SHIFT + x0 - disp[p * sources + s], CHUNK), :]
            summed = summed + warped
            squares = squares + warped * warped
        mean = summed * inv
        store(x0, (squares * inv - mean * mean).astype(jnp.bfloat16))


def plane_taps(p, planes, var, kernel):
    deep = kernel.shape[0] // 3
    first, last = max(p - 1, 0), min(p + 2, planes)
    lhs = jnp.concatenate([var[q] for q in range(first, last)], axis=1)
    a0 = first - (p - 1)
    rhs = kernel[a0 * deep : (a0 + last - first) * deep, :]
    return jnp.dot(lhs, rhs, preferred_element_type=jnp.float32)


def own_kernel(at_slots, at_live, sources, scalars, arrived, ref, kernel, taps, wide, ref_wide, var):
    planes, cols, lanes = var.shape
    groups = lanes // LANES
    channels = ref.shape[1]
    per_group = LANES // channels
    blocks = ref.shape[0] * channels // arrived.shape[1]
    group_blocks = blocks // groups
    live = scalars[at_live]
    for g in range(groups):
        rows = [ref[g * per_group + i] for i in range(per_group)]
        ref_wide[g] = jnp.concatenate(rows, axis=0).astype(jnp.float32).T
        for s in range(sources):
            at = at_slots + s * blocks + g * group_blocks
            slab = jnp.concatenate([arrived[scalars[at + b]] for b in range(group_blocks)], axis=0)
            spread(slab, (s < live).astype(jnp.float32), wide, g * sources + s)
    inv = 1.0 / (live.astype(jnp.float32) + 1.0)
    for step in range(planes + 1):
        if step < planes:
            for g in range(groups):

                def store(x0, value):
                    var[step, x0 : x0 + CHUNK, g * LANES : (g + 1) * LANES] = value

                plane_variance(step, g * sources, sources, cols, scalars, wide, ref_wide, g, inv, store)
        if step > 0:
            taps[step - 1] = plane_taps(step - 1, planes, var, kernel)


def rim_kernel(
    tile_rows,
    c1,
    width,
    at_live,
    scalars,
    far,
    near,
    own_taps,
    kernel,
    bias_one,
    kernel_two,
    bias_two,
    out,
    wide,
    ref_wide,
    var,
    left,
    right,
    cost,
):
    planes, cols, _ = var.shape
    sources, slab_rows = far.shape[0] - 1, far.shape[1]
    channels = slab_rows // tile_rows
    is_below = lax.broadcasted_iota(jnp.int32, (1, LANES), 1) < channels
    live = jnp.where(is_below, scalars[at_live + 2], scalars[at_live + 1])
    filler = jnp.zeros((LANES - channels - slab_rows, cols), jnp.bfloat16)
    odd = scalars[at_live + 4] > 0

    def slab(s):
        below = jnp.where(odd, far[s, 0:channels, :], near[s, 0:channels, :])
        above = jnp.where(odd, near[s], far[s])
        return jnp.concatenate([below, above, filler], axis=0)

    ref_wide[0] = slab(sources).astype(jnp.float32).T
    for s in range(sources):
        spread(slab(s), (s < live).astype(jnp.float32), wide, s)
    inv = 1.0 / (live.astype(jnp.float32) + 1.0)

    held = LANES - width
    lane_at = lax.broadcasted_iota(jnp.int32, (cols, LANES), 1)
    keep = jnp.where((lane_at[:1] >= c1) | (scalars[at_live + 3] > 0), 1.0, 0.0)
    zeros = jnp.zeros((PAD, LANES), jnp.float32)
    out_w = out.shape[2]
    for step in range(planes + 1):
        if step < planes:

            def store(x0, value):
                var[step, x0 : x0 + CHUNK, :] = value

            plane_variance(step, 0, sources, cols, scalars, wide, ref_wide, 0, inv, store)
        if step == 0:
            continue
        p = step - 1
        taps = own_taps[p] + plane_taps(p, planes, var, kernel)
        t_left, t_right = taps[:, 0:LANES], taps[:, LANES : 2 * LANES]
        left[p, 0:PAD, :] = zeros
        left[p, PAD : PAD + cols, :] = t_left
        right[p, PAD : PAD + cols, :] = t_right
        right[p, PAD + cols : 2 * PAD + cols, :] = zeros
        center = jnp.where(
            lane_at < held,
            pltpu.roll(t_left, LANES - width, 1),
            pltpu.roll(t_right, LANES - (width - held), 1),
        )
        total = left[p, PAD - 1 : PAD - 1 + cols, :] + center + right[p, PAD + 1 : PAD + 1 + cols, :]
        cost[p, 0:PAD, :] = zeros
        cost[p, PAD : PAD + cols, :] = jnp.maximum(total + bias_one[...], 0.0) * keep
        if p % 2 == 0:
            continue
        q = p // 2
        parts = []
        a0 = 0
        for a in range(3):
            plane = 2 * q + a - 1
            if plane < 0:
                a0 = 1
                continue
            for d in range(3):
                parts.append(cost[plane, pl.ds(PAD + d - 1, out_w, stride=2), :].astype(jnp.bfloat16))
        lhs = jnp.concatenate(parts, axis=1)
        rhs = kernel_two[:, a0 * 3 * LANES :]
        result = lax.dot_general(rhs, lhs, (((1,), (1,)), ((), ())), preferred_element_type=jnp.float32)
        out[q] = result + bias_two[...]


def on_device(
    ref_features,
    source_tiles,
    pair_lists,
    view_counts,
    disparities,
    conv_first,
    bias_first,
    conv_second,
    bias_second,
):
    n_view = lax.axis_size("view")
    me = lax.axis_index("view").reshape(1)
    rows_n, channels, cols = ref_features.shape
    tiles_dev, tile_rows = source_tiles.shape[0], source_tiles.shape[1]
    sources, blocks = pair_lists.shape[1], pair_lists.shape[2]
    planes = disparities.shape[0]
    slab = tile_rows * channels
    groups = rows_n * channels // LANES
    c1, c2 = conv_first.shape[2], conv_second.shape[0]
    width = (rows_n + 1) * c1
    half_r, half_p, half_x = rows_n // 2, planes // 2, cols // 2
    own_deep = groups * LANES
    smem = pl.BlockSpec(memory_space=pltpu.SMEM)
    vmem = pl.BlockSpec(memory_space=pltpu.VMEM)
    anywhere = pl.BlockSpec(memory_space=pl.ANY)
    params = pltpu.CompilerParams(vmem_limit_bytes=VMEM_LIMIT)
    bf16, f32, i32 = jnp.bfloat16, jnp.float32, jnp.int32

    table = pl.pallas_call(
        functools.partial(request_kernel, tiles_dev),
        out_shape=jax.ShapeDtypeStruct((n_view, 1, CAP + 1), i32),
        in_specs=[smem, smem],
        out_specs=vmem,
        compiler_params=params,
        name="request_table",
    )(pair_lists, view_counts)
    table = lax.all_to_all(table, "view", split_axis=0, concat_axis=0, tiled=True)
    outgoing = source_tiles.reshape(tiles_dev, slab, cols)[table[:, 0, :CAP]]
    arrived = lax.all_to_all(outgoing, "view", split_axis=0, concat_axis=0, tiled=True)
    arrived = arrived.reshape(n_view * CAP, slab, cols)

    at_slots = planes * sources
    at_live = at_slots + sources * blocks
    places = {row: row for row in range(rows_n + 1)}
    places.update({row - tile_rows: rows_n + 1 + row for row in range(tile_rows)})
    shape = jax.ShapeDtypeStruct
    prepared = pl.pallas_call(
        functools.partial(prepare_kernel, tiles_dev, places),
        out_shape=[
            shape((3 * own_deep, 2 * LANES), bf16),
            shape((3 * LANES, 2 * LANES), bf16),
            shape((half_r * c2, 9 * LANES), bf16),
            shape((1, LANES), f32),
            shape((half_r * c2, half_x), f32),
            shape((at_live + 5,), i32),
        ],
        in_specs=[vmem, vmem] + [smem] * 7,
        out_specs=[vmem] * 5 + [smem],
        scratch_shapes=[pltpu.VMEM((2 * LANES, own_deep + LANES), f32)],
        compiler_params=params,
        name="weights_and_scalars",
    )(
        conv_first.transpose(0, 1, 3, 2, 4),
        conv_second.transpose(1, 2, 3, 4, 0),
        bias_first,
        bias_second,
        disparities,
        pair_lists,
        view_counts,
        table,
        me,
    )
    kernel_own, kernel_rim, kernel_two, bias_one, bias_two, scalars = prepared

    payload = shape((sources + 1, slab, cols), bf16)
    far, near = pl.pallas_call(
        functools.partial(edge_kernel, blocks, at_slots, at_live),
        out_shape=[payload, payload],
        in_specs=[smem, vmem, vmem, anywhere],
        out_specs=[vmem, vmem],
        compiler_params=params,
        name="edge_tiles",
    )(scalars, arrived, ref_features.reshape(blocks, slab, cols), bias_one)
    far = swapped(far, "view", 1)
    near = swapped(near, "view", 0)

    own_taps = pl.pallas_call(
        functools.partial(own_kernel, at_slots, at_live, sources),
        out_shape=shape((planes, cols, 2 * LANES), f32),
        in_specs=[smem] + [vmem] * 3,
        out_specs=vmem,
        scratch_shapes=[
            pltpu.VMEM((groups * sources, cols + 2 * SHIFT, LANES), f32),
            pltpu.VMEM((groups, cols, LANES), f32),
            pltpu.VMEM((planes, cols, own_deep), bf16),
        ],
        compiler_params=params,
        name="own_rows",
    )(scalars, arrived, ref_features, kernel_own)

    out = pl.pallas_call(
        functools.partial(rim_kernel, tile_rows, c1, width, at_live),
        out_shape=shape((half_p, half_r * c2, half_x), f32),
        in_specs=[smem] + [vmem] * 7,
        out_specs=vmem,
        scratch_shapes=[
            pltpu.VMEM((sources, cols + 2 * SHIFT, LANES), f32),
            pltpu.VMEM((1, cols, LANES), f32),
            pltpu.VMEM((planes, cols, LANES), bf16),
            pltpu.VMEM((planes, cols + 2 * PAD, LANES), f32),
            pltpu.VMEM((planes, cols + 2 * PAD, LANES), f32),
            pltpu.VMEM((planes, cols + PAD, LANES), f32),
        ],
        compiler_params=params,
        name="rim_and_convolutions",
    )(scalars, far, near, own_taps, kernel_rim, bias_one, kernel_two, bias_two)
    return out.reshape(half_p, half_r, c2, half_x)


def solution(mesh):
    return jax.shard_map(
        on_device,
        mesh=mesh,
        in_specs=(
            P(("groups", "view"), None, None),
            P(("groups", "view"), None, None, None),
            P(("groups", "view"), None, None),
            P(("groups", "view")),
            P("groups", None),
            P(),
            P(),
            P(),
            P(),
        ),
        out_specs=P("groups", "view", None, None),
        check_vma=False,
    )
```

```python
import functools

import numpy as np

import jax
import jax.numpy as jnp
from jax import lax
from jax.experimental import pallas as pl
from jax.experimental.pallas import tpu as pltpu
from jax.sharding import PartitionSpec as P

SHIFT = 48
CAP = 2
LANES = 128
PAD = 8
CHUNK = 64
VMEM_LIMIT = 40 * 1024 * 1024


def swapped(x, axis, parity):
    count = lax.axis_size(axis)
    pairs = [(i, i + 1) for i in range(parity, count - 1, 2)]
    return lax.ppermute(x, axis, pairs + [(j, i) for i, j in pairs])


def request_places(pair_lists, tiles_dev):
    owners, ranks, tiles = [], [], []
    for s in range(pair_lists.shape[1]):
        for b in range(pair_lists.shape[2]):
            tile = pair_lists[0, s, b]
            whole = jnp.maximum(tile, 0)
            owner = jnp.where(tile >= 0, lax.div(whole, tiles_dev), -1)
            rank = jnp.int32(0)
            for other in owners:
                rank = rank + jnp.where(other == owner, 1, 0)
            owners.append(owner)
            ranks.append(rank)
            tiles.append(lax.rem(whole, tiles_dev))
    return owners, ranks, tiles


def request_kernel(tiles_dev, pair_lists, table):
    owners, ranks, tiles = request_places(pair_lists, tiles_dev)
    row = lax.broadcasted_iota(jnp.int32, table.shape, 0)
    lane = lax.broadcasted_iota(jnp.int32, table.shape, 2)
    total = jnp.zeros(table.shape, jnp.int32)
    for owner, rank, tile in zip(owners, ranks, tiles):
        total = jnp.where((row == owner) & (lane == rank), tile, total)
    table[...] = total


def prepare_kernel(
    tiles_dev,
    edge_rows,
    mid_rows,
    first,
    second,
    bias_first,
    bias_second,
    disparities,
    pair_lists,
    view_counts,
    me,
    _,
    kernel_edge,
    kernel_mid,
    two_mid,
    two_edge,
    bias_lanes,
    bias_rows,
    bias_two,
    scalars,
    turned,
    stacked,
):
    planes, sources = disparities.shape
    owners, ranks, _ = request_places(pair_lists, tiles_dev)
    at = 0
    for p in range(planes):
        for s in range(sources):
            scalars[at] = disparities[p, s]
            at += 1
    for owner, rank in zip(owners, ranks):
        scalars[at] = jnp.where(owner >= 0, owner * CAP + rank, 0)
        at += 1
    scalars[at] = view_counts[0]
    scalars[at + 1] = me[0]
    scalars[at + 2] = lax.rem(me[0], 2)

    c1, channels = first.shape[3], first.shape[4]
    c2 = second.shape[4]
    rows_n = len(edge_rows) + len(mid_rows)
    half_r = rows_n // 2
    place = {row: i for i, row in enumerate(edge_rows + mid_rows)}
    per_group = LANES // channels
    filler = jnp.zeros((c1, LANES - channels), jnp.float32)
    taps = {}
    for a in range(3):
        for b in range(3):
            for d in range(3):
                tap = jnp.concatenate([first[a, b, d].astype(jnp.float32), filler], axis=1)
                for turn in range(per_group):
                    lane = turn * channels
                    taps[a, b, d, turn] = pltpu.roll(tap, lane, 1) if lane else tap

    def band(a, d, r, group):
        total = jnp.zeros((c1, LANES), jnp.float32)
        for b in range(3):
            at_place = place.get(r - 1 + b, -1)
            if at_place >= 0 and at_place // per_group == group:
                total = total + taps[a, b, d, at_place % per_group]
        return total

    rim = (-1, 0, rows_n - 1, rows_n)
    for d in range(3):
        for i, r in enumerate(rim):
            at = (d * len(rim) + i) * c1
            for a in range(3):
                kernel_edge[at : at + c1, a * LANES : (a + 1) * LANES] = band(a, d, r, 0)
    inner = range(1, rows_n - 1)
    width = len(inner) * c1
    for a in range(3):
        turned[...] = jnp.zeros(turned.shape, jnp.float32)
        for d, start in ((0, 0), (2, width), (1, LANES)):
            for r in inner:
                at = start + (r - 1) * c1
                for group in range(2):
                    turned[at : at + c1, group * LANES : (group + 1) * LANES] = band(a, d, r, group)
        kernel_mid[a * 2 * LANES : (a + 1) * 2 * LANES, :] = turned[...].T.astype(jnp.bfloat16)

    def second_rows(a, d, rows):
        parts = []
        for r in rows:
            blocks = []
            for g in range(half_r):
                b = -1 if r is None else r - 2 * g + 1
                hit = 0 <= b < 3
                blocks.append(second[a, b, d].astype(jnp.float32) if hit else jnp.zeros((c1, c2), jnp.float32))
            blocks.append(jnp.zeros((c1, LANES - half_r * c2), jnp.float32))
            parts.append(jnp.concatenate(blocks, axis=1))
        return jnp.concatenate(parts, axis=0)

    lane_rows = list(inner) + [None] * (LANES // c1 - len(inner))
    stacked[...] = jnp.zeros(stacked.shape, jnp.float32)
    for a in range(3):
        for d in range(3):
            at = (a * 3 + d) * LANES
            two_mid[:, at : at + LANES] = second_rows(a, d, lane_rows).T[: half_r * c2].astype(jnp.bfloat16)
            at = (a * 3 + d) * len(rim) * c1
            stacked[at : at + len(rim) * c1, :] = second_rows(a, d, rim[:3] + (None,))
    two_edge[...] = stacked[...].T[: half_r * c2].astype(jnp.bfloat16)

    def spread_bias(like, axis, bias):
        index = lax.broadcasted_iota(jnp.int32, like.shape, axis)
        total = jnp.zeros(like.shape, jnp.float32)
        for i in range(bias.shape[0]):
            total = jnp.where(index % bias.shape[0] == i, bias[i], total)
        like[...] = total

    spread_bias(bias_lanes, 1, bias_first)
    spread_bias(bias_rows, 0, bias_first)
    spread_bias(bias_two, 0, bias_second)


def spread(slab, scale, wide, at):
    cols = slab.shape[1]
    band = jnp.zeros((SHIFT, LANES), jnp.float32)
    wide[at, 0:SHIFT, :] = band
    wide[at, SHIFT + cols : 2 * SHIFT + cols, :] = band
    wide[at, SHIFT : SHIFT + cols, :] = slab.astype(jnp.float32).T * scale


def plane_variance(p, at, sources, cols, disp, wide, ref_wide, ref_at, inv, store):
    for x0 in range(0, cols, CHUNK):
        ref = ref_wide[ref_at, x0 : x0 + CHUNK, :]
        summed = ref
        squares = ref * ref
        for s in range(sources):
            warped = wide[at + s, pl.ds(SHIFT + x0 - disp[p * sources + s], CHUNK), :]
            summed = summed + warped
            squares = squares + warped * warped
        mean = summed * inv
        store(x0, (squares * inv - mean * mean).astype(jnp.bfloat16))


def load_group(at_slots, live, sources, blocks, picks, scalars, arrived, ref, wide, ref_wide):
    tile_rows = ref.shape[0] // blocks
    rows = [ref[block * tile_rows + i] for block in picks for i in range(tile_rows)]
    ref_wide[0] = jnp.concatenate(rows, axis=0).astype(jnp.float32).T
    for s in range(sources):
        slab = jnp.concatenate([arrived[scalars[at_slots + s * blocks + block]] for block in picks], axis=0)
        spread(slab, (s < live).astype(jnp.float32), wide, s)


def near_planes(p, planes, deep):
    first, last = max(p - 1, 0), min(p + 2, planes)
    return range(first, last), (first - p + 1) * deep, (last - p + 1) * deep


def edge_kernel(
    at_slots, at_live, sources, blocks, picks, scalars, arrived, ref, kernel, var, own, far, near, wide, ref_wide
):
    planes, cols, _ = var.shape
    c1 = kernel.shape[0] // 12
    live = scalars[at_live]
    odd = scalars[at_live + 2] > 0
    load_group(at_slots, live, sources, blocks, picks, scalars, arrived, ref, wide, ref_wide)
    inv = 1.0 / (live.astype(jnp.float32) + 1.0)
    weights = kernel[...].astype(jnp.bfloat16)
    column = lax.broadcasted_iota(jnp.int32, (4 * c1, cols), 1)
    empty = jnp.zeros((c1, cols), jnp.float32)
    for step in range(planes + 1):
        if step < planes:

            def store(x0, value):
                var[step, x0 : x0 + CHUNK, :] = value

            plane_variance(step, 0, sources, cols, scalars, wide, ref_wide, 0, inv, store)
        if step == 0:
            continue
        p = step - 1
        read, start, stop = near_planes(p, planes, LANES)
        lhs = jnp.concatenate([var[q] for q in read], axis=1)
        taps = lax.dot_general(
            weights[:, start:stop], lhs, (((1,), (1,)), ((), ())), preferred_element_type=jnp.float32
        )
        left, center, right = taps[: 4 * c1], taps[4 * c1 : 8 * c1], taps[8 * c1 :]
        total = center + jnp.where(column > 0, pltpu.roll(left, 1, 1), 0.0)
        total = total + jnp.where(column < cols - 1, pltpu.roll(right, cols - 1, 1), 0.0)
        own[p] = total[: 3 * c1]
        downward = total[2 * c1 :]
        upward = jnp.concatenate([total[:c1], empty], axis=0)
        far[p] = jnp.where(odd, downward, upward).astype(jnp.bfloat16)
        near[p] = jnp.where(odd, upward, downward).astype(jnp.bfloat16)


def mid_kernel(
    at_slots,
    at_live,
    sources,
    blocks,
    picks,
    width,
    scalars,
    arrived,
    ref,
    edge_var,
    kernel,
    bias_lanes,
    kernel_two,
    bias_two,
    out,
    wide,
    ref_wide,
    var,
    sides,
    cost,
):
    planes, cols, _ = var.shape
    live = scalars[at_live]
    load_group(at_slots, live, sources, blocks, picks, scalars, arrived, ref, wide, ref_wide)
    inv = 1.0 / (live.astype(jnp.float32) + 1.0)
    zeros = jnp.zeros((PAD, LANES), jnp.float32)
    out_w = out.shape[2]
    for step in range(planes + 1):
        if step < planes:

            def store(x0, value):
                var[step, x0 : x0 + CHUNK, :] = value

            plane_variance(step, 0, sources, cols, scalars, wide, ref_wide, 0, inv, store)
        if step == 0:
            continue
        p = step - 1
        read, start, stop = near_planes(p, planes, 2 * LANES)
        lhs = jnp.concatenate([part for q in read for part in (edge_var[q], var[q])], axis=1)
        taps = jnp.dot(lhs, kernel[start:stop, :], preferred_element_type=jnp.float32)
        sides[p, 0:PAD, :] = zeros
        sides[p, PAD : PAD + cols, :] = taps[:, :LANES]
        sides[p, PAD + cols : 2 * PAD + cols, :] = zeros
        right = pltpu.roll(sides[p, PAD + 1 : PAD + 1 + cols, :], LANES - width, 1)
        total = sides[p, PAD - 1 : PAD - 1 + cols, :] + taps[:, LANES:] + right
        cost[p, 0:PAD, :] = zeros
        cost[p, PAD : PAD + cols, :] = jnp.maximum(total + bias_lanes[...], 0.0)
        if p % 2 == 0:
            continue
        q = p // 2
        read, start, stop = near_planes(2 * q, planes, 3 * LANES)
        parts = [
            cost[plane, pl.ds(PAD + d - 1, out_w, stride=2), :].astype(jnp.bfloat16) for plane in read for d in range(3)
        ]
        lhs = jnp.concatenate(parts, axis=1)
        result = lax.dot_general(
            kernel_two[:, start:stop], lhs, (((1,), (1,)), ((), ())), preferred_element_type=jnp.float32
        )
        out[q] = result + bias_two[...]


def end_kernel(at_live, scalars, far, near, own, partial, bias_rows, kernel_two, out):
    planes, ends, cols = own.shape
    c1 = ends // 3
    out_w = out.shape[2]
    odd = scalars[at_live + 2] > 0
    not_top = (scalars[at_live + 1] > 0).astype(jnp.float32)
    empty = jnp.zeros((c1, cols), jnp.float32)
    bias = bias_rows[...]
    rows = []
    for p in range(planes):
        lower, upper = far[p].astype(jnp.float32), near[p].astype(jnp.float32)
        above = jnp.where(odd, upper, lower)
        below = jnp.where(odd, lower, upper)
        ready = jnp.maximum(own[p] + jnp.concatenate([above, below[:c1]], axis=0) + bias, 0.0)
        rows += [ready[:c1] * not_top, ready[c1:], empty]
    cost = jnp.concatenate(rows, axis=0).astype(jnp.bfloat16)
    column = lax.broadcasted_iota(jnp.int32, (cols, out_w), 0)
    target = 2 * lax.broadcasted_iota(jnp.int32, (cols, out_w), 1)
    taken = []
    for d in range(3):
        choice = jnp.where(column == target + (d - 1), 1.0, 0.0).astype(jnp.bfloat16)
        taken.append(jnp.dot(cost, choice, preferred_element_type=jnp.float32).astype(jnp.bfloat16))
    deep = 4 * c1
    for q in range(planes // 2):
        read, start, stop = near_planes(2 * q, planes, 3 * deep)
        rhs = jnp.concatenate([taken[d][plane * deep : (plane + 1) * deep] for plane in read for d in range(3)], axis=0)
        result = jnp.dot(kernel_two[:, start:stop], rhs, preferred_element_type=jnp.float32)
        out[q] = partial[q] + result


def on_device(
    ref_features,
    source_tiles,
    pair_lists,
    view_counts,
    disparities,
    conv_first,
    bias_first,
    conv_second,
    bias_second,
):
    n_view = lax.axis_size("view")
    me = lax.axis_index("view").reshape(1)
    rows_n, channels, cols = ref_features.shape
    tiles_dev, tile_rows = source_tiles.shape[0], source_tiles.shape[1]
    sources, blocks = pair_lists.shape[1], pair_lists.shape[2]
    planes = disparities.shape[0]
    slab = tile_rows * channels
    c1, c2 = conv_first.shape[2], conv_second.shape[0]
    half_r, half_p, half_x = rows_n // 2, planes // 2, cols // 2
    smem = pl.BlockSpec(memory_space=pltpu.SMEM)
    vmem = pl.BlockSpec(memory_space=pltpu.VMEM)
    anywhere = pl.BlockSpec(memory_space=pl.ANY)
    params = pltpu.CompilerParams(vmem_limit_bytes=VMEM_LIMIT)
    bf16, f32, i32 = jnp.bfloat16, jnp.float32, jnp.int32
    shape = jax.ShapeDtypeStruct

    table = pl.pallas_call(
        functools.partial(request_kernel, tiles_dev),
        out_shape=shape((n_view, 1, CAP), i32),
        in_specs=[smem],
        out_specs=vmem,
        compiler_params=params,
        name="request_table",
    )(pair_lists)
    table = lax.all_to_all(table, "view", split_axis=0, concat_axis=0, tiled=True)
    outgoing = source_tiles.reshape(tiles_dev, slab, cols)[table[:, 0]]
    arrived = lax.all_to_all(outgoing, "view", split_axis=0, concat_axis=0, tiled=True)
    arrived = arrived.reshape(n_view * CAP, slab, cols)

    at_slots = planes * sources
    at_live = at_slots + sources * blocks
    edge_blocks, mid_blocks = (0, blocks - 1), tuple(range(1, blocks - 1))
    rows_of = lambda picks: [block * tile_rows + i for block in picks for i in range(tile_rows)]
    edge_rows, mid_rows = rows_of(edge_blocks), rows_of(mid_blocks)
    prepared = pl.pallas_call(
        functools.partial(prepare_kernel, tiles_dev, edge_rows, mid_rows),
        out_shape=[
            shape((12 * c1, 3 * LANES), f32),
            shape((6 * LANES, 2 * LANES), bf16),
            shape((half_r * c2, 9 * LANES), bf16),
            shape((half_r * c2, 3 * LANES), bf16),
            shape((1, LANES), f32),
            shape((3 * c1, cols), f32),
            shape((half_r * c2, half_x), f32),
            shape((at_live + 3,), i32),
        ],
        in_specs=[vmem, vmem] + [smem] * 6 + [anywhere],
        out_specs=[vmem] * 7 + [smem],
        scratch_shapes=[pltpu.VMEM((2 * LANES, 2 * LANES), f32), pltpu.VMEM((3 * LANES, LANES), f32)],
        compiler_params=params,
        name="weights_and_scalars",
    )(
        conv_first.transpose(0, 1, 3, 2, 4),
        conv_second.transpose(1, 2, 3, 4, 0),
        bias_first,
        bias_second,
        disparities,
        pair_lists,
        view_counts,
        me,
        table,
    )
    kernel_edge, kernel_mid, two_mid, two_edge, bias_lanes, bias_rows, bias_two, scalars = prepared

    band_scratch = [pltpu.VMEM((sources, cols + 2 * SHIFT, LANES), f32), pltpu.VMEM((1, cols, LANES), f32)]
    payload = shape((planes, 2 * c1, cols), bf16)
    edge_var, own, far, near = pl.pallas_call(
        functools.partial(edge_kernel, at_slots, at_live, sources, blocks, edge_blocks),
        out_shape=[shape((planes, cols, LANES), bf16), shape((planes, 3 * c1, cols), f32), payload, payload],
        in_specs=[smem] + [vmem] * 3,
        out_specs=[vmem] * 4,
        scratch_shapes=band_scratch,
        compiler_params=params,
        name="edge_rows",
    )(scalars, arrived, ref_features, kernel_edge)
    far = swapped(far, "view", 1)
    near = swapped(near, "view", 0)

    partial = pl.pallas_call(
        functools.partial(mid_kernel, at_slots, at_live, sources, blocks, mid_blocks, (rows_n - 2) * c1),
        out_shape=shape((half_p, half_r * c2, half_x), f32),
        in_specs=[smem] + [vmem] * 7,
        out_specs=vmem,
        scratch_shapes=band_scratch
        + [
            pltpu.VMEM((planes, cols, LANES), bf16),
            pltpu.VMEM((planes, cols + 2 * PAD, LANES), f32),
            pltpu.VMEM((planes, cols + PAD, LANES), f32),
        ],
        compiler_params=params,
        name="middle_rows",
    )(scalars, arrived, ref_features, edge_var, kernel_mid, bias_lanes, two_mid, bias_two)

    out = pl.pallas_call(
        functools.partial(end_kernel, at_live),
        out_shape=shape((half_p, half_r * c2, half_x), f32),
        in_specs=[smem] + [vmem] * 6,
        out_specs=vmem,
        compiler_params=params,
        name="end_rows",
    )(scalars, far, near, own, partial, bias_rows, two_edge)
    return out.reshape(half_p, half_r, c2, half_x)


def solution(mesh):
    return jax.shard_map(
        on_device,
        mesh=mesh,
        in_specs=(
            P(("groups", "view"), None, None),
            P(("groups", "view"), None, None, None),
            P(("groups", "view"), None, None),
            P(("groups", "view")),
            P("groups", None),
            P(),
            P(),
            P(),
            P(),
        ),
        out_specs=P("groups", "view", None, None),
        check_vma=False,
    )
```

```python
import functools

import numpy as np

import jax
import jax.numpy as jnp
from jax import lax
from jax.experimental import pallas as pl
from jax.experimental.pallas import tpu as pltpu
from jax.sharding import PartitionSpec as P

SHIFT = 48
CAP = 2
LANES = 128
CHUNK = 64
VMEM_LIMIT = 24 * 1024 * 1024


def swapped(x, axis, parity):
    count = lax.axis_size(axis)
    pairs = [(i, i + 1) for i in range(parity, count - 1, 2)]
    return lax.ppermute(x, axis, pairs + [(j, i) for i, j in pairs])


def request_places(pair_lists, tiles_dev):
    owners, ranks, tiles = [], [], []
    for s in range(pair_lists.shape[1]):
        for b in range(pair_lists.shape[2]):
            tile = pair_lists[0, s, b]
            whole = jnp.maximum(tile, 0)
            owner = jnp.where(tile >= 0, lax.div(whole, tiles_dev), -1)
            rank = jnp.int32(0)
            for other in owners:
                rank = rank + jnp.where(other == owner, 1, 0)
            owners.append(owner)
            ranks.append(rank)
            tiles.append(lax.rem(whole, tiles_dev))
    return owners, ranks, tiles


def request_kernel(tiles_dev, pair_lists, table, held, sem):
    copy = pltpu.make_async_copy(pair_lists, held, sem)
    copy.start()
    copy.wait()
    owners, ranks, tiles = request_places(held, tiles_dev)
    row = lax.broadcasted_iota(jnp.int32, table.shape, 0)
    lane = lax.broadcasted_iota(jnp.int32, table.shape, 2)
    total = jnp.zeros(table.shape, jnp.int32)
    for owner, rank, tile in zip(owners, ranks, tiles):
        total = jnp.where((row == owner) & (lane == rank), tile, total)
    table[...] = total


def prepare_kernel(
    tiles_dev,
    edge_rows,
    mid_rows,
    first,
    second,
    bias_first,
    bias_second,
    disparities,
    pair_lists,
    view_counts,
    me,
    _,
    kernel_edge,
    kernel_mid,
    two_mid,
    two_edge,
    bias_rows,
    bias_two,
    scalars,
    stacked_mid,
    stacked_edge,
):
    planes, sources = disparities.shape
    owners, ranks, _ = request_places(pair_lists, tiles_dev)
    at = 0
    for p in range(planes):
        for s in range(sources):
            scalars[at] = disparities[p, s]
            at += 1
    for owner, rank in zip(owners, ranks):
        scalars[at] = jnp.where(owner >= 0, owner * CAP + rank, 0)
        at += 1
    scalars[at] = view_counts[0]
    scalars[at + 1] = me[0]
    scalars[at + 2] = lax.rem(me[0], 2)

    c1, channels = first.shape[3], first.shape[4]
    c2 = second.shape[4]
    rows_n = len(edge_rows) + len(mid_rows)
    half_r = rows_n // 2
    place = {row: i for i, row in enumerate(edge_rows + mid_rows)}
    per_group = LANES // channels
    filler = jnp.zeros((c1, LANES - channels), jnp.float32)
    taps = {}
    for a in range(3):
        for b in range(3):
            for d in range(3):
                tap = jnp.concatenate([first[a, b, d].astype(jnp.float32), filler], axis=1)
                for turn in range(per_group):
                    lane = turn * channels
                    taps[a, b, d, turn] = pltpu.roll(tap, lane, 1) if lane else tap

    def band(a, d, r, group):
        total = jnp.zeros((c1, LANES), jnp.float32)
        for b in range(3):
            at_place = place.get(r - 1 + b, -1)
            if at_place >= 0 and at_place // per_group == group:
                total = total + taps[a, b, d, at_place % per_group]
        return total

    rim = (-1, 0, rows_n - 1, rows_n)
    inner = tuple(range(1, rows_n - 1))
    for kernel, rows, groups in ((kernel_edge, rim, 1), (kernel_mid, inner, 2)):
        for d in range(3):
            for i, r in enumerate(rows):
                at = (d * len(rows) + i) * c1
                for a in range(3):
                    for group in range(groups):
                        lane = (a * groups + group) * LANES
                        kernel[at : at + c1, lane : lane + LANES] = band(a, d, r, group)

    def second_row(a, d, r):
        blocks = []
        for g in range(half_r):
            b = -1 if r is None else r - 2 * g + 1
            hit = 0 <= b < 3
            blocks.append(second[a, b, d].astype(jnp.float32) if hit else jnp.zeros((c1, c2), jnp.float32))
        blocks.append(jnp.zeros((c1, LANES - half_r * c2), jnp.float32))
        return jnp.concatenate(blocks, axis=1)

    for two, stacked, rows in ((two_mid, stacked_mid, inner), (two_edge, stacked_edge, rim[:3] + (None,))):
        stacked[...] = jnp.zeros(stacked.shape, jnp.float32)
        for a in range(3):
            for d in range(3):
                for i, r in enumerate(rows):
                    at = ((a * 3 + d) * len(rows) + i) * c1
                    stacked[at : at + c1, :] = second_row(a, d, r)
        two[...] = stacked[...].T[: half_r * c2].astype(jnp.bfloat16)

    def spread_bias(like, bias):
        index = lax.broadcasted_iota(jnp.int32, like.shape, 0)
        total = jnp.zeros(like.shape, jnp.float32)
        for i in range(bias.shape[0]):
            total = jnp.where(index % bias.shape[0] == i, bias[i], total)
        like[...] = total

    spread_bias(bias_rows, bias_first)
    spread_bias(bias_two, bias_second)


def spread(slab, scale, wide, at):
    cols = slab.shape[1]
    band = jnp.zeros((SHIFT, LANES), jnp.float32)
    wide[at, 0:SHIFT, :] = band
    wide[at, SHIFT + cols : 2 * SHIFT + cols, :] = band
    wide[at, SHIFT : SHIFT + cols, :] = slab.astype(jnp.float32).T * scale


def plane_variance(p, at, sources, cols, disp, wide, ref_wide, ref_at, inv, store):
    for x0 in range(0, cols, CHUNK):
        ref = ref_wide[ref_at, x0 : x0 + CHUNK, :]
        summed = ref
        squares = ref * ref
        for s in range(sources):
            warped = wide[at + s, pl.ds(SHIFT + x0 - disp[p * sources + s], CHUNK), :]
            summed = summed + warped
            squares = squares + warped * warped
        mean = summed * inv
        store(x0, (squares * inv - mean * mean).astype(jnp.bfloat16))


def load_reference(ref, blocks, picks, ref_wide):
    tile_rows = ref.shape[0] // blocks
    rows = [ref[block * tile_rows + i] for block in picks for i in range(tile_rows)]
    ref_wide[0] = jnp.concatenate(rows, axis=0).astype(jnp.float32).T


def load_tiles(at_slots, live, sources, blocks, picks, scalars, arrived, wide):
    for s in range(sources):
        slab = jnp.concatenate([arrived[scalars[at_slots + s * blocks + block]] for block in picks], axis=0)
        spread(slab, (s < live).astype(jnp.float32), wide, s)


def plane_sums(p, planes, parts, weights, column):
    cols = column.shape[1]
    first, last = max(p - 1, 0), min(p + 2, planes)
    lhs = jnp.concatenate([part[q] for q in range(first, last) for part in parts], axis=1)
    deep = lhs.shape[1] // (last - first)
    start = (first - p + 1) * deep
    taps = lax.dot_general(
        weights[:, start : start + lhs.shape[1]], lhs, (((1,), (1,)), ((), ())), preferred_element_type=jnp.float32
    )
    rows = taps.shape[0] // 3
    left, center, right = taps[:rows], taps[rows : 2 * rows], taps[2 * rows :]
    total = center + jnp.where(column[:rows] > 0, pltpu.roll(left, 1, 1), 0.0)
    return total + jnp.where(column[:rows] < cols - 1, pltpu.roll(right, cols - 1, 1), 0.0)


def strided_planes(q, planes, taken, rows, weights):
    parts = []
    for plane in range(2 * q - 1, 2 * q + 2):
        for d in range(3):
            if 0 <= plane < planes:
                parts.append(taken[d][plane * rows : (plane + 1) * rows])
            else:
                parts.append(jnp.zeros((rows, taken[d].shape[1]), jnp.bfloat16))
    rhs = jnp.concatenate(parts, axis=0)
    return jnp.dot(weights[:, : rhs.shape[0]], rhs, preferred_element_type=jnp.float32)


def edge_kernel(
    at_slots,
    at_live,
    sources,
    blocks,
    picks,
    scalars_hbm,
    arrived,
    ref,
    kernel_hbm,
    var,
    own,
    far,
    near,
    flags,
    wide,
    ref_wide,
    scalars,
    kernel,
    sem,
):
    copy_scalars = pltpu.make_async_copy(scalars_hbm, scalars, sem.at[0])
    copy_kernel = pltpu.make_async_copy(kernel_hbm, kernel, sem.at[1])
    copy_scalars.start()
    copy_kernel.start()
    planes, cols, _ = var.shape
    c1 = kernel.shape[0] // 12
    load_reference(ref, blocks, picks, ref_wide)
    copy_scalars.wait()
    live = scalars[at_live]
    odd = scalars[at_live + 2] > 0
    flags[0] = jnp.where(odd, 1.0, 0.0) * jnp.ones((c1, LANES), jnp.float32)
    flags[1] = jnp.where(scalars[at_live + 1] > 0, 1.0, 0.0) * jnp.ones((c1, LANES), jnp.float32)
    load_tiles(at_slots, live, sources, blocks, picks, scalars, arrived, wide)
    inv = 1.0 / (live.astype(jnp.float32) + 1.0)
    copy_kernel.wait()
    weights = kernel[...].astype(jnp.bfloat16)
    column = lax.broadcasted_iota(jnp.int32, (4 * c1, cols), 1)
    empty = jnp.zeros((c1, cols), jnp.float32)
    for step in range(planes + 1):
        if step < planes:

            def store(x0, value):
                var[step, x0 : x0 + CHUNK, :] = value

            plane_variance(step, 0, sources, cols, scalars, wide, ref_wide, 0, inv, store)
        if step == 0:
            continue
        p = step - 1
        total = plane_sums(p, planes, (var,), weights, column)
        own[p] = total[: 3 * c1]
        downward = total[2 * c1 :]
        upward = jnp.concatenate([total[:c1], empty], axis=0)
        far[p] = jnp.where(odd, downward, upward).astype(jnp.bfloat16)
        near[p] = jnp.where(odd, upward, downward).astype(jnp.bfloat16)


def mid_kernel(
    at_slots,
    at_live,
    sources,
    blocks,
    picks,
    scalars,
    arrived,
    ref,
    edge_var,
    kernel,
    bias_rows,
    kernel_two,
    bias_two,
    out,
    choices,
    wide,
    ref_wide,
    var,
    cost,
):
    planes, cols, _ = var.shape
    out_w = out.shape[2]
    inner = cost.shape[0] // planes
    live = scalars[at_live]
    load_reference(ref, blocks, picks, ref_wide)
    load_tiles(at_slots, live, sources, blocks, picks, scalars, arrived, wide)
    inv = 1.0 / (live.astype(jnp.float32) + 1.0)
    weights = kernel[...].astype(jnp.bfloat16)
    bias = bias_rows[:inner]
    column = lax.broadcasted_iota(jnp.int32, (inner, cols), 1)
    row = lax.broadcasted_iota(jnp.int32, (cols, out_w), 0)
    target = 2 * lax.broadcasted_iota(jnp.int32, (cols, out_w), 1)
    for d in range(3):
        choices[d] = jnp.where(row == target + (d - 1), 1.0, 0.0).astype(jnp.bfloat16)
    for step in range(planes + 1):
        if step < planes:

            def store(x0, value):
                var[step, x0 : x0 + CHUNK, :] = value

            plane_variance(step, 0, sources, cols, scalars, wide, ref_wide, 0, inv, store)
        if step == 0:
            continue
        p = step - 1
        total = plane_sums(p, planes, (edge_var, var), weights, column)
        cost[p * inner : (p + 1) * inner, :] = jnp.maximum(total + bias, 0.0).astype(jnp.bfloat16)
    taken = [
        jnp.dot(cost[...], choices[d], preferred_element_type=jnp.float32).astype(jnp.bfloat16) for d in range(3)
    ]
    for q in range(planes // 2):
        out[q] = strided_planes(q, planes, taken, inner, kernel_two) + bias_two[...]


def end_kernel(far, near, flags, own, partial, bias_rows, kernel_two, choices, out):
    planes, ends, cols = own.shape
    c1 = ends // 3
    odd = jnp.concatenate([flags[0]] * (cols // LANES), axis=1) > 0.5
    not_top = jnp.concatenate([flags[1]] * (cols // LANES), axis=1)
    empty = jnp.zeros((c1, cols), jnp.float32)
    bias = bias_rows[:c1]
    rows = []
    for p in range(planes):
        lower, upper = far[p].astype(jnp.float32), near[p].astype(jnp.float32)
        before = own[p, :c1] + jnp.where(odd, upper[:c1], lower[:c1])
        top = own[p, c1 : 2 * c1] + jnp.where(odd, upper[c1:], lower[c1:])
        bottom = own[p, 2 * c1 :] + jnp.where(odd, lower[:c1], upper[:c1])
        rows += [jnp.maximum(before + bias, 0.0) * not_top]
        rows += [jnp.maximum(top + bias, 0.0), jnp.maximum(bottom + bias, 0.0), empty]
    cost = jnp.concatenate(rows, axis=0).astype(jnp.bfloat16)
    taken = [jnp.dot(cost, choices[d], preferred_element_type=jnp.float32).astype(jnp.bfloat16) for d in range(3)]
    for q in range(planes // 2):
        out[q] = partial[q] + strided_planes(q, planes, taken, 4 * c1, kernel_two)


def on_device(
    ref_features,
    source_tiles,
    pair_lists,
    view_counts,
    disparities,
    conv_first,
    bias_first,
    conv_second,
    bias_second,
):
    n_view = lax.axis_size("view")
    me = lax.axis_index("view").reshape(1)
    rows_n, channels, cols = ref_features.shape
    tiles_dev, tile_rows = source_tiles.shape[0], source_tiles.shape[1]
    sources, blocks = pair_lists.shape[1], pair_lists.shape[2]
    planes = disparities.shape[0]
    slab = tile_rows * channels
    c1, c2 = conv_first.shape[2], conv_second.shape[0]
    half_r, half_p, half_x = rows_n // 2, planes // 2, cols // 2
    smem = pl.BlockSpec(memory_space=pltpu.SMEM)
    vmem = pl.BlockSpec(memory_space=pltpu.VMEM)
    anywhere = pl.BlockSpec(memory_space=pl.ANY)
    hbm = pl.BlockSpec(memory_space=pltpu.HBM)
    params = pltpu.CompilerParams(vmem_limit_bytes=VMEM_LIMIT)
    bf16, f32, i32 = jnp.bfloat16, jnp.float32, jnp.int32
    shape = jax.ShapeDtypeStruct

    table = pl.pallas_call(
        functools.partial(request_kernel, tiles_dev),
        out_shape=shape((n_view, 1, CAP), i32),
        in_specs=[hbm],
        out_specs=vmem,
        scratch_shapes=[pltpu.SMEM(pair_lists.shape, i32), pltpu.SemaphoreType.DMA],
        compiler_params=params,
        name="request_table",
    )(pair_lists)
    table = lax.all_to_all(table, "view", split_axis=0, concat_axis=0, tiled=True)
    outgoing = source_tiles.reshape(tiles_dev, slab, cols)[table[:, 0]]
    arrived = lax.all_to_all(outgoing, "view", split_axis=0, concat_axis=0, tiled=True)
    arrived = arrived.reshape(n_view * CAP, slab, cols)

    at_slots = planes * sources
    at_live = at_slots + sources * blocks
    edge_blocks, mid_blocks = (0, blocks - 1), tuple(range(1, blocks - 1))
    rows_of = lambda picks: [block * tile_rows + i for block in picks for i in range(tile_rows)]
    edge_rows, mid_rows = rows_of(edge_blocks), rows_of(mid_blocks)
    inner = (rows_n - 2) * c1
    mid_deep, edge_deep = (-(-9 * rows // LANES) * LANES for rows in (inner, 4 * c1))
    prepared = pl.pallas_call(
        functools.partial(prepare_kernel, tiles_dev, edge_rows, mid_rows),
        out_shape=[
            shape((12 * c1, 3 * LANES), f32),
            shape((3 * inner, 6 * LANES), f32),
            shape((half_r * c2, mid_deep), bf16),
            shape((half_r * c2, edge_deep), bf16),
            shape((inner, cols), f32),
            shape((half_r * c2, half_x), f32),
            shape((LANES,), i32),
        ],
        in_specs=[vmem, vmem] + [smem] * 6 + [anywhere],
        out_specs=[vmem] * 6 + [smem],
        scratch_shapes=[pltpu.VMEM((mid_deep, LANES), f32), pltpu.VMEM((edge_deep, LANES), f32)],
        compiler_params=params,
        name="weights_and_scalars",
    )(
        conv_first.transpose(0, 1, 3, 2, 4),
        conv_second.transpose(1, 2, 3, 4, 0),
        bias_first,
        bias_second,
        disparities,
        pair_lists,
        view_counts,
        me,
        table,
    )
    kernel_edge, kernel_mid, two_mid, two_edge, bias_rows, bias_two, scalars = prepared

    band_scratch = [pltpu.VMEM((sources, cols + 2 * SHIFT, LANES), f32), pltpu.VMEM((1, cols, LANES), f32)]
    payload = shape((planes, 2 * c1, cols), bf16)
    edge_var, own, far, near, flags = pl.pallas_call(
        functools.partial(edge_kernel, at_slots, at_live, sources, blocks, edge_blocks),
        out_shape=[
            shape((planes, cols, LANES), bf16),
            shape((planes, 3 * c1, cols), f32),
            payload,
            payload,
            shape((2, c1, LANES), f32),
        ],
        in_specs=[hbm, vmem, vmem, hbm],
        out_specs=[vmem] * 5,
        scratch_shapes=band_scratch
        + [
            pltpu.SMEM(scalars.shape, i32),
            pltpu.VMEM(kernel_edge.shape, f32),
            pltpu.SemaphoreType.DMA((2,)),
        ],
        compiler_params=params,
        name="edge_rows",
    )(scalars, arrived, ref_features, kernel_edge)
    far = swapped(far, "view", 1)
    near = swapped(near, "view", 0)

    partial, choices = pl.pallas_call(
        functools.partial(mid_kernel, at_slots, at_live, sources, blocks, mid_blocks),
        out_shape=[shape((half_p, half_r * c2, half_x), f32), shape((3, cols, half_x), bf16)],
        in_specs=[smem] + [vmem] * 7,
        out_specs=[vmem, vmem],
        scratch_shapes=band_scratch
        + [pltpu.VMEM((planes, cols, LANES), bf16), pltpu.VMEM((planes * inner, cols), bf16)],
        compiler_params=params,
        name="middle_rows",
    )(scalars, arrived, ref_features, edge_var, kernel_mid, bias_rows, two_mid, bias_two)

    out = pl.pallas_call(
        end_kernel,
        out_shape=shape((half_p, half_r * c2, half_x), f32),
        in_specs=[vmem] * 8,
        out_specs=vmem,
        compiler_params=params,
        name="end_rows",
    )(far, near, flags, own, partial, bias_rows, two_edge, choices)
    return out.reshape(half_p, half_r, c2, half_x)


def solution(mesh):
    return jax.shard_map(
        on_device,
        mesh=mesh,
        in_specs=(
            P(("groups", "view"), None, None),
            P(("groups", "view"), None, None, None),
            P(("groups", "view"), None, None),
            P(("groups", "view")),
            P("groups", None),
            P(),
            P(),
            P(),
            P(),
        ),
        out_specs=P("groups", "view", None, None),
        check_vma=False,
    )
```

```python
import functools

import numpy as np

import jax
import jax.numpy as jnp
from jax import lax
from jax.experimental import pallas as pl
from jax.experimental.pallas import tpu as pltpu
from jax.sharding import PartitionSpec as P

SHIFT = 48
CAP = 2
LANES = 128
CHUNK = 64
VMEM_LIMIT = 10 * 1024 * 1024


def swapped(x, axis, parity):
    count = lax.axis_size(axis)
    pairs = [(i, i + 1) for i in range(parity, count - 1, 2)]
    return lax.ppermute(x, axis, pairs + [(j, i) for i, j in pairs])


def request_places(pair_lists, tiles_dev):
    owners, ranks, tiles = [], [], []
    for s in range(pair_lists.shape[1]):
        for b in range(pair_lists.shape[2]):
            tile = pair_lists[0, s, b]
            whole = jnp.maximum(tile, 0)
            owner = jnp.where(tile >= 0, lax.div(whole, tiles_dev), -1)
            rank = jnp.int32(0)
            for other in owners:
                rank = rank + jnp.where(other == owner, 1, 0)
            owners.append(owner)
            ranks.append(rank)
            tiles.append(lax.rem(whole, tiles_dev))
    return owners, ranks, tiles


def request_kernel(tiles_dev, pair_lists, table, held, sem):
    copy = pltpu.make_async_copy(pair_lists, held, sem)
    copy.start()
    copy.wait()
    owners, ranks, tiles = request_places(held, tiles_dev)
    row = lax.broadcasted_iota(jnp.int32, table.shape, 0)
    lane = lax.broadcasted_iota(jnp.int32, table.shape, 2)
    total = jnp.zeros(table.shape, jnp.int32)
    for owner, rank, tile in zip(owners, ranks, tiles):
        total = jnp.where((row == owner) & (lane == rank), tile, total)
    table[...] = total


def prepare_kernel(
    tiles_dev,
    edge_rows,
    mid_rows,
    first,
    second,
    bias_first,
    bias_second,
    disparities,
    pair_lists,
    view_counts,
    me,
    _,
    kernel_edge,
    kernel_mid,
    two_mid,
    two_edge,
    bias_rows,
    bias_two,
    scalars,
    stacked_mid,
    stacked_edge,
):
    planes, sources = disparities.shape
    owners, ranks, _ = request_places(pair_lists, tiles_dev)
    at = 0
    for p in range(planes):
        for s in range(sources):
            scalars[at] = disparities[p, s]
            at += 1
    for owner, rank in zip(owners, ranks):
        scalars[at] = jnp.where(owner >= 0, owner * CAP + rank, 0)
        at += 1
    scalars[at] = view_counts[0]
    scalars[at + 1] = me[0]
    scalars[at + 2] = lax.rem(me[0], 2)

    c1, channels = first.shape[3], first.shape[4]
    c2 = second.shape[4]
    rows_n = len(edge_rows) + len(mid_rows)
    half_r = rows_n // 2
    place = {row: i for i, row in enumerate(edge_rows + mid_rows)}
    per_group = LANES // channels
    filler = jnp.zeros((c1, LANES - channels), jnp.float32)
    taps = {}
    for a in range(3):
        for b in range(3):
            for d in range(3):
                tap = jnp.concatenate([first[a, b, d].astype(jnp.float32), filler], axis=1)
                for turn in range(per_group):
                    lane = turn * channels
                    taps[a, b, d, turn] = pltpu.roll(tap, lane, 1) if lane else tap

    def band(a, d, r, group):
        total = jnp.zeros((c1, LANES), jnp.float32)
        for b in range(3):
            at_place = place.get(r - 1 + b, -1)
            if at_place >= 0 and at_place // per_group == group:
                total = total + taps[a, b, d, at_place % per_group]
        return total

    rim = (-1, 0, rows_n - 1, rows_n)
    inner = tuple(range(1, rows_n - 1))
    for kernel, rows, groups in ((kernel_edge, rim, 1), (kernel_mid, inner, 2)):
        for d in range(3):
            for i, r in enumerate(rows):
                at = (d * len(rows) + i) * c1
                for a in range(3):
                    for group in range(groups):
                        lane = (a * groups + group) * LANES
                        kernel[at : at + c1, lane : lane + LANES] = band(a, d, r, group)

    def second_row(a, d, r):
        blocks = []
        for g in range(half_r):
            b = -1 if r is None else r - 2 * g + 1
            hit = 0 <= b < 3
            blocks.append(second[a, b, d].astype(jnp.float32) if hit else jnp.zeros((c1, c2), jnp.float32))
        blocks.append(jnp.zeros((c1, LANES - half_r * c2), jnp.float32))
        return jnp.concatenate(blocks, axis=1)

    for two, stacked, rows in ((two_mid, stacked_mid, inner), (two_edge, stacked_edge, rim[:3] + (None,))):
        stacked[...] = jnp.zeros(stacked.shape, jnp.float32)
        for a in range(3):
            for d in range(3):
                for i, r in enumerate(rows):
                    at = ((a * 3 + d) * len(rows) + i) * c1
                    stacked[at : at + c1, :] = second_row(a, d, r)
        two[...] = stacked[...].T[: half_r * c2].astype(jnp.bfloat16)

    def spread_bias(like, bias):
        index = lax.broadcasted_iota(jnp.int32, like.shape, 0)
        total = jnp.zeros(like.shape, jnp.float32)
        for i in range(bias.shape[0]):
            total = jnp.where(index % bias.shape[0] == i, bias[i], total)
        like[...] = total

    spread_bias(bias_rows, bias_first)
    spread_bias(bias_two, bias_second)


def spread(slab, scale, wide, at):
    cols = slab.shape[1]
    band = jnp.zeros((SHIFT, LANES), jnp.float32)
    wide[at, 0:SHIFT, :] = band
    wide[at, SHIFT + cols : 2 * SHIFT + cols, :] = band
    wide[at, SHIFT : SHIFT + cols, :] = slab.T.astype(jnp.float32) * scale


def plane_variance(p, at, sources, cols, disp, wide, ref_wide, ref_at, inv, store):
    for x0 in range(0, cols, CHUNK):
        ref = ref_wide[ref_at, x0 : x0 + CHUNK, :]
        summed = ref
        squares = ref * ref
        for s in range(sources):
            warped = wide[at + s, pl.ds(SHIFT + x0 - disp[p * sources + s], CHUNK), :]
            summed = summed + warped
            squares = squares + warped * warped
        store(x0, (squares - summed * summed * inv).astype(jnp.bfloat16))


def view_weights(live):
    total = live.astype(jnp.float32) + jnp.ones((1, LANES), jnp.float32)
    return 1.0 / total, lax.rsqrt(total)


def load_reference(ref, blocks, picks, scale, ref_wide):
    tile_rows = ref.shape[0] // blocks
    rows = [ref[block * tile_rows + i] for block in picks for i in range(tile_rows)]
    ref_wide[0] = jnp.concatenate(rows, axis=0).T.astype(jnp.float32) * scale


def load_tiles(at_slots, live, sources, blocks, picks, scale, scalars, arrived, wide):
    for s in range(sources):
        slab = jnp.concatenate([arrived[scalars[at_slots + s * blocks + block]] for block in picks], axis=0)
        spread(slab, jnp.where(s < live, scale, 0.0), wide, s)


def plane_sums(p, planes, parts, weights, column):
    cols = column.shape[1]
    first, last = max(p - 1, 0), min(p + 2, planes)
    lhs = jnp.concatenate([part[q] for q in range(first, last) for part in parts], axis=1)
    deep = lhs.shape[1] // (last - first)
    start = (first - p + 1) * deep
    taps = lax.dot_general(
        weights[:, start : start + lhs.shape[1]], lhs, (((1,), (1,)), ((), ())), preferred_element_type=jnp.float32
    )
    rows = taps.shape[0] // 3
    left, center, right = taps[:rows], taps[rows : 2 * rows], taps[2 * rows :]
    total = center + jnp.where(column[:rows] > 0, pltpu.roll(left, 1, 1), 0.0)
    return total + jnp.where(column[:rows] < cols - 1, pltpu.roll(right, cols - 1, 1), 0.0)


def strided_planes(q, planes, taken, rows, weights):
    parts = []
    for plane in range(2 * q - 1, 2 * q + 2):
        for d in range(3):
            if 0 <= plane < planes:
                parts.append(taken[d][plane * rows : (plane + 1) * rows])
            else:
                parts.append(jnp.zeros((rows, taken[d].shape[1]), jnp.bfloat16))
    rhs = jnp.concatenate(parts, axis=0)
    return jnp.dot(weights[:, : rhs.shape[0]], rhs, preferred_element_type=jnp.float32)


def edge_kernel(
    at_slots,
    at_live,
    sources,
    blocks,
    picks,
    scalars_hbm,
    arrived,
    ref,
    kernel_hbm,
    var,
    own,
    far,
    near,
    flags,
    wide,
    ref_wide,
    scalars,
    kernel,
    sem,
):
    copy_scalars = pltpu.make_async_copy(scalars_hbm, scalars, sem.at[0])
    copy_kernel = pltpu.make_async_copy(kernel_hbm, kernel, sem.at[1])
    copy_scalars.start()
    copy_kernel.start()
    planes, cols, _ = var.shape
    c1 = kernel.shape[0] // 12
    copy_scalars.wait()
    live = scalars[at_live]
    inv, scale = view_weights(live)
    load_reference(ref, blocks, picks, scale, ref_wide)
    odd = scalars[at_live + 2] > 0
    flags[0] = jnp.where(odd, 1.0, 0.0) * jnp.ones((c1, LANES), jnp.float32)
    flags[1] = jnp.where(scalars[at_live + 1] > 0, 1.0, 0.0) * jnp.ones((c1, LANES), jnp.float32)
    load_tiles(at_slots, live, sources, blocks, picks, scale, scalars, arrived, wide)
    copy_kernel.wait()
    weights = kernel[...].astype(jnp.bfloat16)
    column = lax.broadcasted_iota(jnp.int32, (4 * c1, cols), 1)
    empty = jnp.zeros((c1, cols), jnp.float32)
    for step in range(planes + 1):
        if step < planes:

            def store(x0, value):
                var[step, x0 : x0 + CHUNK, :] = value

            plane_variance(step, 0, sources, cols, scalars, wide, ref_wide, 0, inv, store)
        if step == 0:
            continue
        p = step - 1
        total = plane_sums(p, planes, (var,), weights, column)
        own[p] = total[: 3 * c1]
        downward = total[2 * c1 :]
        upward = jnp.concatenate([total[:c1], empty], axis=0)
        far[p] = jnp.where(odd, downward, upward).astype(jnp.bfloat16)
        near[p] = jnp.where(odd, upward, downward).astype(jnp.bfloat16)


def mid_kernel(
    at_slots,
    at_live,
    sources,
    blocks,
    picks,
    scalars,
    arrived,
    ref,
    edge_var,
    kernel,
    bias_rows,
    kernel_two,
    bias_two,
    out,
    choices,
    wide,
    ref_wide,
    var,
    cost,
):
    planes, cols, _ = var.shape
    out_w = out.shape[2]
    inner = cost.shape[0] // planes
    live = scalars[at_live]
    inv, scale = view_weights(live)
    load_reference(ref, blocks, picks, scale, ref_wide)
    load_tiles(at_slots, live, sources, blocks, picks, scale, scalars, arrived, wide)
    weights = kernel[...].astype(jnp.bfloat16)
    bias = bias_rows[:inner]
    column = lax.broadcasted_iota(jnp.int32, (inner, cols), 1)
    row = lax.broadcasted_iota(jnp.int32, (cols, out_w), 0)
    target = 2 * lax.broadcasted_iota(jnp.int32, (cols, out_w), 1)
    for d in range(3):
        choices[d] = jnp.where(row == target + (d - 1), 1.0, 0.0).astype(jnp.bfloat16)
    for step in range(planes + 1):
        if step < planes:

            def store(x0, value):
                var[step, x0 : x0 + CHUNK, :] = value

            plane_variance(step, 0, sources, cols, scalars, wide, ref_wide, 0, inv, store)
        if step == 0:
            continue
        p = step - 1
        total = plane_sums(p, planes, (edge_var, var), weights, column)
        cost[p * inner : (p + 1) * inner, :] = jnp.maximum(total + bias, 0.0).astype(jnp.bfloat16)
    taken = [
        jnp.dot(cost[...], choices[d], preferred_element_type=jnp.float32).astype(jnp.bfloat16) for d in range(3)
    ]
    for q in range(planes // 2):
        out[q] = strided_planes(q, planes, taken, inner, kernel_two) + bias_two[...]


def end_kernel(far, near, flags, own, partial, bias_rows, kernel_two, choices, out):
    planes, ends, cols = own.shape
    c1 = ends // 3
    odd = jnp.concatenate([flags[0]] * (cols // LANES), axis=1) > 0.5
    not_top = jnp.concatenate([flags[1]] * (cols // LANES), axis=1)
    empty = jnp.zeros((c1, cols), jnp.float32)
    bias = bias_rows[:c1]
    rows = []
    for p in range(planes):
        lower, upper = far[p].astype(jnp.float32), near[p].astype(jnp.float32)
        before = own[p, :c1] + jnp.where(odd, upper[:c1], lower[:c1])
        top = own[p, c1 : 2 * c1] + jnp.where(odd, upper[c1:], lower[c1:])
        bottom = own[p, 2 * c1 :] + jnp.where(odd, lower[:c1], upper[:c1])
        rows += [jnp.maximum(before + bias, 0.0) * not_top]
        rows += [jnp.maximum(top + bias, 0.0), jnp.maximum(bottom + bias, 0.0), empty]
    cost = jnp.concatenate(rows, axis=0).astype(jnp.bfloat16)
    taken = [jnp.dot(cost, choices[d], preferred_element_type=jnp.float32).astype(jnp.bfloat16) for d in range(3)]
    for q in range(planes // 2):
        out[q] = partial[q] + strided_planes(q, planes, taken, 4 * c1, kernel_two)


def on_device(
    ref_features,
    source_tiles,
    pair_lists,
    view_counts,
    disparities,
    conv_first,
    bias_first,
    conv_second,
    bias_second,
):
    n_view = lax.axis_size("view")
    me = lax.axis_index("view").reshape(1)
    rows_n, channels, cols = ref_features.shape
    tiles_dev, tile_rows = source_tiles.shape[0], source_tiles.shape[1]
    sources, blocks = pair_lists.shape[1], pair_lists.shape[2]
    planes = disparities.shape[0]
    slab = tile_rows * channels
    c1, c2 = conv_first.shape[2], conv_second.shape[0]
    half_r, half_p, half_x = rows_n // 2, planes // 2, cols // 2
    smem = pl.BlockSpec(memory_space=pltpu.SMEM)
    vmem = pl.BlockSpec(memory_space=pltpu.VMEM)
    anywhere = pl.BlockSpec(memory_space=pl.ANY)
    hbm = pl.BlockSpec(memory_space=pltpu.HBM)
    params = pltpu.CompilerParams(vmem_limit_bytes=VMEM_LIMIT)
    bf16, f32, i32 = jnp.bfloat16, jnp.float32, jnp.int32
    shape = jax.ShapeDtypeStruct

    table = pl.pallas_call(
        functools.partial(request_kernel, tiles_dev),
        out_shape=shape((n_view, 1, CAP), i32),
        in_specs=[hbm],
        out_specs=vmem,
        scratch_shapes=[pltpu.SMEM(pair_lists.shape, i32), pltpu.SemaphoreType.DMA],
        compiler_params=params,
        name="request_table",
    )(pair_lists)
    table = lax.all_to_all(table, "view", split_axis=0, concat_axis=0, tiled=True)
    outgoing = source_tiles.reshape(tiles_dev, slab, cols)[table[:, 0]]
    arrived = lax.all_to_all(outgoing, "view", split_axis=0, concat_axis=0, tiled=True)
    arrived = arrived.reshape(n_view * CAP, slab, cols)

    at_slots = planes * sources
    at_live = at_slots + sources * blocks
    edge_blocks, mid_blocks = (0, blocks - 1), tuple(range(1, blocks - 1))
    rows_of = lambda picks: [block * tile_rows + i for block in picks for i in range(tile_rows)]
    edge_rows, mid_rows = rows_of(edge_blocks), rows_of(mid_blocks)
    inner = (rows_n - 2) * c1
    mid_deep, edge_deep = (-(-9 * rows // LANES) * LANES for rows in (inner, 4 * c1))
    prepared = pl.pallas_call(
        functools.partial(prepare_kernel, tiles_dev, edge_rows, mid_rows),
        out_shape=[
            shape((12 * c1, 3 * LANES), f32),
            shape((3 * inner, 6 * LANES), f32),
            shape((half_r * c2, mid_deep), bf16),
            shape((half_r * c2, edge_deep), bf16),
            shape((inner, cols), f32),
            shape((half_r * c2, half_x), f32),
            shape((LANES,), i32),
        ],
        in_specs=[vmem, vmem] + [smem] * 6 + [anywhere],
        out_specs=[vmem] * 6 + [smem],
        scratch_shapes=[pltpu.VMEM((mid_deep, LANES), f32), pltpu.VMEM((edge_deep, LANES), f32)],
        compiler_params=params,
        name="weights_and_scalars",
    )(
        conv_first.transpose(0, 1, 3, 2, 4),
        conv_second.transpose(1, 2, 3, 4, 0),
        bias_first,
        bias_second,
        disparities,
        pair_lists,
        view_counts,
        me,
        table,
    )
    kernel_edge, kernel_mid, two_mid, two_edge, bias_rows, bias_two, scalars = prepared

    band_scratch = [pltpu.VMEM((sources, cols + 2 * SHIFT, LANES), f32), pltpu.VMEM((1, cols, LANES), f32)]
    payload = shape((planes, 2 * c1, cols), bf16)
    edge_var, own, far, near, flags = pl.pallas_call(
        functools.partial(edge_kernel, at_slots, at_live, sources, blocks, edge_blocks),
        out_shape=[
            shape((planes, cols, LANES), bf16),
            shape((planes, 3 * c1, cols), f32),
            payload,
            payload,
            shape((2, c1, LANES), f32),
        ],
        in_specs=[hbm, vmem, vmem, hbm],
        out_specs=[vmem] * 5,
        scratch_shapes=band_scratch
        + [
            pltpu.SMEM(scalars.shape, i32),
            pltpu.VMEM(kernel_edge.shape, f32),
            pltpu.SemaphoreType.DMA((2,)),
        ],
        compiler_params=params,
        name="edge_rows",
    )(scalars, arrived, ref_features, kernel_edge)
    far = swapped(far, "view", 1)
    near = swapped(near, "view", 0)

    partial, choices = pl.pallas_call(
        functools.partial(mid_kernel, at_slots, at_live, sources, blocks, mid_blocks),
        out_shape=[shape((half_p, half_r * c2, half_x), f32), shape((3, cols, half_x), bf16)],
        in_specs=[smem] + [vmem] * 7,
        out_specs=[vmem, vmem],
        scratch_shapes=band_scratch
        + [pltpu.VMEM((planes, cols, LANES), bf16), pltpu.VMEM((planes * inner, cols), bf16)],
        compiler_params=params,
        name="middle_rows",
    )(scalars, arrived, ref_features, edge_var, kernel_mid, bias_rows, two_mid, bias_two)

    out = pl.pallas_call(
        end_kernel,
        out_shape=shape((half_p, half_r * c2, half_x), f32),
        in_specs=[vmem] * 8,
        out_specs=vmem,
        compiler_params=params,
        name="end_rows",
    )(far, near, flags, own, partial, bias_rows, two_edge, choices)
    return out.reshape(half_p, half_r, c2, half_x)


def solution(mesh):
    return jax.shard_map(
        on_device,
        mesh=mesh,
        in_specs=(
            P(("groups", "view"), None, None),
            P(("groups", "view"), None, None, None),
            P(("groups", "view"), None, None),
            P(("groups", "view")),
            P("groups", None),
            P(),
            P(),
            P(),
            P(),
        ),
        out_specs=P("groups", "view", None, None),
        check_vma=False,
    )
```

```python
import functools

import numpy as np

import jax
import jax.numpy as jnp
from jax import lax
from jax.experimental import pallas as pl
from jax.experimental.pallas import tpu as pltpu
from jax.sharding import PartitionSpec as P

SHIFT = 48
CAP = 2
LANES = 128
CHUNK = 64
VMEM_LIMIT = 10 * 1024 * 1024


def swapped(x, axis, parity):
    count = lax.axis_size(axis)
    pairs = [(i, i + 1) for i in range(parity, count - 1, 2)]
    return lax.ppermute(x, axis, pairs + [(j, i) for i, j in pairs])


def request_places(pair_lists, tiles_dev):
    owners, ranks, tiles = [], [], []
    for s in range(pair_lists.shape[1]):
        for b in range(pair_lists.shape[2]):
            tile = pair_lists[0, s, b]
            whole = jnp.maximum(tile, 0)
            owner = jnp.where(tile >= 0, lax.div(whole, tiles_dev), -1)
            rank = jnp.int32(0)
            for other in owners:
                rank = rank + jnp.where(other == owner, 1, 0)
            owners.append(owner)
            ranks.append(rank)
            tiles.append(lax.rem(whole, tiles_dev))
    return owners, ranks, tiles


def request_kernel(tiles_dev, pair_lists, table):
    n_view = table.shape[0]
    row = lax.broadcasted_iota(jnp.int32, (n_view, LANES), 0) * tiles_dev
    lane = lax.broadcasted_iota(jnp.int32, (n_view, LANES), 1)
    total = jnp.zeros((n_view, LANES), jnp.int32)
    count = jnp.zeros((n_view, LANES), jnp.int32)
    for s in range(pair_lists.shape[1]):
        for b in range(pair_lists.shape[2]):
            tile = pair_lists[0, s : s + 1, b : b + 1] - row
            owned = (tile >= 0) & (tile < tiles_dev)
            total = jnp.where(owned & (lane == count), tile, total)
            count = count + jnp.where(owned, 1, 0)
    for d in range(n_view):
        table[d] = total[d : d + 1, : table.shape[2]]


def prepare_kernel(
    tiles_dev,
    edge_rows,
    mid_rows,
    first,
    second,
    bias_first,
    bias_second,
    disparities,
    pair_lists,
    view_counts,
    me,
    _,
    kernel_edge,
    kernel_mid,
    two_mid,
    two_edge,
    bias_rows,
    bias_two,
    scalars,
    stacked_mid,
    stacked_edge,
):
    planes, sources = disparities.shape
    owners, ranks, _ = request_places(pair_lists, tiles_dev)
    at = 0
    for p in range(planes):
        for s in range(sources):
            scalars[at] = disparities[p, s]
            at += 1
    for owner, rank in zip(owners, ranks):
        scalars[at] = jnp.where(owner >= 0, owner * CAP + rank, 0)
        at += 1
    scalars[at] = view_counts[0]
    scalars[at + 1] = me[0]
    scalars[at + 2] = lax.rem(me[0], 2)
    tail = kernel_edge.shape[0] - 8
    lane_at = lax.broadcasted_iota(jnp.int32, (8, LANES), 1)
    numbers = jnp.zeros((8, LANES), jnp.float32)
    for i in range(at + 3):
        numbers = jnp.where(lane_at == i, scalars[i].astype(jnp.float32), numbers)
    kernel_edge[tail:, :] = numbers

    c1, channels = first.shape[3], first.shape[4]
    c2 = second.shape[4]
    rows_n = len(edge_rows) + len(mid_rows)
    half_r = rows_n // 2
    place = {row: i for i, row in enumerate(edge_rows + mid_rows)}
    per_group = LANES // channels
    filler = jnp.zeros((c1, LANES - channels), jnp.float32)
    taps = {}
    for a in range(3):
        for b in range(3):
            for d in range(3):
                tap = jnp.concatenate([first[a, b, d].astype(jnp.float32), filler], axis=1)
                for turn in range(per_group):
                    lane = turn * channels
                    taps[a, b, d, turn] = pltpu.roll(tap, lane, 1) if lane else tap

    def band(a, d, r, group):
        total = jnp.zeros((c1, LANES), jnp.float32)
        for b in range(3):
            at_place = place.get(r - 1 + b, -1)
            if at_place >= 0 and at_place // per_group == group:
                total = total + taps[a, b, d, at_place % per_group]
        return total

    rim = (-1, 0, rows_n - 1, rows_n)
    inner = tuple(range(1, rows_n - 1))
    for kernel, rows, groups in ((kernel_edge, rim, 1), (kernel_mid, inner, 2)):
        for d in range(3):
            for i, r in enumerate(rows):
                for a in range(3):
                    at = ((a * 3 + d) * len(rows) + i) * c1
                    for group in range(groups):
                        kernel[at : at + c1, group * LANES : (group + 1) * LANES] = band(a, d, r, group)

    def second_row(a, d, r):
        blocks = []
        for g in range(half_r):
            b = -1 if r is None else r - 2 * g + 1
            hit = 0 <= b < 3
            blocks.append(second[a, b, d].astype(jnp.float32) if hit else jnp.zeros((c1, c2), jnp.float32))
        blocks.append(jnp.zeros((c1, LANES - half_r * c2), jnp.float32))
        return jnp.concatenate(blocks, axis=1)

    for two, stacked, rows in ((two_mid, stacked_mid, inner), (two_edge, stacked_edge, rim[:3] + (None,))):
        stacked[...] = jnp.zeros(stacked.shape, jnp.float32)
        for a in range(3):
            for d in range(3):
                for i, r in enumerate(rows):
                    at = ((a * 3 + d) * len(rows) + i) * c1
                    stacked[at : at + c1, :] = second_row(a, d, r)
        two[...] = stacked[...].T[: half_r * c2].astype(jnp.bfloat16)

    def spread_bias(like, bias):
        index = lax.broadcasted_iota(jnp.int32, like.shape, 0)
        total = jnp.zeros(like.shape, jnp.float32)
        for i in range(bias.shape[0]):
            total = jnp.where(index % bias.shape[0] == i, bias[i], total)
        like[...] = total

    spread_bias(bias_rows, bias_first)
    spread_bias(bias_two, bias_second)


def plane_variance(p, at, sources, cols, disp, wide, ref_wide, ref_at, inv, store):
    for x0 in range(0, cols, CHUNK):
        ref = ref_wide[ref_at, x0 : x0 + CHUNK, :]
        summed = ref
        squares = ref * ref
        for s in range(sources):
            warped = wide[at + s, pl.ds(SHIFT + x0 - disp[p * sources + s], CHUNK), :]
            summed = summed + warped
            squares = squares + warped * warped
        store(x0, (squares - summed * summed * inv).astype(jnp.bfloat16))


def view_weights(live):
    total = live.astype(jnp.float32) + jnp.ones((1, LANES), jnp.float32)
    return 1.0 / total, lax.rsqrt(total)


def turned_reference(ref, blocks, picks):
    tile_rows = ref.shape[0] // blocks
    rows = [ref[block * tile_rows + i] for block in picks for i in range(tile_rows)]
    return jnp.concatenate(rows, axis=0).T.astype(jnp.float32)


def clear_bands(wide, cols):
    band = jnp.zeros((SHIFT, LANES), jnp.float32)
    for at in range(wide.shape[0]):
        wide[at, 0:SHIFT, :] = band
        wide[at, SHIFT + cols : 2 * SHIFT + cols, :] = band


def load_tiles(at_slots, live, sources, blocks, picks, scale, scalars, arrived, wide):
    for s in range(sources):
        slab = jnp.concatenate([arrived[scalars[at_slots + s * blocks + block]] for block in picks], axis=0)
        cols = slab.shape[1]
        wide[s, SHIFT : SHIFT + cols, :] = slab.T.astype(jnp.float32) * jnp.where(s < live, scale, 0.0)


def add_plane(q, planes, lhs, weights, sums):
    taps = lax.dot_general(weights, lhs, (((1,), (1,)), ((), ())), preferred_element_type=jnp.float32)
    rows = taps.shape[0] // 3
    if q + 1 < planes:
        sums[q + 1] = taps[:rows]
    if q == 0:
        sums[q] = taps[rows : 2 * rows]
    else:
        sums[q] += taps[rows : 2 * rows]
        sums[q - 1] += taps[2 * rows :]


def joined_columns(taps, column):
    rows, cols = column.shape
    left, center, right = taps[:rows], taps[rows : 2 * rows], taps[2 * rows :]
    total = center + jnp.where(column > 0, pltpu.roll(left, 1, 1), 0.0)
    return total + jnp.where(column < cols - 1, pltpu.roll(right, cols - 1, 1), 0.0)


def strided_planes(q, planes, taken, rows, weights):
    parts = []
    for plane in range(2 * q - 1, 2 * q + 2):
        for d in range(3):
            if 0 <= plane < planes:
                parts.append(taken[d][plane * rows : (plane + 1) * rows])
            else:
                parts.append(jnp.zeros((rows, taken[d].shape[1]), jnp.bfloat16))
    rhs = jnp.concatenate(parts, axis=0)
    return jnp.dot(weights[:, : rhs.shape[0]], rhs, preferred_element_type=jnp.float32)


def edge_kernel(
    at_slots, at_live, sources, blocks, picks, packed, arrived, ref, var, own, far, near, flags, wide, ref_wide, sums, held, sem
):
    planes, cols, _ = var.shape
    tail = packed.shape[0] - 8
    c1 = tail // 36
    copy = pltpu.make_async_copy(packed.at[pl.ds(tail, 8)], held, sem)
    copy.start()
    weights = packed[:tail].astype(jnp.bfloat16)
    turned = turned_reference(ref, blocks, picks)
    clear_bands(wide, cols)
    copy.wait()
    scalars = [held[0, i].astype(jnp.int32) for i in range(at_live + 3)]
    live = scalars[at_live]
    inv, scale = view_weights(live)
    ref_wide[0] = turned * scale
    load_tiles(at_slots, live, sources, blocks, picks, scale, scalars, arrived, wide)
    odd = scalars[at_live + 2] > 0
    flags[0] = jnp.where(odd, 1.0, 0.0) * jnp.ones((c1, LANES), jnp.float32)
    flags[1] = jnp.where(scalars[at_live + 1] > 0, 1.0, 0.0) * jnp.ones((c1, LANES), jnp.float32)
    column = lax.broadcasted_iota(jnp.int32, (4 * c1, cols), 1)
    empty = jnp.zeros((c1, cols), jnp.float32)

    def finish(p):
        total = joined_columns(sums[p], column)
        own[p] = total[: 3 * c1]
        downward = total[2 * c1 :]
        upward = jnp.concatenate([total[:c1], empty], axis=0)
        far[p] = jnp.where(odd, downward, upward).astype(jnp.bfloat16)
        near[p] = jnp.where(odd, upward, downward).astype(jnp.bfloat16)

    for q in range(planes):

        def store(x0, value):
            var[q, x0 : x0 + CHUNK, :] = value

        plane_variance(q, 0, sources, cols, scalars, wide, ref_wide, 0, inv, store)
        add_plane(q, planes, var[q], weights, sums)
        if q > 0:
            finish(q - 1)
    finish(planes - 1)


def mid_kernel(
    at_slots,
    at_live,
    sources,
    blocks,
    picks,
    scalars,
    arrived,
    ref,
    edge_var,
    kernel,
    bias_rows,
    kernel_two,
    bias_two,
    out,
    choices,
    wide,
    ref_wide,
    var,
    cost,
    sums,
):
    planes, cols, _ = var.shape
    out_w = out.shape[2]
    inner = cost.shape[0] // planes
    live = scalars[at_live]
    inv, scale = view_weights(live)
    ref_wide[0] = turned_reference(ref, blocks, picks) * scale
    clear_bands(wide, cols)
    load_tiles(at_slots, live, sources, blocks, picks, scale, scalars, arrived, wide)
    weights = kernel[...].astype(jnp.bfloat16)
    bias = bias_rows[:inner]
    column = lax.broadcasted_iota(jnp.int32, (inner, cols), 1)
    row = lax.broadcasted_iota(jnp.int32, (cols, out_w), 0)
    target = 2 * lax.broadcasted_iota(jnp.int32, (cols, out_w), 1)
    for d in range(3):
        choices[d] = jnp.where(row == target + (d - 1), 1.0, 0.0).astype(jnp.bfloat16)

    def finish(p):
        total = joined_columns(sums[p], column)
        cost[p * inner : (p + 1) * inner, :] = jnp.maximum(total + bias, 0.0).astype(jnp.bfloat16)

    for q in range(planes):

        def store(x0, value):
            var[q, x0 : x0 + CHUNK, :] = value

        plane_variance(q, 0, sources, cols, scalars, wide, ref_wide, 0, inv, store)
        add_plane(q, planes, jnp.concatenate([edge_var[q], var[q]], axis=1), weights, sums)
        if q > 0:
            finish(q - 1)
    finish(planes - 1)
    taken = [
        jnp.dot(cost[...], choices[d], preferred_element_type=jnp.float32).astype(jnp.bfloat16) for d in range(3)
    ]
    for q in range(planes // 2):
        out[q] = strided_planes(q, planes, taken, inner, kernel_two) + bias_two[...]


def end_kernel(far, near, flags, own, partial, bias_rows, kernel_two, choices, out):
    planes, ends, cols = own.shape
    c1 = ends // 3
    odd = jnp.concatenate([flags[0]] * (cols // LANES), axis=1) > 0.5
    not_top = jnp.concatenate([flags[1]] * (cols // LANES), axis=1)
    empty = jnp.zeros((c1, cols), jnp.float32)
    bias = bias_rows[:c1]
    rows = []
    for p in range(planes):
        lower, upper = far[p].astype(jnp.float32), near[p].astype(jnp.float32)
        before = own[p, :c1] + jnp.where(odd, upper[:c1], lower[:c1])
        top = own[p, c1 : 2 * c1] + jnp.where(odd, upper[c1:], lower[c1:])
        bottom = own[p, 2 * c1 :] + jnp.where(odd, lower[:c1], upper[:c1])
        rows += [jnp.maximum(before + bias, 0.0) * not_top]
        rows += [jnp.maximum(top + bias, 0.0), jnp.maximum(bottom + bias, 0.0), empty]
    cost = jnp.concatenate(rows, axis=0).astype(jnp.bfloat16)
    taken = [jnp.dot(cost, choices[d], preferred_element_type=jnp.float32).astype(jnp.bfloat16) for d in range(3)]
    for q in range(planes // 2):
        out[q] = partial[q] + strided_planes(q, planes, taken, 4 * c1, kernel_two)


def on_device(
    ref_features,
    source_tiles,
    pair_lists,
    view_counts,
    disparities,
    conv_first,
    bias_first,
    conv_second,
    bias_second,
):
    n_view = lax.axis_size("view")
    me = lax.axis_index("view").reshape(1)
    rows_n, channels, cols = ref_features.shape
    tiles_dev, tile_rows = source_tiles.shape[0], source_tiles.shape[1]
    sources, blocks = pair_lists.shape[1], pair_lists.shape[2]
    planes = disparities.shape[0]
    slab = tile_rows * channels
    c1, c2 = conv_first.shape[2], conv_second.shape[0]
    half_r, half_p, half_x = rows_n // 2, planes // 2, cols // 2
    smem = pl.BlockSpec(memory_space=pltpu.SMEM)
    vmem = pl.BlockSpec(memory_space=pltpu.VMEM)
    anywhere = pl.BlockSpec(memory_space=pl.ANY)
    params = pltpu.CompilerParams(vmem_limit_bytes=VMEM_LIMIT)
    bf16, f32, i32 = jnp.bfloat16, jnp.float32, jnp.int32
    shape = jax.ShapeDtypeStruct

    table = pl.pallas_call(
        functools.partial(request_kernel, tiles_dev),
        out_shape=shape((n_view, 1, CAP), i32),
        in_specs=[vmem],
        out_specs=vmem,
        compiler_params=params,
        name="request_table",
    )(pair_lists)
    table = lax.all_to_all(table, "view", split_axis=0, concat_axis=0, tiled=True)
    outgoing = source_tiles.reshape(tiles_dev, slab, cols)[table[:, 0]]
    arrived = lax.all_to_all(outgoing, "view", split_axis=0, concat_axis=0, tiled=True)
    arrived = arrived.reshape(n_view * CAP, slab, cols)

    at_slots = planes * sources
    at_live = at_slots + sources * blocks
    edge_blocks, mid_blocks = (0, blocks - 1), tuple(range(1, blocks - 1))
    rows_of = lambda picks: [block * tile_rows + i for block in picks for i in range(tile_rows)]
    edge_rows, mid_rows = rows_of(edge_blocks), rows_of(mid_blocks)
    inner = (rows_n - 2) * c1
    mid_deep, edge_deep = (-(-9 * rows // LANES) * LANES for rows in (inner, 4 * c1))
    prepared = pl.pallas_call(
        functools.partial(prepare_kernel, tiles_dev, edge_rows, mid_rows),
        out_shape=[
            shape((36 * c1 + 8, LANES), f32),
            shape((9 * inner, 2 * LANES), f32),
            shape((half_r * c2, mid_deep), bf16),
            shape((half_r * c2, edge_deep), bf16),
            shape((inner, cols), f32),
            shape((half_r * c2, half_x), f32),
            shape((LANES,), i32),
        ],
        in_specs=[vmem, vmem] + [smem] * 6 + [anywhere],
        out_specs=[vmem] * 6 + [smem],
        scratch_shapes=[pltpu.VMEM((mid_deep, LANES), f32), pltpu.VMEM((edge_deep, LANES), f32)],
        compiler_params=params,
        name="weights_and_scalars",
    )(
        conv_first.transpose(0, 1, 3, 2, 4),
        conv_second.transpose(1, 2, 3, 4, 0),
        bias_first,
        bias_second,
        disparities,
        pair_lists,
        view_counts,
        me,
        table,
    )
    kernel_edge, kernel_mid, two_mid, two_edge, bias_rows, bias_two, scalars = prepared

    band_scratch = [pltpu.VMEM((sources, cols + 2 * SHIFT, LANES), f32), pltpu.VMEM((1, cols, LANES), f32)]
    payload = shape((planes, 2 * c1, cols), bf16)
    edge_var, own, far, near, flags = pl.pallas_call(
        functools.partial(edge_kernel, at_slots, at_live, sources, blocks, edge_blocks),
        out_shape=[
            shape((planes, cols, LANES), bf16),
            shape((planes, 3 * c1, cols), f32),
            payload,
            payload,
            shape((2, c1, LANES), f32),
        ],
        in_specs=[vmem] * 3,
        out_specs=[vmem] * 5,
        scratch_shapes=band_scratch
        + [
            pltpu.VMEM((planes, 12 * c1, cols), f32),
            pltpu.SMEM((8, LANES), f32),
            pltpu.SemaphoreType.DMA,
        ],
        compiler_params=params,
        name="edge_rows",
    )(kernel_edge, arrived, ref_features)
    far = swapped(far, "view", 1)
    near = swapped(near, "view", 0)

    partial, choices = pl.pallas_call(
        functools.partial(mid_kernel, at_slots, at_live, sources, blocks, mid_blocks),
        out_shape=[shape((half_p, half_r * c2, half_x), f32), shape((3, cols, half_x), bf16)],
        in_specs=[smem] + [vmem] * 7,
        out_specs=[vmem, vmem],
        scratch_shapes=band_scratch
        + [
            pltpu.VMEM((planes, cols, LANES), bf16),
            pltpu.VMEM((planes * inner, cols), bf16),
            pltpu.VMEM((planes, 3 * inner, cols), f32),
        ],
        compiler_params=params,
        name="middle_rows",
    )(scalars, arrived, ref_features, edge_var, kernel_mid, bias_rows, two_mid, bias_two)

    out = pl.pallas_call(
        end_kernel,
        out_shape=shape((half_p, half_r * c2, half_x), f32),
        in_specs=[vmem] * 8,
        out_specs=vmem,
        compiler_params=params,
        name="end_rows",
    )(far, near, flags, own, partial, bias_rows, two_edge, choices)
    return out.reshape(half_p, half_r, c2, half_x)


def solution(mesh):
    return jax.shard_map(
        on_device,
        mesh=mesh,
        in_specs=(
            P(("groups", "view"), None, None),
            P(("groups", "view"), None, None, None),
            P(("groups", "view"), None, None),
            P(("groups", "view")),
            P("groups", None),
            P(),
            P(),
            P(),
            P(),
        ),
        out_specs=P("groups", "view", None, None),
        check_vma=False,
    )
```

```python
import functools

import numpy as np

import jax
import jax.numpy as jnp
from jax import lax
from jax.experimental import pallas as pl
from jax.experimental.pallas import tpu as pltpu
from jax.sharding import PartitionSpec as P

SHIFT = 48
CAP = 2
SHIFT_BITS = 7
SLOT_BITS = 15
LANES = 128
CHUNK = 64
VMEM_LIMIT = 10 * 1024 * 1024


def swapped(x, axis, parity):
    count = lax.axis_size(axis)
    pairs = [(i, i + 1) for i in range(parity, count - 1, 2)]
    return lax.ppermute(x, axis, pairs + [(j, i) for i, j in pairs])


def pack(values, bits):
    total = values[0]
    for i, value in enumerate(values[1:]):
        total = total + value * (1 << (bits * (i + 1)))
    return total


def unpack(total, count, bits):
    return [lax.shift_right_logical(total, bits * i) & ((1 << bits) - 1) for i in range(count)]


def unpacked(numbers, planes, sources, blocks):
    shifts = [[value - SHIFT for value in unpack(numbers[p][0], sources, SHIFT_BITS)] for p in range(planes)]
    pairs = [unpack(numbers[planes + i][0], 2, SLOT_BITS) for i in range(sources * blocks // 2)]
    flat = [slot for pair in pairs for slot in pair]
    slots = [flat[s * blocks : (s + 1) * blocks] for s in range(sources)]
    last = numbers[-1][0]
    return shifts, slots, lax.shift_right_logical(last, 2), (last & 2) > 0, (last & 1) > 0


def request_places(pair_lists, tiles_dev):
    owners, ranks, tiles = [], [], []
    for s in range(pair_lists.shape[1]):
        for b in range(pair_lists.shape[2]):
            tile = pair_lists[0, s, b]
            whole = jnp.maximum(tile, 0)
            owner = jnp.where(tile >= 0, lax.div(whole, tiles_dev), -1)
            rank = jnp.int32(0)
            for other in owners:
                rank = rank + jnp.where(other == owner, 1, 0)
            owners.append(owner)
            ranks.append(rank)
            tiles.append(lax.rem(whole, tiles_dev))
    return owners, ranks, tiles


def request_kernel(tiles_dev, pair_lists, table):
    n_view = table.shape[0]
    row = lax.broadcasted_iota(jnp.int32, (n_view, LANES), 0) * tiles_dev
    lane = lax.broadcasted_iota(jnp.int32, (n_view, LANES), 1)
    total = jnp.zeros((n_view, LANES), jnp.int32)
    count = jnp.zeros((n_view, LANES), jnp.int32)
    for s in range(pair_lists.shape[1]):
        for b in range(pair_lists.shape[2]):
            tile = pair_lists[0, s : s + 1, b : b + 1] - row
            owned = (tile >= 0) & (tile < tiles_dev)
            total = jnp.where(owned & (lane == count), tile, total)
            count = count + jnp.where(owned, 1, 0)
    for d in range(n_view):
        table[d] = total[d : d + 1, : table.shape[2]]


def prepare_kernel(
    tiles_dev,
    edge_rows,
    mid_rows,
    first,
    second,
    bias_first,
    bias_second,
    disparities,
    pair_lists,
    view_counts,
    me,
    _,
    kernel_edge,
    kernel_mid,
    two_mid,
    two_edge,
    bias_rows,
    bias_two,
    *rest,
):
    numbers, (stacked_mid, stacked_edge) = rest[:-2], rest[-2:]
    planes, sources = disparities.shape
    blocks = pair_lists.shape[2]
    owners, ranks, _ = request_places(pair_lists, tiles_dev)
    for p in range(planes):
        numbers[p][0] = pack([disparities[p, s] + SHIFT for s in range(sources)], SHIFT_BITS)
    slots = [jnp.where(owner >= 0, owner * CAP + rank, 0) for owner, rank in zip(owners, ranks)]
    for i in range(len(slots) // 2):
        numbers[planes + i][0] = pack(slots[2 * i : 2 * i + 2], SLOT_BITS)
    numbers[-1][0] = view_counts[0] * 4 + jnp.where(me[0] > 0, 2, 0) + lax.rem(me[0], 2)

    c1, channels = first.shape[3], first.shape[4]
    c2 = second.shape[4]
    rows_n = len(edge_rows) + len(mid_rows)
    half_r = rows_n // 2
    place = {row: i for i, row in enumerate(edge_rows + mid_rows)}
    per_group = LANES // channels
    filler = jnp.zeros((c1, LANES - channels), jnp.float32)
    taps = {}
    for a in range(3):
        for b in range(3):
            for d in range(3):
                tap = jnp.concatenate([first[a, b, d].astype(jnp.float32), filler], axis=1)
                for turn in range(per_group):
                    lane = turn * channels
                    taps[a, b, d, turn] = pltpu.roll(tap, lane, 1) if lane else tap

    def band(a, d, r, group):
        total = jnp.zeros((c1, LANES), jnp.float32)
        for b in range(3):
            at_place = place.get(r - 1 + b, -1)
            if at_place >= 0 and at_place // per_group == group:
                total = total + taps[a, b, d, at_place % per_group]
        return total

    rim = (-1, 0, rows_n - 1, rows_n)
    inner = tuple(range(1, rows_n - 1))
    for kernel, rows, groups in ((kernel_edge, rim, 1), (kernel_mid, inner, 2)):
        for d in range(3):
            for i, r in enumerate(rows):
                for a in range(3):
                    at = ((a * 3 + d) * len(rows) + i) * c1
                    for group in range(groups):
                        kernel[at : at + c1, group * LANES : (group + 1) * LANES] = band(a, d, r, group)

    def second_row(a, d, r):
        blocks = []
        for g in range(half_r):
            b = -1 if r is None else r - 2 * g + 1
            hit = 0 <= b < 3
            blocks.append(second[a, b, d].astype(jnp.float32) if hit else jnp.zeros((c1, c2), jnp.float32))
        blocks.append(jnp.zeros((c1, LANES - half_r * c2), jnp.float32))
        return jnp.concatenate(blocks, axis=1)

    for two, stacked, rows in ((two_mid, stacked_mid, inner), (two_edge, stacked_edge, rim[:3] + (None,))):
        stacked[...] = jnp.zeros(stacked.shape, jnp.float32)
        for a in range(3):
            for d in range(3):
                for i, r in enumerate(rows):
                    at = ((a * 3 + d) * len(rows) + i) * c1
                    stacked[at : at + c1, :] = second_row(a, d, r)
        two[...] = stacked[...].T[: half_r * c2].astype(jnp.bfloat16)

    def spread_bias(like, bias):
        index = lax.broadcasted_iota(jnp.int32, like.shape, 0)
        total = jnp.zeros(like.shape, jnp.float32)
        for i in range(bias.shape[0]):
            total = jnp.where(index % bias.shape[0] == i, bias[i], total)
        like[...] = total

    spread_bias(bias_rows, bias_first)
    spread_bias(bias_two, bias_second)


def plane_variance(shifts, cols, wide, ref_wide, inv, store):
    for x0 in range(0, cols, CHUNK):
        ref = ref_wide[x0 : x0 + CHUNK, :]
        summed = ref
        squares = ref * ref
        for s, shift in enumerate(shifts):
            warped = wide[s, pl.ds(SHIFT + x0 - shift, CHUNK), :]
            summed = summed + warped
            squares = squares + warped * warped
        store(x0, (squares - summed * summed * inv).astype(jnp.bfloat16))


def view_weights(live):
    total = live.astype(jnp.float32) + jnp.ones((1, LANES), jnp.float32)
    return 1.0 / total, lax.rsqrt(total)


def turned_reference(ref, blocks, picks):
    tile_rows = ref.shape[0] // blocks
    rows = [ref[block * tile_rows + i] for block in picks for i in range(tile_rows)]
    return jnp.concatenate(rows, axis=0).T.astype(jnp.float32)


def clear_bands(wide, cols):
    band = jnp.zeros((SHIFT, LANES), jnp.float32)
    for at in range(wide.shape[0]):
        wide[at, 0:SHIFT, :] = band
        wide[at, SHIFT + cols : 2 * SHIFT + cols, :] = band


def load_tiles(slots, live, picks, scale, arrived, wide):
    for s, places in enumerate(slots):
        slab = jnp.concatenate([arrived[places[block]] for block in picks], axis=0)
        cols = slab.shape[1]
        wide[s, SHIFT : SHIFT + cols, :] = slab.T.astype(jnp.float32) * jnp.where(s < live, scale, 0.0)


def add_plane(q, planes, lhs, weights, sums):
    taps = lax.dot_general(weights, lhs, (((1,), (1,)), ((), ())), preferred_element_type=jnp.float32)
    rows = taps.shape[0] // 3
    if q + 1 < planes:
        sums[q + 1] = taps[:rows]
    if q == 0:
        sums[q] = taps[rows : 2 * rows]
    else:
        sums[q] += taps[rows : 2 * rows]
        sums[q - 1] += taps[2 * rows :]


def joined_columns(taps, column):
    rows, cols = column.shape
    left, center, right = taps[:rows], taps[rows : 2 * rows], taps[2 * rows :]
    total = center + jnp.where(column > 0, pltpu.roll(left, 1, 1), 0.0)
    return total + jnp.where(column < cols - 1, pltpu.roll(right, cols - 1, 1), 0.0)


def strided_planes(q, planes, taken, rows, weights):
    parts = []
    for plane in range(2 * q - 1, 2 * q + 2):
        for d in range(3):
            if 0 <= plane < planes:
                parts.append(taken[d][plane * rows : (plane + 1) * rows])
            else:
                parts.append(jnp.zeros((rows, taken[d].shape[1]), jnp.bfloat16))
    rhs = jnp.concatenate(parts, axis=0)
    return jnp.dot(weights[:, : rhs.shape[0]], rhs, preferred_element_type=jnp.float32)


def warp_kernel(n_numbers, sources, blocks, picks, *refs):
    arrived, ref, var, flags, wide, ref_wide = refs[n_numbers:]
    planes, cols, _ = var.shape
    shifts, slots, live, not_top, odd = unpacked(refs[:n_numbers], planes, sources, blocks)
    inv, scale = view_weights(live)
    ref_wide[...] = turned_reference(ref, blocks, picks) * scale
    clear_bands(wide, cols)
    load_tiles(slots, live, picks, scale, arrived, wide)
    flags[0] = jnp.where(odd, 1.0, 0.0) * jnp.ones(flags.shape[1:], jnp.float32)
    flags[1] = jnp.where(not_top, 1.0, 0.0) * jnp.ones(flags.shape[1:], jnp.float32)
    for p in range(planes):

        def store(x0, value):
            var[p, x0 : x0 + CHUNK, :] = value

        plane_variance(shifts[p], cols, wide, ref_wide, inv, store)


def edge_kernel(var, kernel, flags, own, far, near, sums):
    planes, cols, _ = var.shape
    c1 = kernel.shape[0] // 36
    odd = jnp.concatenate([flags[0]] * 2, axis=0)[:, :1] > 0.5
    weights = kernel[...].astype(jnp.bfloat16)
    column = lax.broadcasted_iota(jnp.int32, (4 * c1, cols), 1)
    empty = jnp.zeros((c1, cols), jnp.float32)

    def finish(p):
        total = joined_columns(sums[p], column)
        own[p] = total[: 3 * c1]
        downward = total[2 * c1 :]
        upward = jnp.concatenate([total[:c1], empty], axis=0)
        far[p] = jnp.where(odd, downward, upward).astype(jnp.bfloat16)
        near[p] = jnp.where(odd, upward, downward).astype(jnp.bfloat16)

    for q in range(planes):
        add_plane(q, planes, var[q], weights, sums)
        if q > 0:
            finish(q - 1)
    finish(planes - 1)


def mid_kernel(n_numbers, sources, blocks, picks, *refs):
    arrived, ref, edge_var, kernel, bias_rows, kernel_two, bias_two = refs[n_numbers : n_numbers + 7]
    out, choices, wide, ref_wide, var, cost, sums = refs[n_numbers + 7 :]
    planes, cols, _ = var.shape
    out_w = out.shape[2]
    inner = cost.shape[0] // planes
    shifts, slots, live, _, _ = unpacked(refs[:n_numbers], planes, sources, blocks)
    inv, scale = view_weights(live)
    ref_wide[...] = turned_reference(ref, blocks, picks) * scale
    clear_bands(wide, cols)
    load_tiles(slots, live, picks, scale, arrived, wide)
    weights = kernel[...].astype(jnp.bfloat16)
    bias = bias_rows[:inner]
    column = lax.broadcasted_iota(jnp.int32, (inner, cols), 1)
    row = lax.broadcasted_iota(jnp.int32, (cols, out_w), 0)
    target = 2 * lax.broadcasted_iota(jnp.int32, (cols, out_w), 1)
    for d in range(3):
        choices[d] = jnp.where(row == target + (d - 1), 1.0, 0.0).astype(jnp.bfloat16)

    def finish(p):
        total = joined_columns(sums[p], column)
        cost[p * inner : (p + 1) * inner, :] = jnp.maximum(total + bias, 0.0).astype(jnp.bfloat16)

    for q in range(planes):

        def store(x0, value):
            var[q, x0 : x0 + CHUNK, :] = value

        plane_variance(shifts[q], cols, wide, ref_wide, inv, store)
        add_plane(q, planes, jnp.concatenate([edge_var[q], var[q]], axis=1), weights, sums)
        if q > 0:
            finish(q - 1)
    finish(planes - 1)
    taken = [
        jnp.dot(cost[...], choices[d], preferred_element_type=jnp.float32).astype(jnp.bfloat16) for d in range(3)
    ]
    for q in range(planes // 2):
        out[q] = strided_planes(q, planes, taken, inner, kernel_two) + bias_two[...]


def end_kernel(far, near, flags, own, partial, bias_rows, kernel_two, choices, out):
    planes, ends, cols = own.shape
    c1 = ends // 3
    odd = jnp.concatenate([flags[0]] * (cols // LANES), axis=1) > 0.5
    not_top = jnp.concatenate([flags[1]] * (cols // LANES), axis=1)
    empty = jnp.zeros((c1, cols), jnp.float32)
    bias = bias_rows[:c1]
    rows = []
    for p in range(planes):
        lower, upper = far[p].astype(jnp.float32), near[p].astype(jnp.float32)
        before = own[p, :c1] + jnp.where(odd, upper[:c1], lower[:c1])
        top = own[p, c1 : 2 * c1] + jnp.where(odd, upper[c1:], lower[c1:])
        bottom = own[p, 2 * c1 :] + jnp.where(odd, lower[:c1], upper[:c1])
        rows += [jnp.maximum(before + bias, 0.0) * not_top]
        rows += [jnp.maximum(top + bias, 0.0), jnp.maximum(bottom + bias, 0.0), empty]
    cost = jnp.concatenate(rows, axis=0).astype(jnp.bfloat16)
    taken = [jnp.dot(cost, choices[d], preferred_element_type=jnp.float32).astype(jnp.bfloat16) for d in range(3)]
    for q in range(planes // 2):
        out[q] = partial[q] + strided_planes(q, planes, taken, 4 * c1, kernel_two)


def on_device(
    ref_features,
    source_tiles,
    pair_lists,
    view_counts,
    disparities,
    conv_first,
    bias_first,
    conv_second,
    bias_second,
):
    n_view = lax.axis_size("view")
    me = lax.axis_index("view").reshape(1)
    rows_n, channels, cols = ref_features.shape
    tiles_dev, tile_rows = source_tiles.shape[0], source_tiles.shape[1]
    sources, blocks = pair_lists.shape[1], pair_lists.shape[2]
    planes = disparities.shape[0]
    slab = tile_rows * channels
    c1, c2 = conv_first.shape[2], conv_second.shape[0]
    half_r, half_p, half_x = rows_n // 2, planes // 2, cols // 2
    smem = pl.BlockSpec(memory_space=pltpu.SMEM)
    vmem = pl.BlockSpec(memory_space=pltpu.VMEM)
    anywhere = pl.BlockSpec(memory_space=pl.ANY)
    params = pltpu.CompilerParams(vmem_limit_bytes=VMEM_LIMIT)
    bf16, f32, i32 = jnp.bfloat16, jnp.float32, jnp.int32
    shape = jax.ShapeDtypeStruct

    table = pl.pallas_call(
        functools.partial(request_kernel, tiles_dev),
        out_shape=shape((n_view, 1, CAP), i32),
        in_specs=[vmem],
        out_specs=vmem,
        compiler_params=params,
        name="request_table",
    )(pair_lists)
    table = lax.all_to_all(table, "view", split_axis=0, concat_axis=0, tiled=True)
    outgoing = source_tiles.reshape(tiles_dev, slab, cols)[table[:, 0]]
    arrived = lax.all_to_all(outgoing, "view", split_axis=0, concat_axis=0, tiled=True)
    arrived = arrived.reshape(n_view * CAP, slab, cols)

    n_numbers = planes + sources * blocks // 2 + 1
    edge_blocks, mid_blocks = (0, blocks - 1), tuple(range(1, blocks - 1))
    rows_of = lambda picks: [block * tile_rows + i for block in picks for i in range(tile_rows)]
    edge_rows, mid_rows = rows_of(edge_blocks), rows_of(mid_blocks)
    inner = (rows_n - 2) * c1
    mid_deep, edge_deep = (-(-9 * rows // LANES) * LANES for rows in (inner, 4 * c1))
    prepared = pl.pallas_call(
        functools.partial(prepare_kernel, tiles_dev, edge_rows, mid_rows),
        out_shape=[
            shape((36 * c1, LANES), f32),
            shape((9 * inner, 2 * LANES), f32),
            shape((half_r * c2, mid_deep), bf16),
            shape((half_r * c2, edge_deep), bf16),
            shape((inner, cols), f32),
            shape((half_r * c2, half_x), f32),
        ]
        + [shape((1,), i32)] * n_numbers,
        in_specs=[vmem, vmem] + [smem] * 6 + [anywhere],
        out_specs=[vmem] * 6 + [smem] * n_numbers,
        scratch_shapes=[pltpu.VMEM((mid_deep, LANES), f32), pltpu.VMEM((edge_deep, LANES), f32)],
        compiler_params=params,
        name="weights_and_scalars",
    )(
        conv_first.transpose(0, 1, 3, 2, 4),
        conv_second.transpose(1, 2, 3, 4, 0),
        bias_first,
        bias_second,
        disparities,
        pair_lists,
        view_counts,
        me,
        table,
    )
    kernel_edge, kernel_mid, two_mid, two_edge, bias_rows, bias_two, *numbers = prepared

    band_scratch = [pltpu.VMEM((sources, cols + 2 * SHIFT, LANES), f32), pltpu.VMEM((cols, LANES), f32)]
    payload = shape((planes, 2 * c1, cols), bf16)
    edge_var, flags = pl.pallas_call(
        functools.partial(warp_kernel, n_numbers, sources, blocks, edge_blocks),
        out_shape=[shape((planes, cols, LANES), bf16), shape((2, c1, LANES), f32)],
        in_specs=[smem] * n_numbers + [vmem] * 2,
        out_specs=[vmem] * 2,
        scratch_shapes=band_scratch,
        compiler_params=params,
        name="edge_variance",
    )(*numbers, arrived, ref_features)
    own, far, near = pl.pallas_call(
        edge_kernel,
        out_shape=[shape((planes, 3 * c1, cols), f32), payload, payload],
        in_specs=[vmem] * 3,
        out_specs=[vmem] * 3,
        scratch_shapes=[pltpu.VMEM((planes, 12 * c1, cols), f32)],
        compiler_params=params,
        name="edge_rows",
    )(edge_var, kernel_edge, flags)
    far = swapped(far, "view", 1)
    near = swapped(near, "view", 0)

    partial, choices = pl.pallas_call(
        functools.partial(mid_kernel, n_numbers, sources, blocks, mid_blocks),
        out_shape=[shape((half_p, half_r * c2, half_x), f32), shape((3, cols, half_x), bf16)],
        in_specs=[smem] * n_numbers + [vmem] * 7,
        out_specs=[vmem, vmem],
        scratch_shapes=band_scratch
        + [
            pltpu.VMEM((planes, cols, LANES), bf16),
            pltpu.VMEM((planes * inner, cols), bf16),
            pltpu.VMEM((planes, 3 * inner, cols), f32),
        ],
        compiler_params=params,
        name="middle_rows",
    )(*numbers, arrived, ref_features, edge_var, kernel_mid, bias_rows, two_mid, bias_two)

    out = pl.pallas_call(
        end_kernel,
        out_shape=shape((half_p, half_r * c2, half_x), f32),
        in_specs=[vmem] * 8,
        out_specs=vmem,
        compiler_params=params,
        name="end_rows",
    )(far, near, flags, own, partial, bias_rows, two_edge, choices)
    return out.reshape(half_p, half_r, c2, half_x)


def solution(mesh):
    return jax.shard_map(
        on_device,
        mesh=mesh,
        in_specs=(
            P(("groups", "view"), None, None),
            P(("groups", "view"), None, None, None),
            P(("groups", "view"), None, None),
            P(("groups", "view")),
            P("groups", None),
            P(),
            P(),
            P(),
            P(),
        ),
        out_specs=P("groups", "view", None, None),
        check_vma=False,
    )
```

```python
import functools

import numpy as np

import jax
import jax.numpy as jnp
from jax import lax
from jax.experimental import pallas as pl
from jax.experimental.pallas import tpu as pltpu
from jax.sharding import PartitionSpec as P

SHIFT = 48
CAP = 2
SHIFT_BITS = 7
SLOT_BITS = 15
LANES = 128
CHUNK = 64
VMEM_LIMIT = 10 * 1024 * 1024


def swapped(x, axis, parity):
    count = lax.axis_size(axis)
    pairs = [(i, i + 1) for i in range(parity, count - 1, 2)]
    return lax.ppermute(x, axis, pairs + [(j, i) for i, j in pairs])


def pack(values, bits):
    total = values[0]
    for i, value in enumerate(values[1:]):
        total = total + value * (1 << (bits * (i + 1)))
    return total


def unpack(total, count, bits):
    return [lax.shift_right_logical(total, bits * i) & ((1 << bits) - 1) for i in range(count)]


def unpacked(numbers, planes, sources, blocks):
    shifts = [[value - SHIFT for value in unpack(numbers[p][0], sources, SHIFT_BITS)] for p in range(planes)]
    pairs = [unpack(numbers[planes + i][0], 2, SLOT_BITS) for i in range(sources * blocks // 2)]
    flat = [slot for pair in pairs for slot in pair]
    slots = [flat[s * blocks : (s + 1) * blocks] for s in range(sources)]
    last = numbers[-1][0]
    return shifts, slots, lax.shift_right_logical(last, 2), (last & 2) > 0, (last & 1) > 0


def fetch(numbers, held, sem):
    copies = [pltpu.make_async_copy(number, into, sem.at[i]) for i, (number, into) in enumerate(zip(numbers, held))]
    for copy in copies:
        copy.start()
    return copies


def request_places(pair_lists, tiles_dev):
    owners, ranks, tiles = [], [], []
    for s in range(pair_lists.shape[1]):
        for b in range(pair_lists.shape[2]):
            tile = pair_lists[0, s, b]
            whole = jnp.maximum(tile, 0)
            owner = jnp.where(tile >= 0, lax.div(whole, tiles_dev), -1)
            rank = jnp.int32(0)
            for other in owners:
                rank = rank + jnp.where(other == owner, 1, 0)
            owners.append(owner)
            ranks.append(rank)
            tiles.append(lax.rem(whole, tiles_dev))
    return owners, ranks, tiles


def request_kernel(tiles_dev, pair_lists, table):
    n_view = table.shape[0]
    row = lax.broadcasted_iota(jnp.int32, (n_view, LANES), 0) * tiles_dev
    lane = lax.broadcasted_iota(jnp.int32, (n_view, LANES), 1)
    total = jnp.zeros((n_view, LANES), jnp.int32)
    count = jnp.zeros((n_view, LANES), jnp.int32)
    for s in range(pair_lists.shape[1]):
        for b in range(pair_lists.shape[2]):
            tile = pair_lists[0, s : s + 1, b : b + 1] - row
            owned = (tile >= 0) & (tile < tiles_dev)
            total = jnp.where(owned & (lane == count), tile, total)
            count = count + jnp.where(owned, 1, 0)
    for d in range(n_view):
        table[d] = total[d : d + 1, : table.shape[2]]


def prepare_kernel(
    tiles_dev,
    edge_rows,
    mid_rows,
    first,
    second,
    bias_first,
    bias_second,
    disparities,
    pair_lists,
    view_counts,
    me,
    _,
    kernel_edge,
    kernel_mid,
    two_mid,
    two_edge,
    bias_rows,
    bias_two,
    *rest,
):
    numbers, (stacked_mid, stacked_edge) = rest[:-2], rest[-2:]
    planes, sources = disparities.shape
    blocks = pair_lists.shape[2]
    owners, ranks, _ = request_places(pair_lists, tiles_dev)
    for p in range(planes):
        numbers[p][0] = pack([disparities[p, s] + SHIFT for s in range(sources)], SHIFT_BITS)
    slots = [jnp.where(owner >= 0, owner * CAP + rank, 0) for owner, rank in zip(owners, ranks)]
    for i in range(len(slots) // 2):
        numbers[planes + i][0] = pack(slots[2 * i : 2 * i + 2], SLOT_BITS)
    numbers[-1][0] = view_counts[0] * 4 + jnp.where(me[0] > 0, 2, 0) + lax.rem(me[0], 2)

    c1, channels = first.shape[3], first.shape[4]
    c2 = second.shape[4]
    rows_n = len(edge_rows) + len(mid_rows)
    half_r = rows_n // 2
    place = {row: i for i, row in enumerate(edge_rows + mid_rows)}
    per_group = LANES // channels
    filler = jnp.zeros((c1, LANES - channels), jnp.float32)
    taps = {}
    for a in range(3):
        for b in range(3):
            for d in range(3):
                tap = jnp.concatenate([first[a, b, d].astype(jnp.float32), filler], axis=1)
                for turn in range(per_group):
                    lane = turn * channels
                    taps[a, b, d, turn] = pltpu.roll(tap, lane, 1) if lane else tap

    def band(a, d, r, group):
        total = jnp.zeros((c1, LANES), jnp.float32)
        for b in range(3):
            at_place = place.get(r - 1 + b, -1)
            if at_place >= 0 and at_place // per_group == group:
                total = total + taps[a, b, d, at_place % per_group]
        return total

    rim = (-1, 0, rows_n - 1, rows_n)
    inner = tuple(range(1, rows_n - 1))
    for kernel, rows, groups in ((kernel_edge, rim, 1), (kernel_mid, inner, 2)):
        for d in range(3):
            for i, r in enumerate(rows):
                for a in range(3):
                    at = ((a * 3 + d) * len(rows) + i) * c1
                    for group in range(groups):
                        kernel[at : at + c1, group * LANES : (group + 1) * LANES] = band(a, d, r, group)

    def second_row(a, d, r):
        blocks = []
        for g in range(half_r):
            b = -1 if r is None else r - 2 * g + 1
            hit = 0 <= b < 3
            blocks.append(second[a, b, d].astype(jnp.float32) if hit else jnp.zeros((c1, c2), jnp.float32))
        blocks.append(jnp.zeros((c1, LANES - half_r * c2), jnp.float32))
        return jnp.concatenate(blocks, axis=1)

    for two, stacked, rows in ((two_mid, stacked_mid, inner), (two_edge, stacked_edge, rim[:3] + (None,))):
        stacked[...] = jnp.zeros(stacked.shape, jnp.float32)
        for a in range(3):
            for d in range(3):
                for i, r in enumerate(rows):
                    at = ((a * 3 + d) * len(rows) + i) * c1
                    stacked[at : at + c1, :] = second_row(a, d, r)
        two[...] = stacked[...].T[: half_r * c2].astype(jnp.bfloat16)

    def spread_bias(like, bias):
        index = lax.broadcasted_iota(jnp.int32, like.shape, 0)
        total = jnp.zeros(like.shape, jnp.float32)
        for i in range(bias.shape[0]):
            total = jnp.where(index % bias.shape[0] == i, bias[i], total)
        like[...] = total

    spread_bias(bias_rows, bias_first)
    spread_bias(bias_two, bias_second)


def plane_variance(shifts, cols, wide, ref_wide, inv, store):
    for x0 in range(0, cols, CHUNK):
        ref = ref_wide[x0 : x0 + CHUNK, :]
        summed = ref
        squares = ref * ref
        for s, shift in enumerate(shifts):
            warped = wide[s, pl.ds(SHIFT + x0 - shift, CHUNK), :]
            summed = summed + warped
            squares = squares + warped * warped
        store(x0, (squares - summed * summed * inv).astype(jnp.bfloat16))


def view_weights(live):
    total = live.astype(jnp.float32) + jnp.ones((1, LANES), jnp.float32)
    return 1.0 / total, lax.rsqrt(total)


def turned_reference(ref, blocks, picks):
    tile_rows = ref.shape[0] // blocks
    rows = [ref[block * tile_rows + i] for block in picks for i in range(tile_rows)]
    return jnp.concatenate(rows, axis=0).T.astype(jnp.float32)


def clear_bands(wide, cols):
    band = jnp.zeros((SHIFT, LANES), jnp.float32)
    for at in range(wide.shape[0]):
        wide[at, 0:SHIFT, :] = band
        wide[at, SHIFT + cols : 2 * SHIFT + cols, :] = band


def load_tiles(slots, live, picks, scale, arrived, wide):
    for s, places in enumerate(slots):
        slab = jnp.concatenate([arrived[places[block]] for block in picks], axis=0)
        cols = slab.shape[1]
        wide[s, SHIFT : SHIFT + cols, :] = slab.T.astype(jnp.float32) * jnp.where(s < live, scale, 0.0)


def add_plane(q, planes, lhs, weights, sums):
    taps = lax.dot_general(weights, lhs, (((1,), (1,)), ((), ())), preferred_element_type=jnp.float32)
    rows = taps.shape[0] // 3
    if q + 1 < planes:
        sums[q + 1] = taps[:rows]
    if q == 0:
        sums[q] = taps[rows : 2 * rows]
    else:
        sums[q] += taps[rows : 2 * rows]
        sums[q - 1] += taps[2 * rows :]


def joined_columns(taps, column):
    rows, cols = column.shape
    left, center, right = taps[:rows], taps[rows : 2 * rows], taps[2 * rows :]
    total = center + jnp.where(column > 0, pltpu.roll(left, 1, 1), 0.0)
    return total + jnp.where(column < cols - 1, pltpu.roll(right, cols - 1, 1), 0.0)


def strided_planes(q, planes, taken, rows, weights):
    parts = []
    for plane in range(2 * q - 1, 2 * q + 2):
        for d in range(3):
            if 0 <= plane < planes:
                parts.append(taken[d][plane * rows : (plane + 1) * rows])
            else:
                parts.append(jnp.zeros((rows, taken[d].shape[1]), jnp.bfloat16))
    rhs = jnp.concatenate(parts, axis=0)
    return jnp.dot(weights[:, : rhs.shape[0]], rhs, preferred_element_type=jnp.float32)


def warp_kernel(n_numbers, sources, blocks, picks, *refs):
    arrived, ref, var, flags, wide, ref_wide, sem = refs[n_numbers : n_numbers + 7]
    held = refs[n_numbers + 7 :]
    planes, cols, _ = var.shape
    copies = fetch(refs[:n_numbers], held, sem)
    turned = turned_reference(ref, blocks, picks)
    clear_bands(wide, cols)
    for copy in copies:
        copy.wait()
    shifts, slots, live, not_top, odd = unpacked(held, planes, sources, blocks)
    inv, scale = view_weights(live)
    ref_wide[...] = turned * scale
    load_tiles(slots, live, picks, scale, arrived, wide)
    flags[0] = jnp.where(odd, 1.0, 0.0) * jnp.ones(flags.shape[1:], jnp.float32)
    flags[1] = jnp.where(not_top, 1.0, 0.0) * jnp.ones(flags.shape[1:], jnp.float32)
    for p in range(planes):

        def store(x0, value):
            var[p, x0 : x0 + CHUNK, :] = value

        plane_variance(shifts[p], cols, wide, ref_wide, inv, store)


def edge_kernel(var, kernel, flags, own, far, near, sums):
    planes, cols, _ = var.shape
    c1 = kernel.shape[0] // 36
    odd = jnp.concatenate([flags[0]] * 2, axis=0)[:, :1] > 0.5
    weights = kernel[...].astype(jnp.bfloat16)
    column = lax.broadcasted_iota(jnp.int32, (4 * c1, cols), 1)
    empty = jnp.zeros((c1, cols), jnp.float32)

    def finish(p):
        total = joined_columns(sums[p], column)
        own[p] = total[: 3 * c1]
        downward = total[2 * c1 :]
        upward = jnp.concatenate([total[:c1], empty], axis=0)
        far[p] = jnp.where(odd, downward, upward).astype(jnp.bfloat16)
        near[p] = jnp.where(odd, upward, downward).astype(jnp.bfloat16)

    for q in range(planes):
        add_plane(q, planes, var[q], weights, sums)
        if q > 0:
            finish(q - 1)
    finish(planes - 1)


def mid_kernel(n_numbers, sources, blocks, picks, *refs):
    arrived, ref, edge_var, kernel, bias_rows, kernel_two, bias_two = refs[n_numbers : n_numbers + 7]
    out, choices, wide, ref_wide, sem, var, cost, sums = refs[n_numbers + 7 : n_numbers + 15]
    held = refs[n_numbers + 15 :]
    planes, cols, _ = var.shape
    out_w = out.shape[2]
    inner = cost.shape[0] // planes
    copies = fetch(refs[:n_numbers], held, sem)
    row = lax.broadcasted_iota(jnp.int32, (cols, out_w), 0)
    target = 2 * lax.broadcasted_iota(jnp.int32, (cols, out_w), 1)
    for d in range(3):
        choices[d] = jnp.where(row == target + (d - 1), 1.0, 0.0).astype(jnp.bfloat16)
    turned = turned_reference(ref, blocks, picks)
    clear_bands(wide, cols)
    for copy in copies:
        copy.wait()
    shifts, slots, live, _, _ = unpacked(held, planes, sources, blocks)
    inv, scale = view_weights(live)
    ref_wide[...] = turned * scale
    load_tiles(slots, live, picks, scale, arrived, wide)
    weights = kernel[...].astype(jnp.bfloat16)
    bias = bias_rows[:inner]
    column = lax.broadcasted_iota(jnp.int32, (inner, cols), 1)

    def finish(p):
        total = joined_columns(sums[p], column)
        cost[p * inner : (p + 1) * inner, :] = jnp.maximum(total + bias, 0.0).astype(jnp.bfloat16)

    for q in range(planes):

        def store(x0, value):
            var[q, x0 : x0 + CHUNK, :] = value

        plane_variance(shifts[q], cols, wide, ref_wide, inv, store)
        add_plane(q, planes, jnp.concatenate([edge_var[q], var[q]], axis=1), weights, sums)
        if q > 0:
            finish(q - 1)
    finish(planes - 1)
    taken = [
        jnp.dot(cost[...], choices[d], preferred_element_type=jnp.float32).astype(jnp.bfloat16) for d in range(3)
    ]
    for q in range(planes // 2):
        out[q] = strided_planes(q, planes, taken, inner, kernel_two) + bias_two[...]


def end_kernel(far, near, flags, own, partial, bias_rows, kernel_two, choices, out):
    planes, ends, cols = own.shape
    c1 = ends // 3
    odd = jnp.concatenate([flags[0]] * (cols // LANES), axis=1) > 0.5
    not_top = jnp.concatenate([flags[1]] * (cols // LANES), axis=1)
    empty = jnp.zeros((c1, cols), jnp.float32)
    bias = bias_rows[:c1]
    rows = []
    for p in range(planes):
        lower, upper = far[p].astype(jnp.float32), near[p].astype(jnp.float32)
        before = own[p, :c1] + jnp.where(odd, upper[:c1], lower[:c1])
        top = own[p, c1 : 2 * c1] + jnp.where(odd, upper[c1:], lower[c1:])
        bottom = own[p, 2 * c1 :] + jnp.where(odd, lower[:c1], upper[:c1])
        rows += [jnp.maximum(before + bias, 0.0) * not_top]
        rows += [jnp.maximum(top + bias, 0.0), jnp.maximum(bottom + bias, 0.0), empty]
    cost = jnp.concatenate(rows, axis=0).astype(jnp.bfloat16)
    taken = [jnp.dot(cost, choices[d], preferred_element_type=jnp.float32).astype(jnp.bfloat16) for d in range(3)]
    for q in range(planes // 2):
        out[q] = partial[q] + strided_planes(q, planes, taken, 4 * c1, kernel_two)


def on_device(
    ref_features,
    source_tiles,
    pair_lists,
    view_counts,
    disparities,
    conv_first,
    bias_first,
    conv_second,
    bias_second,
):
    n_view = lax.axis_size("view")
    me = lax.axis_index("view").reshape(1)
    rows_n, channels, cols = ref_features.shape
    tiles_dev, tile_rows = source_tiles.shape[0], source_tiles.shape[1]
    sources, blocks = pair_lists.shape[1], pair_lists.shape[2]
    planes = disparities.shape[0]
    slab = tile_rows * channels
    c1, c2 = conv_first.shape[2], conv_second.shape[0]
    half_r, half_p, half_x = rows_n // 2, planes // 2, cols // 2
    smem = pl.BlockSpec(memory_space=pltpu.SMEM)
    vmem = pl.BlockSpec(memory_space=pltpu.VMEM)
    anywhere = pl.BlockSpec(memory_space=pl.ANY)
    params = pltpu.CompilerParams(vmem_limit_bytes=VMEM_LIMIT)
    bf16, f32, i32 = jnp.bfloat16, jnp.float32, jnp.int32
    shape = jax.ShapeDtypeStruct

    table = pl.pallas_call(
        functools.partial(request_kernel, tiles_dev),
        out_shape=shape((n_view, 1, CAP), i32),
        in_specs=[vmem],
        out_specs=vmem,
        compiler_params=params,
        name="request_table",
    )(pair_lists)
    table = lax.all_to_all(table, "view", split_axis=0, concat_axis=0, tiled=True)
    outgoing = source_tiles.reshape(tiles_dev, slab, cols)[table[:, 0]]
    arrived = lax.all_to_all(outgoing, "view", split_axis=0, concat_axis=0, tiled=True)
    arrived = arrived.reshape(n_view * CAP, slab, cols)

    n_numbers = planes + sources * blocks // 2 + 1
    edge_blocks, mid_blocks = (0, blocks - 1), tuple(range(1, blocks - 1))
    rows_of = lambda picks: [block * tile_rows + i for block in picks for i in range(tile_rows)]
    edge_rows, mid_rows = rows_of(edge_blocks), rows_of(mid_blocks)
    inner = (rows_n - 2) * c1
    mid_deep, edge_deep = (-(-9 * rows // LANES) * LANES for rows in (inner, 4 * c1))
    prepared = pl.pallas_call(
        functools.partial(prepare_kernel, tiles_dev, edge_rows, mid_rows),
        out_shape=[
            shape((36 * c1, LANES), f32),
            shape((9 * inner, 2 * LANES), f32),
            shape((half_r * c2, mid_deep), bf16),
            shape((half_r * c2, edge_deep), bf16),
            shape((inner, cols), f32),
            shape((half_r * c2, half_x), f32),
        ]
        + [shape((1,), i32)] * n_numbers,
        in_specs=[vmem, vmem] + [smem] * 6 + [anywhere],
        out_specs=[vmem] * 6 + [smem] * n_numbers,
        scratch_shapes=[pltpu.VMEM((mid_deep, LANES), f32), pltpu.VMEM((edge_deep, LANES), f32)],
        compiler_params=params,
        name="weights_and_scalars",
    )(
        conv_first.transpose(0, 1, 3, 2, 4),
        conv_second.transpose(1, 2, 3, 4, 0),
        bias_first,
        bias_second,
        disparities,
        pair_lists,
        view_counts,
        me,
        table,
    )
    kernel_edge, kernel_mid, two_mid, two_edge, bias_rows, bias_two, *numbers = prepared

    band_scratch = [
        pltpu.VMEM((sources, cols + 2 * SHIFT, LANES), f32),
        pltpu.VMEM((cols, LANES), f32),
        pltpu.SemaphoreType.DMA((n_numbers,)),
    ]
    held_scratch = [pltpu.SMEM((1,), i32)] * n_numbers
    payload = shape((planes, 2 * c1, cols), bf16)
    edge_var, flags = pl.pallas_call(
        functools.partial(warp_kernel, n_numbers, sources, blocks, edge_blocks),
        out_shape=[shape((planes, cols, LANES), bf16), shape((2, c1, LANES), f32)],
        in_specs=[anywhere] * n_numbers + [vmem] * 2,
        out_specs=[vmem] * 2,
        scratch_shapes=band_scratch + held_scratch,
        compiler_params=params,
        name="edge_variance",
    )(*numbers, arrived, ref_features)
    own, far, near = pl.pallas_call(
        edge_kernel,
        out_shape=[shape((planes, 3 * c1, cols), f32), payload, payload],
        in_specs=[vmem] * 3,
        out_specs=[vmem] * 3,
        scratch_shapes=[pltpu.VMEM((planes, 12 * c1, cols), f32)],
        compiler_params=params,
        name="edge_rows",
    )(edge_var, kernel_edge, flags)
    far = swapped(far, "view", 1)
    near = swapped(near, "view", 0)

    partial, choices = pl.pallas_call(
        functools.partial(mid_kernel, n_numbers, sources, blocks, mid_blocks),
        out_shape=[shape((half_p, half_r * c2, half_x), f32), shape((3, cols, half_x), bf16)],
        in_specs=[anywhere] * n_numbers + [vmem] * 7,
        out_specs=[vmem, vmem],
        scratch_shapes=band_scratch
        + [
            pltpu.VMEM((planes, cols, LANES), bf16),
            pltpu.VMEM((planes * inner, cols), bf16),
            pltpu.VMEM((planes, 3 * inner, cols), f32),
        ]
        + held_scratch,
        compiler_params=params,
        name="middle_rows",
    )(*numbers, arrived, ref_features, edge_var, kernel_mid, bias_rows, two_mid, bias_two)

    out = pl.pallas_call(
        end_kernel,
        out_shape=shape((half_p, half_r * c2, half_x), f32),
        in_specs=[vmem] * 8,
        out_specs=vmem,
        compiler_params=params,
        name="end_rows",
    )(far, near, flags, own, partial, bias_rows, two_edge, choices)
    return out.reshape(half_p, half_r, c2, half_x)


def solution(mesh):
    return jax.shard_map(
        on_device,
        mesh=mesh,
        in_specs=(
            P(("groups", "view"), None, None),
            P(("groups", "view"), None, None, None),
            P(("groups", "view"), None, None),
            P(("groups", "view")),
            P("groups", None),
            P(),
            P(),
            P(),
            P(),
        ),
        out_specs=P("groups", "view", None, None),
        check_vma=False,
    )
```

```python
import functools

import numpy as np

import jax
import jax.numpy as jnp
from jax import lax
from jax.experimental import pallas as pl
from jax.experimental.pallas import tpu as pltpu
from jax.sharding import PartitionSpec as P

SHIFT = 48
CAP = 2
LANES = 128
CHUNK = 64
VMEM_LIMIT = 10 * 1024 * 1024


def swapped(x, axis, parity):
    count = lax.axis_size(axis)
    pairs = [(i, i + 1) for i in range(parity, count - 1, 2)]
    return lax.ppermute(x, axis, pairs + [(j, i) for i, j in pairs])


def request_places(pair_lists, tiles_dev):
    owners, ranks, tiles = [], [], []
    for s in range(pair_lists.shape[1]):
        for b in range(pair_lists.shape[2]):
            tile = pair_lists[0, s, b]
            whole = jnp.maximum(tile, 0)
            owner = jnp.where(tile >= 0, lax.div(whole, tiles_dev), -1)
            rank = jnp.int32(0)
            for other in owners:
                rank = rank + jnp.where(other == owner, 1, 0)
            owners.append(owner)
            ranks.append(rank)
            tiles.append(lax.rem(whole, tiles_dev))
    return owners, ranks, tiles


def request_kernel(tiles_dev, pair_lists, table):
    n_view = table.shape[0]
    row = lax.broadcasted_iota(jnp.int32, (n_view, LANES), 0) * tiles_dev
    lane = lax.broadcasted_iota(jnp.int32, (n_view, LANES), 1)
    total = jnp.zeros((n_view, LANES), jnp.int32)
    count = jnp.zeros((n_view, LANES), jnp.int32)
    for s in range(pair_lists.shape[1]):
        for b in range(pair_lists.shape[2]):
            tile = pair_lists[0, s : s + 1, b : b + 1] - row
            owned = (tile >= 0) & (tile < tiles_dev)
            total = jnp.where(owned & (lane == count), tile, total)
            count = count + jnp.where(owned, 1, 0)
    for d in range(n_view):
        table[d] = total[d : d + 1, : table.shape[2]]


def prepare_kernel(
    tiles_dev,
    edge_rows,
    mid_rows,
    first,
    second,
    bias_first,
    bias_second,
    disparities,
    pair_lists,
    view_counts,
    me,
    _,
    kernel_edge,
    kernel_mid,
    two_mid,
    two_edge,
    bias_rows,
    bias_two,
    scalars,
    stacked_mid,
    stacked_edge,
):
    planes, sources = disparities.shape
    owners, ranks, _ = request_places(pair_lists, tiles_dev)
    at = 0
    for p in range(planes):
        for s in range(sources):
            scalars[at] = disparities[p, s]
            at += 1
    for owner, rank in zip(owners, ranks):
        scalars[at] = jnp.where(owner >= 0, owner * CAP + rank, 0)
        at += 1
    scalars[at] = view_counts[0]
    scalars[at + 1] = me[0]
    scalars[at + 2] = lax.rem(me[0], 2)
    tail = kernel_edge.shape[0] - 8
    lane_at = lax.broadcasted_iota(jnp.int32, (8, LANES), 1)
    numbers = jnp.zeros((8, LANES), jnp.float32)
    for i in range(at + 3):
        numbers = jnp.where(lane_at == i, scalars[i].astype(jnp.float32), numbers)
    kernel_edge[tail:, :] = numbers

    c1, channels = first.shape[3], first.shape[4]
    c2 = second.shape[4]
    rows_n = len(edge_rows) + len(mid_rows)
    half_r = rows_n // 2
    place = {row: i for i, row in enumerate(edge_rows + mid_rows)}
    per_group = LANES // channels
    filler = jnp.zeros((c1, LANES - channels), jnp.float32)
    taps = {}
    for a in range(3):
        for b in range(3):
            for d in range(3):
                tap = jnp.concatenate([first[a, b, d].astype(jnp.float32), filler], axis=1)
                for turn in range(per_group):
                    lane = turn * channels
                    taps[a, b, d, turn] = pltpu.roll(tap, lane, 1) if lane else tap

    def band(a, d, r, group):
        total = jnp.zeros((c1, LANES), jnp.float32)
        for b in range(3):
            at_place = place.get(r - 1 + b, -1)
            if at_place >= 0 and at_place // per_group == group:
                total = total + taps[a, b, d, at_place % per_group]
        return total

    rim = (-1, 0, rows_n - 1, rows_n)
    inner = tuple(range(1, rows_n - 1))
    for kernel, rows, groups in ((kernel_edge, rim, 1), (kernel_mid, inner, 2)):
        for d in range(3):
            for i, r in enumerate(rows):
                for a in range(3):
                    at = ((a * 3 + d) * len(rows) + i) * c1
                    for group in range(groups):
                        kernel[at : at + c1, group * LANES : (group + 1) * LANES] = band(a, d, r, group)

    def second_row(a, d, r):
        blocks = []
        for g in range(half_r):
            b = -1 if r is None else r - 2 * g + 1
            hit = 0 <= b < 3
            blocks.append(second[a, b, d].astype(jnp.float32) if hit else jnp.zeros((c1, c2), jnp.float32))
        blocks.append(jnp.zeros((c1, LANES - half_r * c2), jnp.float32))
        return jnp.concatenate(blocks, axis=1)

    for two, stacked, rows in ((two_mid, stacked_mid, inner), (two_edge, stacked_edge, rim[:3] + (None,))):
        stacked[...] = jnp.zeros(stacked.shape, jnp.float32)
        for a in range(3):
            for d in range(3):
                for i, r in enumerate(rows):
                    at = ((a * 3 + d) * len(rows) + i) * c1
                    stacked[at : at + c1, :] = second_row(a, d, r)
        two[...] = stacked[...].T[: half_r * c2].astype(jnp.bfloat16)

    def spread_bias(like, bias):
        index = lax.broadcasted_iota(jnp.int32, like.shape, 0)
        total = jnp.zeros(like.shape, jnp.float32)
        for i in range(bias.shape[0]):
            total = jnp.where(index % bias.shape[0] == i, bias[i], total)
        like[...] = total

    spread_bias(bias_rows, bias_first)
    spread_bias(bias_two, bias_second)


def plane_variance(p, sources, cols, disp, wide, ref_wide, inv):
    chunks = []
    for x0 in range(0, cols, CHUNK):
        ref = ref_wide[0, x0 : x0 + CHUNK, :]
        summed = ref
        squares = ref * ref
        for s in range(sources):
            warped = wide[s, pl.ds(SHIFT + x0 - disp[p * sources + s], CHUNK), :]
            summed = summed + warped
            squares = squares + warped * warped
        chunks.append((squares - summed * summed * inv).astype(jnp.bfloat16))
    return jnp.concatenate(chunks, axis=0)


def view_weights(live):
    total = live.astype(jnp.float32) + jnp.ones((1, LANES), jnp.float32)
    return 1.0 / total, lax.rsqrt(total)


def turned_reference(ref, blocks, picks):
    tile_rows = ref.shape[0] // blocks
    rows = [ref[block * tile_rows + i] for block in picks for i in range(tile_rows)]
    return jnp.concatenate(rows, axis=0).T.astype(jnp.float32)


def clear_bands(wide, cols):
    band = jnp.zeros((SHIFT, LANES), jnp.float32)
    for at in range(wide.shape[0]):
        wide[at, 0:SHIFT, :] = band
        wide[at, SHIFT + cols : 2 * SHIFT + cols, :] = band


def load_tiles(at_slots, live, sources, blocks, picks, scale, scalars, arrived, wide):
    for s in range(sources):
        slab = jnp.concatenate([arrived[scalars[at_slots + s * blocks + block]] for block in picks], axis=0)
        cols = slab.shape[1]
        wide[s, SHIFT : SHIFT + cols, :] = slab.T.astype(jnp.float32) * jnp.where(s < live, scale, 0.0)


def add_plane(q, planes, lhs, weights, sums):
    taps = lax.dot_general(weights, lhs, (((1,), (1,)), ((), ())), preferred_element_type=jnp.float32)
    rows = taps.shape[0] // 3
    if q + 1 < planes:
        sums[q + 1] = taps[:rows]
    if q == 0:
        sums[q] = taps[rows : 2 * rows]
    else:
        sums[q] += taps[rows : 2 * rows]
        sums[q - 1] += taps[2 * rows :]


def joined_columns(taps, column):
    rows, cols = column.shape
    left, center, right = taps[:rows], taps[rows : 2 * rows], taps[2 * rows :]
    total = center + jnp.where(column > 0, pltpu.roll(left, 1, 1), 0.0)
    return total + jnp.where(column < cols - 1, pltpu.roll(right, cols - 1, 1), 0.0)


def strided_planes(q, planes, taken, rows, weights, out_w):
    step = taken.shape[1] // 3
    parts = []
    for plane in range(2 * q - 1, 2 * q + 2):
        for d in range(3):
            if 0 <= plane < planes:
                parts.append(taken[plane * rows : (plane + 1) * rows, d * step : (d + 1) * step])
            else:
                parts.append(jnp.zeros((rows, step), jnp.bfloat16))
    rhs = jnp.concatenate(parts, axis=0)
    result = jnp.dot(weights[:, : rhs.shape[0]], rhs, preferred_element_type=jnp.float32)
    return result[:, :out_w]


def edge_kernel(
    at_slots, at_live, sources, blocks, picks, packed, arrived, ref, var, own, far, near, flags, wide, ref_wide, sums, held, sem
):
    planes, cols, _ = var.shape
    tail = packed.shape[0] - 8
    c1 = tail // 36
    copy = pltpu.make_async_copy(packed.at[pl.ds(tail, 8)], held, sem)
    copy.start()
    weights = packed[:tail].astype(jnp.bfloat16)
    turned = turned_reference(ref, blocks, picks)
    clear_bands(wide, cols)
    copy.wait()
    scalars = [held[0, i].astype(jnp.int32) for i in range(at_live + 3)]
    live = scalars[at_live]
    inv, scale = view_weights(live)
    ref_wide[0] = turned * scale
    load_tiles(at_slots, live, sources, blocks, picks, scale, scalars, arrived, wide)
    odd = scalars[at_live + 2] > 0
    flags[0] = jnp.where(odd, 1.0, 0.0) * jnp.ones((c1, LANES), jnp.float32)
    flags[1] = jnp.where(scalars[at_live + 1] > 0, 1.0, 0.0) * jnp.ones((c1, LANES), jnp.float32)
    column = lax.broadcasted_iota(jnp.int32, (4 * c1, cols), 1)
    empty = jnp.zeros((c1, cols), jnp.float32)

    def finish(p):
        total = joined_columns(sums[p], column)
        own[p] = total[: 3 * c1]
        downward = total[2 * c1 :]
        upward = jnp.concatenate([total[:c1], empty], axis=0)
        far[p] = jnp.where(odd, downward, upward).astype(jnp.bfloat16)
        near[p] = jnp.where(odd, upward, downward).astype(jnp.bfloat16)

    values = plane_variance(0, sources, cols, scalars, wide, ref_wide, inv)
    for q in range(planes):
        held_values = values
        if q + 1 < planes:
            values = plane_variance(q + 1, sources, cols, scalars, wide, ref_wide, inv)
        add_plane(q, planes, held_values, weights, sums)
        var[q] = held_values
        if q > 0:
            finish(q - 1)
    finish(planes - 1)


def mid_kernel(
    at_slots,
    at_live,
    sources,
    blocks,
    picks,
    numbers,
    arrived,
    ref,
    edge_var,
    kernel,
    bias_rows,
    kernel_two,
    bias_two,
    out,
    choices,
    wide,
    ref_wide,
    cost,
    sums,
    scalars,
    sem,
):
    copy = pltpu.make_async_copy(numbers, scalars, sem)
    copy.start()
    planes, cols, _ = edge_var.shape
    inner = cost.shape[0] // planes
    step = choices.shape[1] // 3
    row = lax.broadcasted_iota(jnp.int32, (cols, step), 0)
    target = 2 * lax.broadcasted_iota(jnp.int32, (cols, step), 1)
    for d in range(3):
        choices[:, d * step : (d + 1) * step] = jnp.where(row == target + (d - 1), 1.0, 0.0).astype(jnp.bfloat16)
    turned = turned_reference(ref, blocks, picks)
    clear_bands(wide, cols)
    copy.wait()
    live = scalars[at_live]
    inv, scale = view_weights(live)
    ref_wide[0] = turned * scale
    load_tiles(at_slots, live, sources, blocks, picks, scale, scalars, arrived, wide)
    weights = kernel[...].astype(jnp.bfloat16)
    bias = bias_rows[:inner]
    column = lax.broadcasted_iota(jnp.int32, (inner, cols), 1)

    def finish(p):
        total = joined_columns(sums[p], column)
        cost[p * inner : (p + 1) * inner, :] = jnp.maximum(total + bias, 0.0).astype(jnp.bfloat16)

    values = plane_variance(0, sources, cols, scalars, wide, ref_wide, inv)
    for q in range(planes):
        held_values = values
        if q + 1 < planes:
            values = plane_variance(q + 1, sources, cols, scalars, wide, ref_wide, inv)
        add_plane(q, planes, jnp.concatenate([edge_var[q], held_values], axis=1), weights, sums)
        if q > 0:
            finish(q - 1)
    finish(planes - 1)
    taken = jnp.dot(cost[...], choices[...], preferred_element_type=jnp.float32).astype(jnp.bfloat16)
    for q in range(planes // 2):
        out[q] = strided_planes(q, planes, taken, inner, kernel_two, out.shape[2]) + bias_two[...]


def end_kernel(far, near, flags, own, partial, bias_rows, kernel_two, choices, out):
    planes, ends, cols = own.shape
    c1 = ends // 3
    odd = jnp.concatenate([flags[0]] * (cols // LANES), axis=1) > 0.5
    not_top = jnp.concatenate([flags[1]] * (cols // LANES), axis=1)
    empty = jnp.zeros((c1, cols), jnp.float32)
    bias = bias_rows[:c1]
    rows = []
    for p in range(planes):
        lower, upper = far[p].astype(jnp.float32), near[p].astype(jnp.float32)
        before = own[p, :c1] + jnp.where(odd, upper[:c1], lower[:c1])
        top = own[p, c1 : 2 * c1] + jnp.where(odd, upper[c1:], lower[c1:])
        bottom = own[p, 2 * c1 :] + jnp.where(odd, lower[:c1], upper[:c1])
        rows += [jnp.maximum(before + bias, 0.0) * not_top]
        rows += [jnp.maximum(top + bias, 0.0), jnp.maximum(bottom + bias, 0.0), empty]
    cost = jnp.concatenate(rows, axis=0).astype(jnp.bfloat16)
    taken = jnp.dot(cost, choices[...], preferred_element_type=jnp.float32).astype(jnp.bfloat16)
    for q in range(planes // 2):
        out[q] = partial[q] + strided_planes(q, planes, taken, 4 * c1, kernel_two, out.shape[2])


def on_device(
    ref_features,
    source_tiles,
    pair_lists,
    view_counts,
    disparities,
    conv_first,
    bias_first,
    conv_second,
    bias_second,
):
    n_view = lax.axis_size("view")
    me = lax.axis_index("view").reshape(1)
    rows_n, channels, cols = ref_features.shape
    tiles_dev, tile_rows = source_tiles.shape[0], source_tiles.shape[1]
    sources, blocks = pair_lists.shape[1], pair_lists.shape[2]
    planes = disparities.shape[0]
    slab = tile_rows * channels
    c1, c2 = conv_first.shape[2], conv_second.shape[0]
    half_r, half_p, half_x = rows_n // 2, planes // 2, cols // 2
    smem = pl.BlockSpec(memory_space=pltpu.SMEM)
    vmem = pl.BlockSpec(memory_space=pltpu.VMEM)
    anywhere = pl.BlockSpec(memory_space=pl.ANY)
    params = pltpu.CompilerParams(vmem_limit_bytes=VMEM_LIMIT)
    bf16, f32, i32 = jnp.bfloat16, jnp.float32, jnp.int32
    shape = jax.ShapeDtypeStruct

    table = pl.pallas_call(
        functools.partial(request_kernel, tiles_dev),
        out_shape=shape((n_view, 1, CAP), i32),
        in_specs=[vmem],
        out_specs=vmem,
        compiler_params=params,
        name="request_table",
    )(pair_lists)
    table = lax.all_to_all(table, "view", split_axis=0, concat_axis=0, tiled=True)
    outgoing = source_tiles.reshape(tiles_dev, slab, cols)[table[:, 0]]
    arrived = lax.all_to_all(outgoing, "view", split_axis=0, concat_axis=0, tiled=True)
    arrived = arrived.reshape(n_view * CAP, slab, cols)

    at_slots = planes * sources
    at_live = at_slots + sources * blocks
    edge_blocks, mid_blocks = (0, blocks - 1), tuple(range(1, blocks - 1))
    rows_of = lambda picks: [block * tile_rows + i for block in picks for i in range(tile_rows)]
    edge_rows, mid_rows = rows_of(edge_blocks), rows_of(mid_blocks)
    inner = (rows_n - 2) * c1
    mid_deep, edge_deep = (-(-9 * rows // LANES) * LANES for rows in (inner, 4 * c1))
    prepared = pl.pallas_call(
        functools.partial(prepare_kernel, tiles_dev, edge_rows, mid_rows),
        out_shape=[
            shape((36 * c1 + 8, LANES), f32),
            shape((9 * inner, 2 * LANES), f32),
            shape((half_r * c2, mid_deep), bf16),
            shape((half_r * c2, edge_deep), bf16),
            shape((inner, cols), f32),
            shape((half_r * c2, half_x), f32),
            shape((LANES,), i32),
        ],
        in_specs=[vmem, vmem] + [smem] * 6 + [anywhere],
        out_specs=[vmem] * 6 + [smem],
        scratch_shapes=[pltpu.VMEM((mid_deep, LANES), f32), pltpu.VMEM((edge_deep, LANES), f32)],
        compiler_params=params,
        name="weights_and_scalars",
    )(
        conv_first.transpose(0, 1, 3, 2, 4),
        conv_second.transpose(1, 2, 3, 4, 0),
        bias_first,
        bias_second,
        disparities,
        pair_lists,
        view_counts,
        me,
        table,
    )
    kernel_edge, kernel_mid, two_mid, two_edge, bias_rows, bias_two, scalars = prepared

    band_scratch = [pltpu.VMEM((sources, cols + 2 * SHIFT, LANES), f32), pltpu.VMEM((1, cols, LANES), f32)]
    payload = shape((planes, 2 * c1, cols), bf16)
    col_step = -(-half_x // LANES) * LANES
    edge_var, own, far, near, flags = pl.pallas_call(
        functools.partial(edge_kernel, at_slots, at_live, sources, blocks, edge_blocks),
        out_shape=[
            shape((planes, cols, LANES), bf16),
            shape((planes, 3 * c1, cols), f32),
            payload,
            payload,
            shape((2, c1, LANES), f32),
        ],
        in_specs=[vmem] * 3,
        out_specs=[vmem] * 5,
        scratch_shapes=band_scratch
        + [
            pltpu.VMEM((planes, 12 * c1, cols), f32),
            pltpu.SMEM((8, LANES), f32),
            pltpu.SemaphoreType.DMA,
        ],
        compiler_params=params,
        name="edge_rows",
    )(kernel_edge, arrived, ref_features)
    far = swapped(far, "view", 1)
    near = swapped(near, "view", 0)

    partial, choices = pl.pallas_call(
        functools.partial(mid_kernel, at_slots, at_live, sources, blocks, mid_blocks),
        out_shape=[shape((half_p, half_r * c2, half_x), f32), shape((cols, 3 * col_step), bf16)],
        in_specs=[anywhere] + [vmem] * 7,
        out_specs=[vmem, vmem],
        scratch_shapes=band_scratch
        + [
            pltpu.VMEM((planes * inner, cols), bf16),
            pltpu.VMEM((planes, 3 * inner, cols), f32),
            pltpu.SMEM(scalars.shape, i32),
            pltpu.SemaphoreType.DMA,
        ],
        compiler_params=params,
        name="middle_rows",
    )(scalars, arrived, ref_features, edge_var, kernel_mid, bias_rows, two_mid, bias_two)

    out = pl.pallas_call(
        end_kernel,
        out_shape=shape((half_p, half_r * c2, half_x), f32),
        in_specs=[vmem] * 8,
        out_specs=vmem,
        compiler_params=params,
        name="end_rows",
    )(far, near, flags, own, partial, bias_rows, two_edge, choices)
    return out.reshape(half_p, half_r, c2, half_x)


def solution(mesh):
    return jax.shard_map(
        on_device,
        mesh=mesh,
        in_specs=(
            P(("groups", "view"), None, None),
            P(("groups", "view"), None, None, None),
            P(("groups", "view"), None, None),
            P(("groups", "view")),
            P("groups", None),
            P(),
            P(),
            P(),
            P(),
        ),
        out_specs=P("groups", "view", None, None),
        check_vma=False,
    )
```

```python
import functools

import numpy as np

import jax
import jax.numpy as jnp
from jax import lax
from jax.experimental import pallas as pl
from jax.experimental.pallas import tpu as pltpu
from jax.sharding import PartitionSpec as P

SHIFT = 48
CAP = 2
LANES = 128
CHUNK = 64
VMEM_LIMIT = 10 * 1024 * 1024


def swapped(x, axis, parity):
    count = lax.axis_size(axis)
    pairs = [(i, i + 1) for i in range(parity, count - 1, 2)]
    return lax.ppermute(x, axis, pairs + [(j, i) for i, j in pairs])


def request_places(pair_lists, tiles_dev):
    owners, ranks, tiles = [], [], []
    for s in range(pair_lists.shape[1]):
        for b in range(pair_lists.shape[2]):
            tile = pair_lists[0, s, b]
            whole = jnp.maximum(tile, 0)
            owner = jnp.where(tile >= 0, lax.div(whole, tiles_dev), -1)
            rank = jnp.int32(0)
            for other in owners:
                rank = rank + jnp.where(other == owner, 1, 0)
            owners.append(owner)
            ranks.append(rank)
            tiles.append(lax.rem(whole, tiles_dev))
    return owners, ranks, tiles


def request_kernel(tiles_dev, pair_lists, table):
    n_view = table.shape[0]
    row = lax.broadcasted_iota(jnp.int32, (n_view, LANES), 0) * tiles_dev
    lane = lax.broadcasted_iota(jnp.int32, (n_view, LANES), 1)
    total = jnp.zeros((n_view, LANES), jnp.int32)
    count = jnp.zeros((n_view, LANES), jnp.int32)
    for s in range(pair_lists.shape[1]):
        for b in range(pair_lists.shape[2]):
            tile = pair_lists[0, s : s + 1, b : b + 1] - row
            owned = (tile >= 0) & (tile < tiles_dev)
            total = jnp.where(owned & (lane == count), tile, total)
            count = count + jnp.where(owned, 1, 0)
    for d in range(n_view):
        table[d] = total[d : d + 1, : table.shape[2]]


def prepare_kernel(
    tiles_dev,
    edge_rows,
    mid_rows,
    first,
    second,
    bias_first,
    bias_second,
    disparities,
    pair_lists,
    view_counts,
    me,
    _,
    kernel_edge,
    kernel_mid,
    two_mid,
    two_edge,
    bias_rows,
    bias_two,
    scalars,
    stacked_mid,
    stacked_edge,
):
    planes, sources = disparities.shape
    owners, ranks, _ = request_places(pair_lists, tiles_dev)
    at = 0
    for p in range(planes):
        for s in range(sources):
            scalars[at] = disparities[p, s]
            at += 1
    for owner, rank in zip(owners, ranks):
        scalars[at] = jnp.where(owner >= 0, owner * CAP + rank, 0)
        at += 1
    scalars[at] = view_counts[0]
    scalars[at + 1] = me[0]
    scalars[at + 2] = lax.rem(me[0], 2)
    tail = kernel_edge.shape[0] - 8
    lane_at = lax.broadcasted_iota(jnp.int32, (8, LANES), 1)
    numbers = jnp.zeros((8, LANES), jnp.float32)
    for i in range(at + 3):
        numbers = jnp.where(lane_at == i, scalars[i].astype(jnp.float32), numbers)
    kernel_edge[tail:, :] = numbers

    c1, channels = first.shape[3], first.shape[4]
    c2 = second.shape[4]
    rows_n = len(edge_rows) + len(mid_rows)
    half_r = rows_n // 2
    place = {row: i for i, row in enumerate(edge_rows + mid_rows)}
    per_group = LANES // channels
    filler = jnp.zeros((c1, LANES - channels), jnp.float32)
    taps = {}
    for a in range(3):
        for b in range(3):
            for d in range(3):
                tap = jnp.concatenate([first[a, b, d].astype(jnp.float32), filler], axis=1)
                for turn in range(per_group):
                    lane = turn * channels
                    taps[a, b, d, turn] = pltpu.roll(tap, lane, 1) if lane else tap

    def band(a, d, r, group):
        total = jnp.zeros((c1, LANES), jnp.float32)
        for b in range(3):
            at_place = place.get(r - 1 + b, -1)
            if at_place >= 0 and at_place // per_group == group:
                total = total + taps[a, b, d, at_place % per_group]
        return total

    rim = (-1, 0, rows_n - 1, rows_n)
    inner = tuple(range(1, rows_n - 1))
    for kernel, rows, groups in ((kernel_edge, rim, 1), (kernel_mid, inner, 2)):
        for d in range(3):
            for i, r in enumerate(rows):
                for a in range(3):
                    at = ((a * 3 + d) * len(rows) + i) * c1
                    for group in range(groups):
                        kernel[at : at + c1, group * LANES : (group + 1) * LANES] = band(a, d, r, group)

    def second_row(a, d, r):
        blocks = []
        for g in range(half_r):
            b = -1 if r is None else r - 2 * g + 1
            hit = 0 <= b < 3
            blocks.append(second[a, b, d].astype(jnp.float32) if hit else jnp.zeros((c1, c2), jnp.float32))
        blocks.append(jnp.zeros((c1, LANES - half_r * c2), jnp.float32))
        return jnp.concatenate(blocks, axis=1)

    for two, stacked, rows in ((two_mid, stacked_mid, inner), (two_edge, stacked_edge, rim[:3] + (None,))):
        deep = two.shape[1]
        stacked[...] = jnp.zeros(stacked.shape, jnp.float32)
        for a in range(3):
            for j, d in enumerate((1, 0, 2)):
                for i, r in enumerate(rows):
                    at = j * deep + (a * len(rows) + i) * c1
                    stacked[at : at + c1, :] = second_row(a, d, r)
        outs = half_r * c2
        for j in range(3):
            two[j * outs : (j + 1) * outs, :] = stacked[j * deep : (j + 1) * deep, :].T[:outs].astype(jnp.bfloat16)

    def spread_bias(like, bias):
        index = lax.broadcasted_iota(jnp.int32, like.shape, 0)
        total = jnp.zeros(like.shape, jnp.float32)
        for i in range(bias.shape[0]):
            total = jnp.where(index % bias.shape[0] == i, bias[i], total)
        like[...] = total

    spread_bias(bias_rows, bias_first)
    spread_bias(bias_two, bias_second)


def plane_variance(p, sources, cols, disp, wide, ref_wide, inv):
    chunks = []
    for x0 in range(0, cols, CHUNK):
        ref = ref_wide[0, x0 : x0 + CHUNK, :]
        summed = ref
        squares = ref * ref
        for s in range(sources):
            warped = wide[s, pl.ds(SHIFT + x0 - disp[p * sources + s], CHUNK), :]
            summed = summed + warped
            squares = squares + warped * warped
        chunks.append((squares - summed * summed * inv).astype(jnp.bfloat16))
    return jnp.concatenate(chunks, axis=0)


def view_weights(live):
    total = live.astype(jnp.float32) + jnp.ones((1, LANES), jnp.float32)
    return 1.0 / total, lax.rsqrt(total)


def turned_reference(ref, blocks, picks):
    tile_rows = ref.shape[0] // blocks
    rows = [ref[block * tile_rows + i] for block in picks for i in range(tile_rows)]
    return jnp.concatenate(rows, axis=0).T.astype(jnp.float32)


def clear_bands(wide, cols):
    band = jnp.zeros((SHIFT, LANES), jnp.float32)
    for at in range(wide.shape[0]):
        wide[at, 0:SHIFT, :] = band
        wide[at, SHIFT + cols : 2 * SHIFT + cols, :] = band


def load_tiles(at_slots, live, sources, blocks, picks, scale, scalars, arrived, wide):
    for s in range(sources):
        slab = jnp.concatenate([arrived[scalars[at_slots + s * blocks + block]] for block in picks], axis=0)
        cols = slab.shape[1]
        wide[s, SHIFT : SHIFT + cols, :] = slab.T.astype(jnp.float32) * jnp.where(s < live, scale, 0.0)


def add_plane(q, planes, lhs, weights, sums):
    taps = lax.dot_general(weights, lhs, (((1,), (1,)), ((), ())), preferred_element_type=jnp.float32)
    rows = taps.shape[0] // 3
    slots = sums.shape[0]
    if q + 1 < planes:
        sums[(q + 1) % slots] = taps[:rows]
    if q == 0:
        sums[q % slots] = taps[rows : 2 * rows]
    else:
        sums[q % slots] += taps[rows : 2 * rows]
        sums[(q - 1) % slots] += taps[2 * rows :]


def joined_columns(taps, column):
    rows, cols = column.shape
    left, center, right = taps[:rows], taps[rows : 2 * rows], taps[2 * rows :]
    total = center + jnp.where(column > 0, pltpu.roll(left, 1, 1), 0.0)
    return total + jnp.where(column < cols - 1, pltpu.roll(right, cols - 1, 1), 0.0)


def strided_planes(q, planes, taken, rows, weights, out_w):
    step = taken.shape[1] // 2
    none = jnp.zeros((rows, 2 * step), jnp.bfloat16)
    near = range(2 * q - 1, 2 * q + 2)
    parts = [taken[p * rows : (p + 1) * rows] if 0 <= p < planes else none for p in near]
    rhs = jnp.concatenate(parts, axis=0)
    deep = rhs.shape[0]
    outs = weights.shape[0] // 3
    even = jnp.dot(weights[:outs, :deep], rhs[:, :step], preferred_element_type=jnp.float32)
    odd = jnp.dot(weights[outs:, :deep], rhs[:, step:], preferred_element_type=jnp.float32)
    result = even + pltpu.roll(odd[:outs], 1, 1) + odd[outs:]
    return result[:, :out_w]


def edge_kernel(
    at_slots, at_live, sources, blocks, picks, packed, arrived, ref, var, own, far, near, flags, wide, ref_wide, sums, held, sem
):
    planes, cols, _ = var.shape
    tail = packed.shape[0] - 8
    c1 = tail // 36
    copy = pltpu.make_async_copy(packed.at[pl.ds(tail, 8)], held, sem)
    copy.start()
    weights = packed[:tail].astype(jnp.bfloat16)
    turned = turned_reference(ref, blocks, picks)
    clear_bands(wide, cols)
    copy.wait()
    scalars = [held[0, i].astype(jnp.int32) for i in range(at_live + 3)]
    live = scalars[at_live]
    inv, scale = view_weights(live)
    ref_wide[0] = turned * scale
    load_tiles(at_slots, live, sources, blocks, picks, scale, scalars, arrived, wide)
    odd = scalars[at_live + 2] > 0
    flags[0] = jnp.where(odd, 1.0, 0.0) * jnp.ones((c1, LANES), jnp.float32)
    flags[1] = jnp.where(scalars[at_live + 1] > 0, 1.0, 0.0) * jnp.ones((c1, LANES), jnp.float32)
    column = lax.broadcasted_iota(jnp.int32, (4 * c1, cols), 1)
    empty = jnp.zeros((c1, cols), jnp.float32)

    def finish(p):
        total = joined_columns(sums[p % sums.shape[0]], column)
        own[p] = total[: 3 * c1]
        downward = total[2 * c1 :]
        upward = jnp.concatenate([total[:c1], empty], axis=0)
        far[p] = jnp.where(odd, downward, upward).astype(jnp.bfloat16)
        near[p] = jnp.where(odd, upward, downward).astype(jnp.bfloat16)

    values = plane_variance(0, sources, cols, scalars, wide, ref_wide, inv)
    for q in range(planes):
        held_values = values
        if q + 1 < planes:
            values = plane_variance(q + 1, sources, cols, scalars, wide, ref_wide, inv)
        add_plane(q, planes, held_values, weights, sums)
        var[q] = held_values
        if q > 0:
            finish(q - 1)
    finish(planes - 1)


def mid_kernel(
    at_slots,
    at_live,
    sources,
    blocks,
    picks,
    numbers,
    arrived,
    ref,
    edge_var,
    kernel,
    bias_rows,
    kernel_two,
    bias_two,
    out,
    choices,
    wide,
    ref_wide,
    cost,
    sums,
    scalars,
    sem,
):
    copy = pltpu.make_async_copy(numbers, scalars, sem)
    copy.start()
    planes, cols, _ = edge_var.shape
    inner = cost.shape[0] // planes
    step = choices.shape[1] // 2
    row = lax.broadcasted_iota(jnp.int32, (cols, step), 0)
    target = 2 * lax.broadcasted_iota(jnp.int32, (cols, step), 1)
    for odd in range(2):
        choices[:, odd * step : (odd + 1) * step] = jnp.where(row == target + odd, 1.0, 0.0).astype(jnp.bfloat16)
    turned = turned_reference(ref, blocks, picks)
    clear_bands(wide, cols)
    copy.wait()
    live = scalars[at_live]
    inv, scale = view_weights(live)
    ref_wide[0] = turned * scale
    load_tiles(at_slots, live, sources, blocks, picks, scale, scalars, arrived, wide)
    weights = kernel[...].astype(jnp.bfloat16)
    bias = bias_rows[:inner]
    column = lax.broadcasted_iota(jnp.int32, (inner, cols), 1)

    def finish(p):
        total = joined_columns(sums[p % sums.shape[0]], column)
        cost[p * inner : (p + 1) * inner, :] = jnp.maximum(total + bias, 0.0).astype(jnp.bfloat16)

    values = plane_variance(0, sources, cols, scalars, wide, ref_wide, inv)
    for q in range(planes):
        held_values = values
        if q + 1 < planes:
            values = plane_variance(q + 1, sources, cols, scalars, wide, ref_wide, inv)
        add_plane(q, planes, jnp.concatenate([edge_var[q], held_values], axis=1), weights, sums)
        if q > 0:
            finish(q - 1)
    finish(planes - 1)
    taken = jnp.dot(cost[...], choices[...], preferred_element_type=jnp.float32).astype(jnp.bfloat16)
    for q in range(planes // 2):
        out[q] = strided_planes(q, planes, taken, inner, kernel_two, out.shape[2]) + bias_two[...]


def end_kernel(far, near, flags, own, partial, bias_rows, kernel_two, choices, out):
    planes, ends, cols = own.shape
    c1 = ends // 3
    odd = jnp.concatenate([flags[0]] * (cols // LANES), axis=1) > 0.5
    not_top = jnp.concatenate([flags[1]] * (cols // LANES), axis=1)
    empty = jnp.zeros((c1, cols), jnp.float32)
    bias = bias_rows[:c1]
    rows = []
    for p in range(planes):
        lower, upper = far[p].astype(jnp.float32), near[p].astype(jnp.float32)
        before = own[p, :c1] + jnp.where(odd, upper[:c1], lower[:c1])
        top = own[p, c1 : 2 * c1] + jnp.where(odd, upper[c1:], lower[c1:])
        bottom = own[p, 2 * c1 :] + jnp.where(odd, lower[:c1], upper[:c1])
        rows += [jnp.maximum(before + bias, 0.0) * not_top]
        rows += [jnp.maximum(top + bias, 0.0), jnp.maximum(bottom + bias, 0.0), empty]
    cost = jnp.concatenate(rows, axis=0).astype(jnp.bfloat16)
    taken = jnp.dot(cost, choices[...], preferred_element_type=jnp.float32).astype(jnp.bfloat16)
    for q in range(planes // 2):
        out[q] = partial[q] + strided_planes(q, planes, taken, 4 * c1, kernel_two, out.shape[2])


def on_device(
    ref_features,
    source_tiles,
    pair_lists,
    view_counts,
    disparities,
    conv_first,
    bias_first,
    conv_second,
    bias_second,
):
    n_view = lax.axis_size("view")
    me = lax.axis_index("view").reshape(1)
    rows_n, channels, cols = ref_features.shape
    tiles_dev, tile_rows = source_tiles.shape[0], source_tiles.shape[1]
    sources, blocks = pair_lists.shape[1], pair_lists.shape[2]
    planes = disparities.shape[0]
    slab = tile_rows * channels
    c1, c2 = conv_first.shape[2], conv_second.shape[0]
    half_r, half_p, half_x = rows_n // 2, planes // 2, cols // 2
    smem = pl.BlockSpec(memory_space=pltpu.SMEM)
    vmem = pl.BlockSpec(memory_space=pltpu.VMEM)
    anywhere = pl.BlockSpec(memory_space=pl.ANY)
    params = pltpu.CompilerParams(vmem_limit_bytes=VMEM_LIMIT)
    bf16, f32, i32 = jnp.bfloat16, jnp.float32, jnp.int32
    shape = jax.ShapeDtypeStruct

    table = pl.pallas_call(
        functools.partial(request_kernel, tiles_dev),
        out_shape=shape((n_view, 1, CAP), i32),
        in_specs=[vmem],
        out_specs=vmem,
        compiler_params=params,
        name="request_table",
    )(pair_lists)
    table = lax.all_to_all(table, "view", split_axis=0, concat_axis=0, tiled=True)
    outgoing = source_tiles.reshape(tiles_dev, slab, cols)[table[:, 0]]
    arrived = lax.all_to_all(outgoing, "view", split_axis=0, concat_axis=0, tiled=True)
    arrived = arrived.reshape(n_view * CAP, slab, cols)

    at_slots = planes * sources
    at_live = at_slots + sources * blocks
    edge_blocks, mid_blocks = (0, blocks - 1), tuple(range(1, blocks - 1))
    rows_of = lambda picks: [block * tile_rows + i for block in picks for i in range(tile_rows)]
    edge_rows, mid_rows = rows_of(edge_blocks), rows_of(mid_blocks)
    inner = (rows_n - 2) * c1
    mid_deep, edge_deep = (-(-3 * rows // LANES) * LANES for rows in (inner, 4 * c1))
    prepared = pl.pallas_call(
        functools.partial(prepare_kernel, tiles_dev, edge_rows, mid_rows),
        out_shape=[
            shape((36 * c1 + 8, LANES), f32),
            shape((9 * inner, 2 * LANES), f32),
            shape((3 * half_r * c2, mid_deep), bf16),
            shape((3 * half_r * c2, edge_deep), bf16),
            shape((inner, cols), f32),
            shape((half_r * c2, half_x), f32),
            shape((LANES,), i32),
        ],
        in_specs=[vmem, vmem] + [smem] * 6 + [anywhere],
        out_specs=[vmem] * 6 + [smem],
        scratch_shapes=[pltpu.VMEM((3 * mid_deep, LANES), f32), pltpu.VMEM((3 * edge_deep, LANES), f32)],
        compiler_params=params,
        name="weights_and_scalars",
    )(
        conv_first.transpose(0, 1, 3, 2, 4),
        conv_second.transpose(1, 2, 3, 4, 0),
        bias_first,
        bias_second,
        disparities,
        pair_lists,
        view_counts,
        me,
        table,
    )
    kernel_edge, kernel_mid, two_mid, two_edge, bias_rows, bias_two, scalars = prepared

    band_scratch = [pltpu.VMEM((sources, cols + 2 * SHIFT, LANES), f32), pltpu.VMEM((1, cols, LANES), f32)]
    payload = shape((planes, 2 * c1, cols), bf16)
    col_step = (half_x // LANES + 1) * LANES
    edge_var, own, far, near, flags = pl.pallas_call(
        functools.partial(edge_kernel, at_slots, at_live, sources, blocks, edge_blocks),
        out_shape=[
            shape((planes, cols, LANES), bf16),
            shape((planes, 3 * c1, cols), f32),
            payload,
            payload,
            shape((2, c1, LANES), f32),
        ],
        in_specs=[vmem] * 3,
        out_specs=[vmem] * 5,
        scratch_shapes=band_scratch
        + [
            pltpu.VMEM((3, 12 * c1, cols), f32),
            pltpu.SMEM((8, LANES), f32),
            pltpu.SemaphoreType.DMA,
        ],
        compiler_params=params,
        name="edge_rows",
    )(kernel_edge, arrived, ref_features)
    far = swapped(far, "view", 1)
    near = swapped(near, "view", 0)

    partial, choices = pl.pallas_call(
        functools.partial(mid_kernel, at_slots, at_live, sources, blocks, mid_blocks),
        out_shape=[shape((half_p, half_r * c2, half_x), f32), shape((cols, 2 * col_step), bf16)],
        in_specs=[anywhere] + [vmem] * 7,
        out_specs=[vmem, vmem],
        scratch_shapes=band_scratch
        + [
            pltpu.VMEM((planes * inner, cols), bf16),
            pltpu.VMEM((3, 3 * inner, cols), f32),
            pltpu.SMEM(scalars.shape, i32),
            pltpu.SemaphoreType.DMA,
        ],
        compiler_params=params,
        name="middle_rows",
    )(scalars, arrived, ref_features, edge_var, kernel_mid, bias_rows, two_mid, bias_two)

    out = pl.pallas_call(
        end_kernel,
        out_shape=shape((half_p, half_r * c2, half_x), f32),
        in_specs=[vmem] * 8,
        out_specs=vmem,
        compiler_params=params,
        name="end_rows",
    )(far, near, flags, own, partial, bias_rows, two_edge, choices)
    return out.reshape(half_p, half_r, c2, half_x)


def solution(mesh):
    return jax.shard_map(
        on_device,
        mesh=mesh,
        in_specs=(
            P(("groups", "view"), None, None),
            P(("groups", "view"), None, None, None),
            P(("groups", "view"), None, None),
            P(("groups", "view")),
            P("groups", None),
            P(),
            P(),
            P(),
            P(),
        ),
        out_specs=P("groups", "view", None, None),
        check_vma=False,
    )
```

```python
import functools

import numpy as np

import jax
import jax.numpy as jnp
from jax import lax
from jax.experimental import pallas as pl
from jax.experimental.pallas import tpu as pltpu
from jax.sharding import PartitionSpec as P

SHIFT = 48
CAP = 2
LANES = 128
CHUNK = 64
VMEM_LIMIT = 10 * 1024 * 1024


def swapped(x, axis, parity):
    count = lax.axis_size(axis)
    pairs = [(i, i + 1) for i in range(parity, count - 1, 2)]
    return lax.ppermute(x, axis, pairs + [(j, i) for i, j in pairs])


def request_places(pair_lists, tiles_dev):
    owners, ranks, tiles = [], [], []
    for s in range(pair_lists.shape[1]):
        for b in range(pair_lists.shape[2]):
            tile = pair_lists[0, s, b]
            whole = jnp.maximum(tile, 0)
            owner = jnp.where(tile >= 0, lax.div(whole, tiles_dev), -1)
            rank = jnp.int32(0)
            for other in owners:
                rank = rank + jnp.where(other == owner, 1, 0)
            owners.append(owner)
            ranks.append(rank)
            tiles.append(lax.rem(whole, tiles_dev))
    return owners, ranks, tiles


def request_kernel(tiles_dev, pair_lists, table):
    n_view = table.shape[0]
    row = lax.broadcasted_iota(jnp.int32, (n_view, LANES), 0) * tiles_dev
    lane = lax.broadcasted_iota(jnp.int32, (n_view, LANES), 1)
    total = jnp.zeros((n_view, LANES), jnp.int32)
    count = jnp.zeros((n_view, LANES), jnp.int32)
    for s in range(pair_lists.shape[1]):
        for b in range(pair_lists.shape[2]):
            tile = pair_lists[0, s : s + 1, b : b + 1] - row
            owned = (tile >= 0) & (tile < tiles_dev)
            total = jnp.where(owned & (lane == count), tile, total)
            count = count + jnp.where(owned, 1, 0)
    for d in range(n_view):
        table[d] = total[d : d + 1, : table.shape[2]]


def prepare_kernel(
    tiles_dev,
    edge_rows,
    mid_rows,
    first,
    second,
    bias_first,
    bias_second,
    disparities,
    pair_lists,
    view_counts,
    me,
    _,
    kernel_edge,
    kernel_mid,
    two_mid,
    two_edge,
    bias_rows,
    bias_two,
    scalars,
    stacked_mid,
    stacked_edge,
):
    planes, sources = disparities.shape
    owners, ranks, _ = request_places(pair_lists, tiles_dev)
    at = 0
    for p in range(planes):
        for s in range(sources):
            scalars[at] = disparities[p, s]
            at += 1
    for owner, rank in zip(owners, ranks):
        scalars[at] = jnp.where(owner >= 0, owner * CAP + rank, 0)
        at += 1
    scalars[at] = view_counts[0]
    scalars[at + 1] = me[0]
    scalars[at + 2] = lax.rem(me[0], 2)
    tail = kernel_edge.shape[0] - 8
    lane_at = lax.broadcasted_iota(jnp.int32, (8, LANES), 1)
    numbers = jnp.zeros((8, LANES), jnp.float32)
    for i in range(at + 3):
        numbers = jnp.where(lane_at == i, scalars[i].astype(jnp.float32), numbers)
    kernel_edge[tail:, :] = numbers

    c1, channels = first.shape[3], first.shape[4]
    c2 = second.shape[4]
    rows_n = len(edge_rows) + len(mid_rows)
    half_r = rows_n // 2
    place = {row: i for i, row in enumerate(edge_rows + mid_rows)}
    per_group = LANES // channels
    filler = jnp.zeros((c1, LANES - channels), jnp.float32)
    taps = {}
    for a in range(3):
        for b in range(3):
            for d in range(3):
                tap = jnp.concatenate([first[a, b, d].astype(jnp.float32), filler], axis=1)
                for turn in range(per_group):
                    lane = turn * channels
                    taps[a, b, d, turn] = pltpu.roll(tap, lane, 1) if lane else tap

    def band(a, d, r, group):
        total = jnp.zeros((c1, LANES), jnp.float32)
        for b in range(3):
            at_place = place.get(r - 1 + b, -1)
            if at_place >= 0 and at_place // per_group == group:
                total = total + taps[a, b, d, at_place % per_group]
        return total

    rim = (-1, 0, rows_n - 1, rows_n)
    inner = tuple(range(1, rows_n - 1))
    for kernel, rows, groups in ((kernel_edge, (rim[0],) + rim[2:], 1), (kernel_mid, (0,) + inner, 2)):
        for d in range(3):
            for i, r in enumerate(rows):
                for a in range(3):
                    at = ((a * 3 + d) * len(rows) + i) * c1
                    for group in range(groups):
                        kernel[at : at + c1, group * LANES : (group + 1) * LANES] = band(a, d, r, group)

    def second_row(a, d, r):
        blocks = []
        for g in range(half_r):
            b = -1 if r is None else r - 2 * g + 1
            hit = 0 <= b < 3
            blocks.append(second[a, b, d].astype(jnp.float32) if hit else jnp.zeros((c1, c2), jnp.float32))
        blocks.append(jnp.zeros((c1, LANES - half_r * c2), jnp.float32))
        return jnp.concatenate(blocks, axis=1)

    for two, stacked, rows in ((two_mid, stacked_mid, inner), (two_edge, stacked_edge, rim[:3] + (None,))):
        deep = two.shape[1]
        stacked[...] = jnp.zeros(stacked.shape, jnp.float32)
        for a in range(3):
            for j, d in enumerate((1, 0, 2)):
                for i, r in enumerate(rows):
                    at = j * deep + (a * len(rows) + i) * c1
                    stacked[at : at + c1, :] = second_row(a, d, r)
        outs = half_r * c2
        for j in range(3):
            two[j * outs : (j + 1) * outs, :] = stacked[j * deep : (j + 1) * deep, :].T[:outs].astype(jnp.bfloat16)

    def spread_bias(like, bias):
        index = lax.broadcasted_iota(jnp.int32, like.shape, 0)
        total = jnp.zeros(like.shape, jnp.float32)
        for i in range(bias.shape[0]):
            total = jnp.where(index % bias.shape[0] == i, bias[i], total)
        like[...] = total

    spread_bias(bias_rows, bias_first)
    spread_bias(bias_two, bias_second)


def plane_variance(p, sources, cols, disp, wide, ref_wide, inv):
    chunks = []
    for x0 in range(0, cols, CHUNK):
        ref = ref_wide[0, x0 : x0 + CHUNK, :]
        summed = ref
        squares = ref * ref
        for s in range(sources):
            warped = wide[s, pl.ds(SHIFT + x0 - disp[p * sources + s], CHUNK), :]
            summed = summed + warped
            squares = squares + warped * warped
        chunks.append((squares - summed * summed * inv).astype(jnp.bfloat16))
    return jnp.concatenate(chunks, axis=0)


def view_weights(live):
    total = live.astype(jnp.float32) + jnp.ones((1, LANES), jnp.float32)
    return 1.0 / total, lax.rsqrt(total)


def turned_reference(ref, blocks, picks):
    tile_rows = ref.shape[0] // blocks
    rows = [ref[block * tile_rows + i] for block in picks for i in range(tile_rows)]
    return jnp.concatenate(rows, axis=0).T.astype(jnp.float32)


def clear_bands(wide, cols):
    band = jnp.zeros((SHIFT, LANES), jnp.float32)
    for at in range(wide.shape[0]):
        wide[at, 0:SHIFT, :] = band
        wide[at, SHIFT + cols : 2 * SHIFT + cols, :] = band


def load_tiles(at_slots, live, sources, blocks, picks, scale, scalars, arrived, wide):
    for s in range(sources):
        slab = jnp.concatenate([arrived[scalars[at_slots + s * blocks + block]] for block in picks], axis=0)
        cols = slab.shape[1]
        wide[s, SHIFT : SHIFT + cols, :] = slab.T.astype(jnp.float32) * jnp.where(s < live, scale, 0.0)


def add_plane(q, planes, lhs, weights, sums):
    taps = lax.dot_general(weights, lhs, (((1,), (1,)), ((), ())), preferred_element_type=jnp.float32)
    rows = taps.shape[0] // 3
    slots = sums.shape[0]
    if q + 1 < planes:
        sums[(q + 1) % slots] = taps[:rows]
    if q == 0:
        sums[q % slots] = taps[rows : 2 * rows]
    else:
        sums[q % slots] += taps[rows : 2 * rows]
        sums[(q - 1) % slots] += taps[2 * rows :]


def joined_columns(taps, column):
    rows, cols = column.shape
    left, center, right = taps[:rows], taps[rows : 2 * rows], taps[2 * rows :]
    total = center + jnp.where(column > 0, pltpu.roll(left, 1, 1), 0.0)
    return total + jnp.where(column < cols - 1, pltpu.roll(right, cols - 1, 1), 0.0)


def strided_planes(q, planes, taken, rows, weights, out_w):
    step = taken.shape[1] // 2
    none = jnp.zeros((rows, 2 * step), jnp.bfloat16)
    near = range(2 * q - 1, 2 * q + 2)
    parts = [taken[p * rows : (p + 1) * rows] if 0 <= p < planes else none for p in near]
    rhs = jnp.concatenate(parts, axis=0)
    deep = rhs.shape[0]
    outs = weights.shape[0] // 3
    even = jnp.dot(weights[:outs, :deep], rhs[:, :step], preferred_element_type=jnp.float32)
    odd = jnp.dot(weights[outs:, :deep], rhs[:, step:], preferred_element_type=jnp.float32)
    result = even + pltpu.roll(odd[:outs], 1, 1) + odd[outs:]
    return result[:, :out_w]


def edge_kernel(
    at_slots, at_live, sources, blocks, picks, packed, arrived, ref, var, own, far, near, flags, wide, ref_wide, sums, held, sem
):
    planes, cols, _ = var.shape
    tail = packed.shape[0] - 8
    c1 = tail // 27
    copy = pltpu.make_async_copy(packed.at[pl.ds(tail, 1)], held, sem)
    copy.start()
    weights = packed[:tail].astype(jnp.bfloat16)
    turned = turned_reference(ref, blocks, picks)
    clear_bands(wide, cols)
    copy.wait()
    scalars = [held[0, i].astype(jnp.int32) for i in range(at_live + 3)]
    live = scalars[at_live]
    inv, scale = view_weights(live)
    ref_wide[0] = turned * scale
    load_tiles(at_slots, live, sources, blocks, picks, scale, scalars, arrived, wide)
    odd = scalars[at_live + 2] > 0
    flags[0] = jnp.where(odd, 1.0, 0.0) * jnp.ones((c1, LANES), jnp.float32)
    flags[1] = jnp.where(scalars[at_live + 1] > 0, 1.0, 0.0) * jnp.ones((c1, LANES), jnp.float32)
    column = lax.broadcasted_iota(jnp.int32, (3 * c1, cols), 1)
    empty = jnp.zeros((c1, cols), jnp.float32)

    def finish(p):
        total = joined_columns(sums[p % sums.shape[0]], column)
        own[p] = total[: 2 * c1]
        downward = total[c1:]
        upward = jnp.concatenate([total[:c1], empty], axis=0)
        far[p] = jnp.where(odd, downward, upward).astype(jnp.bfloat16)
        near[p] = jnp.where(odd, upward, downward).astype(jnp.bfloat16)

    values = plane_variance(0, sources, cols, scalars, wide, ref_wide, inv)
    for q in range(planes):
        held_values = values
        if q + 1 < planes:
            values = plane_variance(q + 1, sources, cols, scalars, wide, ref_wide, inv)
        add_plane(q, planes, held_values, weights, sums)
        var[q] = held_values
        if q > 0:
            finish(q - 1)
    finish(planes - 1)


def mid_kernel(
    at_slots,
    at_live,
    sources,
    blocks,
    picks,
    numbers,
    arrived,
    ref,
    edge_var,
    kernel,
    bias_rows,
    kernel_two,
    bias_two,
    out,
    own,
    choices,
    wide,
    ref_wide,
    cost,
    sums,
    scalars,
    sem,
):
    copy = pltpu.make_async_copy(numbers, scalars, sem)
    copy.start()
    planes, cols, _ = edge_var.shape
    inner = cost.shape[0] // planes
    step = choices.shape[1] // 2
    row = lax.broadcasted_iota(jnp.int32, (cols, step), 0)
    target = 2 * lax.broadcasted_iota(jnp.int32, (cols, step), 1)
    for odd in range(2):
        choices[:, odd * step : (odd + 1) * step] = jnp.where(row == target + odd, 1.0, 0.0).astype(jnp.bfloat16)
    turned = turned_reference(ref, blocks, picks)
    clear_bands(wide, cols)
    copy.wait()
    live = scalars[at_live]
    inv, scale = view_weights(live)
    ref_wide[0] = turned * scale
    load_tiles(at_slots, live, sources, blocks, picks, scale, scalars, arrived, wide)
    weights = kernel[...].astype(jnp.bfloat16)
    bias = bias_rows[:inner]
    ready, cols = own.shape[1:]
    column = lax.broadcasted_iota(jnp.int32, (ready + inner, cols), 1)

    def finish(p):
        total = joined_columns(sums[p % sums.shape[0]], column)
        own[p] = total[:ready]
        cost[p * inner : (p + 1) * inner, :] = jnp.maximum(total[ready:] + bias, 0.0).astype(jnp.bfloat16)

    values = plane_variance(0, sources, cols, scalars, wide, ref_wide, inv)
    for q in range(planes):
        held_values = values
        if q + 1 < planes:
            values = plane_variance(q + 1, sources, cols, scalars, wide, ref_wide, inv)
        add_plane(q, planes, jnp.concatenate([edge_var[q], held_values], axis=1), weights, sums)
        if q > 0:
            finish(q - 1)
    finish(planes - 1)
    taken = jnp.dot(cost[...], choices[...], preferred_element_type=jnp.float32).astype(jnp.bfloat16)
    for q in range(planes // 2):
        out[q] = strided_planes(q, planes, taken, inner, kernel_two, out.shape[2]) + bias_two[...]


def end_kernel(far, near, flags, own, own_top, partial, bias_rows, kernel_two, choices, out):
    planes, c1, cols = own_top.shape
    odd = jnp.concatenate([flags[0]] * (cols // LANES), axis=1) > 0.5
    not_top = jnp.concatenate([flags[1]] * (cols // LANES), axis=1)
    empty = jnp.zeros((c1, cols), jnp.float32)
    bias = bias_rows[:c1]
    rows = []
    for p in range(planes):
        lower, upper = far[p].astype(jnp.float32), near[p].astype(jnp.float32)
        before = own[p, :c1] + jnp.where(odd, upper[:c1], lower[:c1])
        top = own_top[p] + jnp.where(odd, upper[c1:], lower[c1:])
        bottom = own[p, c1:] + jnp.where(odd, lower[:c1], upper[:c1])
        rows += [jnp.maximum(before + bias, 0.0) * not_top]
        rows += [jnp.maximum(top + bias, 0.0), jnp.maximum(bottom + bias, 0.0), empty]
    cost = jnp.concatenate(rows, axis=0).astype(jnp.bfloat16)
    taken = jnp.dot(cost, choices[...], preferred_element_type=jnp.float32).astype(jnp.bfloat16)
    for q in range(planes // 2):
        out[q] = partial[q] + strided_planes(q, planes, taken, 4 * c1, kernel_two, out.shape[2])


def on_device(
    ref_features,
    source_tiles,
    pair_lists,
    view_counts,
    disparities,
    conv_first,
    bias_first,
    conv_second,
    bias_second,
):
    n_view = lax.axis_size("view")
    me = lax.axis_index("view").reshape(1)
    rows_n, channels, cols = ref_features.shape
    tiles_dev, tile_rows = source_tiles.shape[0], source_tiles.shape[1]
    sources, blocks = pair_lists.shape[1], pair_lists.shape[2]
    planes = disparities.shape[0]
    slab = tile_rows * channels
    c1, c2 = conv_first.shape[2], conv_second.shape[0]
    half_r, half_p, half_x = rows_n // 2, planes // 2, cols // 2
    smem = pl.BlockSpec(memory_space=pltpu.SMEM)
    vmem = pl.BlockSpec(memory_space=pltpu.VMEM)
    anywhere = pl.BlockSpec(memory_space=pl.ANY)
    params = pltpu.CompilerParams(vmem_limit_bytes=VMEM_LIMIT)
    bf16, f32, i32 = jnp.bfloat16, jnp.float32, jnp.int32
    shape = jax.ShapeDtypeStruct

    table = pl.pallas_call(
        functools.partial(request_kernel, tiles_dev),
        out_shape=shape((n_view, 1, CAP), i32),
        in_specs=[vmem],
        out_specs=vmem,
        compiler_params=params,
        name="request_table",
    )(pair_lists)
    table = lax.all_to_all(table, "view", split_axis=0, concat_axis=0, tiled=True)
    outgoing = source_tiles.reshape(tiles_dev, slab, cols)[table[:, 0]]
    arrived = lax.all_to_all(outgoing, "view", split_axis=0, concat_axis=0, tiled=True)
    arrived = arrived.reshape(n_view * CAP, slab, cols)

    at_slots = planes * sources
    at_live = at_slots + sources * blocks
    edge_blocks, mid_blocks = (0, blocks - 1), tuple(range(1, blocks - 1))
    rows_of = lambda picks: [block * tile_rows + i for block in picks for i in range(tile_rows)]
    edge_rows, mid_rows = rows_of(edge_blocks), rows_of(mid_blocks)
    inner = (rows_n - 2) * c1
    mid_deep, edge_deep = (-(-3 * rows // LANES) * LANES for rows in (inner, 4 * c1))
    prepared = pl.pallas_call(
        functools.partial(prepare_kernel, tiles_dev, edge_rows, mid_rows),
        out_shape=[
            shape((27 * c1 + 8, LANES), f32),
            shape((9 * (inner + c1), 2 * LANES), f32),
            shape((3 * half_r * c2, mid_deep), bf16),
            shape((3 * half_r * c2, edge_deep), bf16),
            shape((inner, cols), f32),
            shape((half_r * c2, half_x), f32),
            shape((LANES,), i32),
        ],
        in_specs=[vmem, vmem] + [smem] * 6 + [anywhere],
        out_specs=[vmem] * 6 + [smem],
        scratch_shapes=[pltpu.VMEM((3 * mid_deep, LANES), f32), pltpu.VMEM((3 * edge_deep, LANES), f32)],
        compiler_params=params,
        name="weights_and_scalars",
    )(
        conv_first.transpose(0, 1, 3, 2, 4),
        conv_second.transpose(1, 2, 3, 4, 0),
        bias_first,
        bias_second,
        disparities,
        pair_lists,
        view_counts,
        me,
        table,
    )
    kernel_edge, kernel_mid, two_mid, two_edge, bias_rows, bias_two, scalars = prepared

    band_scratch = [pltpu.VMEM((sources, cols + 2 * SHIFT, LANES), f32), pltpu.VMEM((1, cols, LANES), f32)]
    payload = shape((planes, 2 * c1, cols), bf16)
    col_step = (half_x // LANES + 1) * LANES
    edge_var, own, far, near, flags = pl.pallas_call(
        functools.partial(edge_kernel, at_slots, at_live, sources, blocks, edge_blocks),
        out_shape=[
            shape((planes, cols, LANES), bf16),
            shape((planes, 2 * c1, cols), f32),
            payload,
            payload,
            shape((2, c1, LANES), f32),
        ],
        in_specs=[vmem] * 3,
        out_specs=[vmem] * 5,
        scratch_shapes=band_scratch
        + [
            pltpu.VMEM((3, 9 * c1, cols), f32),
            pltpu.SMEM((1, LANES), f32),
            pltpu.SemaphoreType.DMA,
        ],
        compiler_params=params,
        name="edge_rows",
    )(kernel_edge, arrived, ref_features)
    far = swapped(far, "view", 1)
    near = swapped(near, "view", 0)

    partial, own_top, choices = pl.pallas_call(
        functools.partial(mid_kernel, at_slots, at_live, sources, blocks, mid_blocks),
        out_shape=[
            shape((half_p, half_r * c2, half_x), f32),
            shape((planes, c1, cols), f32),
            shape((cols, 2 * col_step), bf16),
        ],
        in_specs=[anywhere] + [vmem] * 7,
        out_specs=[vmem] * 3,
        scratch_shapes=band_scratch
        + [
            pltpu.VMEM((planes * inner, cols), bf16),
            pltpu.VMEM((3, 3 * (inner + c1), cols), f32),
            pltpu.SMEM(scalars.shape, i32),
            pltpu.SemaphoreType.DMA,
        ],
        compiler_params=params,
        name="middle_rows",
    )(scalars, arrived, ref_features, edge_var, kernel_mid, bias_rows, two_mid, bias_two)

    out = pl.pallas_call(
        end_kernel,
        out_shape=shape((half_p, half_r * c2, half_x), f32),
        in_specs=[vmem] * 9,
        out_specs=vmem,
        compiler_params=params,
        name="end_rows",
    )(far, near, flags, own, own_top, partial, bias_rows, two_edge, choices)
    return out.reshape(half_p, half_r, c2, half_x)


def solution(mesh):
    return jax.shard_map(
        on_device,
        mesh=mesh,
        in_specs=(
            P(("groups", "view"), None, None),
            P(("groups", "view"), None, None, None),
            P(("groups", "view"), None, None),
            P(("groups", "view")),
            P("groups", None),
            P(),
            P(),
            P(),
            P(),
        ),
        out_specs=P("groups", "view", None, None),
        check_vma=False,
    )
```

```python
import functools

import numpy as np

import jax
import jax.numpy as jnp
from jax import lax
from jax.experimental import pallas as pl
from jax.experimental.pallas import tpu as pltpu
from jax.sharding import PartitionSpec as P

SHIFT = 48
CAP = 2
LANES = 128
CHUNK = 64
VMEM_LIMIT = 10 * 1024 * 1024


def swapped(x, axis, parity):
    count = lax.axis_size(axis)
    pairs = [(i, i + 1) for i in range(parity, count - 1, 2)]
    return lax.ppermute(x, axis, pairs + [(j, i) for i, j in pairs])


def request_places(pair_lists, tiles_dev):
    owners, ranks, tiles = [], [], []
    for s in range(pair_lists.shape[1]):
        for b in range(pair_lists.shape[2]):
            tile = pair_lists[0, s, b]
            whole = jnp.maximum(tile, 0)
            owner = jnp.where(tile >= 0, lax.div(whole, tiles_dev), -1)
            rank = jnp.int32(0)
            for other in owners:
                rank = rank + jnp.where(other == owner, 1, 0)
            owners.append(owner)
            ranks.append(rank)
            tiles.append(lax.rem(whole, tiles_dev))
    return owners, ranks, tiles


def request_kernel(tiles_dev, pair_lists, table):
    n_view = table.shape[0]
    row = lax.broadcasted_iota(jnp.int32, (n_view, LANES), 0) * tiles_dev
    lane = lax.broadcasted_iota(jnp.int32, (n_view, LANES), 1)
    total = jnp.zeros((n_view, LANES), jnp.int32)
    count = jnp.zeros((n_view, LANES), jnp.int32)
    for s in range(pair_lists.shape[1]):
        for b in range(pair_lists.shape[2]):
            tile = pair_lists[0, s : s + 1, b : b + 1] - row
            owned = (tile >= 0) & (tile < tiles_dev)
            total = jnp.where(owned & (lane == count), tile, total)
            count = count + jnp.where(owned, 1, 0)
    for d in range(n_view):
        table[d] = total[d : d + 1, : table.shape[2]]


def prepare_kernel(
    tiles_dev,
    edge_rows,
    mid_rows,
    first,
    second,
    bias_first,
    bias_second,
    disparities,
    pair_lists,
    view_counts,
    me,
    _,
    kernel_edge,
    kernel_mid,
    two_mid,
    two_edge,
    bias_rows,
    bias_two,
    numbers,
    stacked_mid,
    stacked_edge,
):
    planes, sources = disparities.shape
    owners, ranks, _ = request_places(pair_lists, tiles_dev)
    values = [disparities[p, s] for p in range(planes) for s in range(sources)]
    values += [jnp.where(owner >= 0, owner * CAP + rank, 0) for owner, rank in zip(owners, ranks)]
    values += [view_counts[0], me[0], lax.rem(me[0], 2)]
    lane_at = lax.broadcasted_iota(jnp.int32, (8, LANES), 1)
    row = jnp.zeros((8, LANES), jnp.int32)
    for i, value in enumerate(values):
        row = jnp.where(lane_at == i, value, row)
    for at in range(0, numbers.shape[0], 8):
        numbers[at : at + 8, :] = row

    c1, channels = first.shape[3], first.shape[4]
    c2 = second.shape[4]
    rows_n = len(edge_rows) + len(mid_rows)
    half_r = rows_n // 2
    place = {row: i for i, row in enumerate(edge_rows + mid_rows)}
    per_group = LANES // channels
    filler = jnp.zeros((c1, LANES - channels), jnp.float32)
    taps = {}
    for a in range(3):
        for b in range(3):
            for d in range(3):
                tap = jnp.concatenate([first[a, b, d].astype(jnp.float32), filler], axis=1)
                for turn in range(per_group):
                    lane = turn * channels
                    taps[a, b, d, turn] = pltpu.roll(tap, lane, 1) if lane else tap

    def band(a, d, r, group):
        total = jnp.zeros((c1, LANES), jnp.float32)
        for b in range(3):
            at_place = place.get(r - 1 + b, -1)
            if at_place >= 0 and at_place // per_group == group:
                total = total + taps[a, b, d, at_place % per_group]
        return total

    rim = (-1, 0, rows_n - 1, rows_n)
    inner = tuple(range(1, rows_n - 1))
    for kernel, rows, groups in ((kernel_edge, (rim[0],) + rim[2:], 1), (kernel_mid, (0,) + inner, 2)):
        for d in range(3):
            for i, r in enumerate(rows):
                for a in range(3):
                    at = ((a * 3 + d) * len(rows) + i) * c1
                    for group in range(groups):
                        kernel[at : at + c1, group * LANES : (group + 1) * LANES] = band(a, d, r, group)

    def second_row(a, d, r):
        blocks = []
        for g in range(half_r):
            b = -1 if r is None else r - 2 * g + 1
            hit = 0 <= b < 3
            blocks.append(second[a, b, d].astype(jnp.float32) if hit else jnp.zeros((c1, c2), jnp.float32))
        blocks.append(jnp.zeros((c1, LANES - half_r * c2), jnp.float32))
        return jnp.concatenate(blocks, axis=1)

    for two, stacked, rows in ((two_mid, stacked_mid, inner), (two_edge, stacked_edge, rim[:3] + (None,))):
        deep = two.shape[1]
        stacked[...] = jnp.zeros(stacked.shape, jnp.float32)
        for a in range(3):
            for j, d in enumerate((1, 0, 2)):
                for i, r in enumerate(rows):
                    at = j * deep + (a * len(rows) + i) * c1
                    stacked[at : at + c1, :] = second_row(a, d, r)
        outs = half_r * c2
        for j in range(3):
            two[j * outs : (j + 1) * outs, :] = stacked[j * deep : (j + 1) * deep, :].T[:outs].astype(jnp.bfloat16)

    def spread_bias(like, bias):
        index = lax.broadcasted_iota(jnp.int32, like.shape, 0)
        total = jnp.zeros(like.shape, jnp.float32)
        for i in range(bias.shape[0]):
            total = jnp.where(index % bias.shape[0] == i, bias[i], total)
        like[...] = total

    spread_bias(bias_rows, bias_first)
    spread_bias(bias_two, bias_second)


def plane_variance(p, sources, cols, disp, wide, ref_wide, inv):
    chunks = []
    for x0 in range(0, cols, CHUNK):
        ref = ref_wide[0, x0 : x0 + CHUNK, :]
        summed = ref
        squares = ref * ref
        for s in range(sources):
            warped = wide[s, pl.ds(SHIFT + x0 - disp[p * sources + s], CHUNK), :]
            summed = summed + warped
            squares = squares + warped * warped
        chunks.append((squares - summed * summed * inv).astype(jnp.bfloat16))
    return jnp.concatenate(chunks, axis=0)


def view_weights(live):
    total = live.astype(jnp.float32) + jnp.ones((1, LANES), jnp.float32)
    return 1.0 / total, lax.rsqrt(total)


def turned_reference(ref, blocks, picks):
    tile_rows = ref.shape[0] // blocks
    rows = [ref[block * tile_rows + i] for block in picks for i in range(tile_rows)]
    return jnp.concatenate(rows, axis=0).T.astype(jnp.float32)


def clear_bands(wide, cols):
    band = jnp.zeros((SHIFT, LANES), jnp.float32)
    for at in range(wide.shape[0]):
        wide[at, 0:SHIFT, :] = band
        wide[at, SHIFT + cols : 2 * SHIFT + cols, :] = band


def load_tiles(at_slots, live, sources, blocks, picks, scale, scalars, arrived, wide):
    for s in range(sources):
        slab = jnp.concatenate([arrived[scalars[at_slots + s * blocks + block]] for block in picks], axis=0)
        cols = slab.shape[1]
        wide[s, SHIFT : SHIFT + cols, :] = slab.T.astype(jnp.float32) * jnp.where(s < live, scale, 0.0)


def add_plane(q, planes, lhs, weights, sums):
    taps = lax.dot_general(weights, lhs, (((1,), (1,)), ((), ())), preferred_element_type=jnp.float32)
    rows = taps.shape[0] // 3
    slots = sums.shape[0]
    if q + 1 < planes:
        sums[(q + 1) % slots] = taps[:rows]
    if q == 0:
        sums[q % slots] = taps[rows : 2 * rows]
    else:
        sums[q % slots] += taps[rows : 2 * rows]
        sums[(q - 1) % slots] += taps[2 * rows :]


def joined_columns(taps, column):
    rows, cols = column.shape
    left, center, right = taps[:rows], taps[rows : 2 * rows], taps[2 * rows :]
    total = center + jnp.where(column > 0, pltpu.roll(left, 1, 1), 0.0)
    return total + jnp.where(column < cols - 1, pltpu.roll(right, cols - 1, 1), 0.0)


def strided_planes(q, planes, taken, rows, weights, out_w):
    step = taken.shape[1] // 2
    none = jnp.zeros((rows, 2 * step), jnp.bfloat16)
    near = range(2 * q - 1, 2 * q + 2)
    parts = [taken[p * rows : (p + 1) * rows] if 0 <= p < planes else none for p in near]
    rhs = jnp.concatenate(parts, axis=0)
    deep = rhs.shape[0]
    outs = weights.shape[0] // 3
    even = jnp.dot(weights[:outs, :deep], rhs[:, :step], preferred_element_type=jnp.float32)
    odd = jnp.dot(weights[outs:, :deep], rhs[:, step:], preferred_element_type=jnp.float32)
    result = even + pltpu.roll(odd[:outs], 1, 1) + odd[outs:]
    return result[:, :out_w]


def edge_kernel(
    at_slots, at_live, sources, blocks, picks, numbers, arrived, ref, kernel, var, own, far, near, flags, wide, ref_wide, sums, held, sem
):
    planes, cols, _ = var.shape
    c1 = kernel.shape[0] // 27
    copy = pltpu.make_async_copy(numbers.at[pl.ds(0, 1)], held, sem)
    copy.start()
    weights = kernel[...].astype(jnp.bfloat16)
    turned = turned_reference(ref, blocks, picks)
    clear_bands(wide, cols)
    copy.wait()
    scalars = [held[0, i] for i in range(at_live + 3)]
    live = scalars[at_live]
    inv, scale = view_weights(live)
    ref_wide[0] = turned * scale
    load_tiles(at_slots, live, sources, blocks, picks, scale, scalars, arrived, wide)
    odd = scalars[at_live + 2] > 0
    flags[0] = jnp.where(odd, 1.0, 0.0) * jnp.ones((c1, LANES), jnp.float32)
    flags[1] = jnp.where(scalars[at_live + 1] > 0, 1.0, 0.0) * jnp.ones((c1, LANES), jnp.float32)
    column = lax.broadcasted_iota(jnp.int32, (3 * c1, cols), 1)
    empty = jnp.zeros((c1, cols), jnp.float32)

    def finish(p):
        total = joined_columns(sums[p % sums.shape[0]], column)
        own[p] = total[: 2 * c1]
        downward = total[c1:]
        upward = jnp.concatenate([total[:c1], empty], axis=0)
        far[p] = jnp.where(odd, downward, upward).astype(jnp.bfloat16)
        near[p] = jnp.where(odd, upward, downward).astype(jnp.bfloat16)

    values = plane_variance(0, sources, cols, scalars, wide, ref_wide, inv)
    for q in range(planes):
        held_values = values
        if q + 1 < planes:
            values = plane_variance(q + 1, sources, cols, scalars, wide, ref_wide, inv)
        add_plane(q, planes, held_values, weights, sums)
        var[q] = held_values
        if q > 0:
            finish(q - 1)
    finish(planes - 1)


def mid_kernel(
    at_slots,
    at_live,
    sources,
    blocks,
    picks,
    numbers,
    arrived,
    ref,
    edge_var,
    kernel,
    bias_rows,
    kernel_two,
    bias_two,
    out,
    own,
    choices,
    wide,
    ref_wide,
    cost,
    sums,
    held,
    sem,
):
    copy = pltpu.make_async_copy(numbers.at[pl.ds(0, 1)], held, sem)
    copy.start()
    planes, cols, _ = edge_var.shape
    inner = cost.shape[0] // planes
    step = choices.shape[1] // 2
    row = lax.broadcasted_iota(jnp.int32, (cols, step), 0)
    target = 2 * lax.broadcasted_iota(jnp.int32, (cols, step), 1)
    for odd in range(2):
        choices[:, odd * step : (odd + 1) * step] = jnp.where(row == target + odd, 1.0, 0.0).astype(jnp.bfloat16)
    turned = turned_reference(ref, blocks, picks)
    clear_bands(wide, cols)
    copy.wait()
    scalars = [held[0, i] for i in range(at_live + 1)]
    live = scalars[at_live]
    inv, scale = view_weights(live)
    ref_wide[0] = turned * scale
    load_tiles(at_slots, live, sources, blocks, picks, scale, scalars, arrived, wide)
    weights = kernel[...].astype(jnp.bfloat16)
    bias = bias_rows[:inner]
    ready, cols = own.shape[1:]
    column = lax.broadcasted_iota(jnp.int32, (ready + inner, cols), 1)

    def finish(p):
        total = joined_columns(sums[p % sums.shape[0]], column)
        own[p] = total[:ready]
        cost[p * inner : (p + 1) * inner, :] = jnp.maximum(total[ready:] + bias, 0.0).astype(jnp.bfloat16)

    values = plane_variance(0, sources, cols, scalars, wide, ref_wide, inv)
    for q in range(planes):
        held_values = values
        if q + 1 < planes:
            values = plane_variance(q + 1, sources, cols, scalars, wide, ref_wide, inv)
        add_plane(q, planes, jnp.concatenate([edge_var[q], held_values], axis=1), weights, sums)
        if q > 0:
            finish(q - 1)
    finish(planes - 1)
    taken = jnp.dot(cost[...], choices[...], preferred_element_type=jnp.float32).astype(jnp.bfloat16)
    for q in range(planes // 2):
        out[q] = strided_planes(q, planes, taken, inner, kernel_two, out.shape[2]) + bias_two[...]


def end_kernel(far, near, flags, own, own_top, partial, bias_rows, kernel_two, choices, out):
    planes, c1, cols = own_top.shape
    odd = jnp.concatenate([flags[0]] * (cols // LANES), axis=1) > 0.5
    not_top = jnp.concatenate([flags[1]] * (cols // LANES), axis=1)
    empty = jnp.zeros((c1, cols), jnp.float32)
    bias = bias_rows[:c1]
    rows = []
    for p in range(planes):
        lower, upper = far[p].astype(jnp.float32), near[p].astype(jnp.float32)
        before = own[p, :c1] + jnp.where(odd, upper[:c1], lower[:c1])
        top = own_top[p] + jnp.where(odd, upper[c1:], lower[c1:])
        bottom = own[p, c1:] + jnp.where(odd, lower[:c1], upper[:c1])
        rows += [jnp.maximum(before + bias, 0.0) * not_top]
        rows += [jnp.maximum(top + bias, 0.0), jnp.maximum(bottom + bias, 0.0), empty]
    cost = jnp.concatenate(rows, axis=0).astype(jnp.bfloat16)
    taken = jnp.dot(cost, choices[...], preferred_element_type=jnp.float32).astype(jnp.bfloat16)
    for q in range(planes // 2):
        out[q] = partial[q] + strided_planes(q, planes, taken, 4 * c1, kernel_two, out.shape[2])


def on_device(
    ref_features,
    source_tiles,
    pair_lists,
    view_counts,
    disparities,
    conv_first,
    bias_first,
    conv_second,
    bias_second,
):
    n_view = lax.axis_size("view")
    me = lax.axis_index("view").reshape(1)
    rows_n, channels, cols = ref_features.shape
    tiles_dev, tile_rows = source_tiles.shape[0], source_tiles.shape[1]
    sources, blocks = pair_lists.shape[1], pair_lists.shape[2]
    planes = disparities.shape[0]
    slab = tile_rows * channels
    c1, c2 = conv_first.shape[2], conv_second.shape[0]
    half_r, half_p, half_x = rows_n // 2, planes // 2, cols // 2
    smem = pl.BlockSpec(memory_space=pltpu.SMEM)
    vmem = pl.BlockSpec(memory_space=pltpu.VMEM)
    anywhere = pl.BlockSpec(memory_space=pl.ANY)
    params = pltpu.CompilerParams(vmem_limit_bytes=VMEM_LIMIT)
    bf16, f32, i32 = jnp.bfloat16, jnp.float32, jnp.int32
    shape = jax.ShapeDtypeStruct

    table = pl.pallas_call(
        functools.partial(request_kernel, tiles_dev),
        out_shape=shape((n_view, 1, CAP), i32),
        in_specs=[vmem],
        out_specs=vmem,
        compiler_params=params,
        name="request_table",
    )(pair_lists)
    table = lax.all_to_all(table, "view", split_axis=0, concat_axis=0, tiled=True)
    outgoing = source_tiles.reshape(tiles_dev, slab, cols)[table[:, 0]]
    arrived = lax.all_to_all(outgoing, "view", split_axis=0, concat_axis=0, tiled=True)
    arrived = arrived.reshape(n_view * CAP, slab, cols)

    at_slots = planes * sources
    at_live = at_slots + sources * blocks
    edge_blocks, mid_blocks = (0, blocks - 1), tuple(range(1, blocks - 1))
    rows_of = lambda picks: [block * tile_rows + i for block in picks for i in range(tile_rows)]
    edge_rows, mid_rows = rows_of(edge_blocks), rows_of(mid_blocks)
    inner = (rows_n - 2) * c1
    mid_deep, edge_deep = (-(-3 * rows // LANES) * LANES for rows in (inner, 4 * c1))
    prepared = pl.pallas_call(
        functools.partial(prepare_kernel, tiles_dev, edge_rows, mid_rows),
        out_shape=[
            shape((27 * c1, LANES), f32),
            shape((9 * (inner + c1), 2 * LANES), f32),
            shape((3 * half_r * c2, mid_deep), bf16),
            shape((3 * half_r * c2, edge_deep), bf16),
            shape((inner, cols), f32),
            shape((half_r * c2, half_x), f32),
            shape((12 * 8, LANES), i32),
        ],
        in_specs=[vmem, vmem] + [smem] * 6 + [anywhere],
        out_specs=[vmem] * 7,
        scratch_shapes=[pltpu.VMEM((3 * mid_deep, LANES), f32), pltpu.VMEM((3 * edge_deep, LANES), f32)],
        compiler_params=params,
        name="weights_and_scalars",
    )(
        conv_first.transpose(0, 1, 3, 2, 4),
        conv_second.transpose(1, 2, 3, 4, 0),
        bias_first,
        bias_second,
        disparities,
        pair_lists,
        view_counts,
        me,
        table,
    )
    kernel_edge, kernel_mid, two_mid, two_edge, bias_rows, bias_two, numbers = prepared

    band_scratch = [pltpu.VMEM((sources, cols + 2 * SHIFT, LANES), f32), pltpu.VMEM((1, cols, LANES), f32)]
    payload = shape((planes, 2 * c1, cols), bf16)
    col_step = (half_x // LANES + 1) * LANES
    edge_var, own, far, near, flags = pl.pallas_call(
        functools.partial(edge_kernel, at_slots, at_live, sources, blocks, edge_blocks),
        out_shape=[
            shape((planes, cols, LANES), bf16),
            shape((planes, 2 * c1, cols), f32),
            payload,
            payload,
            shape((2, c1, LANES), f32),
        ],
        in_specs=[vmem] * 4,
        out_specs=[vmem] * 5,
        scratch_shapes=band_scratch
        + [
            pltpu.VMEM((3, 9 * c1, cols), f32),
            pltpu.SMEM((1, LANES), i32),
            pltpu.SemaphoreType.DMA,
        ],
        compiler_params=params,
        name="edge_rows",
    )(numbers, arrived, ref_features, kernel_edge)
    far = swapped(far, "view", 1)
    near = swapped(near, "view", 0)

    partial, own_top, choices = pl.pallas_call(
        functools.partial(mid_kernel, at_slots, at_live, sources, blocks, mid_blocks),
        out_shape=[
            shape((half_p, half_r * c2, half_x), f32),
            shape((planes, c1, cols), f32),
            shape((cols, 2 * col_step), bf16),
        ],
        in_specs=[vmem] * 8,
        out_specs=[vmem] * 3,
        scratch_shapes=band_scratch
        + [
            pltpu.VMEM((planes * inner, cols), bf16),
            pltpu.VMEM((3, 3 * (inner + c1), cols), f32),
            pltpu.SMEM((1, LANES), i32),
            pltpu.SemaphoreType.DMA,
        ],
        compiler_params=params,
        name="middle_rows",
    )(numbers, arrived, ref_features, edge_var, kernel_mid, bias_rows, two_mid, bias_two)

    out = pl.pallas_call(
        end_kernel,
        out_shape=shape((half_p, half_r * c2, half_x), f32),
        in_specs=[vmem] * 9,
        out_specs=vmem,
        compiler_params=params,
        name="end_rows",
    )(far, near, flags, own, own_top, partial, bias_rows, two_edge, choices)
    return out.reshape(half_p, half_r, c2, half_x)


def solution(mesh):
    return jax.shard_map(
        on_device,
        mesh=mesh,
        in_specs=(
            P(("groups", "view"), None, None),
            P(("groups", "view"), None, None, None),
            P(("groups", "view"), None, None),
            P(("groups", "view")),
            P("groups", None),
            P(),
            P(),
            P(),
            P(),
        ),
        out_specs=P("groups", "view", None, None),
        check_vma=False,
    )
```

```python
import functools

import numpy as np

import jax
import jax.numpy as jnp
from jax import lax
from jax.experimental import pallas as pl
from jax.experimental.pallas import tpu as pltpu
from jax.sharding import PartitionSpec as P

SHIFT = 48
CAP = 2
LANES = 128
CHUNK = 64
VMEM_LIMIT = 10 * 1024 * 1024


def swapped(x, axis, parity):
    count = lax.axis_size(axis)
    pairs = [(i, i + 1) for i in range(parity, count - 1, 2)]
    return lax.ppermute(x, axis, pairs + [(j, i) for i, j in pairs])


def request_places(pair_lists, tiles_dev):
    owners, ranks, tiles = [], [], []
    for s in range(pair_lists.shape[1]):
        for b in range(pair_lists.shape[2]):
            tile = pair_lists[0, s, b]
            whole = jnp.maximum(tile, 0)
            owner = jnp.where(tile >= 0, lax.div(whole, tiles_dev), -1)
            rank = jnp.int32(0)
            for other in owners:
                rank = rank + jnp.where(other == owner, 1, 0)
            owners.append(owner)
            ranks.append(rank)
            tiles.append(lax.rem(whole, tiles_dev))
    return owners, ranks, tiles


def request_kernel(tiles_dev, pair_lists, table):
    n_view = table.shape[0]
    row = lax.broadcasted_iota(jnp.int32, (n_view, LANES), 0) * tiles_dev
    lane = lax.broadcasted_iota(jnp.int32, (n_view, LANES), 1)
    total = jnp.zeros((n_view, LANES), jnp.int32)
    count = jnp.zeros((n_view, LANES), jnp.int32)
    for s in range(pair_lists.shape[1]):
        for b in range(pair_lists.shape[2]):
            tile = pair_lists[0, s : s + 1, b : b + 1] - row
            owned = (tile >= 0) & (tile < tiles_dev)
            total = jnp.where(owned & (lane == count), tile, total)
            count = count + jnp.where(owned, 1, 0)
    for d in range(n_view):
        table[d] = total[d : d + 1, : table.shape[2]]


def collect_kernel(*refs):
    arrived = refs[-1]
    for k, bundle in enumerate(refs[:-1]):
        for j in range(CAP):
            arrived[k * CAP + j] = bundle[j]


def prepare_kernel(
    tiles_dev,
    edge_rows,
    mid_rows,
    first,
    second,
    bias_first,
    bias_second,
    disparities,
    pair_lists,
    view_counts,
    me,
    table,
    _,
    kernel_edge,
    kernel_mid,
    two_mid,
    two_edge,
    bias_rows,
    bias_two,
    scalars,
    later,
    stacked_mid,
    stacked_edge,
):
    planes, sources = disparities.shape
    n_view = table.shape[0]
    later[...] = table[...]
    owners, ranks, _ = request_places(pair_lists, tiles_dev)
    at = 0
    for p in range(planes):
        for s in range(sources):
            scalars[at] = disparities[p, s]
            at += 1
    for owner, rank in zip(owners, ranks):
        back = lax.rem(me[0] - owner + n_view, n_view)
        scalars[at] = jnp.where(owner >= 0, back * CAP + rank, 0)
        at += 1
    scalars[at] = view_counts[0]
    scalars[at + 1] = me[0]
    scalars[at + 2] = lax.rem(me[0], 2)
    tail = kernel_edge.shape[0] - 8
    lane_at = lax.broadcasted_iota(jnp.int32, (8, LANES), 1)
    numbers = jnp.zeros((8, LANES), jnp.float32)
    for i in range(at + 3):
        numbers = jnp.where(lane_at == i, scalars[i].astype(jnp.float32), numbers)
    kernel_edge[tail:, :] = numbers

    c1, channels = first.shape[3], first.shape[4]
    c2 = second.shape[4]
    rows_n = len(edge_rows) + len(mid_rows)
    half_r = rows_n // 2
    place = {row: i for i, row in enumerate(edge_rows + mid_rows)}
    per_group = LANES // channels
    filler = jnp.zeros((c1, LANES - channels), jnp.float32)
    taps = {}
    for a in range(3):
        for b in range(3):
            for d in range(3):
                tap = jnp.concatenate([first[a, b, d].astype(jnp.float32), filler], axis=1)
                for turn in range(per_group):
                    lane = turn * channels
                    taps[a, b, d, turn] = pltpu.roll(tap, lane, 1) if lane else tap

    def band(a, d, r, group):
        total = jnp.zeros((c1, LANES), jnp.float32)
        for b in range(3):
            at_place = place.get(r - 1 + b, -1)
            if at_place >= 0 and at_place // per_group == group:
                total = total + taps[a, b, d, at_place % per_group]
        return total

    rim = (-1, 0, rows_n - 1, rows_n)
    inner = tuple(range(1, rows_n - 1))
    for kernel, rows, groups in ((kernel_edge, (rim[0],) + rim[2:], 1), (kernel_mid, (0,) + inner, 2)):
        for d in range(3):
            for i, r in enumerate(rows):
                for a in range(3):
                    at = ((a * 3 + d) * len(rows) + i) * c1
                    for group in range(groups):
                        kernel[at : at + c1, group * LANES : (group + 1) * LANES] = band(a, d, r, group)

    def second_row(a, d, r):
        blocks = []
        for g in range(half_r):
            b = -1 if r is None else r - 2 * g + 1
            hit = 0 <= b < 3
            blocks.append(second[a, b, d].astype(jnp.float32) if hit else jnp.zeros((c1, c2), jnp.float32))
        blocks.append(jnp.zeros((c1, LANES - half_r * c2), jnp.float32))
        return jnp.concatenate(blocks, axis=1)

    for two, stacked, rows in ((two_mid, stacked_mid, inner), (two_edge, stacked_edge, rim[:3] + (None,))):
        deep = two.shape[1]
        stacked[...] = jnp.zeros(stacked.shape, jnp.float32)
        for a in range(3):
            for j, d in enumerate((1, 0, 2)):
                for i, r in enumerate(rows):
                    at = j * deep + (a * len(rows) + i) * c1
                    stacked[at : at + c1, :] = second_row(a, d, r)
        outs = half_r * c2
        for j in range(3):
            two[j * outs : (j + 1) * outs, :] = stacked[j * deep : (j + 1) * deep, :].T[:outs].astype(jnp.bfloat16)

    def spread_bias(like, bias):
        index = lax.broadcasted_iota(jnp.int32, like.shape, 0)
        total = jnp.zeros(like.shape, jnp.float32)
        for i in range(bias.shape[0]):
            total = jnp.where(index % bias.shape[0] == i, bias[i], total)
        like[...] = total

    spread_bias(bias_rows, bias_first)
    spread_bias(bias_two, bias_second)


def plane_variance(p, sources, cols, disp, wide, ref_wide, inv):
    chunks = []
    for x0 in range(0, cols, CHUNK):
        ref = ref_wide[0, x0 : x0 + CHUNK, :]
        summed = ref
        squares = ref * ref
        for s in range(sources):
            warped = wide[s, pl.ds(SHIFT + x0 - disp[p * sources + s], CHUNK), :]
            summed = summed + warped
            squares = squares + warped * warped
        chunks.append((squares - summed * summed * inv).astype(jnp.bfloat16))
    return jnp.concatenate(chunks, axis=0)


def view_weights(live):
    total = live.astype(jnp.float32) + jnp.ones((1, LANES), jnp.float32)
    return 1.0 / total, lax.rsqrt(total)


def turned_reference(ref, blocks, picks):
    tile_rows = ref.shape[0] // blocks
    rows = [ref[block * tile_rows + i] for block in picks for i in range(tile_rows)]
    return jnp.concatenate(rows, axis=0).T.astype(jnp.float32)


def clear_bands(wide, cols):
    band = jnp.zeros((SHIFT, LANES), jnp.float32)
    for at in range(wide.shape[0]):
        wide[at, 0:SHIFT, :] = band
        wide[at, SHIFT + cols : 2 * SHIFT + cols, :] = band


def load_tiles(at_slots, live, sources, blocks, picks, scale, scalars, arrived, wide):
    for s in range(sources):
        slab = jnp.concatenate([arrived[scalars[at_slots + s * blocks + block]] for block in picks], axis=0)
        cols = slab.shape[1]
        wide[s, SHIFT : SHIFT + cols, :] = slab.T.astype(jnp.float32) * jnp.where(s < live, scale, 0.0)


def add_plane(q, planes, lhs, weights, sums):
    taps = lax.dot_general(weights, lhs, (((1,), (1,)), ((), ())), preferred_element_type=jnp.float32)
    rows = taps.shape[0] // 3
    slots = sums.shape[0]
    if q + 1 < planes:
        sums[(q + 1) % slots] = taps[:rows]
    if q == 0:
        sums[q % slots] = taps[rows : 2 * rows]
    else:
        sums[q % slots] += taps[rows : 2 * rows]
        sums[(q - 1) % slots] += taps[2 * rows :]


def joined_columns(taps, column):
    rows, cols = column.shape
    left, center, right = taps[:rows], taps[rows : 2 * rows], taps[2 * rows :]
    total = center + jnp.where(column > 0, pltpu.roll(left, 1, 1), 0.0)
    return total + jnp.where(column < cols - 1, pltpu.roll(right, cols - 1, 1), 0.0)


def strided_planes(q, planes, taken, rows, weights, out_w):
    step = taken.shape[1] // 2
    none = jnp.zeros((rows, 2 * step), jnp.bfloat16)
    near = range(2 * q - 1, 2 * q + 2)
    parts = [taken[p * rows : (p + 1) * rows] if 0 <= p < planes else none for p in near]
    rhs = jnp.concatenate(parts, axis=0)
    deep = rhs.shape[0]
    outs = weights.shape[0] // 3
    even = jnp.dot(weights[:outs, :deep], rhs[:, :step], preferred_element_type=jnp.float32)
    odd = jnp.dot(weights[outs:, :deep], rhs[:, step:], preferred_element_type=jnp.float32)
    result = even + pltpu.roll(odd[:outs], 1, 1) + odd[outs:]
    return result[:, :out_w]


def edge_kernel(
    at_slots, at_live, sources, blocks, picks, packed, arrived, ref, var, own, far, near, flags, wide, ref_wide, sums, held, sem
):
    planes, cols, _ = var.shape
    tail = packed.shape[0] - 8
    c1 = tail // 27
    copy = pltpu.make_async_copy(packed.at[pl.ds(tail, 1)], held, sem)
    copy.start()
    weights = packed[:tail].astype(jnp.bfloat16)
    turned = turned_reference(ref, blocks, picks)
    clear_bands(wide, cols)
    copy.wait()
    scalars = [held[0, i].astype(jnp.int32) for i in range(at_live + 3)]
    live = scalars[at_live]
    inv, scale = view_weights(live)
    ref_wide[0] = turned * scale
    load_tiles(at_slots, live, sources, blocks, picks, scale, scalars, arrived, wide)
    odd = scalars[at_live + 2] > 0
    flags[0] = jnp.where(odd, 1.0, 0.0) * jnp.ones((c1, LANES), jnp.float32)
    flags[1] = jnp.where(scalars[at_live + 1] > 0, 1.0, 0.0) * jnp.ones((c1, LANES), jnp.float32)
    column = lax.broadcasted_iota(jnp.int32, (3 * c1, cols), 1)
    empty = jnp.zeros((c1, cols), jnp.float32)

    def finish(p):
        total = joined_columns(sums[p % sums.shape[0]], column)
        own[p] = total[: 2 * c1]
        downward = total[c1:]
        upward = jnp.concatenate([total[:c1], empty], axis=0)
        far[p] = jnp.where(odd, downward, upward).astype(jnp.bfloat16)
        near[p] = jnp.where(odd, upward, downward).astype(jnp.bfloat16)

    values = plane_variance(0, sources, cols, scalars, wide, ref_wide, inv)
    for q in range(planes):
        held_values = values
        if q + 1 < planes:
            values = plane_variance(q + 1, sources, cols, scalars, wide, ref_wide, inv)
        add_plane(q, planes, held_values, weights, sums)
        var[q] = held_values
        if q > 0:
            finish(q - 1)
    finish(planes - 1)


def mid_kernel(
    at_slots,
    at_live,
    sources,
    blocks,
    picks,
    numbers,
    arrived,
    ref,
    edge_var,
    kernel,
    bias_rows,
    kernel_two,
    bias_two,
    out,
    own,
    choices,
    wide,
    ref_wide,
    cost,
    sums,
    scalars,
    sem,
):
    copy = pltpu.make_async_copy(numbers, scalars, sem)
    copy.start()
    planes, cols, _ = edge_var.shape
    inner = cost.shape[0] // planes
    step = choices.shape[1] // 2
    row = lax.broadcasted_iota(jnp.int32, (cols, step), 0)
    target = 2 * lax.broadcasted_iota(jnp.int32, (cols, step), 1)
    for odd in range(2):
        choices[:, odd * step : (odd + 1) * step] = jnp.where(row == target + odd, 1.0, 0.0).astype(jnp.bfloat16)
    turned = turned_reference(ref, blocks, picks)
    clear_bands(wide, cols)
    copy.wait()
    live = scalars[at_live]
    inv, scale = view_weights(live)
    ref_wide[0] = turned * scale
    load_tiles(at_slots, live, sources, blocks, picks, scale, scalars, arrived, wide)
    weights = kernel[...].astype(jnp.bfloat16)
    bias = bias_rows[:inner]
    ready, cols = own.shape[1:]
    column = lax.broadcasted_iota(jnp.int32, (ready + inner, cols), 1)

    def finish(p):
        total = joined_columns(sums[p % sums.shape[0]], column)
        own[p] = total[:ready]
        cost[p * inner : (p + 1) * inner, :] = jnp.maximum(total[ready:] + bias, 0.0).astype(jnp.bfloat16)

    values = plane_variance(0, sources, cols, scalars, wide, ref_wide, inv)
    for q in range(planes):
        held_values = values
        if q + 1 < planes:
            values = plane_variance(q + 1, sources, cols, scalars, wide, ref_wide, inv)
        add_plane(q, planes, jnp.concatenate([edge_var[q], held_values], axis=1), weights, sums)
        if q > 0:
            finish(q - 1)
    finish(planes - 1)
    taken = jnp.dot(cost[...], choices[...], preferred_element_type=jnp.float32).astype(jnp.bfloat16)
    for q in range(planes // 2):
        out[q] = strided_planes(q, planes, taken, inner, kernel_two, out.shape[2]) + bias_two[...]


def end_kernel(far, near, flags, own, own_top, partial, bias_rows, kernel_two, choices, out):
    planes, c1, cols = own_top.shape
    odd = jnp.concatenate([flags[0]] * (cols // LANES), axis=1) > 0.5
    not_top = jnp.concatenate([flags[1]] * (cols // LANES), axis=1)
    empty = jnp.zeros((c1, cols), jnp.float32)
    bias = bias_rows[:c1]
    rows = []
    for p in range(planes):
        lower, upper = far[p].astype(jnp.float32), near[p].astype(jnp.float32)
        before = own[p, :c1] + jnp.where(odd, upper[:c1], lower[:c1])
        top = own_top[p] + jnp.where(odd, upper[c1:], lower[c1:])
        bottom = own[p, c1:] + jnp.where(odd, lower[:c1], upper[:c1])
        rows += [jnp.maximum(before + bias, 0.0) * not_top]
        rows += [jnp.maximum(top + bias, 0.0), jnp.maximum(bottom + bias, 0.0), empty]
    cost = jnp.concatenate(rows, axis=0).astype(jnp.bfloat16)
    taken = jnp.dot(cost, choices[...], preferred_element_type=jnp.float32).astype(jnp.bfloat16)
    for q in range(planes // 2):
        out[q] = partial[q] + strided_planes(q, planes, taken, 4 * c1, kernel_two, out.shape[2])


def on_device(
    ref_features,
    source_tiles,
    pair_lists,
    view_counts,
    disparities,
    conv_first,
    bias_first,
    conv_second,
    bias_second,
):
    n_view = lax.axis_size("view")
    me = lax.axis_index("view").reshape(1)
    rows_n, channels, cols = ref_features.shape
    tiles_dev, tile_rows = source_tiles.shape[0], source_tiles.shape[1]
    sources, blocks = pair_lists.shape[1], pair_lists.shape[2]
    planes = disparities.shape[0]
    slab = tile_rows * channels
    c1, c2 = conv_first.shape[2], conv_second.shape[0]
    half_r, half_p, half_x = rows_n // 2, planes // 2, cols // 2
    smem = pl.BlockSpec(memory_space=pltpu.SMEM)
    vmem = pl.BlockSpec(memory_space=pltpu.VMEM)
    anywhere = pl.BlockSpec(memory_space=pl.ANY)
    params = pltpu.CompilerParams(vmem_limit_bytes=VMEM_LIMIT)
    bf16, f32, i32 = jnp.bfloat16, jnp.float32, jnp.int32
    shape = jax.ShapeDtypeStruct

    table = pl.pallas_call(
        functools.partial(request_kernel, tiles_dev),
        out_shape=shape((n_view, 1, CAP), i32),
        in_specs=[vmem],
        out_specs=vmem,
        compiler_params=params,
        name="request_table",
    )(pair_lists)
    table = lax.all_to_all(table, "view", split_axis=0, concat_axis=0, tiled=True)
    tiles = source_tiles.reshape(tiles_dev, slab, cols)
    table = jnp.roll(table.reshape(n_view, CAP), -me[0], axis=0)
    far_first = sorted(range(1, n_view), key=lambda k: -min(k, n_view - k))
    half = len(far_first) // 2
    order = [k for pair in zip(far_first, far_first[::-1]) for k in pair][: len(far_first)]
    bundles = [None] * n_view

    def send(wanted, distances):
        for k in distances:
            pairs = [(i, (i + k) % n_view) for i in range(n_view)]
            bundles[k] = lax.ppermute(tiles[wanted[k]], "view", pairs)

    send(table, order[:half])

    at_slots = planes * sources
    at_live = at_slots + sources * blocks
    edge_blocks, mid_blocks = (0, blocks - 1), tuple(range(1, blocks - 1))
    rows_of = lambda picks: [block * tile_rows + i for block in picks for i in range(tile_rows)]
    edge_rows, mid_rows = rows_of(edge_blocks), rows_of(mid_blocks)
    inner = (rows_n - 2) * c1
    mid_deep, edge_deep = (-(-3 * rows // LANES) * LANES for rows in (inner, 4 * c1))
    prepared = pl.pallas_call(
        functools.partial(prepare_kernel, tiles_dev, edge_rows, mid_rows),
        out_shape=[
            shape((27 * c1 + 8, LANES), f32),
            shape((9 * (inner + c1), 2 * LANES), f32),
            shape((3 * half_r * c2, mid_deep), bf16),
            shape((3 * half_r * c2, edge_deep), bf16),
            shape((inner, cols), f32),
            shape((half_r * c2, half_x), f32),
            shape((LANES,), i32),
            shape((n_view, CAP), i32),
        ],
        in_specs=[vmem, vmem] + [smem] * 6 + [vmem, anywhere],
        out_specs=[vmem] * 6 + [smem, vmem],
        scratch_shapes=[pltpu.VMEM((3 * mid_deep, LANES), f32), pltpu.VMEM((3 * edge_deep, LANES), f32)],
        compiler_params=params,
        name="weights_and_scalars",
    )(
        conv_first.transpose(0, 1, 3, 2, 4),
        conv_second.transpose(1, 2, 3, 4, 0),
        bias_first,
        bias_second,
        disparities,
        pair_lists,
        view_counts,
        me,
        table,
        bundles[order[0]],
    )
    kernel_edge, kernel_mid, two_mid, two_edge, bias_rows, bias_two, scalars, later = prepared
    send(later, order[half:])
    bundles[0] = tiles[later[0]]
    arrived = pl.pallas_call(
        collect_kernel,
        out_shape=shape((n_view * CAP, slab, cols), bf16),
        in_specs=[vmem] * n_view,
        out_specs=vmem,
        compiler_params=params,
        name="all_tiles",
    )(*bundles)

    band_scratch = [pltpu.VMEM((sources, cols + 2 * SHIFT, LANES), f32), pltpu.VMEM((1, cols, LANES), f32)]
    payload = shape((planes, 2 * c1, cols), bf16)
    col_step = (half_x // LANES + 1) * LANES
    edge_var, own, far, near, flags = pl.pallas_call(
        functools.partial(edge_kernel, at_slots, at_live, sources, blocks, edge_blocks),
        out_shape=[
            shape((planes, cols, LANES), bf16),
            shape((planes, 2 * c1, cols), f32),
            payload,
            payload,
            shape((2, c1, LANES), f32),
        ],
        in_specs=[vmem] * 3,
        out_specs=[vmem] * 5,
        scratch_shapes=band_scratch
        + [
            pltpu.VMEM((3, 9 * c1, cols), f32),
            pltpu.SMEM((1, LANES), f32),
            pltpu.SemaphoreType.DMA,
        ],
        compiler_params=params,
        name="edge_rows",
    )(kernel_edge, arrived, ref_features)
    far = swapped(far, "view", 1)
    near = swapped(near, "view", 0)

    partial, own_top, choices = pl.pallas_call(
        functools.partial(mid_kernel, at_slots, at_live, sources, blocks, mid_blocks),
        out_shape=[
            shape((half_p, half_r * c2, half_x), f32),
            shape((planes, c1, cols), f32),
            shape((cols, 2 * col_step), bf16),
        ],
        in_specs=[anywhere] + [vmem] * 7,
        out_specs=[vmem] * 3,
        scratch_shapes=band_scratch
        + [
            pltpu.VMEM((planes * inner, cols), bf16),
            pltpu.VMEM((3, 3 * (inner + c1), cols), f32),
            pltpu.SMEM(scalars.shape, i32),
            pltpu.SemaphoreType.DMA,
        ],
        compiler_params=params,
        name="middle_rows",
    )(scalars, arrived, ref_features, edge_var, kernel_mid, bias_rows, two_mid, bias_two)

    out = pl.pallas_call(
        end_kernel,
        out_shape=shape((half_p, half_r * c2, half_x), f32),
        in_specs=[vmem] * 9,
        out_specs=vmem,
        compiler_params=params,
        name="end_rows",
    )(far, near, flags, own, own_top, partial, bias_rows, two_edge, choices)
    return out.reshape(half_p, half_r, c2, half_x)


def solution(mesh):
    return jax.shard_map(
        on_device,
        mesh=mesh,
        in_specs=(
            P(("groups", "view"), None, None),
            P(("groups", "view"), None, None, None),
            P(("groups", "view"), None, None),
            P(("groups", "view")),
            P("groups", None),
            P(),
            P(),
            P(),
            P(),
        ),
        out_specs=P("groups", "view", None, None),
        check_vma=False,
    )
```

```python
import functools

import numpy as np

import jax
import jax.numpy as jnp
from jax import lax
from jax.experimental import pallas as pl
from jax.experimental.pallas import tpu as pltpu
from jax.sharding import PartitionSpec as P

SHIFT = 48
CAP = 2
LANES = 128
CHUNK = 64
VMEM_LIMIT = 10 * 1024 * 1024


def swapped(x, axis, parity):
    count = lax.axis_size(axis)
    pairs = [(i, i + 1) for i in range(parity, count - 1, 2)]
    return lax.ppermute(x, axis, pairs + [(j, i) for i, j in pairs])


def request_places(pair_lists, tiles_dev):
    owners, ranks, tiles = [], [], []
    for s in range(pair_lists.shape[1]):
        for b in range(pair_lists.shape[2]):
            tile = pair_lists[0, s, b]
            whole = jnp.maximum(tile, 0)
            owner = jnp.where(tile >= 0, lax.div(whole, tiles_dev), -1)
            rank = jnp.int32(0)
            for other in owners:
                rank = rank + jnp.where(other == owner, 1, 0)
            owners.append(owner)
            ranks.append(rank)
            tiles.append(lax.rem(whole, tiles_dev))
    return owners, ranks, tiles


def request_kernel(tiles_dev, pair_lists, table):
    n_view = table.shape[0]
    row = lax.broadcasted_iota(jnp.int32, (n_view, LANES), 0) * tiles_dev
    lane = lax.broadcasted_iota(jnp.int32, (n_view, LANES), 1)
    total = jnp.zeros((n_view, LANES), jnp.int32)
    count = jnp.zeros((n_view, LANES), jnp.int32)
    for s in range(pair_lists.shape[1]):
        for b in range(pair_lists.shape[2]):
            tile = pair_lists[0, s : s + 1, b : b + 1] - row
            owned = (tile >= 0) & (tile < tiles_dev)
            total = jnp.where(owned & (lane == count), tile, total)
            count = count + jnp.where(owned, 1, 0)
    total = jnp.where(lane == CAP, lax.broadcasted_iota(jnp.int32, (n_view, LANES), 0), total)
    for d in range(n_view):
        table[d] = total[d : d + 1, : table.shape[2]]


def gather_kernel(distances, n_view, table, tiles, *bundles):
    me = table[0, CAP]
    for k, bundle in zip(distances, bundles):
        at = lax.rem(me + k, n_view) * (CAP + 1)
        for j in range(CAP):
            bundle[j] = tiles[table[0, at + j]]


def collect_kernel(*refs):
    arrived = refs[-1]
    for k, bundle in enumerate(refs[:-1]):
        for j in range(CAP):
            arrived[k * CAP + j] = bundle[j]


def prepare_kernel(
    tiles_dev,
    edge_rows,
    mid_rows,
    first,
    second,
    bias_first,
    bias_second,
    disparities,
    pair_lists,
    view_counts,
    me,
    table,
    _,
    kernel_edge,
    kernel_mid,
    two_mid,
    two_edge,
    bias_rows,
    bias_two,
    scalars,
    later,
    stacked_mid,
    stacked_edge,
):
    planes, sources = disparities.shape
    n_view = table.shape[1] // (CAP + 1)
    later[...] = table[...]
    owners, ranks, _ = request_places(pair_lists, tiles_dev)
    at = 0
    for p in range(planes):
        for s in range(sources):
            scalars[at] = disparities[p, s]
            at += 1
    for owner, rank in zip(owners, ranks):
        back = lax.rem(me[0] - owner + n_view, n_view)
        scalars[at] = jnp.where(owner >= 0, back * CAP + rank, 0)
        at += 1
    scalars[at] = view_counts[0]
    scalars[at + 1] = me[0]
    scalars[at + 2] = lax.rem(me[0], 2)
    tail = kernel_edge.shape[0] - 8
    lane_at = lax.broadcasted_iota(jnp.int32, (8, LANES), 1)
    numbers = jnp.zeros((8, LANES), jnp.float32)
    for i in range(at + 3):
        numbers = jnp.where(lane_at == i, scalars[i].astype(jnp.float32), numbers)
    kernel_edge[tail:, :] = numbers

    c1, channels = first.shape[3], first.shape[4]
    c2 = second.shape[4]
    rows_n = len(edge_rows) + len(mid_rows)
    half_r = rows_n // 2
    place = {row: i for i, row in enumerate(edge_rows + mid_rows)}
    per_group = LANES // channels
    filler = jnp.zeros((c1, LANES - channels), jnp.float32)
    taps = {}
    for a in range(3):
        for b in range(3):
            for d in range(3):
                tap = jnp.concatenate([first[a, b, d].astype(jnp.float32), filler], axis=1)
                for turn in range(per_group):
                    lane = turn * channels
                    taps[a, b, d, turn] = pltpu.roll(tap, lane, 1) if lane else tap

    def band(a, d, r, group):
        total = jnp.zeros((c1, LANES), jnp.float32)
        for b in range(3):
            at_place = place.get(r - 1 + b, -1)
            if at_place >= 0 and at_place // per_group == group:
                total = total + taps[a, b, d, at_place % per_group]
        return total

    rim = (-1, 0, rows_n - 1, rows_n)
    inner = tuple(range(1, rows_n - 1))
    for kernel, rows, groups in ((kernel_edge, (rim[0],) + rim[2:], 1), (kernel_mid, (0,) + inner, 2)):
        for d in range(3):
            for i, r in enumerate(rows):
                for a in range(3):
                    at = ((a * 3 + d) * len(rows) + i) * c1
                    for group in range(groups):
                        kernel[at : at + c1, group * LANES : (group + 1) * LANES] = band(a, d, r, group)

    def second_row(a, d, r):
        blocks = []
        for g in range(half_r):
            b = -1 if r is None else r - 2 * g + 1
            hit = 0 <= b < 3
            blocks.append(second[a, b, d].astype(jnp.float32) if hit else jnp.zeros((c1, c2), jnp.float32))
        blocks.append(jnp.zeros((c1, LANES - half_r * c2), jnp.float32))
        return jnp.concatenate(blocks, axis=1)

    for two, stacked, rows in ((two_mid, stacked_mid, inner), (two_edge, stacked_edge, rim[:3] + (None,))):
        deep = two.shape[1]
        stacked[...] = jnp.zeros(stacked.shape, jnp.float32)
        for a in range(3):
            for j, d in enumerate((1, 0, 2)):
                for i, r in enumerate(rows):
                    at = j * deep + (a * len(rows) + i) * c1
                    stacked[at : at + c1, :] = second_row(a, d, r)
        outs = half_r * c2
        for j in range(3):
            two[j * outs : (j + 1) * outs, :] = stacked[j * deep : (j + 1) * deep, :].T[:outs].astype(jnp.bfloat16)

    def spread_bias(like, bias):
        index = lax.broadcasted_iota(jnp.int32, like.shape, 0)
        total = jnp.zeros(like.shape, jnp.float32)
        for i in range(bias.shape[0]):
            total = jnp.where(index % bias.shape[0] == i, bias[i], total)
        like[...] = total

    spread_bias(bias_rows, bias_first)
    spread_bias(bias_two, bias_second)


def plane_variance(p, sources, cols, disp, wide, ref_wide, inv):
    chunks = []
    for x0 in range(0, cols, CHUNK):
        ref = ref_wide[0, x0 : x0 + CHUNK, :]
        summed = ref
        squares = ref * ref
        for s in range(sources):
            warped = wide[s, pl.ds(SHIFT + x0 - disp[p * sources + s], CHUNK), :]
            summed = summed + warped
            squares = squares + warped * warped
        chunks.append((squares - summed * summed * inv).astype(jnp.bfloat16))
    return jnp.concatenate(chunks, axis=0)


def view_weights(live):
    total = live.astype(jnp.float32) + jnp.ones((1, LANES), jnp.float32)
    return 1.0 / total, lax.rsqrt(total)


def turned_reference(ref, blocks, picks):
    tile_rows = ref.shape[0] // blocks
    rows = [ref[block * tile_rows + i] for block in picks for i in range(tile_rows)]
    return jnp.concatenate(rows, axis=0).T.astype(jnp.float32)


def clear_bands(wide, cols):
    band = jnp.zeros((SHIFT, LANES), jnp.float32)
    for at in range(wide.shape[0]):
        wide[at, 0:SHIFT, :] = band
        wide[at, SHIFT + cols : 2 * SHIFT + cols, :] = band


def load_tiles(at_slots, live, sources, blocks, picks, scale, scalars, arrived, wide):
    for s in range(sources):
        slab = jnp.concatenate([arrived[scalars[at_slots + s * blocks + block]] for block in picks], axis=0)
        cols = slab.shape[1]
        wide[s, SHIFT : SHIFT + cols, :] = slab.T.astype(jnp.float32) * jnp.where(s < live, scale, 0.0)


def add_plane(q, planes, lhs, weights, sums):
    taps = lax.dot_general(weights, lhs, (((1,), (1,)), ((), ())), preferred_element_type=jnp.float32)
    rows = taps.shape[0] // 3
    slots = sums.shape[0]
    if q + 1 < planes:
        sums[(q + 1) % slots] = taps[:rows]
    if q == 0:
        sums[q % slots] = taps[rows : 2 * rows]
    else:
        sums[q % slots] += taps[rows : 2 * rows]
        sums[(q - 1) % slots] += taps[2 * rows :]


def joined_columns(taps, column):
    rows, cols = column.shape
    left, center, right = taps[:rows], taps[rows : 2 * rows], taps[2 * rows :]
    total = center + jnp.where(column > 0, pltpu.roll(left, 1, 1), 0.0)
    return total + jnp.where(column < cols - 1, pltpu.roll(right, cols - 1, 1), 0.0)


def strided_planes(q, planes, taken, rows, weights, out_w):
    step = taken.shape[1] // 2
    none = jnp.zeros((rows, 2 * step), jnp.bfloat16)
    near = range(2 * q - 1, 2 * q + 2)
    parts = [taken[p * rows : (p + 1) * rows] if 0 <= p < planes else none for p in near]
    rhs = jnp.concatenate(parts, axis=0)
    deep = rhs.shape[0]
    outs = weights.shape[0] // 3
    even = jnp.dot(weights[:outs, :deep], rhs[:, :step], preferred_element_type=jnp.float32)
    odd = jnp.dot(weights[outs:, :deep], rhs[:, step:], preferred_element_type=jnp.float32)
    result = even + pltpu.roll(odd[:outs], 1, 1) + odd[outs:]
    return result[:, :out_w]


def edge_kernel(
    at_slots, at_live, sources, blocks, picks, packed, arrived, ref, var, own, far, near, flags, wide, ref_wide, sums, held, sem
):
    planes, cols, _ = var.shape
    tail = packed.shape[0] - 8
    c1 = tail // 27
    copy = pltpu.make_async_copy(packed.at[pl.ds(tail, 1)], held, sem)
    copy.start()
    weights = packed[:tail].astype(jnp.bfloat16)
    turned = turned_reference(ref, blocks, picks)
    clear_bands(wide, cols)
    copy.wait()
    scalars = [held[0, i].astype(jnp.int32) for i in range(at_live + 3)]
    live = scalars[at_live]
    inv, scale = view_weights(live)
    ref_wide[0] = turned * scale
    load_tiles(at_slots, live, sources, blocks, picks, scale, scalars, arrived, wide)
    odd = scalars[at_live + 2] > 0
    flags[0] = jnp.where(odd, 1.0, 0.0) * jnp.ones((c1, LANES), jnp.float32)
    flags[1] = jnp.where(scalars[at_live + 1] > 0, 1.0, 0.0) * jnp.ones((c1, LANES), jnp.float32)
    column = lax.broadcasted_iota(jnp.int32, (3 * c1, cols), 1)
    empty = jnp.zeros((c1, cols), jnp.float32)

    def finish(p):
        total = joined_columns(sums[p % sums.shape[0]], column)
        own[p] = total[: 2 * c1]
        downward = total[c1:]
        upward = jnp.concatenate([total[:c1], empty], axis=0)
        far[p] = jnp.where(odd, downward, upward).astype(jnp.bfloat16)
        near[p] = jnp.where(odd, upward, downward).astype(jnp.bfloat16)

    values = plane_variance(0, sources, cols, scalars, wide, ref_wide, inv)
    for q in range(planes):
        held_values = values
        if q + 1 < planes:
            values = plane_variance(q + 1, sources, cols, scalars, wide, ref_wide, inv)
        add_plane(q, planes, held_values, weights, sums)
        var[q] = held_values
        if q > 0:
            finish(q - 1)
    finish(planes - 1)


def mid_kernel(
    at_slots,
    at_live,
    sources,
    blocks,
    picks,
    numbers,
    arrived,
    ref,
    edge_var,
    kernel,
    bias_rows,
    kernel_two,
    bias_two,
    out,
    own,
    choices,
    wide,
    ref_wide,
    cost,
    sums,
    scalars,
    sem,
):
    copy = pltpu.make_async_copy(numbers, scalars, sem)
    copy.start()
    planes, cols, _ = edge_var.shape
    inner = cost.shape[0] // planes
    step = choices.shape[1] // 2
    row = lax.broadcasted_iota(jnp.int32, (cols, step), 0)
    target = 2 * lax.broadcasted_iota(jnp.int32, (cols, step), 1)
    for odd in range(2):
        choices[:, odd * step : (odd + 1) * step] = jnp.where(row == target + odd, 1.0, 0.0).astype(jnp.bfloat16)
    turned = turned_reference(ref, blocks, picks)
    clear_bands(wide, cols)
    copy.wait()
    live = scalars[at_live]
    inv, scale = view_weights(live)
    ref_wide[0] = turned * scale
    load_tiles(at_slots, live, sources, blocks, picks, scale, scalars, arrived, wide)
    weights = kernel[...].astype(jnp.bfloat16)
    bias = bias_rows[:inner]
    ready, cols = own.shape[1:]
    column = lax.broadcasted_iota(jnp.int32, (ready + inner, cols), 1)

    def finish(p):
        total = joined_columns(sums[p % sums.shape[0]], column)
        own[p] = total[:ready]
        cost[p * inner : (p + 1) * inner, :] = jnp.maximum(total[ready:] + bias, 0.0).astype(jnp.bfloat16)

    values = plane_variance(0, sources, cols, scalars, wide, ref_wide, inv)
    for q in range(planes):
        held_values = values
        if q + 1 < planes:
            values = plane_variance(q + 1, sources, cols, scalars, wide, ref_wide, inv)
        add_plane(q, planes, jnp.concatenate([edge_var[q], held_values], axis=1), weights, sums)
        if q > 0:
            finish(q - 1)
    finish(planes - 1)
    taken = jnp.dot(cost[...], choices[...], preferred_element_type=jnp.float32).astype(jnp.bfloat16)
    for q in range(planes // 2):
        out[q] = strided_planes(q, planes, taken, inner, kernel_two, out.shape[2]) + bias_two[...]


def end_kernel(far, near, flags, own, own_top, partial, bias_rows, kernel_two, choices, out):
    planes, c1, cols = own_top.shape
    odd = jnp.concatenate([flags[0]] * (cols // LANES), axis=1) > 0.5
    not_top = jnp.concatenate([flags[1]] * (cols // LANES), axis=1)
    empty = jnp.zeros((c1, cols), jnp.float32)
    bias = bias_rows[:c1]
    rows = []
    for p in range(planes):
        lower, upper = far[p].astype(jnp.float32), near[p].astype(jnp.float32)
        before = own[p, :c1] + jnp.where(odd, upper[:c1], lower[:c1])
        top = own_top[p] + jnp.where(odd, upper[c1:], lower[c1:])
        bottom = own[p, c1:] + jnp.where(odd, lower[:c1], upper[:c1])
        rows += [jnp.maximum(before + bias, 0.0) * not_top]
        rows += [jnp.maximum(top + bias, 0.0), jnp.maximum(bottom + bias, 0.0), empty]
    cost = jnp.concatenate(rows, axis=0).astype(jnp.bfloat16)
    taken = jnp.dot(cost, choices[...], preferred_element_type=jnp.float32).astype(jnp.bfloat16)
    for q in range(planes // 2):
        out[q] = partial[q] + strided_planes(q, planes, taken, 4 * c1, kernel_two, out.shape[2])


def on_device(
    ref_features,
    source_tiles,
    pair_lists,
    view_counts,
    disparities,
    conv_first,
    bias_first,
    conv_second,
    bias_second,
):
    n_view = lax.axis_size("view")
    me = lax.axis_index("view").reshape(1)
    rows_n, channels, cols = ref_features.shape
    tiles_dev, tile_rows = source_tiles.shape[0], source_tiles.shape[1]
    sources, blocks = pair_lists.shape[1], pair_lists.shape[2]
    planes = disparities.shape[0]
    slab = tile_rows * channels
    c1, c2 = conv_first.shape[2], conv_second.shape[0]
    half_r, half_p, half_x = rows_n // 2, planes // 2, cols // 2
    smem = pl.BlockSpec(memory_space=pltpu.SMEM)
    vmem = pl.BlockSpec(memory_space=pltpu.VMEM)
    anywhere = pl.BlockSpec(memory_space=pl.ANY)
    params = pltpu.CompilerParams(vmem_limit_bytes=VMEM_LIMIT)
    bf16, f32, i32 = jnp.bfloat16, jnp.float32, jnp.int32
    shape = jax.ShapeDtypeStruct

    table = pl.pallas_call(
        functools.partial(request_kernel, tiles_dev),
        out_shape=shape((n_view, 1, CAP + 1), i32),
        in_specs=[vmem],
        out_specs=vmem,
        compiler_params=params,
        name="request_table",
    )(pair_lists)
    table = lax.all_to_all(table, "view", split_axis=0, concat_axis=0, tiled=True)
    tiles = source_tiles.reshape(tiles_dev, slab, cols)
    table = table.reshape(1, n_view * (CAP + 1))
    far_first = sorted(range(1, n_view), key=lambda k: -min(k, n_view - k))
    half = len(far_first) // 2
    order = [k for pair in zip(far_first, far_first[::-1]) for k in pair][: len(far_first)]
    bundles = [None] * n_view

    def send(wanted, distances):
        gathered = pl.pallas_call(
            functools.partial(gather_kernel, distances, n_view),
            out_shape=[shape((CAP, slab, cols), bf16)] * len(distances),
            in_specs=[smem, vmem],
            out_specs=[vmem] * len(distances),
            compiler_params=params,
            name=f"requested_tiles_{distances[0]}",
        )(wanted, tiles)
        for k, bundle in zip(distances, gathered):
            pairs = [(i, (i + k) % n_view) for i in range(n_view)]
            bundles[k] = lax.ppermute(bundle, "view", pairs) if k else bundle

    send(table, order[:half])

    at_slots = planes * sources
    at_live = at_slots + sources * blocks
    edge_blocks, mid_blocks = (0, blocks - 1), tuple(range(1, blocks - 1))
    rows_of = lambda picks: [block * tile_rows + i for block in picks for i in range(tile_rows)]
    edge_rows, mid_rows = rows_of(edge_blocks), rows_of(mid_blocks)
    inner = (rows_n - 2) * c1
    mid_deep, edge_deep = (-(-3 * rows // LANES) * LANES for rows in (inner, 4 * c1))
    prepared = pl.pallas_call(
        functools.partial(prepare_kernel, tiles_dev, edge_rows, mid_rows),
        out_shape=[
            shape((27 * c1 + 8, LANES), f32),
            shape((9 * (inner + c1), 2 * LANES), f32),
            shape((3 * half_r * c2, mid_deep), bf16),
            shape((3 * half_r * c2, edge_deep), bf16),
            shape((inner, cols), f32),
            shape((half_r * c2, half_x), f32),
            shape((LANES,), i32),
            shape((1, n_view * (CAP + 1)), i32),
        ],
        in_specs=[vmem, vmem] + [smem] * 6 + [vmem, anywhere],
        out_specs=[vmem] * 6 + [smem, vmem],
        scratch_shapes=[pltpu.VMEM((3 * mid_deep, LANES), f32), pltpu.VMEM((3 * edge_deep, LANES), f32)],
        compiler_params=params,
        name="weights_and_scalars",
    )(
        conv_first.transpose(0, 1, 3, 2, 4),
        conv_second.transpose(1, 2, 3, 4, 0),
        bias_first,
        bias_second,
        disparities,
        pair_lists,
        view_counts,
        me,
        table,
        bundles[order[0]],
    )
    kernel_edge, kernel_mid, two_mid, two_edge, bias_rows, bias_two, scalars, later = prepared
    send(later, order[half:] + [0])
    arrived = pl.pallas_call(
        collect_kernel,
        out_shape=shape((n_view * CAP, slab, cols), bf16),
        in_specs=[vmem] * n_view,
        out_specs=vmem,
        compiler_params=params,
        name="all_tiles",
    )(*bundles)

    band_scratch = [pltpu.VMEM((sources, cols + 2 * SHIFT, LANES), f32), pltpu.VMEM((1, cols, LANES), f32)]
    payload = shape((planes, 2 * c1, cols), bf16)
    col_step = (half_x // LANES + 1) * LANES
    edge_var, own, far, near, flags = pl.pallas_call(
        functools.partial(edge_kernel, at_slots, at_live, sources, blocks, edge_blocks),
        out_shape=[
            shape((planes, cols, LANES), bf16),
            shape((planes, 2 * c1, cols), f32),
            payload,
            payload,
            shape((2, c1, LANES), f32),
        ],
        in_specs=[vmem] * 3,
        out_specs=[vmem] * 5,
        scratch_shapes=band_scratch
        + [
            pltpu.VMEM((3, 9 * c1, cols), f32),
            pltpu.SMEM((1, LANES), f32),
            pltpu.SemaphoreType.DMA,
        ],
        compiler_params=params,
        name="edge_rows",
    )(kernel_edge, arrived, ref_features)
    far = swapped(far, "view", 1)
    near = swapped(near, "view", 0)

    partial, own_top, choices = pl.pallas_call(
        functools.partial(mid_kernel, at_slots, at_live, sources, blocks, mid_blocks),
        out_shape=[
            shape((half_p, half_r * c2, half_x), f32),
            shape((planes, c1, cols), f32),
            shape((cols, 2 * col_step), bf16),
        ],
        in_specs=[anywhere] + [vmem] * 7,
        out_specs=[vmem] * 3,
        scratch_shapes=band_scratch
        + [
            pltpu.VMEM((planes * inner, cols), bf16),
            pltpu.VMEM((3, 3 * (inner + c1), cols), f32),
            pltpu.SMEM(scalars.shape, i32),
            pltpu.SemaphoreType.DMA,
        ],
        compiler_params=params,
        name="middle_rows",
    )(scalars, arrived, ref_features, edge_var, kernel_mid, bias_rows, two_mid, bias_two)

    out = pl.pallas_call(
        end_kernel,
        out_shape=shape((half_p, half_r * c2, half_x), f32),
        in_specs=[vmem] * 9,
        out_specs=vmem,
        compiler_params=params,
        name="end_rows",
    )(far, near, flags, own, own_top, partial, bias_rows, two_edge, choices)
    return out.reshape(half_p, half_r, c2, half_x)


def solution(mesh):
    return jax.shard_map(
        on_device,
        mesh=mesh,
        in_specs=(
            P(("groups", "view"), None, None),
            P(("groups", "view"), None, None, None),
            P(("groups", "view"), None, None),
            P(("groups", "view")),
            P("groups", None),
            P(),
            P(),
            P(),
            P(),
        ),
        out_specs=P("groups", "view", None, None),
        check_vma=False,
    )
```

```python
import functools

import numpy as np

import jax
import jax.numpy as jnp
from jax import lax
from jax.experimental import pallas as pl
from jax.experimental.pallas import tpu as pltpu
from jax.sharding import PartitionSpec as P

SHIFT = 48
CAP = 2
IN_FLIGHT = 5
LANES = 128
CHUNK = 64
VMEM_LIMIT = 10 * 1024 * 1024


def swapped(x, axis, parity):
    count = lax.axis_size(axis)
    pairs = [(i, i + 1) for i in range(parity, count - 1, 2)]
    return lax.ppermute(x, axis, pairs + [(j, i) for i, j in pairs])


def request_places(pair_lists, tiles_dev):
    owners, ranks, tiles = [], [], []
    for s in range(pair_lists.shape[1]):
        for b in range(pair_lists.shape[2]):
            tile = pair_lists[0, s, b]
            whole = jnp.maximum(tile, 0)
            owner = jnp.where(tile >= 0, lax.div(whole, tiles_dev), -1)
            rank = jnp.int32(0)
            for other in owners:
                rank = rank + jnp.where(other == owner, 1, 0)
            owners.append(owner)
            ranks.append(rank)
            tiles.append(lax.rem(whole, tiles_dev))
    return owners, ranks, tiles


def request_kernel(tiles_dev, pair_lists, table):
    n_view = table.shape[0]
    row = lax.broadcasted_iota(jnp.int32, (n_view, LANES), 0) * tiles_dev
    lane = lax.broadcasted_iota(jnp.int32, (n_view, LANES), 1)
    total = jnp.zeros((n_view, LANES), jnp.int32)
    count = jnp.zeros((n_view, LANES), jnp.int32)
    for s in range(pair_lists.shape[1]):
        for b in range(pair_lists.shape[2]):
            tile = pair_lists[0, s : s + 1, b : b + 1] - row
            owned = (tile >= 0) & (tile < tiles_dev)
            total = jnp.where(owned & (lane == count), tile, total)
            count = count + jnp.where(owned, 1, 0)
    total = jnp.where(lane == CAP, lax.broadcasted_iota(jnp.int32, (n_view, LANES), 0), total)
    for d in range(n_view):
        table[d] = total[d : d + 1, : table.shape[2]]


def gather_kernel(distances, n_view, table, tiles, *bundles):
    me = table[0, CAP]
    for k, bundle in zip(distances, bundles):
        at = lax.rem(me + k, n_view) * (CAP + 1)
        for j in range(CAP):
            bundle[j] = tiles[table[0, at + j]]


def collect_kernel(*refs):
    arrived = refs[-1]
    for k, bundle in enumerate(refs[:-1]):
        for j in range(CAP):
            arrived[k * CAP + j] = bundle[j]


def prepare_kernel(
    tiles_dev,
    edge_rows,
    mid_rows,
    first,
    second,
    bias_first,
    bias_second,
    disparities,
    pair_lists,
    view_counts,
    me,
    table,
    _,
    kernel_edge,
    kernel_mid,
    two_mid,
    two_edge,
    bias_rows,
    bias_two,
    scalars,
    later,
    stacked_mid,
    stacked_edge,
):
    planes, sources = disparities.shape
    n_view = table.shape[1] // (CAP + 1)
    later[...] = table[...]
    owners, ranks, _ = request_places(pair_lists, tiles_dev)
    at = 0
    for p in range(planes):
        for s in range(sources):
            scalars[at] = disparities[p, s]
            at += 1
    for owner, rank in zip(owners, ranks):
        back = lax.rem(me[0] - owner + n_view, n_view)
        scalars[at] = jnp.where(owner >= 0, back * CAP + rank, 0)
        at += 1
    scalars[at] = view_counts[0]
    scalars[at + 1] = me[0]
    scalars[at + 2] = lax.rem(me[0], 2)
    tail = kernel_edge.shape[0] - 8
    lane_at = lax.broadcasted_iota(jnp.int32, (8, LANES), 1)
    numbers = jnp.zeros((8, LANES), jnp.float32)
    for i in range(at + 3):
        numbers = jnp.where(lane_at == i, scalars[i].astype(jnp.float32), numbers)
    kernel_edge[tail:, :] = numbers

    c1, channels = first.shape[3], first.shape[4]
    c2 = second.shape[4]
    rows_n = len(edge_rows) + len(mid_rows)
    half_r = rows_n // 2
    place = {row: i for i, row in enumerate(edge_rows + mid_rows)}
    per_group = LANES // channels
    filler = jnp.zeros((c1, LANES - channels), jnp.float32)
    taps = {}
    for a in range(3):
        for b in range(3):
            for d in range(3):
                tap = jnp.concatenate([first[a, b, d].astype(jnp.float32), filler], axis=1)
                for turn in range(per_group):
                    lane = turn * channels
                    taps[a, b, d, turn] = pltpu.roll(tap, lane, 1) if lane else tap

    def band(a, d, r, group):
        total = jnp.zeros((c1, LANES), jnp.float32)
        for b in range(3):
            at_place = place.get(r - 1 + b, -1)
            if at_place >= 0 and at_place // per_group == group:
                total = total + taps[a, b, d, at_place % per_group]
        return total

    rim = (-1, 0, rows_n - 1, rows_n)
    inner = tuple(range(1, rows_n - 1))
    for kernel, rows, groups in ((kernel_edge, (rim[0],) + rim[2:], 1), (kernel_mid, (0,) + inner, 2)):
        for d in range(3):
            for i, r in enumerate(rows):
                for a in range(3):
                    at = ((a * 3 + d) * len(rows) + i) * c1
                    for group in range(groups):
                        kernel[at : at + c1, group * LANES : (group + 1) * LANES] = band(a, d, r, group)

    def second_row(a, d, r):
        blocks = []
        for g in range(half_r):
            b = -1 if r is None else r - 2 * g + 1
            hit = 0 <= b < 3
            blocks.append(second[a, b, d].astype(jnp.float32) if hit else jnp.zeros((c1, c2), jnp.float32))
        blocks.append(jnp.zeros((c1, LANES - half_r * c2), jnp.float32))
        return jnp.concatenate(blocks, axis=1)

    for two, stacked, rows in ((two_mid, stacked_mid, inner), (two_edge, stacked_edge, rim[:3] + (None,))):
        deep = two.shape[1]
        stacked[...] = jnp.zeros(stacked.shape, jnp.float32)
        for a in range(3):
            for j, d in enumerate((1, 0, 2)):
                for i, r in enumerate(rows):
                    at = j * deep + (a * len(rows) + i) * c1
                    stacked[at : at + c1, :] = second_row(a, d, r)
        outs = half_r * c2
        for j in range(3):
            two[j * outs : (j + 1) * outs, :] = stacked[j * deep : (j + 1) * deep, :].T[:outs].astype(jnp.bfloat16)

    def spread_bias(like, bias):
        index = lax.broadcasted_iota(jnp.int32, like.shape, 0)
        total = jnp.zeros(like.shape, jnp.float32)
        for i in range(bias.shape[0]):
            total = jnp.where(index % bias.shape[0] == i, bias[i], total)
        like[...] = total

    spread_bias(bias_rows, bias_first)
    spread_bias(bias_two, bias_second)


def plane_variance(p, sources, cols, disp, wide, ref_wide, inv):
    chunks = []
    for x0 in range(0, cols, CHUNK):
        ref = ref_wide[0, x0 : x0 + CHUNK, :]
        summed = ref
        squares = ref * ref
        for s in range(sources):
            warped = wide[s, pl.ds(SHIFT + x0 - disp[p * sources + s], CHUNK), :]
            summed = summed + warped
            squares = squares + warped * warped
        chunks.append((squares - summed * summed * inv).astype(jnp.bfloat16))
    return jnp.concatenate(chunks, axis=0)


def view_weights(live):
    total = live.astype(jnp.float32) + jnp.ones((1, LANES), jnp.float32)
    return 1.0 / total, lax.rsqrt(total)


def turned_reference(ref, blocks, picks):
    tile_rows = ref.shape[0] // blocks
    rows = [ref[block * tile_rows + i] for block in picks for i in range(tile_rows)]
    return jnp.concatenate(rows, axis=0).T.astype(jnp.float32)


def clear_bands(wide, cols):
    band = jnp.zeros((SHIFT, LANES), jnp.float32)
    for at in range(wide.shape[0]):
        wide[at, 0:SHIFT, :] = band
        wide[at, SHIFT + cols : 2 * SHIFT + cols, :] = band


def load_tiles(at_slots, live, sources, blocks, picks, scale, scalars, arrived, wide):
    for s in range(sources):
        slab = jnp.concatenate([arrived[scalars[at_slots + s * blocks + block]] for block in picks], axis=0)
        cols = slab.shape[1]
        wide[s, SHIFT : SHIFT + cols, :] = slab.T.astype(jnp.float32) * jnp.where(s < live, scale, 0.0)


def add_plane(q, planes, lhs, weights, sums):
    taps = lax.dot_general(weights, lhs, (((1,), (1,)), ((), ())), preferred_element_type=jnp.float32)
    rows = taps.shape[0] // 3
    slots = sums.shape[0]
    if q + 1 < planes:
        sums[(q + 1) % slots] = taps[:rows]
    if q == 0:
        sums[q % slots] = taps[rows : 2 * rows]
    else:
        sums[q % slots] += taps[rows : 2 * rows]
        sums[(q - 1) % slots] += taps[2 * rows :]


def joined_columns(taps, column):
    rows, cols = column.shape
    left, center, right = taps[:rows], taps[rows : 2 * rows], taps[2 * rows :]
    total = center + jnp.where(column > 0, pltpu.roll(left, 1, 1), 0.0)
    return total + jnp.where(column < cols - 1, pltpu.roll(right, cols - 1, 1), 0.0)


def strided_planes(q, planes, taken, rows, weights, out_w):
    step = taken.shape[1] // 2
    none = jnp.zeros((rows, 2 * step), jnp.bfloat16)
    near = range(2 * q - 1, 2 * q + 2)
    parts = [taken[p * rows : (p + 1) * rows] if 0 <= p < planes else none for p in near]
    rhs = jnp.concatenate(parts, axis=0)
    deep = rhs.shape[0]
    outs = weights.shape[0] // 3
    even = jnp.dot(weights[:outs, :deep], rhs[:, :step], preferred_element_type=jnp.float32)
    odd = jnp.dot(weights[outs:, :deep], rhs[:, step:], preferred_element_type=jnp.float32)
    result = even + pltpu.roll(odd[:outs], 1, 1) + odd[outs:]
    return result[:, :out_w]


def edge_kernel(
    at_slots, at_live, sources, blocks, picks, packed, arrived, ref, var, own, far, near, flags, wide, ref_wide, sums, held, sem
):
    planes, cols, _ = var.shape
    tail = packed.shape[0] - 8
    c1 = tail // 27
    copy = pltpu.make_async_copy(packed.at[pl.ds(tail, 1)], held, sem)
    copy.start()
    weights = packed[:tail].astype(jnp.bfloat16)
    turned = turned_reference(ref, blocks, picks)
    clear_bands(wide, cols)
    copy.wait()
    scalars = [held[0, i].astype(jnp.int32) for i in range(at_live + 3)]
    live = scalars[at_live]
    inv, scale = view_weights(live)
    ref_wide[0] = turned * scale
    load_tiles(at_slots, live, sources, blocks, picks, scale, scalars, arrived, wide)
    odd = scalars[at_live + 2] > 0
    flags[0] = jnp.where(odd, 1.0, 0.0) * jnp.ones((c1, LANES), jnp.float32)
    flags[1] = jnp.where(scalars[at_live + 1] > 0, 1.0, 0.0) * jnp.ones((c1, LANES), jnp.float32)
    column = lax.broadcasted_iota(jnp.int32, (3 * c1, cols), 1)
    empty = jnp.zeros((c1, cols), jnp.float32)

    def finish(p):
        total = joined_columns(sums[p % sums.shape[0]], column)
        own[p] = total[: 2 * c1]
        downward = total[c1:]
        upward = jnp.concatenate([total[:c1], empty], axis=0)
        far[p] = jnp.where(odd, downward, upward).astype(jnp.bfloat16)
        near[p] = jnp.where(odd, upward, downward).astype(jnp.bfloat16)

    values = plane_variance(0, sources, cols, scalars, wide, ref_wide, inv)
    for q in range(planes):
        held_values = values
        if q + 1 < planes:
            values = plane_variance(q + 1, sources, cols, scalars, wide, ref_wide, inv)
        add_plane(q, planes, held_values, weights, sums)
        var[q] = held_values
        if q > 0:
            finish(q - 1)
    finish(planes - 1)


def mid_kernel(
    at_slots,
    at_live,
    sources,
    blocks,
    picks,
    numbers,
    arrived,
    ref,
    edge_var,
    kernel,
    bias_rows,
    kernel_two,
    bias_two,
    out,
    own,
    choices,
    wide,
    ref_wide,
    cost,
    sums,
    scalars,
    sem,
):
    copy = pltpu.make_async_copy(numbers, scalars, sem)
    copy.start()
    planes, cols, _ = edge_var.shape
    inner = cost.shape[0] // planes
    step = choices.shape[1] // 2
    row = lax.broadcasted_iota(jnp.int32, (cols, step), 0)
    target = 2 * lax.broadcasted_iota(jnp.int32, (cols, step), 1)
    for odd in range(2):
        choices[:, odd * step : (odd + 1) * step] = jnp.where(row == target + odd, 1.0, 0.0).astype(jnp.bfloat16)
    turned = turned_reference(ref, blocks, picks)
    clear_bands(wide, cols)
    copy.wait()
    live = scalars[at_live]
    inv, scale = view_weights(live)
    ref_wide[0] = turned * scale
    load_tiles(at_slots, live, sources, blocks, picks, scale, scalars, arrived, wide)
    weights = kernel[...].astype(jnp.bfloat16)
    bias = bias_rows[:inner]
    ready, cols = own.shape[1:]
    column = lax.broadcasted_iota(jnp.int32, (ready + inner, cols), 1)

    def finish(p):
        total = joined_columns(sums[p % sums.shape[0]], column)
        own[p] = total[:ready]
        cost[p * inner : (p + 1) * inner, :] = jnp.maximum(total[ready:] + bias, 0.0).astype(jnp.bfloat16)

    values = plane_variance(0, sources, cols, scalars, wide, ref_wide, inv)
    for q in range(planes):
        held_values = values
        if q + 1 < planes:
            values = plane_variance(q + 1, sources, cols, scalars, wide, ref_wide, inv)
        add_plane(q, planes, jnp.concatenate([edge_var[q], held_values], axis=1), weights, sums)
        if q > 0:
            finish(q - 1)
    finish(planes - 1)
    taken = jnp.dot(cost[...], choices[...], preferred_element_type=jnp.float32).astype(jnp.bfloat16)
    for q in range(planes // 2):
        out[q] = strided_planes(q, planes, taken, inner, kernel_two, out.shape[2]) + bias_two[...]


def end_kernel(far, near, flags, own, own_top, partial, bias_rows, kernel_two, choices, out):
    planes, c1, cols = own_top.shape
    odd = jnp.concatenate([flags[0]] * (cols // LANES), axis=1) > 0.5
    not_top = jnp.concatenate([flags[1]] * (cols // LANES), axis=1)
    empty = jnp.zeros((c1, cols), jnp.float32)
    bias = bias_rows[:c1]
    rows = []
    for p in range(planes):
        lower, upper = far[p].astype(jnp.float32), near[p].astype(jnp.float32)
        before = own[p, :c1] + jnp.where(odd, upper[:c1], lower[:c1])
        top = own_top[p] + jnp.where(odd, upper[c1:], lower[c1:])
        bottom = own[p, c1:] + jnp.where(odd, lower[:c1], upper[:c1])
        rows += [jnp.maximum(before + bias, 0.0) * not_top]
        rows += [jnp.maximum(top + bias, 0.0), jnp.maximum(bottom + bias, 0.0), empty]
    cost = jnp.concatenate(rows, axis=0).astype(jnp.bfloat16)
    taken = jnp.dot(cost, choices[...], preferred_element_type=jnp.float32).astype(jnp.bfloat16)
    for q in range(planes // 2):
        out[q] = partial[q] + strided_planes(q, planes, taken, 4 * c1, kernel_two, out.shape[2])


def on_device(
    ref_features,
    source_tiles,
    pair_lists,
    view_counts,
    disparities,
    conv_first,
    bias_first,
    conv_second,
    bias_second,
):
    n_view = lax.axis_size("view")
    me = lax.axis_index("view").reshape(1)
    rows_n, channels, cols = ref_features.shape
    tiles_dev, tile_rows = source_tiles.shape[0], source_tiles.shape[1]
    sources, blocks = pair_lists.shape[1], pair_lists.shape[2]
    planes = disparities.shape[0]
    slab = tile_rows * channels
    c1, c2 = conv_first.shape[2], conv_second.shape[0]
    half_r, half_p, half_x = rows_n // 2, planes // 2, cols // 2
    smem = pl.BlockSpec(memory_space=pltpu.SMEM)
    vmem = pl.BlockSpec(memory_space=pltpu.VMEM)
    anywhere = pl.BlockSpec(memory_space=pl.ANY)
    params = pltpu.CompilerParams(vmem_limit_bytes=VMEM_LIMIT)
    bf16, f32, i32 = jnp.bfloat16, jnp.float32, jnp.int32
    shape = jax.ShapeDtypeStruct

    table = pl.pallas_call(
        functools.partial(request_kernel, tiles_dev),
        out_shape=shape((n_view, 1, 2 * CAP), i32),
        in_specs=[vmem],
        out_specs=vmem,
        compiler_params=params,
        name="request_table",
    )(pair_lists)
    table = lax.all_to_all(table, "view", split_axis=0, concat_axis=0, tiled=True)
    tiles = source_tiles.reshape(tiles_dev, slab, cols)
    table = table[:, 0, : CAP + 1].reshape(1, n_view * (CAP + 1))
    far_first = sorted(range(1, n_view), key=lambda k: -min(k, n_view - k))
    order = [k for pair in zip(far_first, far_first[::-1]) for k in pair][: len(far_first)]
    half = max(1, len(order) - IN_FLIGHT)
    bundles = [None] * n_view

    def send(wanted, distances):
        gathered = pl.pallas_call(
            functools.partial(gather_kernel, distances, n_view),
            out_shape=[shape((CAP, slab, cols), bf16)] * len(distances),
            in_specs=[smem, vmem],
            out_specs=[vmem] * len(distances),
            compiler_params=params,
            name=f"requested_tiles_{distances[0]}",
        )(wanted, tiles)
        for k, bundle in zip(distances, gathered):
            pairs = [(i, (i + k) % n_view) for i in range(n_view)]
            bundles[k] = lax.ppermute(bundle, "view", pairs) if k else bundle

    send(table, order[:half])

    at_slots = planes * sources
    at_live = at_slots + sources * blocks
    edge_blocks, mid_blocks = (0, blocks - 1), tuple(range(1, blocks - 1))
    rows_of = lambda picks: [block * tile_rows + i for block in picks for i in range(tile_rows)]
    edge_rows, mid_rows = rows_of(edge_blocks), rows_of(mid_blocks)
    inner = (rows_n - 2) * c1
    mid_deep, edge_deep = (-(-3 * rows // LANES) * LANES for rows in (inner, 4 * c1))
    prepared = pl.pallas_call(
        functools.partial(prepare_kernel, tiles_dev, edge_rows, mid_rows),
        out_shape=[
            shape((27 * c1 + 8, LANES), f32),
            shape((9 * (inner + c1), 2 * LANES), f32),
            shape((3 * half_r * c2, mid_deep), bf16),
            shape((3 * half_r * c2, edge_deep), bf16),
            shape((inner, cols), f32),
            shape((half_r * c2, half_x), f32),
            shape((LANES,), i32),
            shape((1, n_view * (CAP + 1)), i32),
        ],
        in_specs=[vmem, vmem] + [smem] * 6 + [vmem, anywhere],
        out_specs=[vmem] * 6 + [smem, vmem],
        scratch_shapes=[pltpu.VMEM((3 * mid_deep, LANES), f32), pltpu.VMEM((3 * edge_deep, LANES), f32)],
        compiler_params=params,
        name="weights_and_scalars",
    )(
        conv_first.transpose(0, 1, 3, 2, 4),
        conv_second.transpose(1, 2, 3, 4, 0),
        bias_first,
        bias_second,
        disparities,
        pair_lists,
        view_counts,
        me,
        table,
        bundles[order[min(IN_FLIGHT, half) - 1]],
    )
    kernel_edge, kernel_mid, two_mid, two_edge, bias_rows, bias_two, scalars, later = prepared
    send(later, order[half:] + [0])
    arrived = pl.pallas_call(
        collect_kernel,
        out_shape=shape((n_view * CAP, slab, cols), bf16),
        in_specs=[vmem] * n_view,
        out_specs=vmem,
        compiler_params=params,
        name="all_tiles",
    )(*bundles)

    band_scratch = [pltpu.VMEM((sources, cols + 2 * SHIFT, LANES), f32), pltpu.VMEM((1, cols, LANES), f32)]
    payload = shape((planes, 2 * c1, cols), bf16)
    col_step = (half_x // LANES + 1) * LANES
    edge_var, own, far, near, flags = pl.pallas_call(
        functools.partial(edge_kernel, at_slots, at_live, sources, blocks, edge_blocks),
        out_shape=[
            shape((planes, cols, LANES), bf16),
            shape((planes, 2 * c1, cols), f32),
            payload,
            payload,
            shape((2, c1, LANES), f32),
        ],
        in_specs=[vmem] * 3,
        out_specs=[vmem] * 5,
        scratch_shapes=band_scratch
        + [
            pltpu.VMEM((3, 9 * c1, cols), f32),
            pltpu.SMEM((1, LANES), f32),
            pltpu.SemaphoreType.DMA,
        ],
        compiler_params=params,
        name="edge_rows",
    )(kernel_edge, arrived, ref_features)
    far = swapped(far, "view", 1)
    near = swapped(near, "view", 0)

    partial, own_top, choices = pl.pallas_call(
        functools.partial(mid_kernel, at_slots, at_live, sources, blocks, mid_blocks),
        out_shape=[
            shape((half_p, half_r * c2, half_x), f32),
            shape((planes, c1, cols), f32),
            shape((cols, 2 * col_step), bf16),
        ],
        in_specs=[anywhere] + [vmem] * 7,
        out_specs=[vmem] * 3,
        scratch_shapes=band_scratch
        + [
            pltpu.VMEM((planes * inner, cols), bf16),
            pltpu.VMEM((3, 3 * (inner + c1), cols), f32),
            pltpu.SMEM(scalars.shape, i32),
            pltpu.SemaphoreType.DMA,
        ],
        compiler_params=params,
        name="middle_rows",
    )(scalars, arrived, ref_features, edge_var, kernel_mid, bias_rows, two_mid, bias_two)

    out = pl.pallas_call(
        end_kernel,
        out_shape=shape((half_p, half_r * c2, half_x), f32),
        in_specs=[vmem] * 9,
        out_specs=vmem,
        compiler_params=params,
        name="end_rows",
    )(far, near, flags, own, own_top, partial, bias_rows, two_edge, choices)
    return out.reshape(half_p, half_r, c2, half_x)


def solution(mesh):
    return jax.shard_map(
        on_device,
        mesh=mesh,
        in_specs=(
            P(("groups", "view"), None, None),
            P(("groups", "view"), None, None, None),
            P(("groups", "view"), None, None),
            P(("groups", "view")),
            P("groups", None),
            P(),
            P(),
            P(),
            P(),
        ),
        out_specs=P("groups", "view", None, None),
        check_vma=False,
    )
```

```python
import functools

import numpy as np

import jax
import jax.numpy as jnp
from jax import lax
from jax.experimental import pallas as pl
from jax.experimental.pallas import tpu as pltpu
from jax.sharding import PartitionSpec as P

SHIFT = 48
CAP = 2
LANES = 128
CHUNK = 64
VMEM_LIMIT = 10 * 1024 * 1024


def swapped(x, axis, parity):
    count = lax.axis_size(axis)
    pairs = [(i, i + 1) for i in range(parity, count - 1, 2)]
    return lax.ppermute(x, axis, pairs + [(j, i) for i, j in pairs])


def request_places(pair_lists, tiles_dev):
    owners, ranks, tiles = [], [], []
    for s in range(pair_lists.shape[1]):
        for b in range(pair_lists.shape[2]):
            tile = pair_lists[0, s, b]
            whole = jnp.maximum(tile, 0)
            owner = jnp.where(tile >= 0, lax.div(whole, tiles_dev), -1)
            rank = jnp.int32(0)
            for other in owners:
                rank = rank + jnp.where(other == owner, 1, 0)
            owners.append(owner)
            ranks.append(rank)
            tiles.append(lax.rem(whole, tiles_dev))
    return owners, ranks, tiles


def request_kernel(tiles_dev, pair_lists, table):
    n_view = table.shape[0]
    row = lax.broadcasted_iota(jnp.int32, (n_view, LANES), 0) * tiles_dev
    lane = lax.broadcasted_iota(jnp.int32, (n_view, LANES), 1)
    total = jnp.zeros((n_view, LANES), jnp.int32)
    count = jnp.zeros((n_view, LANES), jnp.int32)
    for s in range(pair_lists.shape[1]):
        for b in range(pair_lists.shape[2]):
            tile = pair_lists[0, s : s + 1, b : b + 1] - row
            owned = (tile >= 0) & (tile < tiles_dev)
            total = jnp.where(owned & (lane == count), tile, total)
            count = count + jnp.where(owned, 1, 0)
    total = jnp.where(lane == CAP, lax.broadcasted_iota(jnp.int32, (n_view, LANES), 0), total)
    for d in range(n_view):
        table[d] = total[d : d + 1, : table.shape[2]]


def gather_kernel(distances, n_view, table, tiles, *bundles):
    me = table[0, CAP]
    for k, bundle in zip(distances, bundles):
        at = lax.rem(me + k, n_view) * (CAP + 1)
        for j in range(CAP):
            bundle[j] = tiles[table[0, at + j]]


def collect_kernel(distances, *refs):
    arrived = refs[-1]
    for k, bundle in zip(distances, refs[:-1]):
        for j in range(CAP):
            arrived[k * CAP + j] = bundle[j]


def prepare_kernel(
    n_view,
    tiles_dev,
    edge_rows,
    mid_rows,
    first,
    second,
    bias_first,
    bias_second,
    disparities,
    pair_lists,
    view_counts,
    me,
    kernel_edge,
    kernel_mid,
    two_mid,
    two_edge,
    bias_rows,
    bias_two,
    scalars,
    stacked_mid,
    stacked_edge,
):
    planes, sources = disparities.shape
    owners, ranks, _ = request_places(pair_lists, tiles_dev)
    at = 0
    for p in range(planes):
        for s in range(sources):
            scalars[at] = disparities[p, s]
            at += 1
    for owner, rank in zip(owners, ranks):
        back = lax.rem(me[0] - owner + n_view, n_view)
        scalars[at] = jnp.where(owner >= 0, back * CAP + rank, 0)
        at += 1
    scalars[at] = view_counts[0]
    scalars[at + 1] = me[0]
    scalars[at + 2] = lax.rem(me[0], 2)
    tail = kernel_edge.shape[0] - 8
    lane_at = lax.broadcasted_iota(jnp.int32, (8, LANES), 1)
    numbers = jnp.zeros((8, LANES), jnp.float32)
    for i in range(at + 3):
        numbers = jnp.where(lane_at == i, scalars[i].astype(jnp.float32), numbers)
    kernel_edge[tail:, :] = numbers

    c1, channels = first.shape[3], first.shape[4]
    c2 = second.shape[4]
    rows_n = len(edge_rows) + len(mid_rows)
    half_r = rows_n // 2
    place = {row: i for i, row in enumerate(edge_rows + mid_rows)}
    per_group = LANES // channels
    filler = jnp.zeros((c1, LANES - channels), jnp.float32)
    taps = {}
    for a in range(3):
        for b in range(3):
            for d in range(3):
                tap = jnp.concatenate([first[a, b, d].astype(jnp.float32), filler], axis=1)
                for turn in range(per_group):
                    lane = turn * channels
                    taps[a, b, d, turn] = pltpu.roll(tap, lane, 1) if lane else tap

    def band(a, d, r, group):
        total = jnp.zeros((c1, LANES), jnp.float32)
        for b in range(3):
            at_place = place.get(r - 1 + b, -1)
            if at_place >= 0 and at_place // per_group == group:
                total = total + taps[a, b, d, at_place % per_group]
        return total

    rim = (-1, 0, rows_n - 1, rows_n)
    inner = tuple(range(1, rows_n - 1))
    for kernel, rows, groups in ((kernel_edge, (rim[0],) + rim[2:], 1), (kernel_mid, (0,) + inner, 2)):
        for d in range(3):
            for i, r in enumerate(rows):
                for a in range(3):
                    at = ((a * 3 + d) * len(rows) + i) * c1
                    for group in range(groups):
                        kernel[at : at + c1, group * LANES : (group + 1) * LANES] = band(a, d, r, group)

    def second_row(a, d, r):
        blocks = []
        for g in range(half_r):
            b = -1 if r is None else r - 2 * g + 1
            hit = 0 <= b < 3
            blocks.append(second[a, b, d].astype(jnp.float32) if hit else jnp.zeros((c1, c2), jnp.float32))
        blocks.append(jnp.zeros((c1, LANES - half_r * c2), jnp.float32))
        return jnp.concatenate(blocks, axis=1)

    for two, stacked, rows in ((two_mid, stacked_mid, inner), (two_edge, stacked_edge, rim[:3] + (None,))):
        deep = two.shape[1]
        stacked[...] = jnp.zeros(stacked.shape, jnp.float32)
        for a in range(3):
            for j, d in enumerate((1, 0, 2)):
                for i, r in enumerate(rows):
                    at = j * deep + (a * len(rows) + i) * c1
                    stacked[at : at + c1, :] = second_row(a, d, r)
        outs = half_r * c2
        for j in range(3):
            two[j * outs : (j + 1) * outs, :] = stacked[j * deep : (j + 1) * deep, :].T[:outs].astype(jnp.bfloat16)

    def spread_bias(like, bias):
        index = lax.broadcasted_iota(jnp.int32, like.shape, 0)
        total = jnp.zeros(like.shape, jnp.float32)
        for i in range(bias.shape[0]):
            total = jnp.where(index % bias.shape[0] == i, bias[i], total)
        like[...] = total

    spread_bias(bias_rows, bias_first)
    spread_bias(bias_two, bias_second)


def plane_variance(p, sources, cols, disp, wide, ref_wide, inv):
    chunks = []
    for x0 in range(0, cols, CHUNK):
        ref = ref_wide[0, x0 : x0 + CHUNK, :]
        summed = ref
        squares = ref * ref
        for s in range(sources):
            warped = wide[s, pl.ds(SHIFT + x0 - disp[p * sources + s], CHUNK), :]
            summed = summed + warped
            squares = squares + warped * warped
        chunks.append((squares - summed * summed * inv).astype(jnp.bfloat16))
    return jnp.concatenate(chunks, axis=0)


def view_weights(live):
    total = live.astype(jnp.float32) + jnp.ones((1, LANES), jnp.float32)
    return 1.0 / total, lax.rsqrt(total)


def turned_reference(ref, blocks, picks):
    tile_rows = ref.shape[0] // blocks
    rows = [ref[block * tile_rows + i] for block in picks for i in range(tile_rows)]
    return jnp.concatenate(rows, axis=0).T.astype(jnp.float32)


def clear_bands(wide, cols):
    band = jnp.zeros((SHIFT, LANES), jnp.float32)
    for at in range(wide.shape[0]):
        wide[at, 0:SHIFT, :] = band
        wide[at, SHIFT + cols : 2 * SHIFT + cols, :] = band


def load_tiles(at_slots, live, sources, blocks, picks, scale, scalars, arrived, wide):
    for s in range(sources):
        slab = jnp.concatenate([arrived[scalars[at_slots + s * blocks + block]] for block in picks], axis=0)
        cols = slab.shape[1]
        wide[s, SHIFT : SHIFT + cols, :] = slab.T.astype(jnp.float32) * jnp.where(s < live, scale, 0.0)


def add_plane(q, planes, lhs, weights, sums):
    taps = lax.dot_general(weights, lhs, (((1,), (1,)), ((), ())), preferred_element_type=jnp.float32)
    rows = taps.shape[0] // 3
    slots = sums.shape[0]
    if q + 1 < planes:
        sums[(q + 1) % slots] = taps[:rows]
    if q == 0:
        sums[q % slots] = taps[rows : 2 * rows]
    else:
        sums[q % slots] += taps[rows : 2 * rows]
        sums[(q - 1) % slots] += taps[2 * rows :]


def joined_columns(taps, column):
    rows, cols = column.shape
    left, center, right = taps[:rows], taps[rows : 2 * rows], taps[2 * rows :]
    total = center + jnp.where(column > 0, pltpu.roll(left, 1, 1), 0.0)
    return total + jnp.where(column < cols - 1, pltpu.roll(right, cols - 1, 1), 0.0)


def strided_planes(q, planes, taken, rows, weights, out_w):
    step = taken.shape[1] // 2
    none = jnp.zeros((rows, 2 * step), jnp.bfloat16)
    near = range(2 * q - 1, 2 * q + 2)
    parts = [taken[p * rows : (p + 1) * rows] if 0 <= p < planes else none for p in near]
    rhs = jnp.concatenate(parts, axis=0)
    deep = rhs.shape[0]
    outs = weights.shape[0] // 3
    even = jnp.dot(weights[:outs, :deep], rhs[:, :step], preferred_element_type=jnp.float32)
    odd = jnp.dot(weights[outs:, :deep], rhs[:, step:], preferred_element_type=jnp.float32)
    result = even + pltpu.roll(odd[:outs], 1, 1) + odd[outs:]
    return result[:, :out_w]


def edge_kernel(
    at_slots, at_live, sources, blocks, picks, packed, arrived, ref, var, own, far, near, flags, wide, ref_wide, sums, held, sem
):
    planes, cols, _ = var.shape
    tail = packed.shape[0] - 8
    c1 = tail // 27
    copy = pltpu.make_async_copy(packed.at[pl.ds(tail, 1)], held, sem)
    copy.start()
    weights = packed[:tail].astype(jnp.bfloat16)
    turned = turned_reference(ref, blocks, picks)
    clear_bands(wide, cols)
    copy.wait()
    scalars = [held[0, i].astype(jnp.int32) for i in range(at_live + 3)]
    live = scalars[at_live]
    inv, scale = view_weights(live)
    ref_wide[0] = turned * scale
    load_tiles(at_slots, live, sources, blocks, picks, scale, scalars, arrived, wide)
    odd = scalars[at_live + 2] > 0
    flags[0] = jnp.where(odd, 1.0, 0.0) * jnp.ones((c1, LANES), jnp.float32)
    flags[1] = jnp.where(scalars[at_live + 1] > 0, 1.0, 0.0) * jnp.ones((c1, LANES), jnp.float32)
    column = lax.broadcasted_iota(jnp.int32, (3 * c1, cols), 1)
    empty = jnp.zeros((c1, cols), jnp.float32)

    def finish(p):
        total = joined_columns(sums[p % sums.shape[0]], column)
        own[p] = total[: 2 * c1]
        downward = total[c1:]
        upward = jnp.concatenate([total[:c1], empty], axis=0)
        far[p] = jnp.where(odd, downward, upward).astype(jnp.bfloat16)
        near[p] = jnp.where(odd, upward, downward).astype(jnp.bfloat16)

    values = plane_variance(0, sources, cols, scalars, wide, ref_wide, inv)
    for q in range(planes):
        held_values = values
        if q + 1 < planes:
            values = plane_variance(q + 1, sources, cols, scalars, wide, ref_wide, inv)
        add_plane(q, planes, held_values, weights, sums)
        var[q] = held_values
        if q > 0:
            finish(q - 1)
    finish(planes - 1)


def mid_kernel(
    at_slots,
    at_live,
    sources,
    blocks,
    picks,
    numbers,
    arrived,
    ref,
    edge_var,
    kernel,
    bias_rows,
    kernel_two,
    bias_two,
    out,
    own,
    choices,
    wide,
    ref_wide,
    cost,
    sums,
    scalars,
    sem,
):
    copy = pltpu.make_async_copy(numbers, scalars, sem)
    copy.start()
    planes, cols, _ = edge_var.shape
    inner = cost.shape[0] // planes
    step = choices.shape[1] // 2
    row = lax.broadcasted_iota(jnp.int32, (cols, step), 0)
    target = 2 * lax.broadcasted_iota(jnp.int32, (cols, step), 1)
    for odd in range(2):
        choices[:, odd * step : (odd + 1) * step] = jnp.where(row == target + odd, 1.0, 0.0).astype(jnp.bfloat16)
    turned = turned_reference(ref, blocks, picks)
    clear_bands(wide, cols)
    copy.wait()
    live = scalars[at_live]
    inv, scale = view_weights(live)
    ref_wide[0] = turned * scale
    load_tiles(at_slots, live, sources, blocks, picks, scale, scalars, arrived, wide)
    weights = kernel[...].astype(jnp.bfloat16)
    bias = bias_rows[:inner]
    ready, cols = own.shape[1:]
    column = lax.broadcasted_iota(jnp.int32, (ready + inner, cols), 1)

    def finish(p):
        total = joined_columns(sums[p % sums.shape[0]], column)
        own[p] = total[:ready]
        cost[p * inner : (p + 1) * inner, :] = jnp.maximum(total[ready:] + bias, 0.0).astype(jnp.bfloat16)

    values = plane_variance(0, sources, cols, scalars, wide, ref_wide, inv)
    for q in range(planes):
        held_values = values
        if q + 1 < planes:
            values = plane_variance(q + 1, sources, cols, scalars, wide, ref_wide, inv)
        add_plane(q, planes, jnp.concatenate([edge_var[q], held_values], axis=1), weights, sums)
        if q > 0:
            finish(q - 1)
    finish(planes - 1)
    taken = jnp.dot(cost[...], choices[...], preferred_element_type=jnp.float32).astype(jnp.bfloat16)
    for q in range(planes // 2):
        out[q] = strided_planes(q, planes, taken, inner, kernel_two, out.shape[2]) + bias_two[...]


def end_kernel(far, near, flags, own, own_top, partial, bias_rows, kernel_two, choices, out):
    planes, c1, cols = own_top.shape
    odd = jnp.concatenate([flags[0]] * (cols // LANES), axis=1) > 0.5
    not_top = jnp.concatenate([flags[1]] * (cols // LANES), axis=1)
    empty = jnp.zeros((c1, cols), jnp.float32)
    bias = bias_rows[:c1]
    rows = []
    for p in range(planes):
        lower, upper = far[p].astype(jnp.float32), near[p].astype(jnp.float32)
        before = own[p, :c1] + jnp.where(odd, upper[:c1], lower[:c1])
        top = own_top[p] + jnp.where(odd, upper[c1:], lower[c1:])
        bottom = own[p, c1:] + jnp.where(odd, lower[:c1], upper[:c1])
        rows += [jnp.maximum(before + bias, 0.0) * not_top]
        rows += [jnp.maximum(top + bias, 0.0), jnp.maximum(bottom + bias, 0.0), empty]
    cost = jnp.concatenate(rows, axis=0).astype(jnp.bfloat16)
    taken = jnp.dot(cost, choices[...], preferred_element_type=jnp.float32).astype(jnp.bfloat16)
    for q in range(planes // 2):
        out[q] = partial[q] + strided_planes(q, planes, taken, 4 * c1, kernel_two, out.shape[2])


def on_device(
    ref_features,
    source_tiles,
    pair_lists,
    view_counts,
    disparities,
    conv_first,
    bias_first,
    conv_second,
    bias_second,
):
    n_view = lax.axis_size("view")
    me = lax.axis_index("view").reshape(1)
    rows_n, channels, cols = ref_features.shape
    tiles_dev, tile_rows = source_tiles.shape[0], source_tiles.shape[1]
    sources, blocks = pair_lists.shape[1], pair_lists.shape[2]
    planes = disparities.shape[0]
    slab = tile_rows * channels
    c1, c2 = conv_first.shape[2], conv_second.shape[0]
    half_r, half_p, half_x = rows_n // 2, planes // 2, cols // 2
    smem = pl.BlockSpec(memory_space=pltpu.SMEM)
    vmem = pl.BlockSpec(memory_space=pltpu.VMEM)
    anywhere = pl.BlockSpec(memory_space=pl.ANY)
    params = pltpu.CompilerParams(vmem_limit_bytes=VMEM_LIMIT)
    bf16, f32, i32 = jnp.bfloat16, jnp.float32, jnp.int32
    shape = jax.ShapeDtypeStruct

    table = pl.pallas_call(
        functools.partial(request_kernel, tiles_dev),
        out_shape=shape((n_view, 1, 2 * CAP), i32),
        in_specs=[vmem],
        out_specs=vmem,
        compiler_params=params,
        name="request_table",
    )(pair_lists)
    table = lax.all_to_all(table, "view", split_axis=0, concat_axis=0, tiled=True)
    tiles = source_tiles.reshape(tiles_dev, slab, cols)
    table = table[:, 0, : CAP + 1].reshape(1, n_view * (CAP + 1))
    far_first = sorted(range(1, n_view), key=lambda k: -min(k, n_view - k))
    order = [k for pair in zip(far_first, far_first[::-1]) for k in pair][: len(far_first)]
    distances = order + [0]
    bundles = [None] * n_view
    gathered = pl.pallas_call(
        functools.partial(gather_kernel, distances, n_view),
        out_shape=[shape((CAP, slab, cols), bf16)] * n_view,
        in_specs=[smem, vmem],
        out_specs=[vmem] * n_view,
        compiler_params=params,
        name="requested_tiles",
    )(table, tiles)
    for k, bundle in zip(distances, gathered):
        pairs = [(i, (i + k) % n_view) for i in range(n_view)]
        bundles[k] = lax.ppermute(bundle, "view", pairs) if k else bundle

    at_slots = planes * sources
    at_live = at_slots + sources * blocks
    edge_blocks, mid_blocks = (0, blocks - 1), tuple(range(1, blocks - 1))
    rows_of = lambda picks: [block * tile_rows + i for block in picks for i in range(tile_rows)]
    edge_rows, mid_rows = rows_of(edge_blocks), rows_of(mid_blocks)
    inner = (rows_n - 2) * c1
    mid_deep, edge_deep = (-(-3 * rows // LANES) * LANES for rows in (inner, 4 * c1))
    prepared = pl.pallas_call(
        functools.partial(prepare_kernel, n_view, tiles_dev, edge_rows, mid_rows),
        out_shape=[
            shape((27 * c1 + 8, LANES), f32),
            shape((9 * (inner + c1), 2 * LANES), f32),
            shape((3 * half_r * c2, mid_deep), bf16),
            shape((3 * half_r * c2, edge_deep), bf16),
            shape((inner, cols), f32),
            shape((half_r * c2, half_x), f32),
            shape((LANES,), i32),
        ],
        in_specs=[vmem, vmem] + [smem] * 6,
        out_specs=[vmem] * 6 + [smem],
        scratch_shapes=[pltpu.VMEM((3 * mid_deep, LANES), f32), pltpu.VMEM((3 * edge_deep, LANES), f32)],
        compiler_params=params,
        name="weights_and_scalars",
    )(
        conv_first.transpose(0, 1, 3, 2, 4),
        conv_second.transpose(1, 2, 3, 4, 0),
        bias_first,
        bias_second,
        disparities,
        pair_lists,
        view_counts,
        me,
    )
    kernel_edge, kernel_mid, two_mid, two_edge, bias_rows, bias_two, scalars = prepared
    arrived = pl.pallas_call(
        functools.partial(collect_kernel, distances),
        out_shape=shape((n_view * CAP, slab, cols), bf16),
        in_specs=[vmem] * n_view,
        out_specs=vmem,
        compiler_params=params,
        name="all_tiles",
    )(*[bundles[k] for k in distances])

    band_scratch = [pltpu.VMEM((sources, cols + 2 * SHIFT, LANES), f32), pltpu.VMEM((1, cols, LANES), f32)]
    payload = shape((planes, 2 * c1, cols), bf16)
    col_step = (half_x // LANES + 1) * LANES
    edge_var, own, far, near, flags = pl.pallas_call(
        functools.partial(edge_kernel, at_slots, at_live, sources, blocks, edge_blocks),
        out_shape=[
            shape((planes, cols, LANES), bf16),
            shape((planes, 2 * c1, cols), f32),
            payload,
            payload,
            shape((2, c1, LANES), f32),
        ],
        in_specs=[vmem] * 3,
        out_specs=[vmem] * 5,
        scratch_shapes=band_scratch
        + [
            pltpu.VMEM((3, 9 * c1, cols), f32),
            pltpu.SMEM((1, LANES), f32),
            pltpu.SemaphoreType.DMA,
        ],
        compiler_params=params,
        name="edge_rows",
    )(kernel_edge, arrived, ref_features)
    far = swapped(far, "view", 1)
    near = swapped(near, "view", 0)

    partial, own_top, choices = pl.pallas_call(
        functools.partial(mid_kernel, at_slots, at_live, sources, blocks, mid_blocks),
        out_shape=[
            shape((half_p, half_r * c2, half_x), f32),
            shape((planes, c1, cols), f32),
            shape((cols, 2 * col_step), bf16),
        ],
        in_specs=[anywhere] + [vmem] * 7,
        out_specs=[vmem] * 3,
        scratch_shapes=band_scratch
        + [
            pltpu.VMEM((planes * inner, cols), bf16),
            pltpu.VMEM((3, 3 * (inner + c1), cols), f32),
            pltpu.SMEM(scalars.shape, i32),
            pltpu.SemaphoreType.DMA,
        ],
        compiler_params=params,
        name="middle_rows",
    )(scalars, arrived, ref_features, edge_var, kernel_mid, bias_rows, two_mid, bias_two)

    out = pl.pallas_call(
        end_kernel,
        out_shape=shape((half_p, half_r * c2, half_x), f32),
        in_specs=[vmem] * 9,
        out_specs=vmem,
        compiler_params=params,
        name="end_rows",
    )(far, near, flags, own, own_top, partial, bias_rows, two_edge, choices)
    return out.reshape(half_p, half_r, c2, half_x)


def solution(mesh):
    return jax.shard_map(
        on_device,
        mesh=mesh,
        in_specs=(
            P(("groups", "view"), None, None),
            P(("groups", "view"), None, None, None),
            P(("groups", "view"), None, None),
            P(("groups", "view")),
            P("groups", None),
            P(),
            P(),
            P(),
            P(),
        ),
        out_specs=P("groups", "view", None, None),
        check_vma=False,
    )
```

```python
import functools

import numpy as np

import jax
import jax.numpy as jnp
from jax import lax
from jax.experimental import pallas as pl
from jax.experimental.pallas import tpu as pltpu
from jax.sharding import PartitionSpec as P

SHIFT = 48
CAP = 2
LANES = 128
CHUNK = 64
VMEM_LIMIT = 10 * 1024 * 1024


def swapped(x, axis, parity):
    count = lax.axis_size(axis)
    pairs = [(i, i + 1) for i in range(parity, count - 1, 2)]
    return lax.ppermute(x, axis, pairs + [(j, i) for i, j in pairs])


def request_places(pair_lists, tiles_dev):
    owners, ranks, tiles = [], [], []
    for s in range(pair_lists.shape[1]):
        for b in range(pair_lists.shape[2]):
            tile = pair_lists[0, s, b]
            whole = jnp.maximum(tile, 0)
            owner = jnp.where(tile >= 0, lax.div(whole, tiles_dev), -1)
            rank = jnp.int32(0)
            for other in owners:
                rank = rank + jnp.where(other == owner, 1, 0)
            owners.append(owner)
            ranks.append(rank)
            tiles.append(lax.rem(whole, tiles_dev))
    return owners, ranks, tiles


def request_kernel(tiles_dev, pair_lists, table):
    n_view = table.shape[0]
    row = lax.broadcasted_iota(jnp.int32, (n_view, LANES), 0) * tiles_dev
    lane = lax.broadcasted_iota(jnp.int32, (n_view, LANES), 1)
    total = jnp.zeros((n_view, LANES), jnp.int32)
    count = jnp.zeros((n_view, LANES), jnp.int32)
    for s in range(pair_lists.shape[1]):
        for b in range(pair_lists.shape[2]):
            tile = pair_lists[0, s : s + 1, b : b + 1] - row
            owned = (tile >= 0) & (tile < tiles_dev)
            total = jnp.where(owned & (lane == count), tile, total)
            count = count + jnp.where(owned, 1, 0)
    total = jnp.where(lane == CAP, lax.broadcasted_iota(jnp.int32, (n_view, LANES), 0), total)
    for d in range(n_view):
        table[d] = total[d : d + 1, : table.shape[2]]


def gather_kernel(distances, n_view, table, tiles, _, *bundles):
    me = table[0, CAP]
    for k, bundle in zip(distances, bundles):
        at = lax.rem(me + k, n_view) * (CAP + 1)
        for j in range(CAP):
            bundle[j] = tiles[table[0, at + j]]


def collect_kernel(distances, *refs):
    arrived = refs[-1]
    for k, bundle in zip(distances, refs[:-1]):
        for j in range(CAP):
            arrived[k * CAP + j] = bundle[j]


def prepare_kernel(
    n_view,
    tiles_dev,
    edge_rows,
    mid_rows,
    first,
    second,
    bias_first,
    bias_second,
    disparities,
    pair_lists,
    view_counts,
    me,
    kernel_edge,
    kernel_mid,
    two_mid,
    two_edge,
    bias_rows,
    bias_two,
    scalars,
    stacked_mid,
    stacked_edge,
):
    planes, sources = disparities.shape
    owners, ranks, _ = request_places(pair_lists, tiles_dev)
    at = 0
    for p in range(planes):
        for s in range(sources):
            scalars[at] = disparities[p, s]
            at += 1
    for owner, rank in zip(owners, ranks):
        back = lax.rem(me[0] - owner + n_view, n_view)
        scalars[at] = jnp.where(owner >= 0, back * CAP + rank, 0)
        at += 1
    scalars[at] = view_counts[0]
    scalars[at + 1] = me[0]
    scalars[at + 2] = lax.rem(me[0], 2)
    tail = kernel_edge.shape[0] - 8
    lane_at = lax.broadcasted_iota(jnp.int32, (8, LANES), 1)
    numbers = jnp.zeros((8, LANES), jnp.float32)
    for i in range(at + 3):
        numbers = jnp.where(lane_at == i, scalars[i].astype(jnp.float32), numbers)
    kernel_edge[tail:, :] = numbers

    c1, channels = first.shape[3], first.shape[4]
    c2 = second.shape[4]
    rows_n = len(edge_rows) + len(mid_rows)
    half_r = rows_n // 2
    place = {row: i for i, row in enumerate(edge_rows + mid_rows)}
    per_group = LANES // channels
    filler = jnp.zeros((c1, LANES - channels), jnp.float32)
    taps = {}
    for a in range(3):
        for b in range(3):
            for d in range(3):
                tap = jnp.concatenate([first[a, b, d].astype(jnp.float32), filler], axis=1)
                for turn in range(per_group):
                    lane = turn * channels
                    taps[a, b, d, turn] = pltpu.roll(tap, lane, 1) if lane else tap

    def band(a, d, r, group):
        total = jnp.zeros((c1, LANES), jnp.float32)
        for b in range(3):
            at_place = place.get(r - 1 + b, -1)
            if at_place >= 0 and at_place // per_group == group:
                total = total + taps[a, b, d, at_place % per_group]
        return total

    rim = (-1, 0, rows_n - 1, rows_n)
    inner = tuple(range(1, rows_n - 1))
    for kernel, rows, groups in ((kernel_edge, (rim[0],) + rim[2:], 1), (kernel_mid, (0,) + inner, 2)):
        for d in range(3):
            for i, r in enumerate(rows):
                for a in range(3):
                    at = ((a * 3 + d) * len(rows) + i) * c1
                    for group in range(groups):
                        kernel[at : at + c1, group * LANES : (group + 1) * LANES] = band(a, d, r, group)

    def second_row(a, d, r):
        blocks = []
        for g in range(half_r):
            b = -1 if r is None else r - 2 * g + 1
            hit = 0 <= b < 3
            blocks.append(second[a, b, d].astype(jnp.float32) if hit else jnp.zeros((c1, c2), jnp.float32))
        blocks.append(jnp.zeros((c1, LANES - half_r * c2), jnp.float32))
        return jnp.concatenate(blocks, axis=1)

    for two, stacked, rows in ((two_mid, stacked_mid, inner), (two_edge, stacked_edge, rim[:3] + (None,))):
        deep = two.shape[1]
        stacked[...] = jnp.zeros(stacked.shape, jnp.float32)
        for a in range(3):
            for j, d in enumerate((1, 0, 2)):
                for i, r in enumerate(rows):
                    at = j * deep + (a * len(rows) + i) * c1
                    stacked[at : at + c1, :] = second_row(a, d, r)
        outs = half_r * c2
        for j in range(3):
            two[j * outs : (j + 1) * outs, :] = stacked[j * deep : (j + 1) * deep, :].T[:outs].astype(jnp.bfloat16)

    def spread_bias(like, bias):
        index = lax.broadcasted_iota(jnp.int32, like.shape, 0)
        total = jnp.zeros(like.shape, jnp.float32)
        for i in range(bias.shape[0]):
            total = jnp.where(index % bias.shape[0] == i, bias[i], total)
        like[...] = total

    spread_bias(bias_rows, bias_first)
    spread_bias(bias_two, bias_second)


def plane_variance(p, sources, cols, disp, wide, ref_wide, inv):
    chunks = []
    for x0 in range(0, cols, CHUNK):
        ref = ref_wide[0, x0 : x0 + CHUNK, :]
        summed = ref
        squares = ref * ref
        for s in range(sources):
            warped = wide[s, pl.ds(SHIFT + x0 - disp[p * sources + s], CHUNK), :]
            summed = summed + warped
            squares = squares + warped * warped
        chunks.append((squares - summed * summed * inv).astype(jnp.bfloat16))
    return jnp.concatenate(chunks, axis=0)


def view_weights(live):
    total = live.astype(jnp.float32) + jnp.ones((1, LANES), jnp.float32)
    return 1.0 / total, lax.rsqrt(total)


def turned_reference(ref, blocks, picks):
    tile_rows = ref.shape[0] // blocks
    rows = [ref[block * tile_rows + i] for block in picks for i in range(tile_rows)]
    return jnp.concatenate(rows, axis=0).T.astype(jnp.float32)


def clear_bands(wide, cols):
    band = jnp.zeros((SHIFT, LANES), jnp.float32)
    for at in range(wide.shape[0]):
        wide[at, 0:SHIFT, :] = band
        wide[at, SHIFT + cols : 2 * SHIFT + cols, :] = band


def load_tiles(at_slots, live, sources, blocks, picks, scale, scalars, arrived, wide):
    for s in range(sources):
        slab = jnp.concatenate([arrived[scalars[at_slots + s * blocks + block]] for block in picks], axis=0)
        cols = slab.shape[1]
        wide[s, SHIFT : SHIFT + cols, :] = slab.T.astype(jnp.float32) * jnp.where(s < live, scale, 0.0)


def add_plane(q, planes, lhs, weights, sums):
    taps = lax.dot_general(weights, lhs, (((1,), (1,)), ((), ())), preferred_element_type=jnp.float32)
    rows = taps.shape[0] // 3
    slots = sums.shape[0]
    if q + 1 < planes:
        sums[(q + 1) % slots] = taps[:rows]
    if q == 0:
        sums[q % slots] = taps[rows : 2 * rows]
    else:
        sums[q % slots] += taps[rows : 2 * rows]
        sums[(q - 1) % slots] += taps[2 * rows :]


def joined_columns(taps, column):
    rows, cols = column.shape
    left, center, right = taps[:rows], taps[rows : 2 * rows], taps[2 * rows :]
    total = center + jnp.where(column > 0, pltpu.roll(left, 1, 1), 0.0)
    return total + jnp.where(column < cols - 1, pltpu.roll(right, cols - 1, 1), 0.0)


def strided_planes(q, planes, taken, rows, weights, out_w):
    step = taken.shape[1] // 2
    none = jnp.zeros((rows, 2 * step), jnp.bfloat16)
    near = range(2 * q - 1, 2 * q + 2)
    parts = [taken[p * rows : (p + 1) * rows] if 0 <= p < planes else none for p in near]
    rhs = jnp.concatenate(parts, axis=0)
    deep = rhs.shape[0]
    outs = weights.shape[0] // 3
    even = jnp.dot(weights[:outs, :deep], rhs[:, :step], preferred_element_type=jnp.float32)
    odd = jnp.dot(weights[outs:, :deep], rhs[:, step:], preferred_element_type=jnp.float32)
    result = even + pltpu.roll(odd[:outs], 1, 1) + odd[outs:]
    return result[:, :out_w]


def edge_kernel(
    at_slots, at_live, sources, blocks, picks, packed, arrived, ref, var, own, far, near, flags, wide, ref_wide, sums, held, sem
):
    planes, cols, _ = var.shape
    tail = packed.shape[0] - 8
    c1 = tail // 27
    copy = pltpu.make_async_copy(packed.at[pl.ds(tail, 1)], held, sem)
    copy.start()
    weights = packed[:tail].astype(jnp.bfloat16)
    turned = turned_reference(ref, blocks, picks)
    clear_bands(wide, cols)
    copy.wait()
    scalars = [held[0, i].astype(jnp.int32) for i in range(at_live + 3)]
    live = scalars[at_live]
    inv, scale = view_weights(live)
    ref_wide[0] = turned * scale
    load_tiles(at_slots, live, sources, blocks, picks, scale, scalars, arrived, wide)
    odd = scalars[at_live + 2] > 0
    flags[0] = jnp.where(odd, 1.0, 0.0) * jnp.ones((c1, LANES), jnp.float32)
    flags[1] = jnp.where(scalars[at_live + 1] > 0, 1.0, 0.0) * jnp.ones((c1, LANES), jnp.float32)
    column = lax.broadcasted_iota(jnp.int32, (3 * c1, cols), 1)
    empty = jnp.zeros((c1, cols), jnp.float32)

    def finish(p):
        total = joined_columns(sums[p % sums.shape[0]], column)
        own[p] = total[: 2 * c1]
        downward = total[c1:]
        upward = jnp.concatenate([total[:c1], empty], axis=0)
        far[p] = jnp.where(odd, downward, upward).astype(jnp.bfloat16)
        near[p] = jnp.where(odd, upward, downward).astype(jnp.bfloat16)

    values = plane_variance(0, sources, cols, scalars, wide, ref_wide, inv)
    for q in range(planes):
        held_values = values
        if q + 1 < planes:
            values = plane_variance(q + 1, sources, cols, scalars, wide, ref_wide, inv)
        add_plane(q, planes, held_values, weights, sums)
        var[q] = held_values
        if q > 0:
            finish(q - 1)
    finish(planes - 1)


def mid_kernel(
    at_slots,
    at_live,
    sources,
    blocks,
    picks,
    numbers,
    arrived,
    ref,
    edge_var,
    kernel,
    bias_rows,
    kernel_two,
    bias_two,
    out,
    own,
    choices,
    wide,
    ref_wide,
    cost,
    sums,
    scalars,
    sem,
):
    copy = pltpu.make_async_copy(numbers, scalars, sem)
    copy.start()
    planes, cols, _ = edge_var.shape
    inner = cost.shape[0] // planes
    step = choices.shape[1] // 2
    row = lax.broadcasted_iota(jnp.int32, (cols, step), 0)
    target = 2 * lax.broadcasted_iota(jnp.int32, (cols, step), 1)
    for odd in range(2):
        choices[:, odd * step : (odd + 1) * step] = jnp.where(row == target + odd, 1.0, 0.0).astype(jnp.bfloat16)
    turned = turned_reference(ref, blocks, picks)
    clear_bands(wide, cols)
    copy.wait()
    live = scalars[at_live]
    inv, scale = view_weights(live)
    ref_wide[0] = turned * scale
    load_tiles(at_slots, live, sources, blocks, picks, scale, scalars, arrived, wide)
    weights = kernel[...].astype(jnp.bfloat16)
    bias = bias_rows[:inner]
    ready, cols = own.shape[1:]
    column = lax.broadcasted_iota(jnp.int32, (ready + inner, cols), 1)

    def finish(p):
        total = joined_columns(sums[p % sums.shape[0]], column)
        own[p] = total[:ready]
        cost[p * inner : (p + 1) * inner, :] = jnp.maximum(total[ready:] + bias, 0.0).astype(jnp.bfloat16)

    values = plane_variance(0, sources, cols, scalars, wide, ref_wide, inv)
    for q in range(planes):
        held_values = values
        if q + 1 < planes:
            values = plane_variance(q + 1, sources, cols, scalars, wide, ref_wide, inv)
        add_plane(q, planes, jnp.concatenate([edge_var[q], held_values], axis=1), weights, sums)
        if q > 0:
            finish(q - 1)
    finish(planes - 1)
    taken = jnp.dot(cost[...], choices[...], preferred_element_type=jnp.float32).astype(jnp.bfloat16)
    for q in range(planes // 2):
        out[q] = strided_planes(q, planes, taken, inner, kernel_two, out.shape[2]) + bias_two[...]


def end_kernel(far, near, flags, own, own_top, partial, bias_rows, kernel_two, choices, out):
    planes, c1, cols = own_top.shape
    odd = jnp.concatenate([flags[0]] * (cols // LANES), axis=1) > 0.5
    not_top = jnp.concatenate([flags[1]] * (cols // LANES), axis=1)
    empty = jnp.zeros((c1, cols), jnp.float32)
    bias = bias_rows[:c1]
    rows = []
    for p in range(planes):
        lower, upper = far[p].astype(jnp.float32), near[p].astype(jnp.float32)
        before = own[p, :c1] + jnp.where(odd, upper[:c1], lower[:c1])
        top = own_top[p] + jnp.where(odd, upper[c1:], lower[c1:])
        bottom = own[p, c1:] + jnp.where(odd, lower[:c1], upper[:c1])
        rows += [jnp.maximum(before + bias, 0.0) * not_top]
        rows += [jnp.maximum(top + bias, 0.0), jnp.maximum(bottom + bias, 0.0), empty]
    cost = jnp.concatenate(rows, axis=0).astype(jnp.bfloat16)
    taken = jnp.dot(cost, choices[...], preferred_element_type=jnp.float32).astype(jnp.bfloat16)
    for q in range(planes // 2):
        out[q] = partial[q] + strided_planes(q, planes, taken, 4 * c1, kernel_two, out.shape[2])


def on_device(
    ref_features,
    source_tiles,
    pair_lists,
    view_counts,
    disparities,
    conv_first,
    bias_first,
    conv_second,
    bias_second,
):
    n_view = lax.axis_size("view")
    me = lax.axis_index("view").reshape(1)
    rows_n, channels, cols = ref_features.shape
    tiles_dev, tile_rows = source_tiles.shape[0], source_tiles.shape[1]
    sources, blocks = pair_lists.shape[1], pair_lists.shape[2]
    planes = disparities.shape[0]
    slab = tile_rows * channels
    c1, c2 = conv_first.shape[2], conv_second.shape[0]
    half_r, half_p, half_x = rows_n // 2, planes // 2, cols // 2
    smem = pl.BlockSpec(memory_space=pltpu.SMEM)
    vmem = pl.BlockSpec(memory_space=pltpu.VMEM)
    anywhere = pl.BlockSpec(memory_space=pl.ANY)
    params = pltpu.CompilerParams(vmem_limit_bytes=VMEM_LIMIT)
    bf16, f32, i32 = jnp.bfloat16, jnp.float32, jnp.int32
    shape = jax.ShapeDtypeStruct

    table = pl.pallas_call(
        functools.partial(request_kernel, tiles_dev),
        out_shape=shape((n_view, 1, 2 * CAP), i32),
        in_specs=[vmem],
        out_specs=vmem,
        compiler_params=params,
        name="request_table",
    )(pair_lists)
    table = lax.all_to_all(table, "view", split_axis=0, concat_axis=0, tiled=True)
    at_slots = planes * sources
    at_live = at_slots + sources * blocks
    edge_blocks, mid_blocks = (0, blocks - 1), tuple(range(1, blocks - 1))
    rows_of = lambda picks: [block * tile_rows + i for block in picks for i in range(tile_rows)]
    edge_rows, mid_rows = rows_of(edge_blocks), rows_of(mid_blocks)
    inner = (rows_n - 2) * c1
    mid_deep, edge_deep = (-(-3 * rows // LANES) * LANES for rows in (inner, 4 * c1))
    prepared = pl.pallas_call(
        functools.partial(prepare_kernel, n_view, tiles_dev, edge_rows, mid_rows),
        out_shape=[
            shape((27 * c1 + 8, LANES), f32),
            shape((9 * (inner + c1), 2 * LANES), f32),
            shape((3 * half_r * c2, mid_deep), bf16),
            shape((3 * half_r * c2, edge_deep), bf16),
            shape((inner, cols), f32),
            shape((half_r * c2, half_x), f32),
            shape((LANES,), i32),
        ],
        in_specs=[vmem, vmem] + [smem] * 6,
        out_specs=[vmem] * 6 + [smem],
        scratch_shapes=[pltpu.VMEM((3 * mid_deep, LANES), f32), pltpu.VMEM((3 * edge_deep, LANES), f32)],
        compiler_params=params,
        name="weights_and_scalars",
    )(
        conv_first.transpose(0, 1, 3, 2, 4),
        conv_second.transpose(1, 2, 3, 4, 0),
        bias_first,
        bias_second,
        disparities,
        pair_lists,
        view_counts,
        me,
    )
    kernel_edge, kernel_mid, two_mid, two_edge, bias_rows, bias_two, scalars = prepared

    tiles = source_tiles.reshape(tiles_dev, slab, cols)
    table = table[:, 0, : CAP + 1].reshape(1, n_view * (CAP + 1))
    far_first = sorted(range(1, n_view), key=lambda k: -min(k, n_view - k))
    order = [k for pair in zip(far_first, far_first[::-1]) for k in pair][: len(far_first)]
    distances = order + [0]
    bundles = [None] * n_view
    gathered = pl.pallas_call(
        functools.partial(gather_kernel, distances, n_view),
        out_shape=[shape((CAP, slab, cols), bf16)] * n_view,
        in_specs=[smem, vmem, anywhere],
        out_specs=[vmem] * n_view,
        compiler_params=params,
        name="requested_tiles",
    )(table, tiles, bias_two)
    for k, bundle in zip(distances, gathered):
        pairs = [(i, (i + k) % n_view) for i in range(n_view)]
        bundles[k] = lax.ppermute(bundle, "view", pairs) if k else bundle
    arrived = pl.pallas_call(
        functools.partial(collect_kernel, distances),
        out_shape=shape((n_view * CAP, slab, cols), bf16),
        in_specs=[vmem] * n_view,
        out_specs=vmem,
        compiler_params=params,
        name="all_tiles",
    )(*[bundles[k] for k in distances])

    band_scratch = [pltpu.VMEM((sources, cols + 2 * SHIFT, LANES), f32), pltpu.VMEM((1, cols, LANES), f32)]
    payload = shape((planes, 2 * c1, cols), bf16)
    col_step = (half_x // LANES + 1) * LANES
    edge_var, own, far, near, flags = pl.pallas_call(
        functools.partial(edge_kernel, at_slots, at_live, sources, blocks, edge_blocks),
        out_shape=[
            shape((planes, cols, LANES), bf16),
            shape((planes, 2 * c1, cols), f32),
            payload,
            payload,
            shape((2, c1, LANES), f32),
        ],
        in_specs=[vmem] * 3,
        out_specs=[vmem] * 5,
        scratch_shapes=band_scratch
        + [
            pltpu.VMEM((3, 9 * c1, cols), f32),
            pltpu.SMEM((1, LANES), f32),
            pltpu.SemaphoreType.DMA,
        ],
        compiler_params=params,
        name="edge_rows",
    )(kernel_edge, arrived, ref_features)
    far = swapped(far, "view", 1)
    near = swapped(near, "view", 0)

    partial, own_top, choices = pl.pallas_call(
        functools.partial(mid_kernel, at_slots, at_live, sources, blocks, mid_blocks),
        out_shape=[
            shape((half_p, half_r * c2, half_x), f32),
            shape((planes, c1, cols), f32),
            shape((cols, 2 * col_step), bf16),
        ],
        in_specs=[anywhere] + [vmem] * 7,
        out_specs=[vmem] * 3,
        scratch_shapes=band_scratch
        + [
            pltpu.VMEM((planes * inner, cols), bf16),
            pltpu.VMEM((3, 3 * (inner + c1), cols), f32),
            pltpu.SMEM(scalars.shape, i32),
            pltpu.SemaphoreType.DMA,
        ],
        compiler_params=params,
        name="middle_rows",
    )(scalars, arrived, ref_features, edge_var, kernel_mid, bias_rows, two_mid, bias_two)

    out = pl.pallas_call(
        end_kernel,
        out_shape=shape((half_p, half_r * c2, half_x), f32),
        in_specs=[vmem] * 9,
        out_specs=vmem,
        compiler_params=params,
        name="end_rows",
    )(far, near, flags, own, own_top, partial, bias_rows, two_edge, choices)
    return out.reshape(half_p, half_r, c2, half_x)


def solution(mesh):
    return jax.shard_map(
        on_device,
        mesh=mesh,
        in_specs=(
            P(("groups", "view"), None, None),
            P(("groups", "view"), None, None, None),
            P(("groups", "view"), None, None),
            P(("groups", "view")),
            P("groups", None),
            P(),
            P(),
            P(),
            P(),
        ),
        out_specs=P("groups", "view", None, None),
        check_vma=False,
    )
```

```python
import functools

import numpy as np

import jax
import jax.numpy as jnp
from jax import lax
from jax.experimental import pallas as pl
from jax.experimental.pallas import tpu as pltpu
from jax.sharding import PartitionSpec as P

SHIFT = 48
CAP = 2
LANES = 128
CHUNK = 64
VMEM_LIMIT = 10 * 1024 * 1024


def swapped(x, axis, parity):
    count = lax.axis_size(axis)
    pairs = [(i, i + 1) for i in range(parity, count - 1, 2)]
    return lax.ppermute(x, axis, pairs + [(j, i) for i, j in pairs])


def request_places(pair_lists, tiles_dev):
    owners, ranks, tiles = [], [], []
    for s in range(pair_lists.shape[1]):
        for b in range(pair_lists.shape[2]):
            tile = pair_lists[0, s, b]
            whole = jnp.maximum(tile, 0)
            owner = jnp.where(tile >= 0, lax.div(whole, tiles_dev), -1)
            rank = jnp.int32(0)
            for other in owners:
                rank = rank + jnp.where(other == owner, 1, 0)
            owners.append(owner)
            ranks.append(rank)
            tiles.append(lax.rem(whole, tiles_dev))
    return owners, ranks, tiles


def request_kernel(tiles_dev, pair_lists, _, table):
    n_view = table.shape[0]
    row = lax.broadcasted_iota(jnp.int32, (n_view, LANES), 0) * tiles_dev
    lane = lax.broadcasted_iota(jnp.int32, (n_view, LANES), 1)
    total = jnp.zeros((n_view, LANES), jnp.int32)
    count = jnp.zeros((n_view, LANES), jnp.int32)
    for s in range(pair_lists.shape[1]):
        for b in range(pair_lists.shape[2]):
            tile = pair_lists[0, s : s + 1, b : b + 1] - row
            owned = (tile >= 0) & (tile < tiles_dev)
            total = jnp.where(owned & (lane == count), tile, total)
            count = count + jnp.where(owned, 1, 0)
    total = jnp.where(lane == CAP, lax.broadcasted_iota(jnp.int32, (n_view, LANES), 0), total)
    for d in range(n_view):
        table[d] = total[d : d + 1, : table.shape[2]]


def gather_kernel(distances, n_view, table, tiles, *bundles):
    me = table[0, CAP]
    for k, bundle in zip(distances, bundles):
        at = lax.rem(me + k, n_view) * (CAP + 1)
        for j in range(CAP):
            bundle[j] = tiles[table[0, at + j]]


def collect_kernel(distances, *refs):
    arrived = refs[-1]
    for k, bundle in zip(distances, refs[:-1]):
        for j in range(CAP):
            arrived[k * CAP + j] = bundle[j]


def prepare_kernel(
    n_view,
    tiles_dev,
    edge_rows,
    mid_rows,
    first,
    second,
    bias_first,
    bias_second,
    disparities,
    pair_lists,
    view_counts,
    me,
    kernel_edge,
    kernel_mid,
    two_mid,
    two_edge,
    bias_rows,
    bias_two,
    numbers,
    stacked_mid,
    stacked_edge,
):
    planes, sources = disparities.shape
    owners, ranks, _ = request_places(pair_lists, tiles_dev)
    values = [disparities[p, s] for p in range(planes) for s in range(sources)]
    for owner, rank in zip(owners, ranks):
        back = lax.rem(me[0] - owner + n_view, n_view)
        values.append(jnp.where(owner >= 0, back * CAP + rank, 0))
    values += [view_counts[0], me[0], lax.rem(me[0], 2)]
    lane_at = lax.broadcasted_iota(jnp.int32, (8, LANES), 1)
    row = jnp.zeros((8, LANES), jnp.int32)
    for i, value in enumerate(values):
        row = jnp.where(lane_at == i, value, row)
    for at in range(0, numbers.shape[0], 8):
        numbers[at : at + 8, :] = row

    c1, channels = first.shape[3], first.shape[4]
    c2 = second.shape[4]
    rows_n = len(edge_rows) + len(mid_rows)
    half_r = rows_n // 2
    place = {row: i for i, row in enumerate(edge_rows + mid_rows)}
    per_group = LANES // channels
    filler = jnp.zeros((c1, LANES - channels), jnp.float32)
    taps = {}
    for a in range(3):
        for b in range(3):
            for d in range(3):
                tap = jnp.concatenate([first[a, b, d].astype(jnp.float32), filler], axis=1)
                for turn in range(per_group):
                    lane = turn * channels
                    taps[a, b, d, turn] = pltpu.roll(tap, lane, 1) if lane else tap

    def band(a, d, r, group):
        total = jnp.zeros((c1, LANES), jnp.float32)
        for b in range(3):
            at_place = place.get(r - 1 + b, -1)
            if at_place >= 0 and at_place // per_group == group:
                total = total + taps[a, b, d, at_place % per_group]
        return total

    rim = (-1, 0, rows_n - 1, rows_n)
    inner = tuple(range(1, rows_n - 1))
    for kernel, rows, groups in ((kernel_edge, (rim[0],) + rim[2:], 1), (kernel_mid, (0,) + inner, 2)):
        for d in range(3):
            for i, r in enumerate(rows):
                for a in range(3):
                    at = ((a * 3 + d) * len(rows) + i) * c1
                    for group in range(groups):
                        kernel[at : at + c1, group * LANES : (group + 1) * LANES] = band(a, d, r, group)

    def second_row(a, d, r):
        blocks = []
        for g in range(half_r):
            b = -1 if r is None else r - 2 * g + 1
            hit = 0 <= b < 3
            blocks.append(second[a, b, d].astype(jnp.float32) if hit else jnp.zeros((c1, c2), jnp.float32))
        blocks.append(jnp.zeros((c1, LANES - half_r * c2), jnp.float32))
        return jnp.concatenate(blocks, axis=1)

    for two, stacked, rows in ((two_mid, stacked_mid, inner), (two_edge, stacked_edge, rim[:3] + (None,))):
        deep = two.shape[1]
        stacked[...] = jnp.zeros(stacked.shape, jnp.float32)
        for a in range(3):
            for j, d in enumerate((1, 0, 2)):
                for i, r in enumerate(rows):
                    at = j * deep + (a * len(rows) + i) * c1
                    stacked[at : at + c1, :] = second_row(a, d, r)
        outs = half_r * c2
        for j in range(3):
            two[j * outs : (j + 1) * outs, :] = stacked[j * deep : (j + 1) * deep, :].T[:outs].astype(jnp.bfloat16)

    def spread_bias(like, bias):
        index = lax.broadcasted_iota(jnp.int32, like.shape, 0)
        total = jnp.zeros(like.shape, jnp.float32)
        for i in range(bias.shape[0]):
            total = jnp.where(index % bias.shape[0] == i, bias[i], total)
        like[...] = total

    spread_bias(bias_rows, bias_first)
    spread_bias(bias_two, bias_second)


def plane_variance(p, sources, cols, disp, wide, ref_wide, inv):
    chunks = []
    for x0 in range(0, cols, CHUNK):
        ref = ref_wide[0, x0 : x0 + CHUNK, :]
        summed = ref
        squares = ref * ref
        for s in range(sources):
            warped = wide[s, pl.ds(SHIFT + x0 - disp[p * sources + s], CHUNK), :]
            summed = summed + warped
            squares = squares + warped * warped
        chunks.append((squares - summed * summed * inv).astype(jnp.bfloat16))
    return jnp.concatenate(chunks, axis=0)


def view_weights(live):
    total = live.astype(jnp.float32) + jnp.ones((1, LANES), jnp.float32)
    return 1.0 / total, lax.rsqrt(total)


def turned_reference(ref, blocks, picks):
    tile_rows = ref.shape[0] // blocks
    rows = [ref[block * tile_rows + i] for block in picks for i in range(tile_rows)]
    return jnp.concatenate(rows, axis=0).T.astype(jnp.float32)


def clear_bands(wide, cols):
    band = jnp.zeros((SHIFT, LANES), jnp.float32)
    for at in range(wide.shape[0]):
        wide[at, 0:SHIFT, :] = band
        wide[at, SHIFT + cols : 2 * SHIFT + cols, :] = band


def load_tiles(at_slots, live, sources, blocks, picks, scale, scalars, arrived, wide):
    for s in range(sources):
        slab = jnp.concatenate([arrived[scalars[at_slots + s * blocks + block]] for block in picks], axis=0)
        cols = slab.shape[1]
        wide[s, SHIFT : SHIFT + cols, :] = slab.T.astype(jnp.float32) * jnp.where(s < live, scale, 0.0)


def add_plane(q, planes, lhs, weights, sums):
    taps = lax.dot_general(weights, lhs, (((1,), (1,)), ((), ())), preferred_element_type=jnp.float32)
    rows = taps.shape[0] // 3
    slots = sums.shape[0]
    if q + 1 < planes:
        sums[(q + 1) % slots] = taps[:rows]
    if q == 0:
        sums[q % slots] = taps[rows : 2 * rows]
    else:
        sums[q % slots] += taps[rows : 2 * rows]
        sums[(q - 1) % slots] += taps[2 * rows :]


def joined_columns(taps, column):
    rows, cols = column.shape
    left, center, right = taps[:rows], taps[rows : 2 * rows], taps[2 * rows :]
    total = center + jnp.where(column > 0, pltpu.roll(left, 1, 1), 0.0)
    return total + jnp.where(column < cols - 1, pltpu.roll(right, cols - 1, 1), 0.0)


def strided_planes(q, planes, taken, rows, weights, out_w):
    step = taken.shape[1] // 2
    none = jnp.zeros((rows, 2 * step), jnp.bfloat16)
    near = range(2 * q - 1, 2 * q + 2)
    parts = [taken[p * rows : (p + 1) * rows] if 0 <= p < planes else none for p in near]
    rhs = jnp.concatenate(parts, axis=0)
    deep = rhs.shape[0]
    outs = weights.shape[0] // 3
    even = jnp.dot(weights[:outs, :deep], rhs[:, :step], preferred_element_type=jnp.float32)
    odd = jnp.dot(weights[outs:, :deep], rhs[:, step:], preferred_element_type=jnp.float32)
    result = even + pltpu.roll(odd[:outs], 1, 1) + odd[outs:]
    return result[:, :out_w]


def warp_kernel(at_slots, at_live, sources, blocks, picks, numbers, arrived, ref, var, flags, wide, ref_wide, held, sem):
    copy = pltpu.make_async_copy(numbers.at[pl.ds(0, 1)], held, sem)
    copy.start()
    planes, cols, _ = var.shape
    turned = turned_reference(ref, blocks, picks)
    clear_bands(wide, cols)
    copy.wait()
    scalars = [held[0, i] for i in range(at_live + 3)]
    live = scalars[at_live]
    inv, scale = view_weights(live)
    ref_wide[0] = turned * scale
    load_tiles(at_slots, live, sources, blocks, picks, scale, scalars, arrived, wide)
    flags[0] = jnp.where(scalars[at_live + 2] > 0, 1.0, 0.0) * jnp.ones(flags.shape[1:], jnp.float32)
    flags[1] = jnp.where(scalars[at_live + 1] > 0, 1.0, 0.0) * jnp.ones(flags.shape[1:], jnp.float32)
    for p in range(planes):
        var[p] = plane_variance(p, sources, cols, scalars, wide, ref_wide, inv)


def edge_kernel(var, kernel, flags, own, far, near, sums):
    planes, cols, _ = var.shape
    c1 = kernel.shape[0] // 27
    odd = jnp.concatenate([jnp.concatenate([flags[0]] * 2, axis=0)] * (cols // LANES), axis=1) > 0.5
    weights = kernel[...].astype(jnp.bfloat16)
    column = lax.broadcasted_iota(jnp.int32, (3 * c1, cols), 1)
    empty = jnp.zeros((c1, cols), jnp.float32)

    def finish(p):
        total = joined_columns(sums[p % sums.shape[0]], column)
        own[p] = total[: 2 * c1]
        downward = total[c1:]
        upward = jnp.concatenate([total[:c1], empty], axis=0)
        far[p] = jnp.where(odd, downward, upward).astype(jnp.bfloat16)
        near[p] = jnp.where(odd, upward, downward).astype(jnp.bfloat16)

    for q in range(planes):
        add_plane(q, planes, var[q], weights, sums)
        if q > 0:
            finish(q - 1)
    finish(planes - 1)


def mid_kernel(
    at_slots,
    at_live,
    sources,
    blocks,
    picks,
    numbers,
    arrived,
    ref,
    edge_var,
    kernel,
    bias_rows,
    kernel_two,
    bias_two,
    out,
    own,
    choices,
    wide,
    ref_wide,
    cost,
    sums,
    held,
    sem,
):
    copy = pltpu.make_async_copy(numbers.at[pl.ds(0, 1)], held, sem)
    copy.start()
    planes, cols, _ = edge_var.shape
    inner = cost.shape[0] // planes
    step = choices.shape[1] // 2
    row = lax.broadcasted_iota(jnp.int32, (cols, step), 0)
    target = 2 * lax.broadcasted_iota(jnp.int32, (cols, step), 1)
    for odd in range(2):
        choices[:, odd * step : (odd + 1) * step] = jnp.where(row == target + odd, 1.0, 0.0).astype(jnp.bfloat16)
    turned = turned_reference(ref, blocks, picks)
    clear_bands(wide, cols)
    copy.wait()
    scalars = [held[0, i] for i in range(at_live + 1)]
    live = scalars[at_live]
    inv, scale = view_weights(live)
    ref_wide[0] = turned * scale
    load_tiles(at_slots, live, sources, blocks, picks, scale, scalars, arrived, wide)
    weights = kernel[...].astype(jnp.bfloat16)
    bias = bias_rows[:inner]
    ready, cols = own.shape[1:]
    column = lax.broadcasted_iota(jnp.int32, (ready + inner, cols), 1)

    def finish(p):
        total = joined_columns(sums[p % sums.shape[0]], column)
        own[p] = total[:ready]
        cost[p * inner : (p + 1) * inner, :] = jnp.maximum(total[ready:] + bias, 0.0).astype(jnp.bfloat16)

    values = plane_variance(0, sources, cols, scalars, wide, ref_wide, inv)
    for q in range(planes):
        held_values = values
        if q + 1 < planes:
            values = plane_variance(q + 1, sources, cols, scalars, wide, ref_wide, inv)
        add_plane(q, planes, jnp.concatenate([edge_var[q], held_values], axis=1), weights, sums)
        if q > 0:
            finish(q - 1)
    finish(planes - 1)
    taken = jnp.dot(cost[...], choices[...], preferred_element_type=jnp.float32).astype(jnp.bfloat16)
    for q in range(planes // 2):
        out[q] = strided_planes(q, planes, taken, inner, kernel_two, out.shape[2]) + bias_two[...]


def end_kernel(far, near, flags, own, own_top, partial, bias_rows, kernel_two, choices, out):
    planes, c1, cols = own_top.shape
    odd = jnp.concatenate([flags[0]] * (cols // LANES), axis=1) > 0.5
    not_top = jnp.concatenate([flags[1]] * (cols // LANES), axis=1)
    empty = jnp.zeros((c1, cols), jnp.float32)
    bias = bias_rows[:c1]
    rows = []
    for p in range(planes):
        lower, upper = far[p].astype(jnp.float32), near[p].astype(jnp.float32)
        before = own[p, :c1] + jnp.where(odd, upper[:c1], lower[:c1])
        top = own_top[p] + jnp.where(odd, upper[c1:], lower[c1:])
        bottom = own[p, c1:] + jnp.where(odd, lower[:c1], upper[:c1])
        rows += [jnp.maximum(before + bias, 0.0) * not_top]
        rows += [jnp.maximum(top + bias, 0.0), jnp.maximum(bottom + bias, 0.0), empty]
    cost = jnp.concatenate(rows, axis=0).astype(jnp.bfloat16)
    taken = jnp.dot(cost, choices[...], preferred_element_type=jnp.float32).astype(jnp.bfloat16)
    for q in range(planes // 2):
        out[q] = partial[q] + strided_planes(q, planes, taken, 4 * c1, kernel_two, out.shape[2])


def on_device(
    ref_features,
    source_tiles,
    pair_lists,
    view_counts,
    disparities,
    conv_first,
    bias_first,
    conv_second,
    bias_second,
):
    n_view = lax.axis_size("view")
    me = lax.axis_index("view").reshape(1)
    rows_n, channels, cols = ref_features.shape
    tiles_dev, tile_rows = source_tiles.shape[0], source_tiles.shape[1]
    sources, blocks = pair_lists.shape[1], pair_lists.shape[2]
    planes = disparities.shape[0]
    slab = tile_rows * channels
    c1, c2 = conv_first.shape[2], conv_second.shape[0]
    half_r, half_p, half_x = rows_n // 2, planes // 2, cols // 2
    smem = pl.BlockSpec(memory_space=pltpu.SMEM)
    vmem = pl.BlockSpec(memory_space=pltpu.VMEM)
    anywhere = pl.BlockSpec(memory_space=pl.ANY)
    params = pltpu.CompilerParams(vmem_limit_bytes=VMEM_LIMIT)
    bf16, f32, i32 = jnp.bfloat16, jnp.float32, jnp.int32
    shape = jax.ShapeDtypeStruct

    tiles = source_tiles.reshape(tiles_dev, slab, cols)
    table = pl.pallas_call(
        functools.partial(request_kernel, tiles_dev),
        out_shape=shape((n_view, 1, 2 * CAP), i32),
        in_specs=[vmem, vmem],
        out_specs=vmem,
        compiler_params=params,
        name="request_table",
    )(pair_lists, tiles)
    table = lax.all_to_all(table, "view", split_axis=0, concat_axis=0, tiled=True)
    table = table[:, 0, : CAP + 1].reshape(1, n_view * (CAP + 1))
    far_first = sorted(range(1, n_view), key=lambda k: -min(k, n_view - k))
    order = [k for pair in zip(far_first, far_first[::-1]) for k in pair][: len(far_first)]
    distances = order + [0]
    bundles = [None] * n_view
    gathered = pl.pallas_call(
        functools.partial(gather_kernel, distances, n_view),
        out_shape=[shape((CAP, slab, cols), bf16)] * n_view,
        in_specs=[smem, vmem],
        out_specs=[vmem] * n_view,
        compiler_params=params,
        name="requested_tiles",
    )(table, tiles)
    for k, bundle in zip(distances, gathered):
        pairs = [(i, (i + k) % n_view) for i in range(n_view)]
        bundles[k] = lax.ppermute(bundle, "view", pairs) if k else bundle

    at_slots = planes * sources
    at_live = at_slots + sources * blocks
    edge_blocks, mid_blocks = (0, blocks - 1), tuple(range(1, blocks - 1))
    rows_of = lambda picks: [block * tile_rows + i for block in picks for i in range(tile_rows)]
    edge_rows, mid_rows = rows_of(edge_blocks), rows_of(mid_blocks)
    inner = (rows_n - 2) * c1
    mid_deep, edge_deep = (-(-3 * rows // LANES) * LANES for rows in (inner, 4 * c1))
    prepared = pl.pallas_call(
        functools.partial(prepare_kernel, n_view, tiles_dev, edge_rows, mid_rows),
        out_shape=[
            shape((27 * c1, LANES), f32),
            shape((9 * (inner + c1), 2 * LANES), f32),
            shape((3 * half_r * c2, mid_deep), bf16),
            shape((3 * half_r * c2, edge_deep), bf16),
            shape((inner, cols), f32),
            shape((half_r * c2, half_x), f32),
            shape((12 * 8, LANES), i32),
        ],
        in_specs=[vmem, vmem] + [smem] * 6,
        out_specs=[vmem] * 7,
        scratch_shapes=[pltpu.VMEM((3 * mid_deep, LANES), f32), pltpu.VMEM((3 * edge_deep, LANES), f32)],
        compiler_params=params,
        name="weights_and_scalars",
    )(
        conv_first.transpose(0, 1, 3, 2, 4),
        conv_second.transpose(1, 2, 3, 4, 0),
        bias_first,
        bias_second,
        disparities,
        pair_lists,
        view_counts,
        me,
    )
    kernel_edge, kernel_mid, two_mid, two_edge, bias_rows, bias_two, numbers = prepared
    arrived = pl.pallas_call(
        functools.partial(collect_kernel, distances),
        out_shape=shape((n_view * CAP, slab, cols), bf16),
        in_specs=[vmem] * n_view,
        out_specs=vmem,
        compiler_params=params,
        name="all_tiles",
    )(*[bundles[k] for k in distances])

    band_scratch = [pltpu.VMEM((sources, cols + 2 * SHIFT, LANES), f32), pltpu.VMEM((1, cols, LANES), f32)]
    payload = shape((planes, 2 * c1, cols), bf16)
    col_step = (half_x // LANES + 1) * LANES
    edge_var, flags = pl.pallas_call(
        functools.partial(warp_kernel, at_slots, at_live, sources, blocks, edge_blocks),
        out_shape=[shape((planes, cols, LANES), bf16), shape((2, c1, LANES), f32)],
        in_specs=[vmem] * 3,
        out_specs=[vmem] * 2,
        scratch_shapes=band_scratch + [pltpu.SMEM((1, LANES), i32), pltpu.SemaphoreType.DMA],
        compiler_params=params,
        name="edge_variance",
    )(numbers, arrived, ref_features)
    own, far, near = pl.pallas_call(
        edge_kernel,
        out_shape=[shape((planes, 2 * c1, cols), f32), payload, payload],
        in_specs=[vmem] * 3,
        out_specs=[vmem] * 3,
        scratch_shapes=[pltpu.VMEM((3, 9 * c1, cols), f32)],
        compiler_params=params,
        name="edge_rows",
    )(edge_var, kernel_edge, flags)
    far = swapped(far, "view", 1)
    near = swapped(near, "view", 0)

    partial, own_top, choices = pl.pallas_call(
        functools.partial(mid_kernel, at_slots, at_live, sources, blocks, mid_blocks),
        out_shape=[
            shape((half_p, half_r * c2, half_x), f32),
            shape((planes, c1, cols), f32),
            shape((cols, 2 * col_step), bf16),
        ],
        in_specs=[vmem] * 8,
        out_specs=[vmem] * 3,
        scratch_shapes=band_scratch
        + [
            pltpu.VMEM((planes * inner, cols), bf16),
            pltpu.VMEM((3, 3 * (inner + c1), cols), f32),
            pltpu.SMEM((1, LANES), i32),
            pltpu.SemaphoreType.DMA,
        ],
        compiler_params=params,
        name="middle_rows",
    )(numbers, arrived, ref_features, edge_var, kernel_mid, bias_rows, two_mid, bias_two)

    out = pl.pallas_call(
        end_kernel,
        out_shape=shape((half_p, half_r * c2, half_x), f32),
        in_specs=[vmem] * 9,
        out_specs=vmem,
        compiler_params=params,
        name="end_rows",
    )(far, near, flags, own, own_top, partial, bias_rows, two_edge, choices)
    return out.reshape(half_p, half_r, c2, half_x)


def solution(mesh):
    return jax.shard_map(
        on_device,
        mesh=mesh,
        in_specs=(
            P(("groups", "view"), None, None),
            P(("groups", "view"), None, None, None),
            P(("groups", "view"), None, None),
            P(("groups", "view")),
            P("groups", None),
            P(),
            P(),
            P(),
            P(),
        ),
        out_specs=P("groups", "view", None, None),
        check_vma=False,
    )
```

```python
import functools

import numpy as np

import jax
import jax.numpy as jnp
from jax import lax
from jax.experimental import pallas as pl
from jax.experimental.pallas import tpu as pltpu
from jax.sharding import PartitionSpec as P

SHIFT = 48
CAP = 2
LANES = 128
CHUNK = 64
VMEM_LIMIT = 10 * 1024 * 1024


def swapped(x, axis, parity):
    count = lax.axis_size(axis)
    pairs = [(i, i + 1) for i in range(parity, count - 1, 2)]
    return lax.ppermute(x, axis, pairs + [(j, i) for i, j in pairs])


def request_places(pair_lists, tiles_dev):
    owners, ranks, tiles = [], [], []
    for s in range(pair_lists.shape[1]):
        for b in range(pair_lists.shape[2]):
            tile = pair_lists[0, s, b]
            whole = jnp.maximum(tile, 0)
            owner = jnp.where(tile >= 0, lax.div(whole, tiles_dev), -1)
            rank = jnp.int32(0)
            for other in owners:
                rank = rank + jnp.where(other == owner, 1, 0)
            owners.append(owner)
            ranks.append(rank)
            tiles.append(lax.rem(whole, tiles_dev))
    return owners, ranks, tiles


def request_kernel(tiles_dev, pair_lists, table):
    n_view = table.shape[0]
    row = lax.broadcasted_iota(jnp.int32, (n_view, LANES), 0) * tiles_dev
    lane = lax.broadcasted_iota(jnp.int32, (n_view, LANES), 1)
    total = jnp.zeros((n_view, LANES), jnp.int32)
    count = jnp.zeros((n_view, LANES), jnp.int32)
    for s in range(pair_lists.shape[1]):
        for b in range(pair_lists.shape[2]):
            tile = pair_lists[0, s : s + 1, b : b + 1] - row
            owned = (tile >= 0) & (tile < tiles_dev)
            total = jnp.where(owned & (lane == count), tile, total)
            count = count + jnp.where(owned, 1, 0)
    total = jnp.where(lane == CAP, lax.broadcasted_iota(jnp.int32, (n_view, LANES), 0), total)
    for d in range(n_view):
        table[d] = total[d : d + 1, : table.shape[2]]


def gather_kernel(distances, n_view, table, tiles, *bundles):
    me = table[0, CAP]
    for k, bundle in zip(distances, bundles):
        at = lax.rem(me + k, n_view) * (CAP + 1)
        for j in range(CAP):
            bundle[j] = tiles[table[0, at + j]]


def collect_kernel(distances, *refs):
    arrived = refs[-1]
    for k, bundle in zip(distances, refs[:-1]):
        for j in range(CAP):
            arrived[k * CAP + j] = bundle[j]


def prepare_kernel(
    n_view,
    tiles_dev,
    edge_rows,
    mid_rows,
    first,
    second,
    bias_first,
    bias_second,
    disparities,
    pair_lists,
    view_counts,
    me,
    kernel_edge,
    kernel_mid,
    two_mid,
    two_edge,
    bias_rows,
    bias_two,
    scalars,
    stacked_mid,
    stacked_edge,
):
    planes, sources = disparities.shape
    owners, ranks, _ = request_places(pair_lists, tiles_dev)
    at = 0
    for p in range(planes):
        for s in range(sources):
            scalars[at] = disparities[p, s]
            at += 1
    for owner, rank in zip(owners, ranks):
        back = lax.rem(me[0] - owner + n_view, n_view)
        scalars[at] = jnp.where(owner >= 0, back * CAP + rank, 0)
        at += 1
    scalars[at] = view_counts[0]
    scalars[at + 1] = me[0]
    scalars[at + 2] = lax.rem(me[0], 2)
    tail = kernel_edge.shape[0] - 8
    lane_at = lax.broadcasted_iota(jnp.int32, (8, LANES), 1)
    numbers = jnp.zeros((8, LANES), jnp.float32)
    for i in range(at + 3):
        numbers = jnp.where(lane_at == i, scalars[i].astype(jnp.float32), numbers)
    kernel_edge[tail:, :] = numbers

    c1, channels = first.shape[3], first.shape[4]
    c2 = second.shape[4]
    rows_n = len(edge_rows) + len(mid_rows)
    half_r = rows_n // 2
    place = {row: i for i, row in enumerate(edge_rows + mid_rows)}
    per_group = LANES // channels
    filler = jnp.zeros((c1, LANES - channels), jnp.float32)
    taps = {}
    for a in range(3):
        for b in range(3):
            for d in range(3):
                tap = jnp.concatenate([first[a, b, d].astype(jnp.float32), filler], axis=1)
                for turn in range(per_group):
                    lane = turn * channels
                    taps[a, b, d, turn] = pltpu.roll(tap, lane, 1) if lane else tap

    def band(a, d, r, group):
        total = jnp.zeros((c1, LANES), jnp.float32)
        for b in range(3):
            at_place = place.get(r - 1 + b, -1)
            if at_place >= 0 and at_place // per_group == group:
                total = total + taps[a, b, d, at_place % per_group]
        return total

    rim = (-1, 0, rows_n - 1, rows_n)
    inner = tuple(range(1, rows_n - 1))
    for kernel, rows, groups in ((kernel_edge, (rim[0],) + rim[2:], 1), (kernel_mid, (0,) + inner, 2)):
        for d in range(3):
            for i, r in enumerate(rows):
                for a in range(3):
                    at = ((a * 3 + d) * len(rows) + i) * c1
                    for group in range(groups):
                        kernel[at : at + c1, group * LANES : (group + 1) * LANES] = band(a, d, r, group)

    def second_row(a, d, r):
        blocks = []
        for g in range(half_r):
            b = -1 if r is None else r - 2 * g + 1
            hit = 0 <= b < 3
            blocks.append(second[a, b, d].astype(jnp.float32) if hit else jnp.zeros((c1, c2), jnp.float32))
        blocks.append(jnp.zeros((c1, LANES - half_r * c2), jnp.float32))
        return jnp.concatenate(blocks, axis=1)

    for two, stacked, rows in ((two_mid, stacked_mid, inner), (two_edge, stacked_edge, rim[:3] + (None,))):
        deep = two.shape[1]
        stacked[...] = jnp.zeros(stacked.shape, jnp.float32)
        for a in range(3):
            for j, d in enumerate((1, 0, 2)):
                for i, r in enumerate(rows):
                    at = j * deep + (a * len(rows) + i) * c1
                    stacked[at : at + c1, :] = second_row(a, d, r)
        outs = half_r * c2
        for j in range(3):
            two[j * outs : (j + 1) * outs, :] = stacked[j * deep : (j + 1) * deep, :].T[:outs].astype(jnp.bfloat16)

    def spread_bias(like, bias):
        index = lax.broadcasted_iota(jnp.int32, like.shape, 0)
        total = jnp.zeros(like.shape, jnp.float32)
        for i in range(bias.shape[0]):
            total = jnp.where(index % bias.shape[0] == i, bias[i], total)
        like[...] = total

    spread_bias(bias_rows, bias_first)
    spread_bias(bias_two, bias_second)


def plane_variance(p, sources, cols, disp, wide, ref_wide, inv):
    chunks = []
    for x0 in range(0, cols, CHUNK):
        ref = ref_wide[0, x0 : x0 + CHUNK, :]
        summed = ref
        squares = ref * ref
        for s in range(sources):
            warped = wide[s, pl.ds(SHIFT + x0 - disp[p * sources + s], CHUNK), :]
            summed = summed + warped
            squares = squares + warped * warped
        chunks.append((squares - summed * summed * inv).astype(jnp.bfloat16))
    return jnp.concatenate(chunks, axis=0)


def view_weights(live):
    total = live.astype(jnp.float32) + jnp.ones((1, LANES), jnp.float32)
    return 1.0 / total, lax.rsqrt(total)


def turned_reference(ref, blocks, picks):
    tile_rows = ref.shape[0] // blocks
    rows = [ref[block * tile_rows + i] for block in picks for i in range(tile_rows)]
    return jnp.concatenate(rows, axis=0).T.astype(jnp.float32)


def clear_bands(wide, cols):
    band = jnp.zeros((SHIFT, LANES), jnp.float32)
    for at in range(wide.shape[0]):
        wide[at, 0:SHIFT, :] = band
        wide[at, SHIFT + cols : 2 * SHIFT + cols, :] = band


def load_tiles(at_slots, live, sources, blocks, picks, scale, scalars, arrived, wide):
    for s in range(sources):
        slab = jnp.concatenate([arrived[scalars[at_slots + s * blocks + block]] for block in picks], axis=0)
        cols = slab.shape[1]
        wide[s, SHIFT : SHIFT + cols, :] = slab.T.astype(jnp.float32) * jnp.where(s < live, scale, 0.0)


def add_plane(q, planes, lhs, weights, sums):
    taps = lax.dot_general(weights, lhs, (((1,), (1,)), ((), ())), preferred_element_type=jnp.float32)
    rows = taps.shape[0] // 3
    slots = sums.shape[0]
    if q + 1 < planes:
        sums[(q + 1) % slots] = taps[:rows]
    if q == 0:
        sums[q % slots] = taps[rows : 2 * rows]
    else:
        sums[q % slots] += taps[rows : 2 * rows]
        sums[(q - 1) % slots] += taps[2 * rows :]


def joined_columns(taps, column):
    rows, cols = column.shape
    left, center, right = taps[:rows], taps[rows : 2 * rows], taps[2 * rows :]
    total = center + jnp.where(column > 0, pltpu.roll(left, 1, 1), 0.0)
    return total + jnp.where(column < cols - 1, pltpu.roll(right, cols - 1, 1), 0.0)


def strided_planes(q, planes, taken, rows, weights, out_w):
    step = taken.shape[1] // 2
    none = jnp.zeros((rows, 2 * step), jnp.bfloat16)
    near = range(2 * q - 1, 2 * q + 2)
    parts = [taken[p * rows : (p + 1) * rows] if 0 <= p < planes else none for p in near]
    rhs = jnp.concatenate(parts, axis=0)
    deep = rhs.shape[0]
    outs = weights.shape[0] // 3
    even = jnp.dot(weights[:outs, :deep], rhs[:, :step], preferred_element_type=jnp.float32)
    odd = jnp.dot(weights[outs:, :deep], rhs[:, step:], preferred_element_type=jnp.float32)
    result = even + pltpu.roll(odd[:outs], 1, 1) + odd[outs:]
    return result[:, :out_w]


def edge_kernel(
    at_slots, at_live, sources, blocks, picks, packed, arrived, ref, var, own, far, near, flags, wide, ref_wide, sums, held, sem
):
    planes, cols, _ = var.shape
    tail = packed.shape[0] - 8
    c1 = tail // 27
    copy = pltpu.make_async_copy(packed.at[pl.ds(tail, 1)], held, sem)
    copy.start()
    weights = packed[:tail].astype(jnp.bfloat16)
    turned = turned_reference(ref, blocks, picks)
    clear_bands(wide, cols)
    copy.wait()
    scalars = [held[0, i].astype(jnp.int32) for i in range(at_live + 3)]
    live = scalars[at_live]
    inv, scale = view_weights(live)
    ref_wide[0] = turned * scale
    load_tiles(at_slots, live, sources, blocks, picks, scale, scalars, arrived, wide)
    odd = scalars[at_live + 2] > 0
    flags[0] = jnp.where(odd, 1.0, 0.0) * jnp.ones((c1, LANES), jnp.float32)
    flags[1] = jnp.where(scalars[at_live + 1] > 0, 1.0, 0.0) * jnp.ones((c1, LANES), jnp.float32)
    column = lax.broadcasted_iota(jnp.int32, (3 * c1, cols), 1)
    empty = jnp.zeros((c1, cols), jnp.float32)

    def finish(p):
        total = joined_columns(sums[p % sums.shape[0]], column)
        own[p] = total[: 2 * c1]
        downward = total[c1:]
        upward = jnp.concatenate([total[:c1], empty], axis=0)
        far[p] = jnp.where(odd, downward, upward).astype(jnp.bfloat16)
        near[p] = jnp.where(odd, upward, downward).astype(jnp.bfloat16)

    values = plane_variance(0, sources, cols, scalars, wide, ref_wide, inv)
    for q in range(planes):
        held_values = values
        if q + 1 < planes:
            values = plane_variance(q + 1, sources, cols, scalars, wide, ref_wide, inv)
        add_plane(q, planes, held_values, weights, sums)
        var[q] = held_values
        if q > 0:
            finish(q - 1)
    finish(planes - 1)


def mid_kernel(
    at_slots,
    at_live,
    sources,
    blocks,
    picks,
    numbers,
    arrived,
    ref,
    edge_var,
    kernel,
    bias_rows,
    kernel_two,
    bias_two,
    out,
    own,
    choices,
    wide,
    ref_wide,
    cost,
    sums,
    scalars,
    sem,
):
    copy = pltpu.make_async_copy(numbers, scalars, sem)
    copy.start()
    planes, cols, _ = edge_var.shape
    inner = cost.shape[0] // planes
    step = choices.shape[1] // 2
    row = lax.broadcasted_iota(jnp.int32, (cols, step), 0)
    target = 2 * lax.broadcasted_iota(jnp.int32, (cols, step), 1)
    for odd in range(2):
        choices[:, odd * step : (odd + 1) * step] = jnp.where(row == target + odd, 1.0, 0.0).astype(jnp.bfloat16)
    turned = turned_reference(ref, blocks, picks)
    clear_bands(wide, cols)
    copy.wait()
    live = scalars[at_live]
    inv, scale = view_weights(live)
    ref_wide[0] = turned * scale
    load_tiles(at_slots, live, sources, blocks, picks, scale, scalars, arrived, wide)
    weights = kernel[...].astype(jnp.bfloat16)
    bias = bias_rows[:inner]
    ready, cols = own.shape[1:]
    column = lax.broadcasted_iota(jnp.int32, (ready + inner, cols), 1)

    def finish(p):
        total = joined_columns(sums[p % sums.shape[0]], column)
        own[p] = total[:ready]
        cost[p * inner : (p + 1) * inner, :] = jnp.maximum(total[ready:] + bias, 0.0).astype(jnp.bfloat16)

    values = plane_variance(0, sources, cols, scalars, wide, ref_wide, inv)
    for q in range(planes):
        held_values = values
        if q + 1 < planes:
            values = plane_variance(q + 1, sources, cols, scalars, wide, ref_wide, inv)
        add_plane(q, planes, jnp.concatenate([edge_var[q], held_values], axis=1), weights, sums)
        if q > 0:
            finish(q - 1)
    finish(planes - 1)
    taken = jnp.dot(cost[...], choices[...], preferred_element_type=jnp.float32).astype(jnp.bfloat16)
    for q in range(planes // 2):
        out[q] = strided_planes(q, planes, taken, inner, kernel_two, out.shape[2]) + bias_two[...]


def end_kernel(far, near, flags, own, own_top, partial, bias_rows, kernel_two, choices, out):
    planes, c1, cols = own_top.shape
    odd = jnp.concatenate([flags[0]] * (cols // LANES), axis=1) > 0.5
    not_top = jnp.concatenate([flags[1]] * (cols // LANES), axis=1)
    empty = jnp.zeros((c1, cols), jnp.float32)
    bias = bias_rows[:c1]
    rows = []
    for p in range(planes):
        lower, upper = far[p].astype(jnp.float32), near[p].astype(jnp.float32)
        before = own[p, :c1] + jnp.where(odd, upper[:c1], lower[:c1])
        top = own_top[p] + jnp.where(odd, upper[c1:], lower[c1:])
        bottom = own[p, c1:] + jnp.where(odd, lower[:c1], upper[:c1])
        rows += [jnp.maximum(before + bias, 0.0) * not_top]
        rows += [jnp.maximum(top + bias, 0.0), jnp.maximum(bottom + bias, 0.0), empty]
    cost = jnp.concatenate(rows, axis=0).astype(jnp.bfloat16)
    taken = jnp.dot(cost, choices[...], preferred_element_type=jnp.float32).astype(jnp.bfloat16)
    for q in range(planes // 2):
        out[q] = partial[q] + strided_planes(q, planes, taken, 4 * c1, kernel_two, out.shape[2])


def on_device(
    ref_features,
    source_tiles,
    pair_lists,
    view_counts,
    disparities,
    conv_first,
    bias_first,
    conv_second,
    bias_second,
):
    n_view = lax.axis_size("view")
    me = lax.axis_index("view").reshape(1)
    rows_n, channels, cols = ref_features.shape
    tiles_dev, tile_rows = source_tiles.shape[0], source_tiles.shape[1]
    sources, blocks = pair_lists.shape[1], pair_lists.shape[2]
    planes = disparities.shape[0]
    slab = tile_rows * channels
    c1, c2 = conv_first.shape[2], conv_second.shape[0]
    half_r, half_p, half_x = rows_n // 2, planes // 2, cols // 2
    smem = pl.BlockSpec(memory_space=pltpu.SMEM)
    vmem = pl.BlockSpec(memory_space=pltpu.VMEM)
    anywhere = pl.BlockSpec(memory_space=pl.ANY)
    params = pltpu.CompilerParams(vmem_limit_bytes=VMEM_LIMIT)
    bf16, f32, i32 = jnp.bfloat16, jnp.float32, jnp.int32
    shape = jax.ShapeDtypeStruct

    table = pl.pallas_call(
        functools.partial(request_kernel, tiles_dev),
        out_shape=shape((n_view, 1, 2 * CAP), i32),
        in_specs=[vmem],
        out_specs=vmem,
        compiler_params=params,
        name="request_table",
    )(pair_lists)
    table = lax.all_to_all(table, "view", split_axis=0, concat_axis=0, tiled=True)
    tiles = source_tiles.reshape(tiles_dev, slab, cols)
    table = table[:, 0, : CAP + 1].reshape(1, n_view * (CAP + 1))
    far_first = sorted(range(1, n_view), key=lambda k: -min(k, n_view - k))
    half = len(far_first) // 2
    order = [k for pair in zip(far_first[:half], far_first[half:]) for k in pair] + far_first[2 * half :]
    distances = order + [0]
    bundles = [None] * n_view
    gathered = pl.pallas_call(
        functools.partial(gather_kernel, distances, n_view),
        out_shape=[shape((CAP, slab, cols), bf16)] * n_view,
        in_specs=[smem, vmem],
        out_specs=[vmem] * n_view,
        compiler_params=params,
        name="requested_tiles",
    )(table, tiles)
    for k, bundle in zip(distances, gathered):
        pairs = [(i, (i + k) % n_view) for i in range(n_view)]
        bundles[k] = lax.ppermute(bundle, "view", pairs) if k else bundle

    at_slots = planes * sources
    at_live = at_slots + sources * blocks
    edge_blocks, mid_blocks = (0, blocks - 1), tuple(range(1, blocks - 1))
    rows_of = lambda picks: [block * tile_rows + i for block in picks for i in range(tile_rows)]
    edge_rows, mid_rows = rows_of(edge_blocks), rows_of(mid_blocks)
    inner = (rows_n - 2) * c1
    mid_deep, edge_deep = (-(-3 * rows // LANES) * LANES for rows in (inner, 4 * c1))
    prepared = pl.pallas_call(
        functools.partial(prepare_kernel, n_view, tiles_dev, edge_rows, mid_rows),
        out_shape=[
            shape((27 * c1 + 8, LANES), f32),
            shape((9 * (inner + c1), 2 * LANES), f32),
            shape((3 * half_r * c2, mid_deep), bf16),
            shape((3 * half_r * c2, edge_deep), bf16),
            shape((inner, cols), f32),
            shape((half_r * c2, half_x), f32),
            shape((LANES,), i32),
        ],
        in_specs=[vmem, vmem] + [smem] * 6,
        out_specs=[vmem] * 6 + [smem],
        scratch_shapes=[pltpu.VMEM((3 * mid_deep, LANES), f32), pltpu.VMEM((3 * edge_deep, LANES), f32)],
        compiler_params=params,
        name="weights_and_scalars",
    )(
        conv_first.transpose(0, 1, 3, 2, 4),
        conv_second.transpose(1, 2, 3, 4, 0),
        bias_first,
        bias_second,
        disparities,
        pair_lists,
        view_counts,
        me,
    )
    kernel_edge, kernel_mid, two_mid, two_edge, bias_rows, bias_two, scalars = prepared
    arrived = pl.pallas_call(
        functools.partial(collect_kernel, distances),
        out_shape=shape((n_view * CAP, slab, cols), bf16),
        in_specs=[vmem] * n_view,
        out_specs=vmem,
        compiler_params=params,
        name="all_tiles",
    )(*[bundles[k] for k in distances])

    band_scratch = [pltpu.VMEM((sources, cols + 2 * SHIFT, LANES), f32), pltpu.VMEM((1, cols, LANES), f32)]
    payload = shape((planes, 2 * c1, cols), bf16)
    col_step = (half_x // LANES + 1) * LANES
    edge_var, own, far, near, flags = pl.pallas_call(
        functools.partial(edge_kernel, at_slots, at_live, sources, blocks, edge_blocks),
        out_shape=[
            shape((planes, cols, LANES), bf16),
            shape((planes, 2 * c1, cols), f32),
            payload,
            payload,
            shape((2, c1, LANES), f32),
        ],
        in_specs=[vmem] * 3,
        out_specs=[vmem] * 5,
        scratch_shapes=band_scratch
        + [
            pltpu.VMEM((3, 9 * c1, cols), f32),
            pltpu.SMEM((1, LANES), f32),
            pltpu.SemaphoreType.DMA,
        ],
        compiler_params=params,
        name="edge_rows",
    )(kernel_edge, arrived, ref_features)
    far = swapped(far, "view", 1)
    near = swapped(near, "view", 0)

    partial, own_top, choices = pl.pallas_call(
        functools.partial(mid_kernel, at_slots, at_live, sources, blocks, mid_blocks),
        out_shape=[
            shape((half_p, half_r * c2, half_x), f32),
            shape((planes, c1, cols), f32),
            shape((cols, 2 * col_step), bf16),
        ],
        in_specs=[anywhere] + [vmem] * 7,
        out_specs=[vmem] * 3,
        scratch_shapes=band_scratch
        + [
            pltpu.VMEM((planes * inner, cols), bf16),
            pltpu.VMEM((3, 3 * (inner + c1), cols), f32),
            pltpu.SMEM(scalars.shape, i32),
            pltpu.SemaphoreType.DMA,
        ],
        compiler_params=params,
        name="middle_rows",
    )(scalars, arrived, ref_features, edge_var, kernel_mid, bias_rows, two_mid, bias_two)

    out = pl.pallas_call(
        end_kernel,
        out_shape=shape((half_p, half_r * c2, half_x), f32),
        in_specs=[vmem] * 9,
        out_specs=vmem,
        compiler_params=params,
        name="end_rows",
    )(far, near, flags, own, own_top, partial, bias_rows, two_edge, choices)
    return out.reshape(half_p, half_r, c2, half_x)


def solution(mesh):
    return jax.shard_map(
        on_device,
        mesh=mesh,
        in_specs=(
            P(("groups", "view"), None, None),
            P(("groups", "view"), None, None, None),
            P(("groups", "view"), None, None),
            P(("groups", "view")),
            P("groups", None),
            P(),
            P(),
            P(),
            P(),
        ),
        out_specs=P("groups", "view", None, None),
        check_vma=False,
    )
```

```python
import functools

import numpy as np

import jax
import jax.numpy as jnp
from jax import lax
from jax.experimental import pallas as pl
from jax.experimental.pallas import tpu as pltpu
from jax.sharding import PartitionSpec as P

SHIFT = 48
CAP = 2
LANES = 128
CHUNK = 64
VMEM_LIMIT = 10 * 1024 * 1024


def swapped(x, axis, parity):
    count = lax.axis_size(axis)
    pairs = [(i, i + 1) for i in range(parity, count - 1, 2)]
    return lax.ppermute(x, axis, pairs + [(j, i) for i, j in pairs])


def request_places(pair_lists, tiles_dev):
    owners, ranks, tiles = [], [], []
    for s in range(pair_lists.shape[1]):
        for b in range(pair_lists.shape[2]):
            tile = pair_lists[0, s, b]
            whole = jnp.maximum(tile, 0)
            owner = jnp.where(tile >= 0, lax.div(whole, tiles_dev), -1)
            rank = jnp.int32(0)
            for other in owners:
                rank = rank + jnp.where(other == owner, 1, 0)
            owners.append(owner)
            ranks.append(rank)
            tiles.append(lax.rem(whole, tiles_dev))
    return owners, ranks, tiles


def request_kernel(tiles_dev, pair_lists, table):
    n_view = table.shape[0]
    row = lax.broadcasted_iota(jnp.int32, (n_view, LANES), 0) * tiles_dev
    lane = lax.broadcasted_iota(jnp.int32, (n_view, LANES), 1)
    total = jnp.zeros((n_view, LANES), jnp.int32)
    count = jnp.zeros((n_view, LANES), jnp.int32)
    for s in range(pair_lists.shape[1]):
        for b in range(pair_lists.shape[2]):
            tile = pair_lists[0, s : s + 1, b : b + 1] - row
            owned = (tile >= 0) & (tile < tiles_dev)
            total = jnp.where(owned & (lane == count), tile, total)
            count = count + jnp.where(owned, 1, 0)
    total = jnp.where(lane == CAP, lax.broadcasted_iota(jnp.int32, (n_view, LANES), 0), total)
    for d in range(n_view):
        table[d] = total[d : d + 1, : table.shape[2]]


def gather_kernel(distances, n_view, table, tiles, *bundles):
    me = table[0, CAP]
    for k, bundle in zip(distances, bundles):
        at = lax.rem(me + k, n_view) * (CAP + 1)
        for j in range(CAP):
            bundle[j] = tiles[table[0, at + j]]


def collect_kernel(distances, *refs):
    arrived = refs[-1]
    for k, bundle in zip(distances, refs[:-1]):
        for j in range(CAP):
            arrived[k * CAP + j] = bundle[j]


def prepare_kernel(
    n_view,
    tiles_dev,
    edge_rows,
    mid_rows,
    first,
    second,
    bias_first,
    bias_second,
    disparities,
    pair_lists,
    view_counts,
    me,
    kernel_edge,
    kernel_mid,
    two_mid,
    two_edge,
    bias_rows,
    bias_two,
    scalars,
    stacked_mid,
    stacked_edge,
):
    planes, sources = disparities.shape
    owners, ranks, _ = request_places(pair_lists, tiles_dev)
    at = 0
    for p in range(planes):
        for s in range(sources):
            scalars[at] = disparities[p, s]
            at += 1
    for owner, rank in zip(owners, ranks):
        back = lax.rem(me[0] - owner + n_view, n_view)
        scalars[at] = jnp.where(owner >= 0, back * CAP + rank, 0)
        at += 1
    scalars[at] = view_counts[0]
    scalars[at + 1] = me[0]
    scalars[at + 2] = lax.rem(me[0], 2)
    tail = kernel_edge.shape[0] - 8
    lane_at = lax.broadcasted_iota(jnp.int32, (8, LANES), 1)
    numbers = jnp.zeros((8, LANES), jnp.float32)
    for i in range(at + 3):
        numbers = jnp.where(lane_at == i, scalars[i].astype(jnp.float32), numbers)
    kernel_edge[tail:, :] = numbers

    c1, channels = first.shape[3], first.shape[4]
    c2 = second.shape[4]
    rows_n = len(edge_rows) + len(mid_rows)
    half_r = rows_n // 2
    place = {row: i for i, row in enumerate(edge_rows + mid_rows)}
    per_group = LANES // channels
    filler = jnp.zeros((c1, LANES - channels), jnp.float32)
    taps = {}
    for a in range(3):
        for b in range(3):
            for d in range(3):
                tap = jnp.concatenate([first[a, b, d].astype(jnp.float32), filler], axis=1)
                for turn in range(per_group):
                    lane = turn * channels
                    taps[a, b, d, turn] = pltpu.roll(tap, lane, 1) if lane else tap

    def band(a, d, r, group):
        total = jnp.zeros((c1, LANES), jnp.float32)
        for b in range(3):
            at_place = place.get(r - 1 + b, -1)
            if at_place >= 0 and at_place // per_group == group:
                total = total + taps[a, b, d, at_place % per_group]
        return total

    rim = (-1, 0, rows_n - 1, rows_n)
    inner = tuple(range(1, rows_n - 1))
    for kernel, rows, groups in ((kernel_edge, (rim[0],) + rim[2:], 1), (kernel_mid, (0,) + inner, 2)):
        for d in range(3):
            for i, r in enumerate(rows):
                for a in range(3):
                    at = ((a * 3 + d) * len(rows) + i) * c1
                    for group in range(groups):
                        kernel[at : at + c1, group * LANES : (group + 1) * LANES] = band(a, d, r, group)

    def second_row(a, d, r):
        blocks = []
        for g in range(half_r):
            b = -1 if r is None else r - 2 * g + 1
            hit = 0 <= b < 3
            blocks.append(second[a, b, d].astype(jnp.float32) if hit else jnp.zeros((c1, c2), jnp.float32))
        blocks.append(jnp.zeros((c1, LANES - half_r * c2), jnp.float32))
        return jnp.concatenate(blocks, axis=1)

    for two, stacked, rows in ((two_mid, stacked_mid, inner), (two_edge, stacked_edge, rim[:3] + (None,))):
        deep = two.shape[1]
        stacked[...] = jnp.zeros(stacked.shape, jnp.float32)
        for a in range(3):
            for j, d in enumerate((1, 0, 2)):
                for i, r in enumerate(rows):
                    at = j * deep + (a * len(rows) + i) * c1
                    stacked[at : at + c1, :] = second_row(a, d, r)
        outs = half_r * c2
        for j in range(3):
            two[j * outs : (j + 1) * outs, :] = stacked[j * deep : (j + 1) * deep, :].T[:outs].astype(jnp.bfloat16)

    def spread_bias(like, bias):
        index = lax.broadcasted_iota(jnp.int32, like.shape, 0)
        total = jnp.zeros(like.shape, jnp.float32)
        for i in range(bias.shape[0]):
            total = jnp.where(index % bias.shape[0] == i, bias[i], total)
        like[...] = total

    spread_bias(bias_rows, bias_first)
    spread_bias(bias_two, bias_second)


def plane_variance(p, sources, cols, disp, wide, ref_wide, inv):
    chunks = []
    for x0 in range(0, cols, CHUNK):
        ref = ref_wide[0, x0 : x0 + CHUNK, :]
        summed = ref
        squares = ref * ref
        for s in range(sources):
            warped = wide[s, pl.ds(SHIFT + x0 - disp[p * sources + s], CHUNK), :]
            summed = summed + warped
            squares = squares + warped * warped
        chunks.append((squares - summed * summed * inv).astype(jnp.bfloat16))
    return jnp.concatenate(chunks, axis=0)


def view_weights(live):
    total = live.astype(jnp.float32) + jnp.ones((1, LANES), jnp.float32)
    return 1.0 / total, lax.rsqrt(total)


def turned_reference(ref, blocks, picks):
    tile_rows = ref.shape[0] // blocks
    rows = [ref[block * tile_rows + i] for block in picks for i in range(tile_rows)]
    return jnp.concatenate(rows, axis=0).T.astype(jnp.float32)


def clear_bands(wide, cols):
    band = jnp.zeros((SHIFT, LANES), jnp.float32)
    for at in range(wide.shape[0]):
        wide[at, 0:SHIFT, :] = band
        wide[at, SHIFT + cols : 2 * SHIFT + cols, :] = band


def load_tiles(at_slots, live, sources, blocks, picks, scale, scalars, arrived, wide):
    for s in range(sources):
        slab = jnp.concatenate([arrived[scalars[at_slots + s * blocks + block]] for block in picks], axis=0)
        cols = slab.shape[1]
        wide[s, SHIFT : SHIFT + cols, :] = slab.T.astype(jnp.float32) * jnp.where(s < live, scale, 0.0)


def add_plane(q, planes, lhs, weights, sums):
    taps = lax.dot_general(weights, lhs, (((1,), (1,)), ((), ())), preferred_element_type=jnp.float32)
    rows = taps.shape[0] // 3
    slots = sums.shape[0]
    if q + 1 < planes:
        sums[(q + 1) % slots] = taps[:rows]
    if q == 0:
        sums[q % slots] = taps[rows : 2 * rows]
    else:
        sums[q % slots] += taps[rows : 2 * rows]
        sums[(q - 1) % slots] += taps[2 * rows :]


def joined_columns(taps, column):
    rows, cols = column.shape
    left, center, right = taps[:rows], taps[rows : 2 * rows], taps[2 * rows :]
    total = center + jnp.where(column > 0, pltpu.roll(left, 1, 1), 0.0)
    return total + jnp.where(column < cols - 1, pltpu.roll(right, cols - 1, 1), 0.0)


def strided_planes(q, planes, taken, rows, weights, out_w):
    step = taken.shape[1] // 2
    none = jnp.zeros((rows, 2 * step), jnp.bfloat16)
    near = range(2 * q - 1, 2 * q + 2)
    parts = [taken[p * rows : (p + 1) * rows] if 0 <= p < planes else none for p in near]
    rhs = jnp.concatenate(parts, axis=0)
    deep = rhs.shape[0]
    outs = weights.shape[0] // 3
    even = jnp.dot(weights[:outs, :deep], rhs[:, :step], preferred_element_type=jnp.float32)
    odd = jnp.dot(weights[outs:, :deep], rhs[:, step:], preferred_element_type=jnp.float32)
    result = even + pltpu.roll(odd[:outs], 1, 1) + odd[outs:]
    return result[:, :out_w]


def edge_kernel(
    at_slots, at_live, sources, blocks, picks, packed, arrived, ref, var, own, far, near, flags, wide, ref_wide, sums, held, sem
):
    planes, cols, _ = var.shape
    tail = packed.shape[0] - 8
    c1 = tail // 27
    copy = pltpu.make_async_copy(packed.at[pl.ds(tail, 1)], held, sem)
    copy.start()
    weights = packed[:tail].astype(jnp.bfloat16)
    turned = turned_reference(ref, blocks, picks)
    clear_bands(wide, cols)
    copy.wait()
    scalars = [held[0, i].astype(jnp.int32) for i in range(at_live + 3)]
    live = scalars[at_live]
    inv, scale = view_weights(live)
    ref_wide[0] = turned * scale
    load_tiles(at_slots, live, sources, blocks, picks, scale, scalars, arrived, wide)
    odd = scalars[at_live + 2] > 0
    flags[0] = jnp.where(odd, 1.0, 0.0) * jnp.ones((c1, LANES), jnp.float32)
    flags[1] = jnp.where(scalars[at_live + 1] > 0, 1.0, 0.0) * jnp.ones((c1, LANES), jnp.float32)
    column = lax.broadcasted_iota(jnp.int32, (3 * c1, cols), 1)
    empty = jnp.zeros((c1, cols), jnp.float32)

    def finish(p):
        total = joined_columns(sums[p % sums.shape[0]], column)
        own[p] = total[: 2 * c1]
        downward = total[c1:]
        upward = jnp.concatenate([total[:c1], empty], axis=0)
        far[p] = jnp.where(odd, downward, upward).astype(jnp.bfloat16)
        near[p] = jnp.where(odd, upward, downward).astype(jnp.bfloat16)

    values = plane_variance(0, sources, cols, scalars, wide, ref_wide, inv)
    for q in range(planes):
        held_values = values
        if q + 1 < planes:
            values = plane_variance(q + 1, sources, cols, scalars, wide, ref_wide, inv)
        add_plane(q, planes, held_values, weights, sums)
        var[q] = held_values
        if q > 0:
            finish(q - 1)
    finish(planes - 1)


def mid_kernel(
    at_slots,
    at_live,
    sources,
    blocks,
    picks,
    numbers,
    arrived,
    ref,
    edge_var,
    kernel,
    bias_rows,
    kernel_two,
    bias_two,
    out,
    own,
    choices,
    wide,
    ref_wide,
    cost,
    sums,
    scalars,
    sem,
):
    copy = pltpu.make_async_copy(numbers, scalars, sem)
    copy.start()
    planes, cols, _ = edge_var.shape
    inner = cost.shape[0] // planes
    step = choices.shape[1] // 2
    row = lax.broadcasted_iota(jnp.int32, (cols, step), 0)
    target = 2 * lax.broadcasted_iota(jnp.int32, (cols, step), 1)
    for odd in range(2):
        choices[:, odd * step : (odd + 1) * step] = jnp.where(row == target + odd, 1.0, 0.0).astype(jnp.bfloat16)
    turned = turned_reference(ref, blocks, picks)
    clear_bands(wide, cols)
    copy.wait()
    live = scalars[at_live]
    inv, scale = view_weights(live)
    ref_wide[0] = turned * scale
    load_tiles(at_slots, live, sources, blocks, picks, scale, scalars, arrived, wide)
    weights = kernel[...].astype(jnp.bfloat16)
    bias = bias_rows[:inner]
    ready, cols = own.shape[1:]
    column = lax.broadcasted_iota(jnp.int32, (ready + inner, cols), 1)

    def finish(p):
        total = joined_columns(sums[p % sums.shape[0]], column)
        own[p] = total[:ready]
        cost[p * inner : (p + 1) * inner, :] = jnp.maximum(total[ready:] + bias, 0.0).astype(jnp.bfloat16)

    values = plane_variance(0, sources, cols, scalars, wide, ref_wide, inv)
    for q in range(planes):
        held_values = values
        if q + 1 < planes:
            values = plane_variance(q + 1, sources, cols, scalars, wide, ref_wide, inv)
        add_plane(q, planes, jnp.concatenate([edge_var[q], held_values], axis=1), weights, sums)
        if q > 0:
            finish(q - 1)
    finish(planes - 1)
    taken = jnp.dot(cost[...], choices[...], preferred_element_type=jnp.float32).astype(jnp.bfloat16)
    for q in range(planes // 2):
        out[q] = strided_planes(q, planes, taken, inner, kernel_two, out.shape[2]) + bias_two[...]


def end_kernel(far, near, flags, own, own_top, partial, bias_rows, kernel_two, choices, out):
    planes, c1, cols = own_top.shape
    odd = jnp.concatenate([flags[0]] * (cols // LANES), axis=1) > 0.5
    not_top = jnp.concatenate([flags[1]] * (cols // LANES), axis=1)
    empty = jnp.zeros((c1, cols), jnp.float32)
    bias = bias_rows[:c1]
    rows = []
    for p in range(planes):
        lower, upper = far[p].astype(jnp.float32), near[p].astype(jnp.float32)
        before = own[p, :c1] + jnp.where(odd, upper[:c1], lower[:c1])
        top = own_top[p] + jnp.where(odd, upper[c1:], lower[c1:])
        bottom = own[p, c1:] + jnp.where(odd, lower[:c1], upper[:c1])
        rows += [jnp.maximum(before + bias, 0.0) * not_top]
        rows += [jnp.maximum(top + bias, 0.0), jnp.maximum(bottom + bias, 0.0), empty]
    cost = jnp.concatenate(rows, axis=0).astype(jnp.bfloat16)
    taken = jnp.dot(cost, choices[...], preferred_element_type=jnp.float32).astype(jnp.bfloat16)
    for q in range(planes // 2):
        out[q] = partial[q] + strided_planes(q, planes, taken, 4 * c1, kernel_two, out.shape[2])


def on_device(
    ref_features,
    source_tiles,
    pair_lists,
    view_counts,
    disparities,
    conv_first,
    bias_first,
    conv_second,
    bias_second,
):
    n_view = lax.axis_size("view")
    me = lax.axis_index("view").reshape(1)
    rows_n, channels, cols = ref_features.shape
    tiles_dev, tile_rows = source_tiles.shape[0], source_tiles.shape[1]
    sources, blocks = pair_lists.shape[1], pair_lists.shape[2]
    planes = disparities.shape[0]
    slab = tile_rows * channels
    c1, c2 = conv_first.shape[2], conv_second.shape[0]
    half_r, half_p, half_x = rows_n // 2, planes // 2, cols // 2
    smem = pl.BlockSpec(memory_space=pltpu.SMEM)
    vmem = pl.BlockSpec(memory_space=pltpu.VMEM)
    anywhere = pl.BlockSpec(memory_space=pl.ANY)
    params = pltpu.CompilerParams(vmem_limit_bytes=VMEM_LIMIT)
    bf16, f32, i32 = jnp.bfloat16, jnp.float32, jnp.int32
    shape = jax.ShapeDtypeStruct

    table = pl.pallas_call(
        functools.partial(request_kernel, tiles_dev),
        out_shape=shape((n_view, 1, 2 * CAP), i32),
        in_specs=[vmem],
        out_specs=vmem,
        compiler_params=params,
        name="request_table",
    )(pair_lists)
    table = lax.all_to_all(table, "view", split_axis=0, concat_axis=0, tiled=True)
    tiles = source_tiles.reshape(tiles_dev, slab, cols)
    table = table[:, 0, : CAP + 1].reshape(1, n_view * (CAP + 1))
    far_first = sorted(range(1, n_view), key=lambda k: -min(k, n_view - k))
    order = [k for pair in zip(far_first[::-1], far_first) for k in pair][: len(far_first)]
    distances = order + [0]
    bundles = [None] * n_view
    gathered = pl.pallas_call(
        functools.partial(gather_kernel, distances, n_view),
        out_shape=[shape((CAP, slab, cols), bf16)] * n_view,
        in_specs=[smem, vmem],
        out_specs=[vmem] * n_view,
        compiler_params=params,
        name="requested_tiles",
    )(table, tiles)
    for k, bundle in zip(distances, gathered):
        pairs = [(i, (i + k) % n_view) for i in range(n_view)]
        bundles[k] = lax.ppermute(bundle, "view", pairs) if k else bundle

    at_slots = planes * sources
    at_live = at_slots + sources * blocks
    edge_blocks, mid_blocks = (0, blocks - 1), tuple(range(1, blocks - 1))
    rows_of = lambda picks: [block * tile_rows + i for block in picks for i in range(tile_rows)]
    edge_rows, mid_rows = rows_of(edge_blocks), rows_of(mid_blocks)
    inner = (rows_n - 2) * c1
    mid_deep, edge_deep = (-(-3 * rows // LANES) * LANES for rows in (inner, 4 * c1))
    prepared = pl.pallas_call(
        functools.partial(prepare_kernel, n_view, tiles_dev, edge_rows, mid_rows),
        out_shape=[
            shape((27 * c1 + 8, LANES), f32),
            shape((9 * (inner + c1), 2 * LANES), f32),
            shape((3 * half_r * c2, mid_deep), bf16),
            shape((3 * half_r * c2, edge_deep), bf16),
            shape((inner, cols), f32),
            shape((half_r * c2, half_x), f32),
            shape((LANES,), i32),
        ],
        in_specs=[vmem, vmem] + [smem] * 6,
        out_specs=[vmem] * 6 + [smem],
        scratch_shapes=[pltpu.VMEM((3 * mid_deep, LANES), f32), pltpu.VMEM((3 * edge_deep, LANES), f32)],
        compiler_params=params,
        name="weights_and_scalars",
    )(
        conv_first.transpose(0, 1, 3, 2, 4),
        conv_second.transpose(1, 2, 3, 4, 0),
        bias_first,
        bias_second,
        disparities,
        pair_lists,
        view_counts,
        me,
    )
    kernel_edge, kernel_mid, two_mid, two_edge, bias_rows, bias_two, scalars = prepared
    arrived = pl.pallas_call(
        functools.partial(collect_kernel, distances),
        out_shape=shape((n_view * CAP, slab, cols), bf16),
        in_specs=[vmem] * n_view,
        out_specs=vmem,
        compiler_params=params,
        name="all_tiles",
    )(*[bundles[k] for k in distances])

    band_scratch = [pltpu.VMEM((sources, cols + 2 * SHIFT, LANES), f32), pltpu.VMEM((1, cols, LANES), f32)]
    payload = shape((planes, 2 * c1, cols), bf16)
    col_step = (half_x // LANES + 1) * LANES
    edge_var, own, far, near, flags = pl.pallas_call(
        functools.partial(edge_kernel, at_slots, at_live, sources, blocks, edge_blocks),
        out_shape=[
            shape((planes, cols, LANES), bf16),
            shape((planes, 2 * c1, cols), f32),
            payload,
            payload,
            shape((2, c1, LANES), f32),
        ],
        in_specs=[vmem] * 3,
        out_specs=[vmem] * 5,
        scratch_shapes=band_scratch
        + [
            pltpu.VMEM((3, 9 * c1, cols), f32),
            pltpu.SMEM((1, LANES), f32),
            pltpu.SemaphoreType.DMA,
        ],
        compiler_params=params,
        name="edge_rows",
    )(kernel_edge, arrived, ref_features)
    far = swapped(far, "view", 1)
    near = swapped(near, "view", 0)

    partial, own_top, choices = pl.pallas_call(
        functools.partial(mid_kernel, at_slots, at_live, sources, blocks, mid_blocks),
        out_shape=[
            shape((half_p, half_r * c2, half_x), f32),
            shape((planes, c1, cols), f32),
            shape((cols, 2 * col_step), bf16),
        ],
        in_specs=[anywhere] + [vmem] * 7,
        out_specs=[vmem] * 3,
        scratch_shapes=band_scratch
        + [
            pltpu.VMEM((planes * inner, cols), bf16),
            pltpu.VMEM((3, 3 * (inner + c1), cols), f32),
            pltpu.SMEM(scalars.shape, i32),
            pltpu.SemaphoreType.DMA,
        ],
        compiler_params=params,
        name="middle_rows",
    )(scalars, arrived, ref_features, edge_var, kernel_mid, bias_rows, two_mid, bias_two)

    out = pl.pallas_call(
        end_kernel,
        out_shape=shape((half_p, half_r * c2, half_x), f32),
        in_specs=[vmem] * 9,
        out_specs=vmem,
        compiler_params=params,
        name="end_rows",
    )(far, near, flags, own, own_top, partial, bias_rows, two_edge, choices)
    return out.reshape(half_p, half_r, c2, half_x)


def solution(mesh):
    return jax.shard_map(
        on_device,
        mesh=mesh,
        in_specs=(
            P(("groups", "view"), None, None),
            P(("groups", "view"), None, None, None),
            P(("groups", "view"), None, None),
            P(("groups", "view")),
            P("groups", None),
            P(),
            P(),
            P(),
            P(),
        ),
        out_specs=P("groups", "view", None, None),
        check_vma=False,
    )
```

```python
import functools

import numpy as np

import jax
import jax.numpy as jnp
from jax import lax
from jax.experimental import pallas as pl
from jax.experimental.pallas import tpu as pltpu
from jax.sharding import PartitionSpec as P

SHIFT = 48
CAP = 2
LANES = 128
CHUNK = 32
VMEM_LIMIT = 10 * 1024 * 1024


def swapped(x, axis, parity):
    count = lax.axis_size(axis)
    pairs = [(i, i + 1) for i in range(parity, count - 1, 2)]
    return lax.ppermute(x, axis, pairs + [(j, i) for i, j in pairs])


def request_places(pair_lists, tiles_dev):
    owners, ranks, tiles = [], [], []
    for s in range(pair_lists.shape[1]):
        for b in range(pair_lists.shape[2]):
            tile = pair_lists[0, s, b]
            whole = jnp.maximum(tile, 0)
            owner = jnp.where(tile >= 0, lax.div(whole, tiles_dev), -1)
            rank = jnp.int32(0)
            for other in owners:
                rank = rank + jnp.where(other == owner, 1, 0)
            owners.append(owner)
            ranks.append(rank)
            tiles.append(lax.rem(whole, tiles_dev))
    return owners, ranks, tiles


def request_kernel(tiles_dev, pair_lists, table):
    n_view = table.shape[0]
    row = lax.broadcasted_iota(jnp.int32, (n_view, LANES), 0) * tiles_dev
    lane = lax.broadcasted_iota(jnp.int32, (n_view, LANES), 1)
    total = jnp.zeros((n_view, LANES), jnp.int32)
    count = jnp.zeros((n_view, LANES), jnp.int32)
    for s in range(pair_lists.shape[1]):
        for b in range(pair_lists.shape[2]):
            tile = pair_lists[0, s : s + 1, b : b + 1] - row
            owned = (tile >= 0) & (tile < tiles_dev)
            total = jnp.where(owned & (lane == count), tile, total)
            count = count + jnp.where(owned, 1, 0)
    total = jnp.where(lane == CAP, lax.broadcasted_iota(jnp.int32, (n_view, LANES), 0), total)
    for d in range(n_view):
        table[d] = total[d : d + 1, : table.shape[2]]


def gather_kernel(distances, n_view, table, tiles, *bundles):
    me = table[0, CAP]
    for k, bundle in zip(distances, bundles):
        at = lax.rem(me + k, n_view) * (CAP + 1)
        for j in range(CAP):
            bundle[j] = tiles[table[0, at + j]]


def collect_kernel(distances, *refs):
    arrived = refs[-1]
    for k, bundle in zip(distances, refs[:-1]):
        for j in range(CAP):
            arrived[k * CAP + j] = bundle[j]


def prepare_kernel(
    n_view,
    tiles_dev,
    edge_rows,
    mid_rows,
    first,
    second,
    bias_first,
    bias_second,
    disparities,
    pair_lists,
    view_counts,
    me,
    kernel_edge,
    kernel_mid,
    two_mid,
    two_edge,
    bias_rows,
    bias_two,
    scalars,
    stacked_mid,
    stacked_edge,
):
    planes, sources = disparities.shape
    owners, ranks, _ = request_places(pair_lists, tiles_dev)
    at = 0
    for p in range(planes):
        for s in range(sources):
            scalars[at] = disparities[p, s]
            at += 1
    for owner, rank in zip(owners, ranks):
        back = lax.rem(me[0] - owner + n_view, n_view)
        scalars[at] = jnp.where(owner >= 0, back * CAP + rank, 0)
        at += 1
    scalars[at] = view_counts[0]
    scalars[at + 1] = me[0]
    scalars[at + 2] = lax.rem(me[0], 2)
    tail = kernel_edge.shape[0] - 8
    lane_at = lax.broadcasted_iota(jnp.int32, (8, LANES), 1)
    numbers = jnp.zeros((8, LANES), jnp.float32)
    for i in range(at + 3):
        numbers = jnp.where(lane_at == i, scalars[i].astype(jnp.float32), numbers)
    kernel_edge[tail:, :] = numbers

    c1, channels = first.shape[3], first.shape[4]
    c2 = second.shape[4]
    rows_n = len(edge_rows) + len(mid_rows)
    half_r = rows_n // 2
    place = {row: i for i, row in enumerate(edge_rows + mid_rows)}
    per_group = LANES // channels
    filler = jnp.zeros((c1, LANES - channels), jnp.float32)
    taps = {}
    for a in range(3):
        for b in range(3):
            for d in range(3):
                tap = jnp.concatenate([first[a, b, d].astype(jnp.float32), filler], axis=1)
                for turn in range(per_group):
                    lane = turn * channels
                    taps[a, b, d, turn] = pltpu.roll(tap, lane, 1) if lane else tap

    def band(a, d, r, group):
        total = jnp.zeros((c1, LANES), jnp.float32)
        for b in range(3):
            at_place = place.get(r - 1 + b, -1)
            if at_place >= 0 and at_place // per_group == group:
                total = total + taps[a, b, d, at_place % per_group]
        return total

    rim = (-1, 0, rows_n - 1, rows_n)
    inner = tuple(range(1, rows_n - 1))
    for kernel, rows, groups in ((kernel_edge, (rim[0],) + rim[2:], 1), (kernel_mid, (0,) + inner, 2)):
        for d in range(3):
            for i, r in enumerate(rows):
                for a in range(3):
                    at = ((a * 3 + d) * len(rows) + i) * c1
                    for group in range(groups):
                        kernel[at : at + c1, group * LANES : (group + 1) * LANES] = band(a, d, r, group)

    def second_row(a, d, r):
        blocks = []
        for g in range(half_r):
            b = -1 if r is None else r - 2 * g + 1
            hit = 0 <= b < 3
            blocks.append(second[a, b, d].astype(jnp.float32) if hit else jnp.zeros((c1, c2), jnp.float32))
        blocks.append(jnp.zeros((c1, LANES - half_r * c2), jnp.float32))
        return jnp.concatenate(blocks, axis=1)

    for two, stacked, rows in ((two_mid, stacked_mid, inner), (two_edge, stacked_edge, rim[:3] + (None,))):
        deep = two.shape[1]
        stacked[...] = jnp.zeros(stacked.shape, jnp.float32)
        for a in range(3):
            for j, d in enumerate((1, 0, 2)):
                for i, r in enumerate(rows):
                    at = j * deep + (a * len(rows) + i) * c1
                    stacked[at : at + c1, :] = second_row(a, d, r)
        outs = half_r * c2
        for j in range(3):
            two[j * outs : (j + 1) * outs, :] = stacked[j * deep : (j + 1) * deep, :].T[:outs].astype(jnp.bfloat16)

    def spread_bias(like, bias):
        index = lax.broadcasted_iota(jnp.int32, like.shape, 0)
        total = jnp.zeros(like.shape, jnp.float32)
        for i in range(bias.shape[0]):
            total = jnp.where(index % bias.shape[0] == i, bias[i], total)
        like[...] = total

    spread_bias(bias_rows, bias_first)
    spread_bias(bias_two, bias_second)


def plane_variance(p, sources, cols, disp, wide, ref_wide, inv):
    chunks = []
    for x0 in range(0, cols, CHUNK):
        ref = ref_wide[0, x0 : x0 + CHUNK, :]
        summed = ref
        squares = ref * ref
        for s in range(sources):
            warped = wide[s, pl.ds(SHIFT + x0 - disp[p * sources + s], CHUNK), :]
            summed = summed + warped
            squares = squares + warped * warped
        chunks.append((squares - summed * summed * inv).astype(jnp.bfloat16))
    return jnp.concatenate(chunks, axis=0)


def view_weights(live):
    total = live.astype(jnp.float32) + jnp.ones((1, LANES), jnp.float32)
    return 1.0 / total, lax.rsqrt(total)


def turned_reference(ref, blocks, picks):
    tile_rows = ref.shape[0] // blocks
    rows = [ref[block * tile_rows + i] for block in picks for i in range(tile_rows)]
    return jnp.concatenate(rows, axis=0).T.astype(jnp.float32)


def clear_bands(wide, cols):
    band = jnp.zeros((SHIFT, LANES), jnp.float32)
    for at in range(wide.shape[0]):
        wide[at, 0:SHIFT, :] = band
        wide[at, SHIFT + cols : 2 * SHIFT + cols, :] = band


def load_tiles(at_slots, live, sources, blocks, picks, scale, scalars, arrived, wide):
    for s in range(sources):
        slab = jnp.concatenate([arrived[scalars[at_slots + s * blocks + block]] for block in picks], axis=0)
        cols = slab.shape[1]
        wide[s, SHIFT : SHIFT + cols, :] = slab.T.astype(jnp.float32) * jnp.where(s < live, scale, 0.0)


def add_plane(q, planes, lhs, weights, sums):
    taps = lax.dot_general(weights, lhs, (((1,), (1,)), ((), ())), preferred_element_type=jnp.float32)
    rows = taps.shape[0] // 3
    slots = sums.shape[0]
    if q + 1 < planes:
        sums[(q + 1) % slots] = taps[:rows]
    if q == 0:
        sums[q % slots] = taps[rows : 2 * rows]
    else:
        sums[q % slots] += taps[rows : 2 * rows]
        sums[(q - 1) % slots] += taps[2 * rows :]


def joined_columns(taps, column):
    rows, cols = column.shape
    left, center, right = taps[:rows], taps[rows : 2 * rows], taps[2 * rows :]
    total = center + jnp.where(column > 0, pltpu.roll(left, 1, 1), 0.0)
    return total + jnp.where(column < cols - 1, pltpu.roll(right, cols - 1, 1), 0.0)


def strided_planes(q, planes, taken, rows, weights, out_w):
    step = taken.shape[1] // 2
    none = jnp.zeros((rows, 2 * step), jnp.bfloat16)
    near = range(2 * q - 1, 2 * q + 2)
    parts = [taken[p * rows : (p + 1) * rows] if 0 <= p < planes else none for p in near]
    rhs = jnp.concatenate(parts, axis=0)
    deep = rhs.shape[0]
    outs = weights.shape[0] // 3
    even = jnp.dot(weights[:outs, :deep], rhs[:, :step], preferred_element_type=jnp.float32)
    odd = jnp.dot(weights[outs:, :deep], rhs[:, step:], preferred_element_type=jnp.float32)
    result = even + pltpu.roll(odd[:outs], 1, 1) + odd[outs:]
    return result[:, :out_w]


def edge_kernel(
    at_slots, at_live, sources, blocks, picks, packed, arrived, ref, var, own, far, near, flags, wide, ref_wide, sums, held, sem
):
    planes, cols, _ = var.shape
    tail = packed.shape[0] - 8
    c1 = tail // 27
    copy = pltpu.make_async_copy(packed.at[pl.ds(tail, 1)], held, sem)
    copy.start()
    weights = packed[:tail].astype(jnp.bfloat16)
    turned = turned_reference(ref, blocks, picks)
    clear_bands(wide, cols)
    copy.wait()
    scalars = [held[0, i].astype(jnp.int32) for i in range(at_live + 3)]
    live = scalars[at_live]
    inv, scale = view_weights(live)
    ref_wide[0] = turned * scale
    load_tiles(at_slots, live, sources, blocks, picks, scale, scalars, arrived, wide)
    odd = scalars[at_live + 2] > 0
    flags[0] = jnp.where(odd, 1.0, 0.0) * jnp.ones((c1, LANES), jnp.float32)
    flags[1] = jnp.where(scalars[at_live + 1] > 0, 1.0, 0.0) * jnp.ones((c1, LANES), jnp.float32)
    column = lax.broadcasted_iota(jnp.int32, (3 * c1, cols), 1)
    empty = jnp.zeros((c1, cols), jnp.float32)

    def finish(p):
        total = joined_columns(sums[p % sums.shape[0]], column)
        own[p] = total[: 2 * c1]
        downward = total[c1:]
        upward = jnp.concatenate([total[:c1], empty], axis=0)
        far[p] = jnp.where(odd, downward, upward).astype(jnp.bfloat16)
        near[p] = jnp.where(odd, upward, downward).astype(jnp.bfloat16)

    values = plane_variance(0, sources, cols, scalars, wide, ref_wide, inv)
    for q in range(planes):
        held_values = values
        if q + 1 < planes:
            values = plane_variance(q + 1, sources, cols, scalars, wide, ref_wide, inv)
        add_plane(q, planes, held_values, weights, sums)
        var[q] = held_values
        if q > 0:
            finish(q - 1)
    finish(planes - 1)


def mid_kernel(
    at_slots,
    at_live,
    sources,
    blocks,
    picks,
    numbers,
    arrived,
    ref,
    edge_var,
    kernel,
    bias_rows,
    kernel_two,
    bias_two,
    out,
    own,
    choices,
    wide,
    ref_wide,
    cost,
    sums,
    scalars,
    sem,
):
    copy = pltpu.make_async_copy(numbers, scalars, sem)
    copy.start()
    planes, cols, _ = edge_var.shape
    inner = cost.shape[0] // planes
    step = choices.shape[1] // 2
    row = lax.broadcasted_iota(jnp.int32, (cols, step), 0)
    target = 2 * lax.broadcasted_iota(jnp.int32, (cols, step), 1)
    for odd in range(2):
        choices[:, odd * step : (odd + 1) * step] = jnp.where(row == target + odd, 1.0, 0.0).astype(jnp.bfloat16)
    turned = turned_reference(ref, blocks, picks)
    clear_bands(wide, cols)
    copy.wait()
    live = scalars[at_live]
    inv, scale = view_weights(live)
    ref_wide[0] = turned * scale
    load_tiles(at_slots, live, sources, blocks, picks, scale, scalars, arrived, wide)
    weights = kernel[...].astype(jnp.bfloat16)
    bias = bias_rows[:inner]
    ready, cols = own.shape[1:]
    column = lax.broadcasted_iota(jnp.int32, (ready + inner, cols), 1)

    def finish(p):
        total = joined_columns(sums[p % sums.shape[0]], column)
        own[p] = total[:ready]
        cost[p * inner : (p + 1) * inner, :] = jnp.maximum(total[ready:] + bias, 0.0).astype(jnp.bfloat16)

    values = plane_variance(0, sources, cols, scalars, wide, ref_wide, inv)
    for q in range(planes):
        held_values = values
        if q + 1 < planes:
            values = plane_variance(q + 1, sources, cols, scalars, wide, ref_wide, inv)
        add_plane(q, planes, jnp.concatenate([edge_var[q], held_values], axis=1), weights, sums)
        if q > 0:
            finish(q - 1)
    finish(planes - 1)
    taken = jnp.dot(cost[...], choices[...], preferred_element_type=jnp.float32).astype(jnp.bfloat16)
    for q in range(planes // 2):
        out[q] = strided_planes(q, planes, taken, inner, kernel_two, out.shape[2]) + bias_two[...]


def end_kernel(far, near, flags, own, own_top, partial, bias_rows, kernel_two, choices, out):
    planes, c1, cols = own_top.shape
    odd = jnp.concatenate([flags[0]] * (cols // LANES), axis=1) > 0.5
    not_top = jnp.concatenate([flags[1]] * (cols // LANES), axis=1)
    empty = jnp.zeros((c1, cols), jnp.float32)
    bias = bias_rows[:c1]
    rows = []
    for p in range(planes):
        lower, upper = far[p].astype(jnp.float32), near[p].astype(jnp.float32)
        before = own[p, :c1] + jnp.where(odd, upper[:c1], lower[:c1])
        top = own_top[p] + jnp.where(odd, upper[c1:], lower[c1:])
        bottom = own[p, c1:] + jnp.where(odd, lower[:c1], upper[:c1])
        rows += [jnp.maximum(before + bias, 0.0) * not_top]
        rows += [jnp.maximum(top + bias, 0.0), jnp.maximum(bottom + bias, 0.0), empty]
    cost = jnp.concatenate(rows, axis=0).astype(jnp.bfloat16)
    taken = jnp.dot(cost, choices[...], preferred_element_type=jnp.float32).astype(jnp.bfloat16)
    for q in range(planes // 2):
        out[q] = partial[q] + strided_planes(q, planes, taken, 4 * c1, kernel_two, out.shape[2])


def on_device(
    ref_features,
    source_tiles,
    pair_lists,
    view_counts,
    disparities,
    conv_first,
    bias_first,
    conv_second,
    bias_second,
):
    n_view = lax.axis_size("view")
    me = lax.axis_index("view").reshape(1)
    rows_n, channels, cols = ref_features.shape
    tiles_dev, tile_rows = source_tiles.shape[0], source_tiles.shape[1]
    sources, blocks = pair_lists.shape[1], pair_lists.shape[2]
    planes = disparities.shape[0]
    slab = tile_rows * channels
    c1, c2 = conv_first.shape[2], conv_second.shape[0]
    half_r, half_p, half_x = rows_n // 2, planes // 2, cols // 2
    smem = pl.BlockSpec(memory_space=pltpu.SMEM)
    vmem = pl.BlockSpec(memory_space=pltpu.VMEM)
    anywhere = pl.BlockSpec(memory_space=pl.ANY)
    params = pltpu.CompilerParams(vmem_limit_bytes=VMEM_LIMIT)
    bf16, f32, i32 = jnp.bfloat16, jnp.float32, jnp.int32
    shape = jax.ShapeDtypeStruct

    table = pl.pallas_call(
        functools.partial(request_kernel, tiles_dev),
        out_shape=shape((n_view, 1, 2 * CAP), i32),
        in_specs=[vmem],
        out_specs=vmem,
        compiler_params=params,
        name="request_table",
    )(pair_lists)
    table = lax.all_to_all(table, "view", split_axis=0, concat_axis=0, tiled=True)
    tiles = source_tiles.reshape(tiles_dev, slab, cols)
    table = table[:, 0, : CAP + 1].reshape(1, n_view * (CAP + 1))
    far_first = sorted(range(1, n_view), key=lambda k: -min(k, n_view - k))
    order = [k for pair in zip(far_first[::-1], far_first) for k in pair][: len(far_first)]
    distances = order + [0]
    bundles = [None] * n_view
    gathered = pl.pallas_call(
        functools.partial(gather_kernel, distances, n_view),
        out_shape=[shape((CAP, slab, cols), bf16)] * n_view,
        in_specs=[smem, vmem],
        out_specs=[vmem] * n_view,
        compiler_params=params,
        name="requested_tiles",
    )(table, tiles)
    for k, bundle in zip(distances, gathered):
        pairs = [(i, (i + k) % n_view) for i in range(n_view)]
        bundles[k] = lax.ppermute(bundle, "view", pairs) if k else bundle

    at_slots = planes * sources
    at_live = at_slots + sources * blocks
    edge_blocks, mid_blocks = (0, blocks - 1), tuple(range(1, blocks - 1))
    rows_of = lambda picks: [block * tile_rows + i for block in picks for i in range(tile_rows)]
    edge_rows, mid_rows = rows_of(edge_blocks), rows_of(mid_blocks)
    inner = (rows_n - 2) * c1
    mid_deep, edge_deep = (-(-3 * rows // LANES) * LANES for rows in (inner, 4 * c1))
    prepared = pl.pallas_call(
        functools.partial(prepare_kernel, n_view, tiles_dev, edge_rows, mid_rows),
        out_shape=[
            shape((27 * c1 + 8, LANES), f32),
            shape((9 * (inner + c1), 2 * LANES), f32),
            shape((3 * half_r * c2, mid_deep), bf16),
            shape((3 * half_r * c2, edge_deep), bf16),
            shape((inner, cols), f32),
            shape((half_r * c2, half_x), f32),
            shape((LANES,), i32),
        ],
        in_specs=[vmem, vmem] + [smem] * 6,
        out_specs=[vmem] * 6 + [smem],
        scratch_shapes=[pltpu.VMEM((3 * mid_deep, LANES), f32), pltpu.VMEM((3 * edge_deep, LANES), f32)],
        compiler_params=params,
        name="weights_and_scalars",
    )(
        conv_first.transpose(0, 1, 3, 2, 4),
        conv_second.transpose(1, 2, 3, 4, 0),
        bias_first,
        bias_second,
        disparities,
        pair_lists,
        view_counts,
        me,
    )
    kernel_edge, kernel_mid, two_mid, two_edge, bias_rows, bias_two, scalars = prepared
    arrived = pl.pallas_call(
        functools.partial(collect_kernel, distances),
        out_shape=shape((n_view * CAP, slab, cols), bf16),
        in_specs=[vmem] * n_view,
        out_specs=vmem,
        compiler_params=params,
        name="all_tiles",
    )(*[bundles[k] for k in distances])

    band_scratch = [pltpu.VMEM((sources, cols + 2 * SHIFT, LANES), f32), pltpu.VMEM((1, cols, LANES), f32)]
    payload = shape((planes, 2 * c1, cols), bf16)
    col_step = (half_x // LANES + 1) * LANES
    edge_var, own, far, near, flags = pl.pallas_call(
        functools.partial(edge_kernel, at_slots, at_live, sources, blocks, edge_blocks),
        out_shape=[
            shape((planes, cols, LANES), bf16),
            shape((planes, 2 * c1, cols), f32),
            payload,
            payload,
            shape((2, c1, LANES), f32),
        ],
        in_specs=[vmem] * 3,
        out_specs=[vmem] * 5,
        scratch_shapes=band_scratch
        + [
            pltpu.VMEM((3, 9 * c1, cols), f32),
            pltpu.SMEM((1, LANES), f32),
            pltpu.SemaphoreType.DMA,
        ],
        compiler_params=params,
        name="edge_rows",
    )(kernel_edge, arrived, ref_features)
    far = swapped(far, "view", 1)
    near = swapped(near, "view", 0)

    partial, own_top, choices = pl.pallas_call(
        functools.partial(mid_kernel, at_slots, at_live, sources, blocks, mid_blocks),
        out_shape=[
            shape((half_p, half_r * c2, half_x), f32),
            shape((planes, c1, cols), f32),
            shape((cols, 2 * col_step), bf16),
        ],
        in_specs=[anywhere] + [vmem] * 7,
        out_specs=[vmem] * 3,
        scratch_shapes=band_scratch
        + [
            pltpu.VMEM((planes * inner, cols), bf16),
            pltpu.VMEM((3, 3 * (inner + c1), cols), f32),
            pltpu.SMEM(scalars.shape, i32),
            pltpu.SemaphoreType.DMA,
        ],
        compiler_params=params,
        name="middle_rows",
    )(scalars, arrived, ref_features, edge_var, kernel_mid, bias_rows, two_mid, bias_two)

    out = pl.pallas_call(
        end_kernel,
        out_shape=shape((half_p, half_r * c2, half_x), f32),
        in_specs=[vmem] * 9,
        out_specs=vmem,
        compiler_params=params,
        name="end_rows",
    )(far, near, flags, own, own_top, partial, bias_rows, two_edge, choices)
    return out.reshape(half_p, half_r, c2, half_x)


def solution(mesh):
    return jax.shard_map(
        on_device,
        mesh=mesh,
        in_specs=(
            P(("groups", "view"), None, None),
            P(("groups", "view"), None, None, None),
            P(("groups", "view"), None, None),
            P(("groups", "view")),
            P("groups", None),
            P(),
            P(),
            P(),
            P(),
        ),
        out_specs=P("groups", "view", None, None),
        check_vma=False,
    )
```
